32 devices in a mesh: expert: 16 (over z, y, core), tensor: 2 (over x).
Axes of the slice: x: 2, y: 2, z: 4, core: 2. Of those that a mesh axis runs over, the one named last changes fastest.
Arguments:
- tokens: bfloat16 [25216, 512], P('expert'), may hold values from -6 to 6
- routes: int32 [25216, 2], P('expert'), may hold values from 0 to 15, all different within a row
- gain_attn: float32 [512], replicated, may hold values from 0.5 to 1.5
- w_qkv: bfloat16 [3, 512, 512], P(None, None, 'tensor'), may hold values from -0.25 to 0.25
- w_attn_out: bfloat16 [512, 512], P('tensor'), may hold values from -1.5 to 1.5
- gain_moe: float32 [512], replicated, may hold values from 0.5 to 1.5
- w_router: bfloat16 [512, 16], replicated, may hold values from -0.25 to 0.25
- w_expert_in: bfloat16 [16, 512, 2048], P('expert', None, 'tensor'), may hold values from -0.25 to 0.25
- w_expert_out: bfloat16 [16, 2048, 512], P('expert', 'tensor'), may hold values from -1.75 to 1.75
- cotangent: bfloat16 [25216, 512], P('expert'), may hold values from -6 to 6
Outputs:
- result: bfloat16 [25216, 512], P('expert')
- grad_tokens: float32 [25216, 512], P('expert')
- grad_gain_attn: float32 [512], replicated
- grad_w_qkv: float32 [3, 512, 512], P(None, None, 'tensor')
- grad_w_attn_out: float32 [512, 512], P('tensor')
- grad_gain_moe: float32 [512], replicated
- grad_w_router: float32 [512, 16], replicated
- grad_w_expert_in: float32 [16, 512, 2048], P('expert', None, 'tensor')
- grad_w_expert_out: float32 [16, 2048, 512], P('expert', 'tensor')
The draws below stay inside these ranges and needn't reach their ends.
Inputs may be any that keep to these rules, and one draw needn't show every extreme that they name: `routes`: each token names two different experts.
All inputs are finite; a program needn't handle non-finite values.
Results may differ from the reference program's by a relative error of at most 0.025.
Values may be sent and summed in bfloat16 or wider, within the bound.
No kernel may reach another device: no remote copies, remote signals or barrier semaphores. Data moves between devices by JAX's collectives and lax.ppermute only.
A program may use at most 192 MiB of HBM per device.

```python
import jax
import jax.numpy as jnp
from jax import lax

D = 512
HEADS = 8
HEAD_DIM = 64
FF = 2048
SEQ = 197
EXPERTS = 16
TOK_DEV = 1576
IMAGES = 128
TOKENS = 25216
CAP = 248
N_EXPERT = 16


def levels(key, extent, split, low, high):
    def one(axis_at, parts):
        draws = jax.random.uniform(jax.random.fold_in(jax.random.fold_in(key, 6), axis_at), (parts,), jnp.float32, low / len(split), high / len(split))
        return jnp.repeat(jnp.exp(draws), extent[axis_at] // parts).reshape((-1,) + (1,) * (len(extent) - axis_at - 1))

    factor_of = one(*split[0])
    for cut in split[1:]:
        factor_of = factor_of * one(*cut)
    return factor_of


def different_ones(rng, rows, amount, top, lift):
    sequence = jax.random.permutation(jax.random.fold_in(rng, 1), amount)
    boost = sequence
    for power in range(3):
        boost = boost * boost // amount
    boost = boost * lift // amount
    lots = jax.random.randint(jax.random.fold_in(rng, 2), (rows, amount), 0, 4096) + boost
    sure = jax.random.permutation(jax.random.fold_in(rng, 3), rows)[jnp.arange(amount) % rows]
    lots = jnp.where(jnp.arange(rows)[:, None] == sure[None, :], 1 << 14, lots)
    merit = lots * amount + jnp.arange(amount)
    return lax.top_k(merit.astype(jnp.int32), top)[1].astype(jnp.int32)


def bell_draw(key, dims, scale, limit, pieces=(), kind=jnp.bfloat16):
    values = scale * jax.random.normal(key, dims, jnp.float32)
    if pieces:
        values = values * levels(key, dims, pieces, -0.22, 0.18)
    return jnp.clip(values, -limit, limit).astype(kind)


def setup_inputs(seed: int = 0) -> dict:
    key_of = jax.random.split(jax.random.key(seed), 11)
    tokens = bell_draw(key_of[0], (TOKENS, D), 1.0, 6.0, ((0, 16),))
    routes = different_ones(key_of[1], TOKENS, EXPERTS, 2, 1024)
    gain_attn = jnp.clip(1.0 + 0.1 * jax.random.normal(key_of[2], (D,), jnp.float32), 0.5, 1.5)
    w_qkv = bell_draw(key_of[3], (3, D, D), D ** -0.5, 0.25, ((2, 2),))
    w_attn_out = bell_draw(key_of[4], (D, D), (D // 32) ** -0.5, 1.5, ((0, 2),))
    gain_moe = jnp.clip(1.0 + 0.1 * jax.random.normal(key_of[5], (D,), jnp.float32), 0.5, 1.5)
    w_router = bell_draw(key_of[6], (D, EXPERTS), D ** -0.5, 0.25)
    w_expert_in = bell_draw(key_of[7], (EXPERTS, D, FF), D ** -0.5, 0.25, ((0, 16), (2, 2)))
    w_expert_out = bell_draw(key_of[8], (EXPERTS, FF, D), ((3 * FF) // (2 * EXPERTS * EXPERTS) + 1) ** -0.5, 1.75, ((0, 16), (1, 2)))
    cotangent = bell_draw(key_of[9], (TOKENS, D), 1.0, 6.0, ((0, 16),))
    return dict(tokens=tokens, routes=routes, gain_attn=gain_attn, w_qkv=w_qkv, w_attn_out=w_attn_out, gain_moe=gain_moe, w_router=w_router, w_expert_in=w_expert_in, w_expert_out=w_expert_out, cotangent=cotangent)


norm_eps = 1e-06
highest = lax.Precision.HIGHEST

@jax.custom_vjp
def low(v):
    return lax.optimization_barrier(v.astype(jnp.bfloat16)).astype(jnp.float32)

@jax.custom_vjp
def low_back(v):
    return v

def low_keep(v):
    return (low(v), None)

def low_pass(kept, grad):
    return (grad,)

def back_keep(v):
    return (v, None)

def back_low(kept, grad):
    return (low(grad),)
low.defvjp(low_keep, low_pass)
low_back.defvjp(back_keep, back_low)

def norm_rows(values, gain_vector):
    center = values - lax.optimization_barrier(jnp.mean(values, axis=-1, keepdims=True))
    spread = lax.optimization_barrier(jnp.mean(center * center, axis=-1, keepdims=True))
    return center * lax.rsqrt(spread + norm_eps) * gain_vector

def slot_table(routes):
    picked = jnp.concatenate([routes[:, 0], routes[:, 1]]).astype(jnp.int32)
    columns = jnp.arange(EXPERTS, dtype=jnp.int32)
    matches = (picked[:, None] == columns[None, :]).astype(jnp.int32)
    earlier = (jnp.cumsum(matches, axis=0) - matches).astype(jnp.int32)
    position = lax.optimization_barrier(jnp.sum(earlier * matches, axis=1)).astype(jnp.int32)
    kept_flat = position < CAP
    slot_flat = jnp.where(kept_flat, picked * CAP + position, EXPERTS * CAP).astype(jnp.int32)
    return (slot_flat, kept_flat)

def spread_group(row_values, slot_group):
    buffer = jnp.zeros((EXPERTS * CAP, D), row_values.dtype)
    return buffer.at[slot_group].set(jnp.concatenate([row_values, row_values], axis=0), mode='drop')

def pick_group(flat_rows, slot_group, kept_group):
    safe_slots = jnp.minimum(slot_group, EXPERTS * CAP - 1).astype(jnp.int32)
    row_values = jnp.take(flat_rows, safe_slots, axis=0) * kept_group[:, None].astype(flat_rows.dtype)
    return row_values.reshape(2, TOK_DEV, D)

def forward(tokens, gain_attn, w_qkv, w_attn_out, gain_moe, w_router, w_expert_in, w_expert_out, slot_flat, kept_flat, routes):
    normed_in = low(norm_rows(tokens, gain_attn))
    projected = jnp.einsum('td,jde->jte', normed_in, w_qkv, precision=highest)
    projected = low_back(low(projected))
    head_blocks = projected.reshape(3, IMAGES, SEQ, HEADS, HEAD_DIM)
    scores = jnp.einsum('bqhe,bkhe->bhqk', head_blocks[0], head_blocks[1], precision=highest)
    scores = low_back(scores * HEAD_DIM ** (-0.5))
    attn_low = low(jax.nn.softmax(scores, axis=-1))
    attended = jnp.einsum('bhqk,bkhe->bqhe', attn_low, head_blocks[2], precision=highest).reshape(TOKENS, D)
    attended = low_back(low(attended))
    residual = tokens + low_back(jnp.dot(attended, w_attn_out, precision=highest))
    routed = low(norm_rows(residual, gain_moe))
    router_probs = jax.nn.softmax(jnp.dot(routed, w_router, precision=highest), axis=-1)
    matches = routes[:, :, None] == jnp.arange(EXPERTS, dtype=jnp.int32)[None, None, :]
    gate_values = lax.optimization_barrier(jnp.sum(jnp.where(matches, router_probs[:, None, :], 0.0), axis=2))
    grouped = routed.reshape(N_EXPERT, TOK_DEV, D)
    buffers = jax.vmap(spread_group)(grouped, slot_flat)
    expert_in = buffers.reshape(N_EXPERT, EXPERTS, CAP, D).transpose(1, 0, 2, 3).reshape(EXPERTS, N_EXPERT * CAP, D)
    pre_active = low_back(jnp.einsum('ecd,edf->ecf', expert_in, w_expert_in, precision=highest))
    active = low(jax.nn.gelu(pre_active, approximate=True))
    expert_out = low_back(jnp.einsum('ecf,efd->ecd', active, w_expert_out, precision=highest))
    returned = expert_out.reshape(EXPERTS, N_EXPERT, CAP, D).transpose(1, 0, 2, 3).reshape(N_EXPERT, EXPERTS * CAP, D)
    pair_out = jax.vmap(pick_group)(returned, slot_flat, kept_flat)
    group_gates = gate_values.reshape(N_EXPERT, TOK_DEV, 2)
    mixture = jnp.einsum('gctd,gtc->gtd', pair_out, group_gates, precision=highest).reshape(TOKENS, D)
    return residual + mixture

def reference(tokens, routes, gain_attn, w_qkv, w_attn_out, gain_moe, w_router, w_expert_in, w_expert_out, cotangent):
    slot_flat, kept_flat = jax.vmap(slot_table)(routes.reshape(N_EXPERT, TOK_DEV, 2))

    def forward_full(*weights):
        return forward(*weights, slot_flat, kept_flat, routes)
    result, pull_back = jax.vjp(forward_full, tokens.astype(jnp.float32), gain_attn, w_qkv.astype(jnp.float32), w_attn_out.astype(jnp.float32), gain_moe, w_router.astype(jnp.float32), w_expert_in.astype(jnp.float32), w_expert_out.astype(jnp.float32))
    gradients = pull_back(cotangent.astype(jnp.float32))
    return (result.astype(jnp.bfloat16), gradients[0], gradients[1], gradients[2], gradients[3], gradients[4], gradients[5], gradients[6], gradients[7])
```

```python
import functools

import jax
import jax.numpy as jnp
from jax import lax
from jax.experimental import pallas as pl
from jax.experimental.pallas import tpu as pltpu
from jax.sharding import PartitionSpec as P

HEAD_DIM = 64
SEQ = 197
PAD = 208
EPS = 1e-06
F32 = jnp.float32
BF16 = jnp.bfloat16
VMEM = pl.BlockSpec(memory_space=pltpu.VMEM)


def nn(a, b):
    return lax.dot_general(a, b, (((1,), (0,)), ((), ())), preferred_element_type=F32)


def nt(a, b):
    return lax.dot_general(a, b, (((1,), (1,)), ((), ())), preferred_element_type=F32)


def tn(a, b):
    return lax.dot_general(a, b, (((0,), (0,)), ((), ())), preferred_element_type=F32)


def params(mib=56):
    return pltpu.CompilerParams(vmem_limit_bytes=mib << 20)


def cost(flops, moved):
    return pl.CostEstimate(flops=int(flops), bytes_accessed=int(moved), transcendentals=0)


def full(shape):
    return pl.BlockSpec(shape, lambda *_: (0,) * len(shape))


def prep_kernel(rank_ref, tok_ref, cot_ref, col_ref, row_ref, tok_out, cot_out, col_out, row_out, wide, *, experts, cap, half, block):
    images = tok_out.shape[0]
    rows = tok_ref.shape[0]
    for source, target in ((cot_ref, cot_out), (tok_ref, tok_out)):
        wide[0:rows, :] = source[...].astype(F32)
        for i in range(images):
            window = wide[i * SEQ : i * SEQ + PAD, :]
            inside = lax.broadcasted_iota(jnp.int32, window.shape, 0) < SEQ
            target[i] = jnp.where(inside, window, 0.0).astype(BF16)
    first_slot = rank_ref[0] * half

    def code(expert, position):
        place = position.astype(jnp.int32) - first_slot
        good = (expert >= 0) & (position < cap) & (place >= 0) & (place < half)
        return jnp.where(good, expert * block + place, -1)

    step = PAD
    lower = (
        lax.broadcasted_iota(jnp.int32, (step, step), 0)
        > lax.broadcasted_iota(jnp.int32, (step, step), 1)
    ).astype(BF16)
    base = jnp.zeros((1, experts), F32)
    for choice in range(2):
        for b in range(images):
            picked = col_ref[b * step : (b + 1) * step, choice : choice + 1]
            chosen = picked == lax.broadcasted_iota(jnp.int32, (step, experts), 1)
            ones = chosen.astype(F32)
            before = nn(lower, ones.astype(BF16)) + base
            position = jnp.sum(before * ones, axis=1, keepdims=True)
            col_out[b * step : (b + 1) * step, choice : choice + 1] = code(picked, position)
            base = base + jnp.sum(ones, axis=0, keepdims=True)
    step = 128
    upper = (
        lax.broadcasted_iota(jnp.int32, (step, step), 0)
        < lax.broadcasted_iota(jnp.int32, (step, step), 1)
    ).astype(BF16)
    base = jnp.zeros((experts, 1), F32)
    for choice in range(2):
        for b in range(row_ref.shape[1] // step):
            picked = row_ref[choice : choice + 1, b * step : (b + 1) * step]
            chosen = picked == lax.broadcasted_iota(jnp.int32, (experts, step), 0)
            ones = chosen.astype(F32)
            before = nn(ones.astype(BF16), upper) + base
            position = jnp.sum(before * ones, axis=0, keepdims=True)
            row_out[choice : choice + 1, b * step : (b + 1) * step] = code(picked, position)
            base = base + jnp.sum(ones, axis=1, keepdims=True)


def prep(rank, tokens, cotangent, routes, experts, cap, half, block):
    rows, width = tokens.shape
    images = rows // SEQ
    padded = jnp.pad(
        routes.reshape(images, SEQ, 2), ((0, 0), (0, PAD - SEQ), (0, 0)), constant_values=-1
    ).reshape(images * PAD, 2)
    wide_rows = -(-((images - 1) * SEQ + PAD) // 16) * 16
    return pl.pallas_call(
        functools.partial(prep_kernel, experts=experts, cap=cap, half=half, block=block),
        out_shape=(
            jax.ShapeDtypeStruct((images, PAD, width), BF16),
            jax.ShapeDtypeStruct((images, PAD, width), BF16),
            jax.ShapeDtypeStruct((images * PAD, 2), jnp.int32),
            jax.ShapeDtypeStruct((2, images * PAD), jnp.int32),
        ),
        in_specs=[pl.BlockSpec(memory_space=pltpu.SMEM)] + [VMEM] * 4,
        out_specs=(VMEM,) * 4,
        scratch_shapes=[pltpu.VMEM((wide_rows, width), F32)],
        compiler_params=params(40),
        cost_estimate=cost(1e8, 1e7),
        name="prep",
    )(rank, tokens, cotangent, padded, padded.T)


def spread_kernel(code_ref, rows_ref, out_ref):
    step = out_ref.shape[0]
    slot = lax.broadcasted_iota(jnp.int32, (step, rows_ref.shape[0]), 0) + pl.program_id(0) * step
    match = (slot == code_ref[0:1, :]) | (slot == code_ref[1:2, :])
    out_ref[...] = nn(match.astype(BF16), rows_ref[...]).astype(BF16)


def spread(code_row, rows, slots, step=256):
    count, width = rows.shape
    return pl.pallas_call(
        spread_kernel,
        out_shape=jax.ShapeDtypeStruct((slots, width), BF16),
        grid=(slots // step,),
        in_specs=[full((2, count)), full((count, width))],
        out_specs=pl.BlockSpec((step, width), lambda i: (i, 0)),
        compiler_params=params(40),
        cost_estimate=cost(2 * slots * count * width, 2 * width * (slots + count)),
        name="spread",
    )(code_row, rows)


def row_mean(v):
    return jnp.mean(v, axis=-1, keepdims=True)


def attend_kernel(first_ref, tok_ref, ga_ref, gm_ref, *rest, shards, own):
    wq, wo = rest[:shards], rest[shards : 2 * shards]
    routed_ref, qkv_ref, prob_ref, att_ref, res_ref = rest[2 * shards :]
    keep = pl.program_id(0) < own
    tok = tok_ref[0].astype(F32)
    center = tok - row_mean(tok)
    normed = (center * lax.rsqrt(row_mean(center * center) + EPS) * ga_ref[...]).astype(BF16)
    key_ok = lax.broadcasted_iota(jnp.int32, (PAD, PAD), 1) < SEQ
    left = lax.broadcasted_iota(jnp.int32, (PAD, 2 * HEAD_DIM), 1) < HEAD_DIM
    residual = tok
    width = wq[0].shape[2]
    for s in range(shards):
        queries, keys, values = (nn(normed, wq[s][j]) for j in range(3))
        queries = queries.astype(BF16) * BF16(HEAD_DIM**-0.5)
        keys = keys.astype(BF16)
        values = values.astype(BF16)
        mixed = []
        for pair in range(width // (2 * HEAD_DIM)):
            cols = slice(pair * 2 * HEAD_DIM, (pair + 1) * 2 * HEAD_DIM)
            qp, kp, vp = queries[:, cols], keys[:, cols], values[:, cols]
            outs = []
            for side in range(2):
                qm = jnp.where(left if side == 0 else ~left, qp, BF16(0))
                scores = jnp.where(key_ok, nt(qm, kp), -jnp.inf)
                ex = jnp.exp(scores - jnp.max(scores, axis=1, keepdims=True))
                probs = (ex * (1.0 / jnp.sum(ex, axis=1, keepdims=True))).astype(BF16)
                head = s * (width // HEAD_DIM) + pair * 2 + side

                @pl.when(keep)
                def _():
                    prob_ref[0, head] = probs

                outs.append(nn(probs, vp))
            mixed.append(jnp.where(left, outs[0], outs[1]).astype(BF16))
        attended = jnp.concatenate(mixed, axis=1)
        residual = residual + nn(attended, wo[s][...])

        @pl.when(keep)
        def _():
            for j, part in enumerate((queries, keys, values)):
                qkv_ref[0, s, j] = part
            att_ref[0, s] = attended

    @pl.when(keep)
    def _():
        res_ref[0] = residual

    center = residual - row_mean(residual)
    normed = center * lax.rsqrt(row_mean(center * center) + EPS) * gm_ref[...]
    routed_ref[0] = normed.astype(BF16)


def attend(first, tok_pad, gain_attn, gain_moe, wq, wo, own):
    images, _, width = tok_pad.shape
    shards = len(wq)
    part = wq[0].shape[2]
    heads = shards * part // HEAD_DIM

    def image(i, first_ref):
        return (lax.rem(i + first_ref[0], images), 0, 0)

    def kept(ndim):
        return lambda i, first_ref: (jnp.minimum(i, own - 1),) + (0,) * (ndim - 1)

    return pl.pallas_call(
        functools.partial(attend_kernel, shards=shards, own=own),
        out_shape=(
            jax.ShapeDtypeStruct((images, PAD, width), BF16),
            jax.ShapeDtypeStruct((own, shards, 3, PAD, part), BF16),
            jax.ShapeDtypeStruct((own, heads, PAD, PAD), BF16),
            jax.ShapeDtypeStruct((own, shards, PAD, part), BF16),
            jax.ShapeDtypeStruct((own, PAD, width), F32),
        ),
        grid_spec=pltpu.PrefetchScalarGridSpec(
            num_scalar_prefetch=1,
            grid=(images,),
            in_specs=[
                pl.BlockSpec((1, PAD, width), image),
                full((1, width)),
                full((1, width)),
            ]
            + [full((3, width, part))] * shards
            + [full((part, width))] * shards,
            out_specs=(
                pl.BlockSpec((1, PAD, width), image),
                pl.BlockSpec((1, shards, 3, PAD, part), kept(5)),
                pl.BlockSpec((1, heads, PAD, PAD), kept(4)),
                pl.BlockSpec((1, shards, PAD, part), kept(4)),
                pl.BlockSpec((1, PAD, width), kept(3)),
            ),
        ),
        compiler_params=params(),
        cost_estimate=cost(images * PAD * width * width * 10, 2e7),
        name="attend",
    )(first, tok_pad, gain_attn.reshape(1, -1), gain_moe.reshape(1, -1), *wq, *wo)


def expert_kernel(expert_ref, x_ref, cot_ref, wr_ref, *rest, shards, half, block, chunk):
    w1, w2 = rest[:shards], rest[shards : 2 * shards]
    gin_ref, out_ref = rest[2 * shards : 2 * shards + 2]
    dw1, dw2 = rest[2 * shards + 2 : 3 * shards + 2], rest[3 * shards + 2 :]
    expert = expert_ref[0]

    @pl.when(pl.program_id(0) == 0)
    def _():
        for ref in dw1 + dw2:
            ref[...] = jnp.zeros_like(ref)

    x = x_ref[...]
    rows, width = x.shape
    cot = cot_ref[...].astype(F32)
    logits = nn(x, wr_ref[...])
    ex = jnp.exp(logits - jnp.max(logits, axis=1, keepdims=True))
    mine = lax.broadcasted_iota(jnp.int32, ex.shape, 1) == expert
    gate = jnp.sum(jnp.where(mine, ex, 0.0), axis=1, keepdims=True) / jnp.sum(
        ex, axis=1, keepdims=True
    )
    grad_out = (gate * cot).astype(BF16)
    out = jnp.zeros((rows, width), F32)
    gin = jnp.zeros((rows, width), F32)
    c0 = (2.0 / jnp.pi) ** 0.5
    for s in range(shards):
        hidden = w1[s].shape[1]
        size = min(chunk, hidden)
        for c in range(hidden // size):
            cols = slice(c * size, (c + 1) * size)
            u = nn(x, w1[s][:, cols])
            square = u * u
            t = jnp.tanh(u * (c0 + (c0 * 0.044715) * square))
            h = 0.5 + 0.5 * t
            slope = h + (0.5 * u) * (1.0 - t * t) * (c0 + (3 * c0 * 0.044715) * square)
            active = (u * h).astype(BF16)
            out = out + nn(active, w2[s][cols, :])
            grad_pre = (nt(grad_out, w2[s][cols, :]) * slope).astype(BF16)
            gin = gin + nt(grad_pre, w1[s][:, cols])
            dw2[s][cols, :] += tn(active, grad_out)
            dw1[s][:, cols] += tn(x, grad_pre)
    out_ref[...] = (gate * out).astype(BF16)
    gate_grad = jnp.sum(cot * out, axis=1, keepdims=True)
    shift = lax.rem(expert * block, width)
    down = lax.broadcasted_iota(jnp.int32, (block, width), 0)
    across = lax.broadcasted_iota(jnp.int32, (block, width), 1)
    diagonal = down + shift == across
    for g in range(rows // block):
        span = slice(g * block, (g + 1) * block)
        line = jnp.sum(jnp.where(diagonal, gate_grad[span], 0.0), axis=0, keepdims=True)
        high = line.astype(BF16).astype(F32)
        value = jnp.where(down == half, high, jnp.where(down == half + 1, line - high, gin[span]))
        gin_ref[span, :] = value.astype(BF16)


def experts_step(expert, x, cot, w_router, w1, w2, half, block, step=512, chunk=512):
    rows, width = x.shape
    shards = len(w1)
    hidden = w1[0].shape[1]
    step = min(step, rows)
    row_spec = pl.BlockSpec((step, width), lambda i, _: (i, 0))
    return pl.pallas_call(
        functools.partial(expert_kernel, shards=shards, half=half, block=block, chunk=chunk),
        out_shape=(jax.ShapeDtypeStruct((rows, width), BF16),) * 2
        + (jax.ShapeDtypeStruct((width, hidden), F32),) * shards
        + (jax.ShapeDtypeStruct((hidden, width), F32),) * shards,
        grid_spec=pltpu.PrefetchScalarGridSpec(
            num_scalar_prefetch=1,
            grid=(rows // step,),
            in_specs=[row_spec, row_spec, full(w_router.shape)]
            + [full((width, hidden))] * shards
            + [full((hidden, width))] * shards,
            out_specs=(row_spec, row_spec)
            + (full((width, hidden)),) * shards
            + (full((hidden, width)),) * shards,
        ),
        compiler_params=params(60),
        cost_estimate=cost(12 * rows * width * hidden * shards, 2e7),
        name="experts",
    )(expert, x, cot, w_router, *w1, *w2)


def collect_kernel(first_ref, code_ref, slots_ref, out_ref, *rest, experts, half, block):
    slots = slots_ref.shape[0]
    lane = lax.broadcasted_iota(jnp.int32, (PAD, slots), 1)
    match = ((lane == code_ref[:, 0:1]) | (lane == code_ref[:, 1:2])).astype(BF16)
    out_ref[0] = nn(match, slots_ref[...]).astype(out_ref.dtype)
    if rest:
        prob_ref, lines = rest
        width = slots_ref.shape[1]

        @pl.when(pl.program_id(0) == 0)
        def _():
            row = lax.broadcasted_iota(jnp.int32, (experts, slots), 0) * block + half
            place = lax.broadcasted_iota(jnp.int32, (experts, slots), 1)
            for k in range(2):
                picked = nn((place == row + k).astype(BF16), slots_ref[...])
                lines[k] = picked.astype(BF16)

        chunk_of = lax.broadcasted_iota(jnp.int32, (experts, width), 0) * block // width
        total = jnp.zeros((experts, PAD), F32)
        for c in range(slots // width):
            cols = slice(c * width, (c + 1) * width)
            for k in range(2):
                total = total + nt(jnp.where(chunk_of == c, lines[k], BF16(0)), match[:, cols])
        prob_ref[0] = total


def collect(first, code_col, slots, own, dtype, experts=None, half=0, block=0):
    count, width = slots.shape
    outs = [jax.ShapeDtypeStruct((own, PAD, width), dtype)]
    specs = [pl.BlockSpec((1, PAD, width), lambda i, f: (i, 0, 0))]
    scratch = []
    if experts:
        outs.append(jax.ShapeDtypeStruct((own, experts, PAD), F32))
        specs.append(pl.BlockSpec((1, experts, PAD), lambda i, f: (i, 0, 0)))
        scratch.append(pltpu.VMEM((2, experts, width), BF16))
    return pl.pallas_call(
        functools.partial(collect_kernel, experts=experts, half=half, block=block),
        out_shape=tuple(outs),
        grid_spec=pltpu.PrefetchScalarGridSpec(
            num_scalar_prefetch=1,
            grid=(own,),
            in_specs=[
                pl.BlockSpec((PAD, 2), lambda i, f: (i + f[0], 0)),
                full((count, width)),
            ],
            out_specs=tuple(specs),
            scratch_shapes=scratch,
        ),
        compiler_params=params(40),
        cost_estimate=cost(2 * own * PAD * count * width, 2 * count * width),
        name="collect",
    )(first, code_col, slots)


def back_kernel(first_ref, *rest, shards, steps, received):
    (sum_ref, gp_ref), rest = rest[:2], rest[2:]
    more, rest = rest[: 2 * received], rest[2 * received :]
    (res_ref, cot_ref, tok_ref, qkv_ref, prob_ref, att_ref, ga_ref, gm_ref, wrt_ref), rest = rest[:9], rest[9:]
    wq, wo, rest = rest[:shards], rest[shards : 2 * shards], rest[2 * shards :]
    gtok_ref, pack_ref, rest = rest[0], rest[1], rest[2:]
    dwq, dwo, small = rest[:shards], rest[shards : 2 * shards], rest[2 * shards]
    experts = wrt_ref.shape[0]
    step = pl.program_id(0)

    @pl.when(step == 0)
    def _():
        for ref in rest:
            ref[...] = jnp.zeros_like(ref)

    residual = res_ref[0]
    center = residual - row_mean(residual)
    scale = lax.rsqrt(row_mean(center * center) + EPS)
    xhat = center * scale
    gm = gm_ref[...]
    routed = (xhat * gm).astype(BF16)
    logits = nt(wrt_ref[...], routed)
    ex = jnp.exp(logits - jnp.max(logits, axis=0, keepdims=True))
    probs = ex / jnp.sum(ex, axis=0, keepdims=True)
    grad_probs = gp_ref[0]
    grad_routed = sum_ref[0]
    if received:
        grad_routed = grad_routed + more[0][0].astype(F32)
        grad_probs = grad_probs + more[1][0]
    grad_logits = probs * (grad_probs - jnp.sum(probs * grad_probs, axis=0, keepdims=True))
    high = grad_logits.astype(BF16)
    low = (grad_logits - high.astype(F32)).astype(BF16)
    small[0:experts, :] += nn(high, routed) + nn(low, routed)
    grad_routed = grad_routed + tn(high, wrt_ref[...]) + tn(low, wrt_ref[...])
    small[experts + 1 : experts + 2, :] += jnp.sum(grad_routed * xhat, axis=0, keepdims=True)
    g = grad_routed * gm
    grad_res = cot_ref[0].astype(F32) + scale * (g - row_mean(g) - xhat * row_mean(g * xhat))
    grad_mixed = grad_res.astype(BF16)

    tok = tok_ref[0].astype(F32)
    center = tok - row_mean(tok)
    tok_scale = lax.rsqrt(row_mean(center * center) + EPS)
    xin = center * tok_scale
    ga = ga_ref[...]
    normed = (xin * ga).astype(BF16)
    left = lax.broadcasted_iota(jnp.int32, (PAD, 2 * HEAD_DIM), 1) < HEAD_DIM
    grad_normed = jnp.zeros(tok.shape, F32)
    width = wq[0].shape[2]
    for s in range(shards):
        dwo[s][...] += tn(att_ref[0, s], grad_mixed)
        grad_att = nt(grad_mixed, wo[s][...]).astype(BF16)
        parts = ([], [], [])
        for pair in range(width // (2 * HEAD_DIM)):
            cols = slice(pair * 2 * HEAD_DIM, (pair + 1) * 2 * HEAD_DIM)
            qp, kp, vp = (qkv_ref[0, s, j, :, cols] for j in range(3))
            gp = grad_att[:, cols]
            totals = None
            for side in range(2):
                mask = left if side == 0 else ~left
                qm, km, gm_ = (jnp.where(mask, v, BF16(0)) for v in (qp, kp, gp))
                low_probs = prob_ref[0, s * (width // HEAD_DIM) + pair * 2 + side]
                p = low_probs.astype(F32)
                gw = nt(gm_, vp)
                ds = (p * (gw - jnp.sum(p * gw, axis=1, keepdims=True))).astype(BF16)
                new = (nn(ds, km), tn(ds, qm), tn(low_probs, gm_))
                totals = new if totals is None else tuple(a + b for a, b in zip(totals, new))
            scaled = (totals[0] * HEAD_DIM**-0.5, totals[1], totals[2])
            for j in range(3):
                parts[j].append(scaled[j].astype(BF16))
        for j in range(3):
            grad_part = jnp.concatenate(parts[j], axis=1)
            dwq[s][j] += tn(normed, grad_part)
            grad_normed = grad_normed + nt(grad_part, wq[s][j])
    small[experts : experts + 1, :] += jnp.sum(grad_normed * xin, axis=0, keepdims=True)
    h = grad_normed * ga
    gtok_ref[0] = (
        grad_res + tok_scale * (h - row_mean(h) - xin * row_mean(h * xin))
    ).astype(BF16)

    @pl.when(step == steps - 1)
    def _():
        at = 0
        for ref, count in ((dwq, 3), (dwo, 1), (small, 0)):
            for j in range(max(count, 1)):
                for s in range(shards):
                    value = ref[s][j] if count == 3 else ref[s][...] if count == 1 else ref[...]
                    for c in range(value.shape[1] // 256):
                        rows = value.shape[0]
                        start = at + c * rows
                        pack_ref[s, start : start + rows, :] = value[:, c * 256 : (c + 1) * 256].astype(BF16)
                at += rows * (value.shape[1] // 256)
        if at < pack_ref.shape[1]:
            for s in range(shards):
                pack_ref[s, at:, :] = jnp.zeros((pack_ref.shape[1] - at, 256), BF16)


def small_rows(experts):
    return -(-(experts + 2) // 16) * 16


def pack_rows(width, part, experts, align):
    rows = 3 * width * (part // 256) + part * (width // 256) + small_rows(experts) * (width // 256)
    return -(-rows // align) * align


def back(first, sums, residual, cot_pad, tok_pad, qkv, probs, att, gain_attn, gain_moe, w_router, wq, wo, align):
    own, _, width = residual.shape
    shards = len(wq)
    part = wq[0].shape[2]
    experts = w_router.shape[1]
    heads = probs.shape[1]
    rows = pack_rows(width, part, experts, align)

    def mine(shape):
        return pl.BlockSpec((1,) + shape, lambda i, f: (i,) + (0,) * len(shape))

    image = pl.BlockSpec((1, PAD, width), lambda i, f: (i + f[0], 0, 0))
    flat = [v for pair in sums for v in pair]
    return pl.pallas_call(
        functools.partial(back_kernel, shards=shards, steps=own, received=len(sums) - 1),
        out_shape=(
            jax.ShapeDtypeStruct((own, PAD, width), BF16),
            jax.ShapeDtypeStruct((shards, rows, 256), BF16),
        ),
        grid_spec=pltpu.PrefetchScalarGridSpec(
            num_scalar_prefetch=1,
            grid=(own,),
            in_specs=[mine((PAD, width)), mine((experts, PAD))] * len(sums)
            + [
                mine((PAD, width)),
                image,
                image,
                mine((shards, 3, PAD, part)),
                mine((heads, PAD, PAD)),
                mine((shards, PAD, part)),
                full((1, width)),
                full((1, width)),
                full((experts, width)),
            ]
            + [full((3, width, part))] * shards
            + [full((part, width))] * shards,
            out_specs=(mine((PAD, width)), full((shards, rows, 256))),
            scratch_shapes=[pltpu.VMEM((3, width, part), F32)] * shards
            + [pltpu.VMEM((part, width), F32)] * shards
            + [pltpu.VMEM((small_rows(experts), width), F32)],
        ),
        compiler_params=params(),
        cost_estimate=cost(own * PAD * width * width * 24, 2e7),
        name="back",
    )(
        first,
        *flat,
        residual,
        cot_pad,
        tok_pad,
        qkv,
        probs,
        att,
        gain_attn.reshape(1, -1),
        gain_moe.reshape(1, -1),
        w_router.T,
        *wq,
        *wo,
    )


def unpad_kernel(first_ref, own_ref, peer_ref, out_ref, *, images):
    own = own_ref.shape[0]
    for i in range(images):
        inner = i % own
        mine = first_ref[0] == i - inner
        value = jnp.where(mine, own_ref[inner].astype(F32), peer_ref[inner].astype(F32))
        out_ref[i * SEQ : (i + 1) * SEQ, :] = value[:SEQ]


def unpad(first, own, peer):
    images, width = 2 * own.shape[0], own.shape[2]
    return pl.pallas_call(
        functools.partial(unpad_kernel, images=images),
        out_shape=jax.ShapeDtypeStruct((images * SEQ, width), F32),
        in_specs=[pl.BlockSpec(memory_space=pltpu.SMEM), VMEM, VMEM],
        out_specs=VMEM,
        compiler_params=params(40),
        cost_estimate=cost(1e6, 6e6),
        name="unpad",
    )(first, own, peer)


def body(tokens, routes, gain_attn, w_qkv, w_attn_out, gain_moe, w_router, w_expert_in, w_expert_out, cotangent, *, ways, groups):
    tok_rows, width = tokens.shape
    experts = w_router.shape[1]
    cap = max(4, (5 * tok_rows // (2 * experts) + 7) // 8 * 8)
    half = -(-cap // ways)
    block = -(-(half + 2) // 32) * 32
    slots = experts * block
    images = tok_rows // SEQ
    own = images // ways
    rank = lax.axis_index("tensor")
    expert = lax.axis_index("expert")
    first = (rank * own).astype(jnp.int32).reshape(1)
    swap = [(0, 1), (1, 0)]

    def other(v):
        return lax.ppermute(v, "tensor", swap)

    def shards_of(v, axis):
        if ways == 2:
            return [v, other(v)]
        return [lax.all_gather(v, "tensor", axis=axis, tiled=True)]

    def exchange(rows):
        shape = rows.shape
        rows = rows.reshape(experts, block, width)
        rows = lax.all_to_all(rows, "expert", split_axis=0, concat_axis=0, tiled=True)
        return rows.reshape(shape)

    tok_pad, cot_pad, code_col, code_row = prep(
        rank.astype(jnp.int32).reshape(1), tokens, cotangent, routes, experts, cap, half, block
    )
    wq = shards_of(w_qkv, 2)
    wo = shards_of(w_attn_out, 0)
    cot_slots = exchange(spread(code_row, cot_pad.reshape(images * PAD, width), slots))
    w1 = shards_of(w_expert_in[0], 1)
    w2 = shards_of(w_expert_out[0], 0)
    routed, qkv, probs, att, residual = attend(first, tok_pad, gain_attn, gain_moe, wq, wo, own)
    x_slots = exchange(spread(code_row, routed.reshape(images * PAD, width), slots))
    gin, gated, *dw = experts_step(
        expert.astype(jnp.int32).reshape(1), x_slots, cot_slots, w_router, w1, w2, half, block
    )
    dw1, dw2 = dw[: len(w1)], dw[len(w1) :]
    gin = exchange(gin)
    gated = exchange(gated)
    if ways == 2:
        there = ((1 - rank) * own).astype(jnp.int32).reshape(1)
        sent = collect(there, code_col, gin, own, BF16, experts, half, block)
        received = tuple(other(v) for v in sent)
        sums = [collect(first, code_col, gin, own, F32, experts, half, block), received]
        grad_w1 = dw1[0] + other(dw1[1].astype(BF16)).astype(F32)
        grad_w2 = dw2[0] + other(dw2[1].astype(BF16)).astype(F32)
        (mix_there,) = collect(there, code_col, gated, own, BF16)
        (mix_here,) = collect(first, code_col, gated, own, F32)
        mixture = mix_here + other(mix_there).astype(F32)
    else:
        every = [collect(jnp.full((1,), r * own, jnp.int32), code_col, gin, own, F32, experts, half, block) for r in range(ways)]
        sums = [
            tuple(
                lax.psum_scatter(jnp.stack([v[k] for v in every]).astype(t), "tensor", scatter_dimension=0).astype(F32)
                for k, t in ((0, BF16), (1, F32))
            )
        ]
        grad_w1 = lax.psum_scatter(dw1[0].astype(BF16), "tensor", scatter_dimension=1, tiled=True).astype(F32)
        grad_w2 = lax.psum_scatter(dw2[0].astype(BF16), "tensor", scatter_dimension=0, tiled=True).astype(F32)
        every = [collect(jnp.full((1,), r * own, jnp.int32), code_col, gated, own, BF16)[0] for r in range(ways)]
        mixture = lax.psum_scatter(jnp.stack(every), "tensor", scatter_dimension=0).astype(F32)
    result = (residual + mixture).astype(BF16)
    grad_tok, pack = back(
        first, sums, residual, cot_pad, tok_pad, qkv, probs, att, gain_attn, gain_moe, w_router, wq, wo, groups * 8
    )
    if ways == 2:
        result = unpad(first, result, other(result)).astype(BF16)
        grad_tokens = unpad(first, grad_tok, other(grad_tok))
    else:

        def whole(v):
            v = lax.all_gather(v, "tensor", axis=0, tiled=True)
            return v[:, :SEQ].reshape(tok_rows, width)

        result = whole(result)
        grad_tokens = whole(grad_tok).astype(F32)

    bits = [1 << b for b in range(groups.bit_length() - 1)]
    if ways == 2:

        def swap_bit(v, bit):
            return lax.ppermute(v, "expert", [(i, i ^ bit) for i in range(groups)])

        def add(a, b):
            return (a.astype(F32) + b.astype(F32)).astype(BF16)

        def halves(v, bit):
            size = v.shape[-2] // 2
            upper = (expert // bit) % 2
            keep = lax.dynamic_slice_in_dim(v, upper * size, size, v.ndim - 2)
            give = lax.dynamic_slice_in_dim(v, (1 - upper) * size, size, v.ndim - 2)
            return keep, give

        keep, give = halves(pack, bits[0])
        pack = add(keep, swap_bit(give, bits[0]))
        total = add(pack[0], other(pack[1]))
        for bit in bits[1:]:
            keep, give = halves(total, bit)
            total = add(keep, swap_bit(give, bit))
        for bit in bits[::-1]:
            got = swap_bit(total, bit)
            upper = (expert // bit) % 2 == 1
            total = jnp.where(upper, jnp.concatenate([got, total]), jnp.concatenate([total, got]))
        total = total.astype(F32)
        part = w_qkv.shape[2]
    else:
        total = lax.psum(pack[0], ("expert", "tensor")).astype(F32)
        part = width

    def take(at, rows, cols):
        blocks = [total[at + b * rows : at + (b + 1) * rows] for b in range(cols // 256)]
        return jnp.concatenate(blocks, axis=1) if len(blocks) > 1 else blocks[0]

    step = width * (part // 256)
    grad_w_qkv = jnp.stack([take(j * step, width, part) for j in range(3)])
    grad_w_attn_out = take(3 * step, part, width)
    small = take(3 * step + part * (width // 256), small_rows(experts), width)
    if ways != 2:
        grad_w_qkv = lax.dynamic_slice_in_dim(grad_w_qkv, rank * w_qkv.shape[2], w_qkv.shape[2], 2)
        grad_w_attn_out = lax.dynamic_slice_in_dim(grad_w_attn_out, rank * w_qkv.shape[2], w_qkv.shape[2], 0)
    return (
        result,
        grad_tokens,
        small[experts],
        grad_w_qkv,
        grad_w_attn_out,
        small[experts + 1],
        small[:experts].T,
        grad_w1[None],
        grad_w2[None],
    )


def solution(mesh):
    placed = (
        P("expert", None),
        P("expert", None),
        P(),
        P(None, None, "tensor"),
        P("tensor", None),
        P(),
        P(),
        P("expert", None, "tensor"),
        P("expert", "tensor", None),
        P("expert", None),
    )
    return jax.shard_map(
        functools.partial(body, ways=mesh.shape["tensor"], groups=mesh.shape["expert"]),
        mesh=mesh,
        in_specs=placed,
        out_specs=(
            P("expert", None),
            P("expert", None),
            P(),
            P(None, None, "tensor"),
            P("tensor", None),
            P(),
            P(),
            P("expert", None, "tensor"),
            P("expert", "tensor", None),
        ),
        check_vma=False,
    )
```

```python
import functools

import jax
import jax.numpy as jnp
from jax import lax
from jax.experimental import pallas as pl
from jax.experimental.pallas import tpu as pltpu
from jax.sharding import PartitionSpec as P

HEAD_DIM = 64
SEQ = 197
PAD = 208
EPS = 1e-06
F32 = jnp.float32
BF16 = jnp.bfloat16
VMEM = pl.BlockSpec(memory_space=pltpu.VMEM)


def nn(a, b):
    return lax.dot_general(a, b, (((1,), (0,)), ((), ())), preferred_element_type=F32)


def nt(a, b):
    return lax.dot_general(a, b, (((1,), (1,)), ((), ())), preferred_element_type=F32)


def tn(a, b):
    return lax.dot_general(a, b, (((0,), (0,)), ((), ())), preferred_element_type=F32)


def params(mib=56):
    return pltpu.CompilerParams(vmem_limit_bytes=mib << 20)


def cost(flops, moved):
    return pl.CostEstimate(flops=int(flops), bytes_accessed=int(moved), transcendentals=0)


def full(shape):
    return pl.BlockSpec(shape, lambda *_: (0,) * len(shape))


def prep_kernel(rank_ref, tok_ref, cot_ref, col_ref, row_ref, tok_out, cot_out, col_out, row_out, wide, *, experts, cap, half, block):
    images = tok_out.shape[0]
    rows = tok_ref.shape[0]
    for source, target in ((cot_ref, cot_out), (tok_ref, tok_out)):
        wide[0:rows, :] = source[...].astype(F32)
        for i in range(images):
            window = wide[i * SEQ : i * SEQ + PAD, :]
            inside = lax.broadcasted_iota(jnp.int32, window.shape, 0) < SEQ
            target[i] = jnp.where(inside, window, 0.0).astype(BF16)
    first_slot = rank_ref[0] * half

    def code(expert, position):
        place = position.astype(jnp.int32) - first_slot
        good = (expert >= 0) & (position < cap) & (place >= 0) & (place < half)
        return jnp.where(good, expert * block + place, -1)

    step = PAD
    lower = (
        lax.broadcasted_iota(jnp.int32, (step, step), 0)
        > lax.broadcasted_iota(jnp.int32, (step, step), 1)
    ).astype(BF16)
    base = jnp.zeros((1, experts), F32)
    for choice in range(2):
        for b in range(images):
            picked = col_ref[b * step : (b + 1) * step, choice : choice + 1]
            chosen = picked == lax.broadcasted_iota(jnp.int32, (step, experts), 1)
            ones = chosen.astype(F32)
            before = nn(lower, ones.astype(BF16)) + base
            position = jnp.sum(before * ones, axis=1, keepdims=True)
            col_out[b * step : (b + 1) * step, choice : choice + 1] = code(picked, position)
            base = base + jnp.sum(ones, axis=0, keepdims=True)
    step = 128
    upper = (
        lax.broadcasted_iota(jnp.int32, (step, step), 0)
        < lax.broadcasted_iota(jnp.int32, (step, step), 1)
    ).astype(BF16)
    base = jnp.zeros((experts, 1), F32)
    for choice in range(2):
        for b in range(row_ref.shape[1] // step):
            picked = row_ref[choice : choice + 1, b * step : (b + 1) * step]
            chosen = picked == lax.broadcasted_iota(jnp.int32, (experts, step), 0)
            ones = chosen.astype(F32)
            before = nn(ones.astype(BF16), upper) + base
            position = jnp.sum(before * ones, axis=0, keepdims=True)
            row_out[choice : choice + 1, b * step : (b + 1) * step] = code(picked, position)
            base = base + jnp.sum(ones, axis=1, keepdims=True)


def prep(rank, tokens, cotangent, routes, experts, cap, half, block):
    rows, width = tokens.shape
    images = rows // SEQ
    padded = jnp.pad(
        routes.reshape(images, SEQ, 2), ((0, 0), (0, PAD - SEQ), (0, 0)), constant_values=-1
    ).reshape(images * PAD, 2)
    wide_rows = -(-((images - 1) * SEQ + PAD) // 16) * 16
    return pl.pallas_call(
        functools.partial(prep_kernel, experts=experts, cap=cap, half=half, block=block),
        out_shape=(
            jax.ShapeDtypeStruct((images, PAD, width), BF16),
            jax.ShapeDtypeStruct((images, PAD, width), BF16),
            jax.ShapeDtypeStruct((images * PAD, 2), jnp.int32),
            jax.ShapeDtypeStruct((2, images * PAD), jnp.int32),
        ),
        in_specs=[pl.BlockSpec(memory_space=pltpu.SMEM)] + [VMEM] * 4,
        out_specs=(VMEM,) * 4,
        scratch_shapes=[pltpu.VMEM((wide_rows, width), F32)],
        compiler_params=params(40),
        cost_estimate=cost(1e8, 1e7),
        name="prep",
    )(rank, tokens, cotangent, padded, padded.T)


def spread_kernel(code_ref, rows_ref, out_ref):
    step = out_ref.shape[0]
    slot = lax.broadcasted_iota(jnp.int32, (step, rows_ref.shape[0]), 0) + pl.program_id(0) * step
    match = (slot == code_ref[0:1, :]) | (slot == code_ref[1:2, :])
    out_ref[...] = nn(match.astype(BF16), rows_ref[...]).astype(BF16)


def spread(code_row, rows, slots, step=256):
    count, width = rows.shape
    return pl.pallas_call(
        spread_kernel,
        out_shape=jax.ShapeDtypeStruct((slots, width), BF16),
        grid=(slots // step,),
        in_specs=[full((2, count)), full((count, width))],
        out_specs=pl.BlockSpec((step, width), lambda i: (i, 0)),
        compiler_params=params(40),
        cost_estimate=cost(2 * slots * count * width, 2 * width * (slots + count)),
        name="spread",
    )(code_row, rows)


def row_mean(v):
    return jnp.mean(v, axis=-1, keepdims=True)


def attend_kernel(first_ref, tok_ref, ga_ref, gm_ref, *rest, shards, own):
    wq, wo = rest[:shards], rest[shards : 2 * shards]
    routed_ref, qkv_ref, prob_ref, att_ref, res_ref = rest[2 * shards :]
    keep = pl.program_id(0) < own
    tok = tok_ref[0].astype(F32)
    center = tok - row_mean(tok)
    normed = (center * lax.rsqrt(row_mean(center * center) + EPS) * ga_ref[...]).astype(BF16)
    key_ok = lax.broadcasted_iota(jnp.int32, (PAD, PAD), 1) < SEQ
    left = lax.broadcasted_iota(jnp.int32, (PAD, 2 * HEAD_DIM), 1) < HEAD_DIM
    residual = tok
    width = wq[0].shape[2]
    for s in range(shards):
        queries, keys, values = (nn(normed, wq[s][j]) for j in range(3))
        queries = queries.astype(BF16) * BF16(HEAD_DIM**-0.5)
        keys = keys.astype(BF16)
        values = values.astype(BF16)
        mixed = []
        for pair in range(width // (2 * HEAD_DIM)):
            cols = slice(pair * 2 * HEAD_DIM, (pair + 1) * 2 * HEAD_DIM)
            qp, kp, vp = queries[:, cols], keys[:, cols], values[:, cols]
            outs = []
            for side in range(2):
                qm = jnp.where(left if side == 0 else ~left, qp, BF16(0))
                scores = jnp.where(key_ok, nt(qm, kp), -jnp.inf)
                ex = jnp.exp(scores - jnp.max(scores, axis=1, keepdims=True))
                probs = (ex * (1.0 / jnp.sum(ex, axis=1, keepdims=True))).astype(BF16)
                head = s * (width // HEAD_DIM) + pair * 2 + side

                @pl.when(keep)
                def _():
                    prob_ref[0, head] = probs

                outs.append(nn(probs, vp))
            mixed.append(jnp.where(left, outs[0], outs[1]).astype(BF16))
        attended = jnp.concatenate(mixed, axis=1)
        residual = residual + nn(attended, wo[s][...])

        @pl.when(keep)
        def _():
            for j, part in enumerate((queries, keys, values)):
                qkv_ref[0, s, j] = part
            att_ref[0, s] = attended

    @pl.when(keep)
    def _():
        res_ref[0] = residual

    center = residual - row_mean(residual)
    normed = center * lax.rsqrt(row_mean(center * center) + EPS) * gm_ref[...]
    routed_ref[0] = normed.astype(BF16)


def attend(first, tok_pad, gain_attn, gain_moe, wq, wo, own):
    images, _, width = tok_pad.shape
    shards = len(wq)
    part = wq[0].shape[2]
    heads = shards * part // HEAD_DIM

    def image(i, first_ref):
        return (lax.rem(i + first_ref[0], images), 0, 0)

    def kept(ndim):
        return lambda i, first_ref: (jnp.minimum(i, own - 1),) + (0,) * (ndim - 1)

    return pl.pallas_call(
        functools.partial(attend_kernel, shards=shards, own=own),
        out_shape=(
            jax.ShapeDtypeStruct((images, PAD, width), BF16),
            jax.ShapeDtypeStruct((own, shards, 3, PAD, part), BF16),
            jax.ShapeDtypeStruct((own, heads, PAD, PAD), BF16),
            jax.ShapeDtypeStruct((own, shards, PAD, part), BF16),
            jax.ShapeDtypeStruct((own, PAD, width), F32),
        ),
        grid_spec=pltpu.PrefetchScalarGridSpec(
            num_scalar_prefetch=1,
            grid=(images,),
            in_specs=[
                pl.BlockSpec((1, PAD, width), image),
                full((1, width)),
                full((1, width)),
            ]
            + [full((3, width, part))] * shards
            + [full((part, width))] * shards,
            out_specs=(
                pl.BlockSpec((1, PAD, width), image),
                pl.BlockSpec((1, shards, 3, PAD, part), kept(5)),
                pl.BlockSpec((1, heads, PAD, PAD), kept(4)),
                pl.BlockSpec((1, shards, PAD, part), kept(4)),
                pl.BlockSpec((1, PAD, width), kept(3)),
            ),
        ),
        compiler_params=params(),
        cost_estimate=cost(images * PAD * width * width * 10, 2e7),
        name="attend",
    )(first, tok_pad, gain_attn.reshape(1, -1), gain_moe.reshape(1, -1), *wq, *wo)


def expert_kernel(expert_ref, x_ref, cot_ref, wr_ref, *rest, shards, half, block, chunk, steps):
    w1, w2 = rest[:shards], rest[shards : 2 * shards]
    gin_ref, out_ref = rest[2 * shards : 2 * shards + 2]
    given = rest[2 * shards + 2 : 4 * shards + 2]
    sums = given[:1] + rest[4 * shards + 2 : 5 * shards + 1] + given[shards : shards + 1] + rest[5 * shards + 1 :]
    dw1, dw2 = sums[:shards], sums[shards:]
    expert = expert_ref[0]

    @pl.when(pl.program_id(0) == 0)
    def _():
        for ref in sums:
            ref[...] = jnp.zeros_like(ref)

    x = x_ref[...]
    rows, width = x.shape
    cot = cot_ref[...].astype(F32)
    logits = nn(x, wr_ref[...])
    ex = jnp.exp(logits - jnp.max(logits, axis=1, keepdims=True))
    mine = lax.broadcasted_iota(jnp.int32, ex.shape, 1) == expert
    gate = jnp.sum(jnp.where(mine, ex, 0.0), axis=1, keepdims=True) / jnp.sum(
        ex, axis=1, keepdims=True
    )
    grad_out = (gate * cot).astype(BF16)
    out = jnp.zeros((rows, width), F32)
    gin = jnp.zeros((rows, width), F32)
    c0 = (2.0 / jnp.pi) ** 0.5
    for s in range(shards):
        hidden = w1[s].shape[1]
        size = min(chunk, hidden)
        for c in range(hidden // size):
            cols = slice(c * size, (c + 1) * size)
            u = nn(x, w1[s][:, cols])
            square = u * u
            t = jnp.tanh(u * (c0 + (c0 * 0.044715) * square))
            h = 0.5 + 0.5 * t
            slope = h + (0.5 * u) * (1.0 - t * t) * (c0 + (3 * c0 * 0.044715) * square)
            active = (u * h).astype(BF16)
            out = out + nn(active, w2[s][cols, :])
            grad_pre = (nt(grad_out, w2[s][cols, :]) * slope).astype(BF16)
            gin = gin + nt(grad_pre, w1[s][:, cols])
            dw2[s][cols, :] += tn(active, grad_out)
            dw1[s][:, cols] += tn(x, grad_pre)
    out_ref[...] = (gate * out).astype(BF16)
    gate_grad = jnp.sum(cot * out, axis=1, keepdims=True)
    shift = lax.rem(expert * block, width)
    down = lax.broadcasted_iota(jnp.int32, (block, width), 0)
    across = lax.broadcasted_iota(jnp.int32, (block, width), 1)
    diagonal = down + shift == across
    for g in range(rows // block):
        span = slice(g * block, (g + 1) * block)
        line = jnp.sum(jnp.where(diagonal, gate_grad[span], 0.0), axis=0, keepdims=True)
        high = line.astype(BF16).astype(F32)
        value = jnp.where(down == half, high, jnp.where(down == half + 1, line - high, gin[span]))
        gin_ref[span, :] = value.astype(BF16)

    @pl.when(pl.program_id(0) == steps - 1)
    def _():
        for s in range(1, shards):
            given[s][...] = dw1[s][...].astype(BF16)
            given[shards + s][...] = dw2[s][...].astype(BF16)


def experts_step(expert, x, cot, w_router, w1, w2, half, block, step=512, chunk=512):
    rows, width = x.shape
    shards = len(w1)
    hidden = w1[0].shape[1]
    step = min(step, rows)
    row_spec = pl.BlockSpec((step, width), lambda i, _: (i, 0))
    return pl.pallas_call(
        functools.partial(
            expert_kernel, shards=shards, half=half, block=block, chunk=chunk, steps=rows // step
        ),
        out_shape=(jax.ShapeDtypeStruct((rows, width), BF16),) * 2
        + tuple(jax.ShapeDtypeStruct((width, hidden), BF16 if s else F32) for s in range(shards))
        + tuple(jax.ShapeDtypeStruct((hidden, width), BF16 if s else F32) for s in range(shards)),
        grid_spec=pltpu.PrefetchScalarGridSpec(
            num_scalar_prefetch=1,
            grid=(rows // step,),
            in_specs=[row_spec, row_spec, full(w_router.shape)]
            + [full((width, hidden))] * shards
            + [full((hidden, width))] * shards,
            out_specs=(row_spec, row_spec)
            + (full((width, hidden)),) * shards
            + (full((hidden, width)),) * shards,
            scratch_shapes=[pltpu.VMEM((width, hidden), F32)] * (shards - 1)
            + [pltpu.VMEM((hidden, width), F32)] * (shards - 1),
        ),
        compiler_params=params(60),
        cost_estimate=cost(12 * rows * width * hidden * shards, 2e7),
        name="experts",
    )(expert, x, cot, w_router, *w1, *w2)


def collect_kernel(first_ref, code_ref, slots_ref, out_ref, *rest, experts, half, block):
    slots = slots_ref.shape[0]
    lane = lax.broadcasted_iota(jnp.int32, (PAD, slots), 1)
    match = ((lane == code_ref[:, 0:1]) | (lane == code_ref[:, 1:2])).astype(BF16)
    out_ref[0] = nn(match, slots_ref[...]).astype(out_ref.dtype)
    if rest:
        prob_ref, lines = rest
        width = slots_ref.shape[1]

        @pl.when(pl.program_id(0) == 0)
        def _():
            row = lax.broadcasted_iota(jnp.int32, (experts, slots), 0) * block + half
            place = lax.broadcasted_iota(jnp.int32, (experts, slots), 1)
            for k in range(2):
                picked = nn((place == row + k).astype(BF16), slots_ref[...])
                lines[k] = picked.astype(BF16)

        chunk_of = lax.broadcasted_iota(jnp.int32, (experts, width), 0) * block // width
        total = jnp.zeros((experts, PAD), F32)
        for c in range(slots // width):
            cols = slice(c * width, (c + 1) * width)
            for k in range(2):
                total = total + nt(jnp.where(chunk_of == c, lines[k], BF16(0)), match[:, cols])
        prob_ref[0] = total


def collect(first, code_col, slots, own, dtype, experts=None, half=0, block=0):
    count, width = slots.shape
    outs = [jax.ShapeDtypeStruct((own, PAD, width), dtype)]
    specs = [pl.BlockSpec((1, PAD, width), lambda i, f: (i, 0, 0))]
    scratch = []
    if experts:
        outs.append(jax.ShapeDtypeStruct((own, experts, PAD), F32))
        specs.append(pl.BlockSpec((1, experts, PAD), lambda i, f: (i, 0, 0)))
        scratch.append(pltpu.VMEM((2, experts, width), BF16))
    return pl.pallas_call(
        functools.partial(collect_kernel, experts=experts, half=half, block=block),
        out_shape=tuple(outs),
        grid_spec=pltpu.PrefetchScalarGridSpec(
            num_scalar_prefetch=1,
            grid=(own,),
            in_specs=[
                pl.BlockSpec((PAD, 2), lambda i, f: (i + f[0], 0)),
                full((count, width)),
            ],
            out_specs=tuple(specs),
            scratch_shapes=scratch,
        ),
        compiler_params=params(40),
        cost_estimate=cost(2 * own * PAD * count * width, 2 * count * width),
        name="collect",
    )(first, code_col, slots)


def back_kernel(first_ref, *rest, shards, steps, received):
    (sum_ref, gp_ref), rest = rest[:2], rest[2:]
    more, rest = rest[: 2 * received], rest[2 * received :]
    (res_ref, cot_ref, tok_ref, qkv_ref, prob_ref, att_ref, ga_ref, gm_ref, wrt_ref), rest = rest[:9], rest[9:]
    wq, wo, rest = rest[:shards], rest[shards : 2 * shards], rest[2 * shards :]
    gtok_ref, pack_ref, rest = rest[0], rest[1], rest[2:]
    dwq, dwo, small = rest[:shards], rest[shards : 2 * shards], rest[2 * shards]
    experts = wrt_ref.shape[0]
    step = pl.program_id(0)

    @pl.when(step == 0)
    def _():
        for ref in rest:
            ref[...] = jnp.zeros_like(ref)

    residual = res_ref[0]
    center = residual - row_mean(residual)
    scale = lax.rsqrt(row_mean(center * center) + EPS)
    xhat = center * scale
    gm = gm_ref[...]
    routed = (xhat * gm).astype(BF16)
    logits = nt(wrt_ref[...], routed)
    ex = jnp.exp(logits - jnp.max(logits, axis=0, keepdims=True))
    probs = ex / jnp.sum(ex, axis=0, keepdims=True)
    grad_probs = gp_ref[0]
    grad_routed = sum_ref[0]
    if received:
        grad_routed = grad_routed + more[0][0].astype(F32)
        grad_probs = grad_probs + more[1][0]
    grad_logits = probs * (grad_probs - jnp.sum(probs * grad_probs, axis=0, keepdims=True))
    high = grad_logits.astype(BF16)
    low = (grad_logits - high.astype(F32)).astype(BF16)
    small[0:experts, :] += nn(high, routed) + nn(low, routed)
    grad_routed = grad_routed + tn(high, wrt_ref[...]) + tn(low, wrt_ref[...])
    small[experts + 1 : experts + 2, :] += jnp.sum(grad_routed * xhat, axis=0, keepdims=True)
    g = grad_routed * gm
    grad_res = cot_ref[0].astype(F32) + scale * (g - row_mean(g) - xhat * row_mean(g * xhat))
    grad_mixed = grad_res.astype(BF16)

    tok = tok_ref[0].astype(F32)
    center = tok - row_mean(tok)
    tok_scale = lax.rsqrt(row_mean(center * center) + EPS)
    xin = center * tok_scale
    ga = ga_ref[...]
    normed = (xin * ga).astype(BF16)
    left = lax.broadcasted_iota(jnp.int32, (PAD, 2 * HEAD_DIM), 1) < HEAD_DIM
    grad_normed = jnp.zeros(tok.shape, F32)
    width = wq[0].shape[2]
    for s in range(shards):
        dwo[s][...] += tn(att_ref[0, s], grad_mixed)
        grad_att = nt(grad_mixed, wo[s][...]).astype(BF16)
        parts = ([], [], [])
        for pair in range(width // (2 * HEAD_DIM)):
            cols = slice(pair * 2 * HEAD_DIM, (pair + 1) * 2 * HEAD_DIM)
            qp, kp, vp = (qkv_ref[0, s, j, :, cols] for j in range(3))
            gp = grad_att[:, cols]
            totals = None
            for side in range(2):
                mask = left if side == 0 else ~left
                qm, km, gm_ = (jnp.where(mask, v, BF16(0)) for v in (qp, kp, gp))
                low_probs = prob_ref[0, s * (width // HEAD_DIM) + pair * 2 + side]
                p = low_probs.astype(F32)
                gw = nt(gm_, vp)
                ds = (p * (gw - jnp.sum(p * gw, axis=1, keepdims=True))).astype(BF16)
                new = (nn(ds, km), tn(ds, qm), tn(low_probs, gm_))
                totals = new if totals is None else tuple(a + b for a, b in zip(totals, new))
            scaled = (totals[0] * HEAD_DIM**-0.5, totals[1], totals[2])
            for j in range(3):
                parts[j].append(scaled[j].astype(BF16))
        for j in range(3):
            grad_part = jnp.concatenate(parts[j], axis=1)
            dwq[s][j] += tn(normed, grad_part)
            grad_normed = grad_normed + nt(grad_part, wq[s][j])
    small[experts : experts + 1, :] += jnp.sum(grad_normed * xin, axis=0, keepdims=True)
    h = grad_normed * ga
    gtok_ref[0] = (
        grad_res + tok_scale * (h - row_mean(h) - xin * row_mean(h * xin))
    ).astype(BF16)

    @pl.when(step == steps - 1)
    def _():
        at = 0
        for ref, count in ((dwq, 3), (dwo, 1), (small, 0)):
            for j in range(max(count, 1)):
                for s in range(shards):
                    value = ref[s][j] if count == 3 else ref[s][...] if count == 1 else ref[...]
                    for c in range(value.shape[1] // 256):
                        rows = value.shape[0]
                        start = at + c * rows
                        pack_ref[s, start : start + rows, :] = value[:, c * 256 : (c + 1) * 256].astype(BF16)
                at += rows * (value.shape[1] // 256)
        if at < pack_ref.shape[1]:
            for s in range(shards):
                pack_ref[s, at:, :] = jnp.zeros((pack_ref.shape[1] - at, 256), BF16)


def small_rows(experts):
    return -(-(experts + 2) // 16) * 16


def pack_rows(width, part, experts, align):
    rows = 3 * width * (part // 256) + part * (width // 256) + small_rows(experts) * (width // 256)
    return -(-rows // align) * align


def back(first, sums, residual, cot_pad, tok_pad, qkv, probs, att, gain_attn, gain_moe, w_router, wq, wo, align):
    own, _, width = residual.shape
    shards = len(wq)
    part = wq[0].shape[2]
    experts = w_router.shape[1]
    heads = probs.shape[1]
    rows = pack_rows(width, part, experts, align)

    def mine(shape):
        return pl.BlockSpec((1,) + shape, lambda i, f: (i,) + (0,) * len(shape))

    image = pl.BlockSpec((1, PAD, width), lambda i, f: (i + f[0], 0, 0))
    flat = [v for pair in sums for v in pair]
    return pl.pallas_call(
        functools.partial(back_kernel, shards=shards, steps=own, received=len(sums) - 1),
        out_shape=(
            jax.ShapeDtypeStruct((own, PAD, width), BF16),
            jax.ShapeDtypeStruct((shards, rows, 256), BF16),
        ),
        grid_spec=pltpu.PrefetchScalarGridSpec(
            num_scalar_prefetch=1,
            grid=(own,),
            in_specs=[mine((PAD, width)), mine((experts, PAD))] * len(sums)
            + [
                mine((PAD, width)),
                image,
                image,
                mine((shards, 3, PAD, part)),
                mine((heads, PAD, PAD)),
                mine((shards, PAD, part)),
                full((1, width)),
                full((1, width)),
                full((experts, width)),
            ]
            + [full((3, width, part))] * shards
            + [full((part, width))] * shards,
            out_specs=(mine((PAD, width)), full((shards, rows, 256))),
            scratch_shapes=[pltpu.VMEM((3, width, part), F32)] * shards
            + [pltpu.VMEM((part, width), F32)] * shards
            + [pltpu.VMEM((small_rows(experts), width), F32)],
        ),
        compiler_params=params(),
        cost_estimate=cost(own * PAD * width * width * 24, 2e7),
        name="back",
    )(
        first,
        *flat,
        residual,
        cot_pad,
        tok_pad,
        qkv,
        probs,
        att,
        gain_attn.reshape(1, -1),
        gain_moe.reshape(1, -1),
        w_router.T,
        *wq,
        *wo,
    )


def unpad_kernel(first_ref, own_ref, peer_ref, out_ref, *, images):
    own = own_ref.shape[0]
    for i in range(images):
        inner = i % own
        mine = first_ref[0] == i - inner
        value = jnp.where(mine, own_ref[inner].astype(F32), peer_ref[inner].astype(F32))
        out_ref[i * SEQ : (i + 1) * SEQ, :] = value[:SEQ]


def unpad(first, own, peer):
    images, width = 2 * own.shape[0], own.shape[2]
    return pl.pallas_call(
        functools.partial(unpad_kernel, images=images),
        out_shape=jax.ShapeDtypeStruct((images * SEQ, width), F32),
        in_specs=[pl.BlockSpec(memory_space=pltpu.SMEM), VMEM, VMEM],
        out_specs=VMEM,
        compiler_params=params(40),
        cost_estimate=cost(1e6, 6e6),
        name="unpad",
    )(first, own, peer)


def body(tokens, routes, gain_attn, w_qkv, w_attn_out, gain_moe, w_router, w_expert_in, w_expert_out, cotangent, *, ways, groups):
    tok_rows, width = tokens.shape
    experts = w_router.shape[1]
    cap = max(4, (5 * tok_rows // (2 * experts) + 7) // 8 * 8)
    half = -(-cap // ways)
    block = -(-(half + 2) // 32) * 32
    slots = experts * block
    images = tok_rows // SEQ
    own = images // ways
    rank = lax.axis_index("tensor")
    expert = lax.axis_index("expert")
    first = (rank * own).astype(jnp.int32).reshape(1)
    swap = [(0, 1), (1, 0)]

    def other(v):
        return lax.ppermute(v, "tensor", swap)

    def shards_of(v, axis):
        if ways == 2:
            return [v, other(v)]
        return [lax.all_gather(v, "tensor", axis=axis, tiled=True)]

    def exchange(rows):
        shape = rows.shape
        rows = rows.reshape(experts, block, width)
        rows = lax.all_to_all(rows, "expert", split_axis=0, concat_axis=0, tiled=True)
        return rows.reshape(shape)

    def after(v, *others):
        return lax.optimization_barrier((v,) + others)[0]

    tok_pad, cot_pad, code_col, code_row = prep(
        rank.astype(jnp.int32).reshape(1), tokens, cotangent, routes, experts, cap, half, block
    )
    wq = shards_of(w_qkv, 2)
    wo = shards_of(w_attn_out, 0)
    cot_slots = after(spread(code_row, cot_pad.reshape(images * PAD, width), slots), wq[-1], wo[-1])
    cot_slots = exchange(cot_slots)
    w1 = shards_of(after(w_expert_in[0], wq[-1]), 1)
    w2 = shards_of(after(w_expert_out[0], wq[-1]), 0)
    routed, qkv, probs, att, residual = attend(first, tok_pad, gain_attn, gain_moe, wq, wo, own)
    x_slots = after(spread(code_row, routed.reshape(images * PAD, width), slots), w1[-1], w2[-1])
    x_slots = exchange(x_slots)
    gin, gated, *dw = experts_step(
        expert.astype(jnp.int32).reshape(1), x_slots, cot_slots, w_router, w1, w2, half, block
    )
    dw1, dw2 = dw[: len(w1)], dw[len(w1) :]
    gin = exchange(gin)
    if ways == 2:
        dw1_peer, dw2_peer = other(dw1[1]), other(dw2[1])
        gin, gated, dw1_peer, dw2_peer = lax.optimization_barrier((gin, gated, dw1_peer, dw2_peer))
    gated = exchange(after(gated, gin))
    if ways == 2:
        there = ((1 - rank) * own).astype(jnp.int32).reshape(1)
        grad_w1 = dw1[0] + dw1_peer.astype(F32)
        grad_w2 = dw2[0] + dw2_peer.astype(F32)
        sent = collect(there, code_col, gin, own, BF16, experts, half, block)
        received = tuple(other(v) for v in sent)
        sums = [collect(first, code_col, gin, own, F32, experts, half, block), received]
    else:
        every = [collect(jnp.full((1,), r * own, jnp.int32), code_col, gin, own, F32, experts, half, block) for r in range(ways)]
        sums = [
            tuple(
                lax.psum_scatter(jnp.stack([v[k] for v in every]).astype(t), "tensor", scatter_dimension=0).astype(F32)
                for k, t in ((0, BF16), (1, F32))
            )
        ]
        grad_w1 = lax.psum_scatter(dw1[0].astype(BF16), "tensor", scatter_dimension=1, tiled=True).astype(F32)
        grad_w2 = lax.psum_scatter(dw2[0].astype(BF16), "tensor", scatter_dimension=0, tiled=True).astype(F32)
    grad_tok, pack = back(
        first, sums, residual, cot_pad, tok_pad, qkv, probs, att, gain_attn, gain_moe, w_router, wq, wo, groups * 8
    )

    bits = [1 << b for b in range(groups.bit_length() - 1)]
    if ways == 2:

        def swap_bit(v, bit):
            return lax.ppermute(v, "expert", [(i, i ^ bit) for i in range(groups)])

        def add(a, b):
            return (a.astype(F32) + b.astype(F32)).astype(BF16)

        def halves(v, bit):
            size = v.shape[-2] // 2
            upper = (expert // bit) % 2
            keep = lax.dynamic_slice_in_dim(v, upper * size, size, v.ndim - 2)
            give = lax.dynamic_slice_in_dim(v, (1 - upper) * size, size, v.ndim - 2)
            return keep, give

        pack, grad_tok, gated = lax.optimization_barrier((pack, grad_tok, gated))
        keep, give = halves(pack, bits[0])
        pack = add(keep, swap_bit(give, bits[0]))
        swapped = other(pack[1])
        (mix_there,) = collect(there, code_col, gated, own, BF16)
        (mix_here,) = collect(first, code_col, gated, own, F32)
        swapped, mix_there, mix_here = lax.optimization_barrier((swapped, mix_there, mix_here))
        total = add(pack[0], swapped)
        mix_peer = other(mix_there)
        keep, give = halves(total, bits[1])
        total = add(keep, swap_bit(give, bits[1]))
        keep, give = halves(total, bits[2])
        total = add(keep, swap_bit(give, bits[2]))
        total, mix_peer = lax.optimization_barrier((total, mix_peer))
        mixture = mix_here + mix_peer.astype(F32)
        result = (residual + mixture).astype(BF16)
        grad_tok, result = lax.optimization_barrier((grad_tok, result))
        grad_peer = other(grad_tok)
        for bit in bits[3:]:
            keep, give = halves(total, bit)
            total = add(keep, swap_bit(give, bit))

        def gathered(v, bit):
            got = swap_bit(v, bit)
            upper = (expert // bit) % 2 == 1
            return jnp.where(upper, jnp.concatenate([got, v]), jnp.concatenate([v, got]))

        for bit in bits[:1:-1]:
            total = gathered(total, bit)
        total, grad_peer = lax.optimization_barrier((total, grad_peer))
        result_peer = other(result)
        grad_tokens = unpad(first, grad_tok, grad_peer)
        for bit in bits[1::-1]:
            total = gathered(total, bit)
        result = unpad(first, result, result_peer).astype(BF16)
        total = total.astype(F32)
        part = w_qkv.shape[2]
    else:
        every = [collect(jnp.full((1,), r * own, jnp.int32), code_col, gated, own, BF16)[0] for r in range(ways)]
        mixture = lax.psum_scatter(jnp.stack(every), "tensor", scatter_dimension=0).astype(F32)

        def whole(v):
            v = lax.all_gather(v, "tensor", axis=0, tiled=True)
            return v[:, :SEQ].reshape(tok_rows, width)

        result = whole((residual + mixture).astype(BF16))
        grad_tokens = whole(grad_tok).astype(F32)
        total = lax.psum(pack[0], ("expert", "tensor")).astype(F32)
        part = width

    def take(at, rows, cols):
        blocks = [total[at + b * rows : at + (b + 1) * rows] for b in range(cols // 256)]
        return jnp.concatenate(blocks, axis=1) if len(blocks) > 1 else blocks[0]

    step = width * (part // 256)
    grad_w_qkv = jnp.stack([take(j * step, width, part) for j in range(3)])
    grad_w_attn_out = take(3 * step, part, width)
    small = take(3 * step + part * (width // 256), small_rows(experts), width)
    if ways != 2:
        grad_w_qkv = lax.dynamic_slice_in_dim(grad_w_qkv, rank * w_qkv.shape[2], w_qkv.shape[2], 2)
        grad_w_attn_out = lax.dynamic_slice_in_dim(grad_w_attn_out, rank * w_qkv.shape[2], w_qkv.shape[2], 0)
    return (
        result,
        grad_tokens,
        small[experts],
        grad_w_qkv,
        grad_w_attn_out,
        small[experts + 1],
        small[:experts].T,
        grad_w1[None],
        grad_w2[None],
    )


def solution(mesh):
    placed = (
        P("expert", None),
        P("expert", None),
        P(),
        P(None, None, "tensor"),
        P("tensor", None),
        P(),
        P(),
        P("expert", None, "tensor"),
        P("expert", "tensor", None),
        P("expert", None),
    )
    return jax.shard_map(
        functools.partial(body, ways=mesh.shape["tensor"], groups=mesh.shape["expert"]),
        mesh=mesh,
        in_specs=placed,
        out_specs=(
            P("expert", None),
            P("expert", None),
            P(),
            P(None, None, "tensor"),
            P("tensor", None),
            P(),
            P(),
            P("expert", None, "tensor"),
            P("expert", "tensor", None),
        ),
        check_vma=False,
    )
```

```python
import functools

import jax
import jax.numpy as jnp
from jax import lax
from jax.experimental import pallas as pl
from jax.experimental.pallas import tpu as pltpu
from jax.sharding import PartitionSpec as P

HEAD_DIM = 64
SEQ = 197
PAD = 208
EPS = 1e-06
F32 = jnp.float32
BF16 = jnp.bfloat16
VMEM = pl.BlockSpec(memory_space=pltpu.VMEM)


def nn(a, b):
    return lax.dot_general(a, b, (((1,), (0,)), ((), ())), preferred_element_type=F32)


def nt(a, b):
    return lax.dot_general(a, b, (((1,), (1,)), ((), ())), preferred_element_type=F32)


def tn(a, b):
    return lax.dot_general(a, b, (((0,), (0,)), ((), ())), preferred_element_type=F32)


def params(mib=56):
    return pltpu.CompilerParams(vmem_limit_bytes=mib << 20)


def cost(us):
    return pl.CostEstimate(flops=0, bytes_accessed=int(us * 3.69e6), transcendentals=0)


def full(shape):
    return pl.BlockSpec(shape, lambda *_: (0,) * len(shape))


def pad_images(source, wide, target):
    wide[0 : source.shape[0], :] = source[...].astype(F32)
    for i in range(target.shape[0]):
        window = wide[i * SEQ : i * SEQ + PAD, :]
        inside = lax.broadcasted_iota(jnp.int32, window.shape, 0) < SEQ
        target[i] = jnp.where(inside, window, 0.0).astype(BF16)


def pad_kernel(source, target, wide):
    pad_images(source, wide, target)


def wide_scratch(images, width):
    return pltpu.VMEM((-(-((images - 1) * SEQ + PAD) // 16) * 16, width), F32)


def pad(rows):
    images, width = rows.shape[0] // SEQ, rows.shape[1]
    return pl.pallas_call(
        pad_kernel,
        out_shape=jax.ShapeDtypeStruct((images, PAD, width), BF16),
        in_specs=[VMEM],
        out_specs=VMEM,
        scratch_shapes=[wide_scratch(images, width)],
        compiler_params=params(),
        cost_estimate=cost(2),
        name="pad",
    )(rows)


def iota(shape, axis):
    return lax.broadcasted_iota(jnp.int32, shape, axis)


def slot_match(code_ref, start, step):
    slot = iota((step, code_ref.shape[1]), 0) + start
    return ((slot == code_ref[0:1, :]) | (slot == code_ref[1:2, :])).astype(BF16)


def front_kernel(rank_ref, cot_ref, col_ref, row_ref, cot_out, slots_out, col_out, row_out, wide, *, cap, half):
    experts, chunks, block, _ = slots_out.shape
    first_slot = rank_ref[0] * (half * chunks)

    def code(expert, position):
        place = position.astype(jnp.int32) - first_slot
        good = (expert >= 0) & (position < cap) & (place >= 0) & (place < half * chunks)
        slot = expert * block + place
        for c in range(1, chunks):
            slot = jnp.where(place >= c * half, slot + (experts * block - half), slot)
        return jnp.where(good, slot, -1)

    lanes = col_ref.shape[1]
    span = lanes * experts
    routes = col_ref[...]
    spread_lanes = (iota((lanes, span), 1) // experts == iota((lanes, span), 0)).astype(BF16)
    gather_lanes = (iota((span, lanes), 0) // experts == iota((span, lanes), 1)).astype(BF16)
    chosen = nn(routes.astype(F32).astype(BF16), spread_lanes) == (iota((PAD, span), 1) % experts).astype(F32)
    ones = chosen.astype(F32)
    lower = (iota((PAD, PAD), 0) > iota((PAD, PAD), 1)).astype(BF16)
    before = nn(lower, ones.astype(BF16))
    totals = jnp.broadcast_to(jnp.sum(ones, axis=0, keepdims=True), (16, span)).astype(BF16)
    source, target = iota((span, span), 0), iota((span, span), 1)
    order_s = (source // experts % 2) * lanes + source // (2 * experts)
    order_t = (target // experts % 2) * lanes + target // (2 * experts)
    earlier = (source % experts == target % experts) & (order_s < order_t)
    before = before + nn(totals, earlier.astype(BF16))[0:1]
    place = nn((jnp.minimum(before, float(cap)) * ones).astype(BF16), gather_lanes)
    col_out[...] = code(routes, place)

    step = 128
    blocks = row_ref.shape[1] // step
    upper = (iota((step, step), 0) < iota((step, step), 1)).astype(BF16)
    order = [(choice, b) for choice in range(2) for b in range(blocks)]
    picked = [row_ref[choice : choice + 1, b * step : (b + 1) * step] for choice, b in order]
    ones = [(p == iota((experts, step), 0)).astype(F32) for p in picked]
    before = nn(jnp.concatenate(ones, axis=0).astype(BF16), upper)
    base = jnp.zeros((experts, 1), F32)
    for k, (choice, b) in enumerate(order):
        position = jnp.sum((before[k * experts : (k + 1) * experts] + base) * ones[k], axis=0, keepdims=True)
        row_out[choice : choice + 1, b * step : (b + 1) * step] = code(picked[k], position)
        base = base + jnp.sum(ones[k], axis=1, keepdims=True)

    pad_images(cot_ref, wide, cot_out)
    rows = cot_out[...].reshape(-1, cot_out.shape[2])
    step = min(512, experts * block)
    per = step // block
    for c in range(chunks):
        for k in range(experts * block // step):
            value = nn(slot_match(row_out, (c * experts + k * per) * block, step), rows).astype(BF16)
            slots_out[k * per : (k + 1) * per, c] = value.reshape(per, block, -1)


def front(rank, cotangent, routes, experts, cap, half, block, chunks):
    rows, width = cotangent.shape
    images = rows // SEQ
    padded = jnp.pad(
        routes.reshape(images, SEQ, 2), ((0, 0), (0, PAD - SEQ), (0, 0)), constant_values=-1
    )
    down = padded.transpose(1, 0, 2).reshape(PAD, images * 2)
    across = padded.reshape(images * PAD, 2).T
    return pl.pallas_call(
        functools.partial(front_kernel, cap=cap, half=half),
        out_shape=(
            jax.ShapeDtypeStruct((images, PAD, width), BF16),
            jax.ShapeDtypeStruct((experts, chunks, block, width), BF16),
            jax.ShapeDtypeStruct(down.shape, jnp.int32),
            jax.ShapeDtypeStruct(across.shape, jnp.int32),
        ),
        in_specs=[pl.BlockSpec(memory_space=pltpu.SMEM)] + [VMEM] * 3,
        out_specs=(VMEM,) * 4,
        scratch_shapes=[wide_scratch(images, width)],
        compiler_params=params(),
        cost_estimate=cost(10),
        name="front",
    )(rank, cotangent, down, across)


def spread_kernel(code_ref, rows_ref, out_ref, *, start, step):
    match = slot_match(code_ref, pl.program_id(0) * step + start, step)
    out_ref[...] = nn(match, rows_ref[...]).astype(BF16).reshape(out_ref.shape)


def spread(code_row, rows, experts, block, chunks, start=0, step=512):
    count, width = rows.shape
    slots = experts * block
    step = min(step, slots)
    per = step // block
    return pl.pallas_call(
        functools.partial(spread_kernel, start=start * slots, step=step),
        out_shape=jax.ShapeDtypeStruct((experts, chunks, block, width), BF16),
        grid=(chunks * slots // step,),
        in_specs=[full((2, count)), full((count, width))],
        out_specs=pl.BlockSpec(
            (per, 1, block, width), lambda i: (i % (experts // per), i // (experts // per), 0, 0)
        ),
        compiler_params=params(),
        cost_estimate=cost(4 * chunks),
        name="spread",
    )(code_row, rows)


def row_mean(v):
    return jnp.mean(v, axis=-1, keepdims=True)


def key_softmax(scores):
    cut = SEQ // 16 * 16
    head, tail = scores[:cut], scores[cut:]
    valid = lax.broadcasted_iota(jnp.int32, tail.shape, 0) < SEQ - cut
    tail = jnp.where(valid, tail, -jnp.inf)
    top = jnp.maximum(jnp.max(head, axis=0, keepdims=True), jnp.max(tail, axis=0, keepdims=True))
    head, tail = jnp.exp(head - top), jnp.exp(tail - top)
    total = jnp.sum(head, axis=0, keepdims=True) + jnp.sum(tail, axis=0, keepdims=True)
    scale = 1.0 / total
    return jnp.concatenate([head * scale, tail * scale], axis=0)


QUAD = 4 * HEAD_DIM


def quad_masks():
    lane = iota((PAD, QUAD), 1)
    return [(lane >= h * HEAD_DIM) & (lane < (h + 1) * HEAD_DIM) for h in range(4)]


def stacked(value, masks):
    return jnp.concatenate([jnp.where(m, value, jnp.zeros_like(value)) for m in masks], axis=0)


def unstacked(value, masks):
    return sum(jnp.where(m, value[h * PAD : (h + 1) * PAD], 0.0) for h, m in enumerate(masks))


def attend_kernel(place_ref, tok_ref, ga_ref, gm_ref, *rest, pieces, own):
    wq, wo, rest = rest[:pieces], rest[pieces : 2 * pieces], rest[2 * pieces :]
    routed_ref, res_ref, qkv_ref, prob_ref, att_ref, wq_all, wo_all, qkv_all, att_all = rest
    batch, _, model = tok_ref.shape
    keep = pl.program_id(0) * batch < own

    @pl.when(pl.program_id(0) == 0)
    def _():
        at = 0
        size = wo[0].shape[0]
        if pieces == 1:
            places = [0]
        else:
            core, small = place_ref[1], wo[1].shape[0]
            places = [0, size + core * small, size + (1 - core) * small]
        for k, start in enumerate(places):
            cols = wo[k].shape[0]
            for j in range(3):
                to = start + j * model
                if k:
                    to = pl.multiple_of(to, 128)
                wq_all[:, pl.ds(to, cols)] = wq[k][j]
            if k:
                start = pl.multiple_of(start, 128)
            wo_all[pl.ds(start, cols), :] = wo[k][...]

    tok = tok_ref[...].reshape(batch * PAD, model).astype(F32)
    center = tok - row_mean(tok)
    normed = (center * lax.rsqrt(row_mean(center * center) + EPS) * ga_ref[...]).astype(BF16)
    value = nn(normed, wq_all[...])
    qkv_all[:, :model] = (value[:, :model] * HEAD_DIM**-0.5).astype(BF16)
    qkv_all[:, model:] = value[:, model:].astype(BF16)
    masks = quad_masks()
    key_ok = iota((4 * PAD, PAD), 1) < SEQ
    for g in range(batch):
        rows = slice(g * PAD, (g + 1) * PAD)
        for quad in range(model // QUAD):
            q, k, v = (qkv_all[rows, j * model + quad * QUAD : j * model + (quad + 1) * QUAD] for j in range(3))
            scores = jnp.where(key_ok, nt(stacked(q, masks), k), -jnp.inf)
            ex = jnp.exp(scores - jnp.max(scores, axis=1, keepdims=True))
            probs = (ex * (1.0 / jnp.sum(ex, axis=1, keepdims=True))).astype(BF16)

            @pl.when(keep)
            def _():
                prob_ref[g, quad] = probs

            mixed = unstacked(nn(probs, v), masks)
            att_all[rows, quad * QUAD : (quad + 1) * QUAD] = mixed.astype(BF16)

    residual = tok + nn(att_all[...], wo_all[...])

    @pl.when(keep)
    def _():
        res_ref[...] = residual.reshape(batch, PAD, model)
        qkv_ref[...] = qkv_all[...].reshape(batch, PAD, 3 * model)
        att_ref[...] = att_all[...].reshape(batch, PAD, model)

    center = residual - row_mean(residual)
    normed = center * lax.rsqrt(row_mean(center * center) + EPS) * gm_ref[...]
    routed_ref[...] = normed.astype(BF16).reshape(batch, PAD, model)


def attend(place, tok_pad, gain_attn, gain_moe, wq, wo, own, batch=2):
    images, _, width = tok_pad.shape
    batch = batch if own % batch == 0 else 1
    pieces = len(wq)
    steps = images // batch

    def image(i, place_ref):
        return (lax.rem(i + place_ref[0] // batch, steps), 0, 0)

    def kept(*shape):
        return pl.BlockSpec(
            (batch,) + shape, lambda i, place_ref: (jnp.minimum(i, own // batch - 1),) + (0,) * len(shape)
        )

    rows = pl.BlockSpec((batch, PAD, width), image)
    probs = (width // QUAD, 4 * PAD, PAD)
    return pl.pallas_call(
        functools.partial(attend_kernel, pieces=pieces, own=own),
        out_shape=(
            jax.ShapeDtypeStruct((images, PAD, width), BF16),
            jax.ShapeDtypeStruct((own, PAD, width), F32),
            jax.ShapeDtypeStruct((own, PAD, 3 * width), BF16),
            jax.ShapeDtypeStruct((own,) + probs, BF16),
            jax.ShapeDtypeStruct((own, PAD, width), BF16),
            jax.ShapeDtypeStruct((width, 3 * width), BF16),
            jax.ShapeDtypeStruct((width, width), BF16),
        ),
        grid_spec=pltpu.PrefetchScalarGridSpec(
            num_scalar_prefetch=1,
            grid=(steps,),
            in_specs=[rows, full((1, width)), full((1, width))] + [full(v.shape) for v in (*wq, *wo)],
            out_specs=(
                rows,
                kept(PAD, width),
                kept(PAD, 3 * width),
                kept(*probs),
                kept(PAD, width),
                full((width, 3 * width)),
                full((width, width)),
            ),
            scratch_shapes=[
                pltpu.VMEM((batch * PAD, 3 * width), BF16),
                pltpu.VMEM((batch * PAD, width), BF16),
            ],
        ),
        compiler_params=params(),
        cost_estimate=cost(25),
        name="attend",
    )(place, tok_pad, gain_attn.reshape(1, -1), gain_moe.reshape(1, -1), *wq, *wo)


def expert_kernel(expert_ref, x_ref, cot_ref, wr_ref, *rest, shards, half, block, chunk, begins, ends, steps):
    w1, w2, rest = rest[:shards], rest[shards : 2 * shards], rest[2 * shards :]
    before, rest = ((), rest) if begins else (rest[: 2 * shards], rest[2 * shards + 1 :])
    (gin_ref, out_ref), given, scratch = rest[:2], rest[2 : 2 + 2 * shards], rest[2 + 2 * shards :]
    sums = list(given)
    if ends and shards > 1:
        sums[1], sums[3] = scratch
    dw1, dw2 = sums[0::1][:shards], sums[shards:]
    expert = expert_ref[0]

    @pl.when(pl.program_id(0) == 0)
    def _():
        for k, ref in enumerate(sums):
            ref[...] = jnp.zeros_like(ref) if begins else before[k][...]

    x = x_ref[...]
    rows, width = x.shape
    cot = cot_ref[...].reshape(rows, width).astype(F32)
    logits = nn(x, wr_ref[...])
    ex = jnp.exp(logits - jnp.max(logits, axis=1, keepdims=True))
    mine = iota(ex.shape, 1) == expert
    gate = jnp.sum(jnp.where(mine, ex, 0.0), axis=1, keepdims=True) / jnp.sum(
        ex, axis=1, keepdims=True
    )
    grad_out = (gate * cot).astype(BF16)
    x_t = x.T
    out = jnp.zeros((rows, width), F32)
    gin = jnp.zeros((rows, width), F32)
    c0 = (2.0 / jnp.pi) ** 0.5
    for s in range(shards):
        hidden = w1[s].shape[1]
        size = min(chunk, hidden)
        for c in range(hidden // size):
            cols = slice(c * size, (c + 1) * size)
            u = nn(x, w1[s][:, cols])
            square = u * u
            t = jnp.tanh(u * (c0 + (c0 * 0.044715) * square))
            h = 0.5 + 0.5 * t
            slope = h + (0.5 * u) * (1.0 - t * t) * (c0 + (3 * c0 * 0.044715) * square)
            active = (u * h).astype(BF16)
            out = out + nn(active, w2[s][cols, :])
            grad_pre = (nt(grad_out, w2[s][cols, :]) * slope).astype(BF16)
            gin = gin + nt(grad_pre, w1[s][:, cols])
            dw2[s][cols, :] += tn(active, grad_out)
            dw1[s][:, cols] += nn(x_t, grad_pre)
    out_ref[...] = (gate * out).astype(BF16).reshape(out_ref.shape)
    gate_grad = jnp.sum(cot * out, axis=1, keepdims=True)
    down, across = iota((block, width), 0), iota((block, width), 1)
    for g in range(rows // block):
        span = slice(g * block, (g + 1) * block)
        line = jnp.sum(jnp.where(down == across, gate_grad[span], 0.0), axis=0, keepdims=True)
        high = line.astype(BF16).astype(F32)
        value = jnp.where(down == half, high, jnp.where(down == half + 1, line - high, gin[span]))
        gin_ref[span, :] = value.astype(BF16)

    if ends and shards > 1:

        @pl.when(pl.program_id(0) == steps - 1)
        def _():
            given[1][...] = sums[1][...].astype(BF16)
            given[3][...] = sums[3][...].astype(BF16)


def experts_step(expert, x, cot, before, number, ends, w_router, w1, w2, half, block, step=512, chunk=512):
    rows, width = x.shape
    shards = len(w1)
    hidden = w1[0].shape[1]
    step = min(step, rows)
    row_spec = pl.BlockSpec((step, width), lambda i, _: (i, 0))
    chunk_spec = pl.BlockSpec((step // block, 1, block, width), lambda i, _: (i, number, 0, 0))
    old = [] if before is None else [*before[1:], before[0]]
    shapes = [(width, hidden)] * shards + [(hidden, width)] * shards

    def once(shape):
        return pl.BlockSpec(shape, lambda *_: (0, 0), pipeline_mode=pl.Buffered(1))

    at = 4 + 2 * shards
    alias = {at + 2 * shards: 1} if old else {}
    if old:
        alias |= {at + k: 2 + k for k in range(0, 2 * shards, shards)}
    return pl.pallas_call(
        functools.partial(
            expert_kernel,
            shards=shards,
            half=half,
            block=block,
            chunk=chunk,
            begins=before is None,
            ends=ends,
            steps=rows // step,
        ),
        out_shape=(jax.ShapeDtypeStruct((rows, width), BF16), jax.ShapeDtypeStruct(cot.shape, BF16))
        + tuple(
            jax.ShapeDtypeStruct(v, BF16 if ends and k % shards else F32) for k, v in enumerate(shapes)
        ),
        grid_spec=pltpu.PrefetchScalarGridSpec(
            num_scalar_prefetch=1,
            grid=(rows // step,),
            in_specs=[row_spec, chunk_spec, full(w_router.shape)]
            + [once((width, hidden))] * shards
            + [once((hidden, width))] * shards
            + ([once(v) for v in shapes] + [pl.BlockSpec(memory_space=pl.ANY)] if old else []),
            out_specs=(row_spec, chunk_spec) + tuple(once(v) for v in shapes),
            scratch_shapes=[pltpu.VMEM(shapes[k], F32) for k in range(1, 2 * shards, 2)]
            if ends and shards > 1
            else [],
        ),
        input_output_aliases=alias,
        compiler_params=params(62),
        cost_estimate=cost(20),
        name="experts",
    )(expert, x, cot, w_router, *w1, *w2, *old)


def collect_kernel(first_ref, code_ref, *rest, numbers, half, block, probs, before):
    chunks = len(numbers)
    parts, rest = rest[:chunks], rest[chunks:]
    old, rest = rest[:before], rest[before:]
    out_ref, rest = rest[0], rest[1:]
    count, width = parts[0].shape
    experts = count // block
    own = out_ref.shape[0]
    rows = own * PAD
    codes = code_ref[...]
    across = iota(codes.shape, 1)
    columns = [
        jnp.concatenate(
            [
                jnp.sum(jnp.where(across == (first_ref[0] + g) * 2 + c, codes, 0), axis=1, keepdims=True)
                for g in range(own)
            ],
            axis=0,
        )
        for c in range(2)
    ]
    lane = iota((rows, count), 1)
    total = old[0][...].reshape(rows, width) if old else None
    grads = None
    for c in range(chunks):
        shift = numbers[c] * count
        match = ((lane + shift == columns[0]) | (lane + shift == columns[1])).astype(BF16)
        value = nn(match, parts[c][...])
        total = value if total is None else total + value
        if probs:
            lines = jnp.zeros((experts, 128), F32)
            for e in range(experts):
                tail = parts[c][e * block + block - 16 : (e + 1) * block, 0:128].astype(F32)
                at = half - (block - 16)
                lines = jnp.where(iota(lines.shape, 0) == e, tail[at : at + 1] + tail[at + 1 : at + 2], lines)
            turned = lines.T[:block]
            slot_grads = jnp.concatenate(
                [jnp.where(iota(turned.shape, 1) == e, turned, 0.0) for e in range(experts)], axis=0
            )
            high = slot_grads.astype(BF16)
            low = (slot_grads - high.astype(F32)).astype(BF16)
            value = nn(match, high) + nn(match, low)
            grads = value if grads is None else grads + value
    out_ref[...] = total.astype(out_ref.dtype).reshape(out_ref.shape)
    if probs:
        for g in range(own):
            value = grads[g * PAD : (g + 1) * PAD].T
            rest[0][g] = value + old[1][g] if old else value


def collect(first, code_col, parts, own, dtype, half, block, probs=False, numbers=None, before=()):
    numbers = tuple(range(len(parts))) if numbers is None else numbers
    count, width = parts[0].shape
    outs = [jax.ShapeDtypeStruct((own, PAD, width), dtype)]
    if probs:
        outs.append(jax.ShapeDtypeStruct((own, count // block, PAD), F32))
    return pl.pallas_call(
        functools.partial(
            collect_kernel, numbers=numbers, half=half, block=block, probs=probs, before=len(before)
        ),
        out_shape=tuple(outs),
        in_specs=[pl.BlockSpec(memory_space=pltpu.SMEM), VMEM] + [VMEM] * (len(parts) + len(before)),
        out_specs=(VMEM,) * len(outs),
        compiler_params=params(),
        cost_estimate=cost(7),
        name="collect",
    )(first, code_col, *parts, *before)


def back_kernel(first_ref, *rest, steps, received):
    (sum_ref, gp_ref), rest = rest[:2], rest[2:]
    more, rest = rest[: 2 * received], rest[2 * received :]
    (res_ref, cot_ref, tok_ref, ga_ref, gm_ref, wrt_ref, wq, wo, qkv_ref, prob_ref, att_ref), rest = rest[:11], rest[11:]
    gtok_ref, pack_ref, dwq, dwo, small, gatt_all, dqkv_all = rest
    experts = wrt_ref.shape[0]
    batch, _, model = res_ref.shape
    rows = batch * PAD
    step = pl.program_id(0)

    @pl.when(step == 0)
    def _():
        for ref in (dwq, dwo, small):
            ref[...] = jnp.zeros_like(ref)

    def flat(ref):
        return ref[...].reshape(rows, -1).astype(F32)

    residual = flat(res_ref)
    center = residual - row_mean(residual)
    scale = lax.rsqrt(row_mean(center * center) + EPS)
    xhat = center * scale
    gm = gm_ref[...]
    routed = (xhat * gm).astype(BF16)
    logits = nt(wrt_ref[...], routed)
    ex = jnp.exp(logits - jnp.max(logits, axis=0, keepdims=True))
    probs = ex / jnp.sum(ex, axis=0, keepdims=True)
    grad_probs = gp_ref[...]
    grad_routed = flat(sum_ref)
    if received:
        grad_routed = grad_routed + flat(more[0])
        grad_probs = grad_probs + more[1][...]
    grad_probs = jnp.concatenate([grad_probs[g] for g in range(batch)], axis=1)
    grad_logits = probs * (grad_probs - jnp.sum(probs * grad_probs, axis=0, keepdims=True))
    high = grad_logits.astype(BF16)
    low = (grad_logits - high.astype(F32)).astype(BF16)
    both = jnp.concatenate([high, low], axis=0)
    new = nn(both, routed)
    small[0:experts, :] += new[:experts] + new[experts:]
    grad_routed = grad_routed + tn(both, jnp.concatenate([wrt_ref[...]] * 2, axis=0))
    small[experts + 1 : experts + 2, :] += jnp.sum(grad_routed * xhat, axis=0, keepdims=True)
    g = grad_routed * gm
    grad_res = flat(cot_ref) + scale * (g - row_mean(g) - xhat * row_mean(g * xhat))
    grad_mixed = grad_res.astype(BF16)
    dwo[...] += tn(att_ref[...].reshape(rows, model), grad_mixed)
    gatt_all[...] = nt(grad_mixed, wo[...]).astype(BF16)

    masks = quad_masks()
    for b in range(batch):
        span = slice(b * PAD, (b + 1) * PAD)
        for quad in range(model // QUAD):
            q, k, v = (
                qkv_ref[b, :, j * model + quad * QUAD : j * model + (quad + 1) * QUAD] for j in range(3)
            )
            grad_heads = stacked(gatt_all[span, quad * QUAD : (quad + 1) * QUAD], masks)
            low_probs = prob_ref[b, quad]
            p = low_probs.astype(F32)
            gw = nt(grad_heads, v)
            ds = (p * (gw - jnp.sum(p * gw, axis=1, keepdims=True))).astype(BF16)
            grad_q = unstacked(nn(ds, k), masks) * HEAD_DIM**-0.5
            grad_k = tn(ds, stacked(q, masks))
            grad_v = tn(low_probs, grad_heads)
            for j, value in enumerate((grad_q, grad_k, grad_v)):
                dqkv_all[span, j * model + quad * QUAD : j * model + (quad + 1) * QUAD] = value.astype(BF16)

    tok = flat(tok_ref)
    center = tok - row_mean(tok)
    tok_scale = lax.rsqrt(row_mean(center * center) + EPS)
    xin = center * tok_scale
    ga = ga_ref[...]
    normed = (xin * ga).astype(BF16)
    dwq[...] += tn(normed, dqkv_all[...])
    grad_normed = nt(dqkv_all[...], wq[...])
    small[experts : experts + 1, :] += jnp.sum(grad_normed * xin, axis=0, keepdims=True)
    h = grad_normed * ga
    grad_tok = grad_res + tok_scale * (h - row_mean(h) - xin * row_mean(h * xin))
    gtok_ref[...] = grad_tok.astype(BF16).reshape(gtok_ref.shape)

    @pl.when(step == steps - 1)
    def _():
        shards = pack_ref.shape[0]
        part = model // shards
        for s in range(shards):
            at = 0
            blocks = [dwq[:, j * model + s * part : j * model + (s + 1) * part] for j in range(3)]
            for value in blocks + [dwo[s * part : (s + 1) * part, :], small[...]]:
                for c in range(value.shape[1] // 256):
                    pack_ref[s, at : at + value.shape[0], :] = value[:, c * 256 : (c + 1) * 256].astype(BF16)
                    at += value.shape[0]
            if at < pack_ref.shape[1]:
                pack_ref[s, at:, :] = jnp.zeros((pack_ref.shape[1] - at, 256), BF16)


def small_rows(experts):
    return -(-(experts + 2) // 16) * 16


def pack_rows(width, part, experts, align):
    rows = 3 * width * (part // 256) + part * (width // 256) + small_rows(experts) * (width // 256)
    return -(-rows // align) * align


def back(first, sums, residual, cot_pad, tok_pad, qkv, probs, att, gain_attn, gain_moe, w_router, wq, wo, shards, align, batch=2):
    own, _, width = residual.shape
    batch = batch if own % batch == 0 else 1
    experts = w_router.shape[1]
    rows = pack_rows(width, width // shards, experts, align)

    def mine(*shape):
        return pl.BlockSpec((batch,) + shape, lambda i, f: (i,) + (0,) * len(shape))

    image = pl.BlockSpec((batch, PAD, width), lambda i, f: (i + f[0] // batch, 0, 0))
    flat = [v for pair in sums for v in pair]
    return pl.pallas_call(
        functools.partial(back_kernel, steps=own // batch, received=len(sums) - 1),
        out_shape=(
            jax.ShapeDtypeStruct((own, PAD, width), BF16),
            jax.ShapeDtypeStruct((shards, rows, 256), BF16),
        ),
        grid_spec=pltpu.PrefetchScalarGridSpec(
            num_scalar_prefetch=1,
            grid=(own // batch,),
            in_specs=[mine(PAD, width), mine(experts, PAD)] * len(sums)
            + [
                mine(PAD, width),
                image,
                image,
                full((1, width)),
                full((1, width)),
                full((experts, width)),
                full(wq.shape),
                full(wo.shape),
                mine(*qkv.shape[1:]),
                mine(*probs.shape[1:]),
                mine(*att.shape[1:]),
            ],
            out_specs=(mine(PAD, width), full((shards, rows, 256))),
            scratch_shapes=[
                pltpu.VMEM((width, 3 * width), F32),
                pltpu.VMEM((width, width), F32),
                pltpu.VMEM((small_rows(experts), width), F32),
                pltpu.VMEM((batch * PAD, width), BF16),
                pltpu.VMEM((batch * PAD, 3 * width), BF16),
            ],
        ),
        compiler_params=params(),
        cost_estimate=cost(16),
        name="back",
    )(
        first,
        *flat,
        residual,
        cot_pad,
        tok_pad,
        gain_attn.reshape(1, -1),
        gain_moe.reshape(1, -1),
        w_router.T,
        wq,
        wo,
        qkv,
        probs,
        att,
    )


def unpad_kernel(first_ref, own_ref, peer_ref, out_ref, *, images):
    own = own_ref.shape[0]
    for i in range(images):
        inner = i % own
        mine = first_ref[0] == i - inner
        value = jnp.where(mine, own_ref[inner].astype(F32), peer_ref[inner].astype(F32))
        out_ref[i * SEQ : (i + 1) * SEQ, :] = value[:SEQ]


def unpad(first, own, peer):
    images, width = 2 * own.shape[0], own.shape[2]
    return pl.pallas_call(
        functools.partial(unpad_kernel, images=images),
        out_shape=jax.ShapeDtypeStruct((images * SEQ, width), F32),
        in_specs=[pl.BlockSpec(memory_space=pltpu.SMEM), VMEM, VMEM],
        out_specs=VMEM,
        compiler_params=params(40),
        cost_estimate=cost(2),
        name="unpad",
    )(first, own, peer)


def body(tokens, routes, gain_attn, w_qkv, w_attn_out, gain_moe, w_router, w_expert_in, w_expert_out, cotangent, *, ways, groups):
    tok_rows, width = tokens.shape
    experts = w_router.shape[1]
    cap = max(4, (5 * tok_rows // (2 * experts) + 7) // 8 * 8)
    chunks = 2
    half = -(-cap // (ways * chunks))
    block = -(-(half + 2) // 16) * 16
    slots = experts * block
    images = tok_rows // SEQ
    own = images // ways
    rank = lax.axis_index("tensor")
    expert = lax.axis_index("expert")
    first = (rank * own).astype(jnp.int32).reshape(1)
    swap = [(0, 1), (1, 0)]

    def other(v):
        return lax.ppermute(v, "tensor", swap)

    def shards_of(v, axis):
        if ways == 2:
            return [v, other(v)]
        return [lax.all_gather(v, "tensor", axis=axis, tiled=True)]

    def exchange(rows):
        return lax.all_to_all(rows, "expert", split_axis=0, concat_axis=0, tiled=True)

    def after(v, *others):
        return lax.optimization_barrier((v,) + others)[0]

    def rows_of(v):
        return v.reshape(-1, width)

    def collected(number, parts, dtype, probs=False, numbers=None, before=()):
        return collect(number, code_col, parts, own, dtype, half, block, probs, numbers, before)

    if ways == 2:
        core = expert % 2
        near = [(i, i ^ 1) for i in range(groups)]

        def part_of(v, axis):
            size = v.shape[axis] // 2
            return other(lax.dynamic_slice_in_dim(v, core * size, size, axis))

        got_q, got_o = part_of(w_qkv, 2), part_of(w_attn_out, 0)
    else:
        core = 0 * expert
        wq, wo = shards_of(w_qkv, 2), shards_of(w_attn_out, 0)
    cot_pad, cot_slots, code_col, code_row = front(
        rank.astype(jnp.int32).reshape(1), cotangent, routes, experts, cap, half, block, chunks
    )
    if ways == 2:
        cot_slots, got_q, got_o = lax.optimization_barrier((cot_slots, got_q, got_o))
        wq = [w_qkv, got_q, lax.ppermute(got_q, "expert", near)]
        wo = [w_attn_out, got_o, lax.ppermute(got_o, "expert", near)]
    cot_slots = exchange(cot_slots)
    tok_pad = pad(after(tokens, cot_pad))
    w1 = shards_of(after(w_expert_in[0], wq[-1]), 1)
    w2 = shards_of(after(w_expert_out[0], wq[-1]), 0)
    place = jnp.stack([rank * own, core]).astype(jnp.int32)
    routed, residual, qkv, probs, att, wq, wo = attend(place, tok_pad, gain_attn, gain_moe, wq, wo, own)
    x_slots = []
    for c in range(chunks):
        sent = spread(code_row, rows_of(routed), experts, block, 1, c)
        if c == 0:
            sent, cot_slots, *_ = lax.optimization_barrier((sent, cot_slots, w1[-1], w2[-1]))
        x_slots.append(exchange(sent))
    gin, more = [], None
    expert_number = expert.astype(jnp.int32).reshape(1)
    for c in range(chunks):
        new, *more = experts_step(
            expert_number, rows_of(x_slots[c]), cot_slots, more, c, c == chunks - 1, w_router, w1, w2, half, block
        )
        gin.append(exchange(new.reshape(experts, block, width)))
    gated, *dw = more
    gin = [rows_of(v) for v in gin]
    if ways == 2:
        there = ((1 - rank) * own).astype(jnp.int32).reshape(1)
        dw1_peer = other(dw[1])
        start = collected(there, gin[:1], F32, True, (0,))
        mine = collected(first, gin[:1], F32, True, (0,))
        gin[1], dw1_peer, *start = lax.optimization_barrier((gin[1], dw1_peer, *start, *mine))
        start, mine = start[:2], start[2:]
        sent = collected(there, gin[1:], BF16, True, (1,), start)
        received = tuple(other(v) for v in sent)
        sums = [collected(first, gin[1:], F32, True, (1,), mine), received]
        gated = exchange(after(gated, *sent))
        grad_w1 = dw[0] + dw1_peer.astype(F32)
        dw2_peer = other(after(dw[3], *received))
    else:
        gated = exchange(gated)
        every = [collected(jnp.full((1,), r * own, jnp.int32), gin, F32, True) for r in range(ways)]
        sums = [
            tuple(
                lax.psum_scatter(jnp.stack([v[k] for v in every]).astype(t), "tensor", scatter_dimension=0).astype(F32)
                for k, t in ((0, BF16), (1, F32))
            )
        ]
        grad_w1 = lax.psum_scatter(dw[0].astype(BF16), "tensor", scatter_dimension=1, tiled=True).astype(F32)
        grad_w2 = lax.psum_scatter(dw[1].astype(BF16), "tensor", scatter_dimension=0, tiled=True).astype(F32)
    grad_tok, pack = back(
        first, sums, residual, cot_pad, tok_pad, qkv, probs, att, gain_attn, gain_moe, w_router, wq, wo,
        2 if ways == 2 else 1, groups * 8,
    )

    bits = [1 << b for b in range(groups.bit_length() - 1)]
    if ways == 2:

        def swap_bit(v, bit):
            return lax.ppermute(v, "expert", [(i, i ^ bit) for i in range(groups)])

        def add(a, b):
            return (a.astype(F32) + b.astype(F32)).astype(BF16)

        def halves(v, bit):
            size = v.shape[-2] // 2
            upper = (expert // bit) % 2
            keep = lax.dynamic_slice_in_dim(v, upper * size, size, v.ndim - 2)
            give = lax.dynamic_slice_in_dim(v, (1 - upper) * size, size, v.ndim - 2)
            return keep, give

        pack, grad_tok, gated, grad_w1, dw2_peer = lax.optimization_barrier((pack, grad_tok, gated, grad_w1, dw2_peer))
        grad_w2 = dw[2] + dw2_peer.astype(F32)
        gated = [rows_of(gated[:, c]) for c in range(chunks)]
        (mix_there,) = collected(there, gated, BF16)
        mix_peer = other(mix_there)
        for bit in bits[:2]:
            keep, give = halves(pack, bit)
            pack = add(keep, swap_bit(give, bit))
        swapped = other(after(pack[1], mix_there))
        total = add(pack[0], swapped)
        (mix_here,) = collected(first, [after(gated[0], mix_there)], F32, False, (0,))
        (mix_here,) = collected(first, gated[1:], F32, False, (1,), (mix_here,))
        total, mix_peer, mix_here = lax.optimization_barrier((total, mix_peer, mix_here))
        grad_peer = other(after(grad_tok, total))
        result = (residual + (mix_here + mix_peer.astype(F32))).astype(BF16)
        keep, give = halves(total, bits[2])
        total = add(keep, swap_bit(give, bits[2]))
        total = add(total, swap_bit(total, bits[3]))

        def gathered(v, bit):
            got = swap_bit(v, bit)
            upper = (expert // bit) % 2 == 1
            return jnp.where(upper, jnp.concatenate([got, v]), jnp.concatenate([v, got]))

        total, result = lax.optimization_barrier((total, result))
        total = gathered(total, bits[2])
        total, grad_peer, result = lax.optimization_barrier((total, grad_peer, result))
        result_peer = other(result)
        grad_tokens = unpad(first, grad_tok, grad_peer)
        for bit in bits[1::-1]:
            total = gathered(total, bit)
        result = unpad(first, result, result_peer).astype(BF16)
        total = total.astype(F32)
        part = w_qkv.shape[2]
    else:
        gated = [rows_of(gated[:, c]) for c in range(chunks)]
        every = [collected(jnp.full((1,), r * own, jnp.int32), gated, BF16)[0] for r in range(ways)]
        mixture = lax.psum_scatter(jnp.stack(every), "tensor", scatter_dimension=0).astype(F32)

        def whole(v):
            v = lax.all_gather(v, "tensor", axis=0, tiled=True)
            return v[:, :SEQ].reshape(tok_rows, width)

        result = whole((residual + mixture).astype(BF16))
        grad_tokens = whole(grad_tok).astype(F32)
        total = lax.psum(pack[0], ("expert", "tensor")).astype(F32)
        part = width

    def take(at, rows, cols):
        blocks = [total[at + b * rows : at + (b + 1) * rows] for b in range(cols // 256)]
        return jnp.concatenate(blocks, axis=1) if len(blocks) > 1 else blocks[0]

    step = width * (part // 256)
    grad_w_qkv = jnp.stack([take(j * step, width, part) for j in range(3)])
    grad_w_attn_out = take(3 * step, part, width)
    small = take(3 * step + part * (width // 256), small_rows(experts), width)
    if ways != 2:
        grad_w_qkv = lax.dynamic_slice_in_dim(grad_w_qkv, rank * w_qkv.shape[2], w_qkv.shape[2], 2)
        grad_w_attn_out = lax.dynamic_slice_in_dim(grad_w_attn_out, rank * w_qkv.shape[2], w_qkv.shape[2], 0)
    return (
        result,
        grad_tokens,
        small[experts],
        grad_w_qkv,
        grad_w_attn_out,
        small[experts + 1],
        small[:experts].T,
        grad_w1[None],
        grad_w2[None],
    )


def solution(mesh):
    placed = (
        P("expert", None),
        P("expert", None),
        P(),
        P(None, None, "tensor"),
        P("tensor", None),
        P(),
        P(),
        P("expert", None, "tensor"),
        P("expert", "tensor", None),
        P("expert", None),
    )
    return jax.shard_map(
        functools.partial(body, ways=mesh.shape["tensor"], groups=mesh.shape["expert"]),
        mesh=mesh,
        in_specs=placed,
        out_specs=(
            P("expert", None),
            P("expert", None),
            P(),
            P(None, None, "tensor"),
            P("tensor", None),
            P(),
            P(),
            P("expert", None, "tensor"),
            P("expert", "tensor", None),
        ),
        check_vma=False,
    )
```

```python
import functools

import jax
import jax.numpy as jnp
from jax import lax
from jax.experimental import pallas as pl
from jax.experimental.pallas import tpu as pltpu
from jax.sharding import PartitionSpec as P

HEAD_DIM = 64
SEQ = 197
PAD = 208
EPS = 1e-06
F32 = jnp.float32
BF16 = jnp.bfloat16
VMEM = pl.BlockSpec(memory_space=pltpu.VMEM)


def nn(a, b):
    return lax.dot_general(a, b, (((1,), (0,)), ((), ())), preferred_element_type=F32)


def nt(a, b):
    return lax.dot_general(a, b, (((1,), (1,)), ((), ())), preferred_element_type=F32)


def tn(a, b):
    return lax.dot_general(a, b, (((0,), (0,)), ((), ())), preferred_element_type=F32)


def params(mib=56):
    return pltpu.CompilerParams(vmem_limit_bytes=mib << 20)


def cost(us):
    return pl.CostEstimate(flops=0, bytes_accessed=int(us * 3.69e6), transcendentals=0)


def full(shape):
    return pl.BlockSpec(shape, lambda *_: (0,) * len(shape))


def pad_images(source, wide, target):
    wide[0 : source.shape[0], :] = source[...].astype(F32)
    for i in range(target.shape[0]):
        window = wide[i * SEQ : i * SEQ + PAD, :]
        inside = lax.broadcasted_iota(jnp.int32, window.shape, 0) < SEQ
        target[i] = jnp.where(inside, window, 0.0).astype(BF16)


def pad_kernel(source, target, wide):
    pad_images(source, wide, target)


def wide_scratch(images, width):
    return pltpu.VMEM((-(-((images - 1) * SEQ + PAD) // 16) * 16, width), F32)


def pad(rows):
    images, width = rows.shape[0] // SEQ, rows.shape[1]
    return pl.pallas_call(
        pad_kernel,
        out_shape=jax.ShapeDtypeStruct((images, PAD, width), BF16),
        in_specs=[VMEM],
        out_specs=VMEM,
        scratch_shapes=[wide_scratch(images, width)],
        compiler_params=params(),
        cost_estimate=cost(2),
        name="pad",
    )(rows)


def iota(shape, axis):
    return lax.broadcasted_iota(jnp.int32, shape, axis)


def slot_match(code_ref, start, step):
    slot = iota((step, code_ref.shape[1]), 0) + start
    return ((slot == code_ref[0:1, :]) | (slot == code_ref[1:2, :])).astype(BF16)


def front_kernel(rank_ref, cot_ref, col_ref, row_ref, cot_out, slots_out, col_out, row_out, wide, *, cap, half):
    experts, chunks, block, _ = slots_out.shape
    first_slot = rank_ref[0] * (half * chunks)

    def code(expert, position):
        place = position.astype(jnp.int32) - first_slot
        good = (expert >= 0) & (position < cap) & (place >= 0) & (place < half * chunks)
        slot = expert * block + place
        for c in range(1, chunks):
            slot = jnp.where(place >= c * half, slot + (experts * block - half), slot)
        return jnp.where(good, slot, -1)

    lanes = col_ref.shape[1]
    span = lanes * experts
    routes = col_ref[...]
    spread_lanes = (iota((lanes, span), 1) // experts == iota((lanes, span), 0)).astype(BF16)
    gather_lanes = (iota((span, lanes), 0) // experts == iota((span, lanes), 1)).astype(BF16)
    chosen = nn(routes.astype(F32).astype(BF16), spread_lanes) == (iota((PAD, span), 1) % experts).astype(F32)
    ones = chosen.astype(F32)
    lower = (iota((PAD, PAD), 0) > iota((PAD, PAD), 1)).astype(BF16)
    before = nn(lower, ones.astype(BF16))
    totals = jnp.broadcast_to(jnp.sum(ones, axis=0, keepdims=True), (16, span)).astype(BF16)
    source, target = iota((span, span), 0), iota((span, span), 1)
    order_s = (source // experts % 2) * lanes + source // (2 * experts)
    order_t = (target // experts % 2) * lanes + target // (2 * experts)
    earlier = (source % experts == target % experts) & (order_s < order_t)
    before = before + nn(totals, earlier.astype(BF16))[0:1]
    place = nn((jnp.minimum(before, float(cap)) * ones).astype(BF16), gather_lanes)
    col_out[...] = code(routes, place)

    step = 128
    blocks = row_ref.shape[1] // step
    upper = (iota((step, step), 0) < iota((step, step), 1)).astype(BF16)
    order = [(choice, b) for choice in range(2) for b in range(blocks)]
    picked = [row_ref[choice : choice + 1, b * step : (b + 1) * step] for choice, b in order]
    ones = [(p == iota((experts, step), 0)).astype(F32) for p in picked]
    before = nn(jnp.concatenate(ones, axis=0).astype(BF16), upper)
    base = jnp.zeros((experts, 1), F32)
    for k, (choice, b) in enumerate(order):
        position = jnp.sum((before[k * experts : (k + 1) * experts] + base) * ones[k], axis=0, keepdims=True)
        row_out[choice : choice + 1, b * step : (b + 1) * step] = code(picked[k], position)
        base = base + jnp.sum(ones[k], axis=1, keepdims=True)

    pad_images(cot_ref, wide, cot_out)
    rows = cot_out[...].reshape(-1, cot_out.shape[2])
    step = min(512, experts * block)
    per = step // block
    for c in range(chunks):
        for k in range(experts * block // step):
            value = nn(slot_match(row_out, (c * experts + k * per) * block, step), rows).astype(BF16)
            slots_out[k * per : (k + 1) * per, c] = value.reshape(per, block, -1)


def front(rank, cotangent, routes, experts, cap, half, block, chunks):
    rows, width = cotangent.shape
    images = rows // SEQ
    padded = jnp.pad(
        routes.reshape(images, SEQ, 2), ((0, 0), (0, PAD - SEQ), (0, 0)), constant_values=-1
    )
    down = padded.transpose(1, 0, 2).reshape(PAD, images * 2)
    across = padded.reshape(images * PAD, 2).T
    return pl.pallas_call(
        functools.partial(front_kernel, cap=cap, half=half),
        out_shape=(
            jax.ShapeDtypeStruct((images, PAD, width), BF16),
            jax.ShapeDtypeStruct((experts, chunks, block, width), BF16),
            jax.ShapeDtypeStruct(down.shape, jnp.int32),
            jax.ShapeDtypeStruct(across.shape, jnp.int32),
        ),
        in_specs=[pl.BlockSpec(memory_space=pltpu.SMEM)] + [VMEM] * 3,
        out_specs=(VMEM,) * 4,
        scratch_shapes=[wide_scratch(images, width)],
        compiler_params=params(),
        cost_estimate=cost(10),
        name="front",
    )(rank, cotangent, down, across)


def spread_kernel(code_ref, rows_ref, out_ref, *, start, step):
    match = slot_match(code_ref, pl.program_id(0) * step + start, step)
    out_ref[...] = nn(match, rows_ref[...]).astype(BF16).reshape(out_ref.shape)


def spread(code_row, rows, experts, block, chunks, start=0, step=512):
    count, width = rows.shape
    slots = experts * block
    step = min(step, slots)
    per = step // block
    return pl.pallas_call(
        functools.partial(spread_kernel, start=start * slots, step=step),
        out_shape=jax.ShapeDtypeStruct((experts, chunks, block, width), BF16),
        grid=(chunks * slots // step,),
        in_specs=[full((2, count)), full((count, width))],
        out_specs=pl.BlockSpec(
            (per, 1, block, width), lambda i: (i % (experts // per), i // (experts // per), 0, 0)
        ),
        compiler_params=params(),
        cost_estimate=cost(4 * chunks),
        name="spread",
    )(code_row, rows)


def row_mean(v):
    return jnp.mean(v, axis=-1, keepdims=True)


def key_softmax(scores):
    cut = SEQ // 16 * 16
    head, tail = scores[:cut], scores[cut:]
    valid = lax.broadcasted_iota(jnp.int32, tail.shape, 0) < SEQ - cut
    tail = jnp.where(valid, tail, -jnp.inf)
    top = jnp.maximum(jnp.max(head, axis=0, keepdims=True), jnp.max(tail, axis=0, keepdims=True))
    head, tail = jnp.exp(head - top), jnp.exp(tail - top)
    total = jnp.sum(head, axis=0, keepdims=True) + jnp.sum(tail, axis=0, keepdims=True)
    scale = 1.0 / total
    return jnp.concatenate([head * scale, tail * scale], axis=0)


QUAD = 4 * HEAD_DIM


def quad_masks():
    lane = iota((PAD, QUAD), 1)
    return [(lane >= h * HEAD_DIM) & (lane < (h + 1) * HEAD_DIM) for h in range(4)]


def stacked(value, masks):
    return jnp.concatenate([jnp.where(m, value, jnp.zeros_like(value)) for m in masks], axis=0)


def unstacked(value, masks):
    return sum(jnp.where(m, value[h * PAD : (h + 1) * PAD], 0.0) for h, m in enumerate(masks))


def attend_kernel(place_ref, tok_ref, ga_ref, gm_ref, *rest, pieces, own):
    wq, wo, rest = rest[:pieces], rest[pieces : 2 * pieces], rest[2 * pieces :]
    routed_ref, res_ref, qkv_ref, prob_ref, att_ref, wq_all, wo_all, qkv_all, att_all = rest
    batch, _, model = tok_ref.shape
    keep = pl.program_id(0) * batch < own

    @pl.when(pl.program_id(0) == 0)
    def _():
        at = 0
        size = wo[0].shape[0]
        if pieces == 1:
            places = [0]
        else:
            core, small = place_ref[1], wo[1].shape[0]
            places = [0, size + core * small, size + (1 - core) * small]
        for k, start in enumerate(places):
            cols = wo[k].shape[0]
            for j in range(3):
                to = start + j * model
                if k:
                    to = pl.multiple_of(to, 128)
                wq_all[:, pl.ds(to, cols)] = wq[k][j]
            if k:
                start = pl.multiple_of(start, 128)
            wo_all[pl.ds(start, cols), :] = wo[k][...]

    tok = tok_ref[...].reshape(batch * PAD, model).astype(F32)
    center = tok - row_mean(tok)
    normed = (center * lax.rsqrt(row_mean(center * center) + EPS) * ga_ref[...]).astype(BF16)
    value = nn(normed, wq_all[...])
    qkv_all[:, :model] = (value[:, :model] * HEAD_DIM**-0.5).astype(BF16)
    qkv_all[:, model:] = value[:, model:].astype(BF16)
    masks = quad_masks()
    key_ok = iota((4 * PAD, PAD), 1) < SEQ
    for g in range(batch):
        rows = slice(g * PAD, (g + 1) * PAD)
        for quad in range(model // QUAD):
            q, k, v = (qkv_all[rows, j * model + quad * QUAD : j * model + (quad + 1) * QUAD] for j in range(3))
            scores = jnp.where(key_ok, nt(stacked(q, masks), k), -jnp.inf)
            ex = jnp.exp(scores - jnp.max(scores, axis=1, keepdims=True))
            probs = (ex * (1.0 / jnp.sum(ex, axis=1, keepdims=True))).astype(BF16)

            @pl.when(keep)
            def _():
                prob_ref[g, quad] = probs

            mixed = unstacked(nn(probs, v), masks)
            att_all[rows, quad * QUAD : (quad + 1) * QUAD] = mixed.astype(BF16)

    residual = tok + nn(att_all[...], wo_all[...])

    @pl.when(keep)
    def _():
        res_ref[...] = residual.reshape(batch, PAD, model)
        qkv_ref[...] = qkv_all[...].reshape(batch, PAD, 3 * model)
        att_ref[...] = att_all[...].reshape(batch, PAD, model)

    center = residual - row_mean(residual)
    normed = center * lax.rsqrt(row_mean(center * center) + EPS) * gm_ref[...]
    routed_ref[...] = normed.astype(BF16).reshape(batch, PAD, model)


def attend(place, tok_pad, gain_attn, gain_moe, wq, wo, own, batch=2):
    images, _, width = tok_pad.shape
    batch = batch if own % batch == 0 else 1
    pieces = len(wq)
    steps = images // batch

    def image(i, place_ref):
        return (lax.rem(i + place_ref[0] // batch, steps), 0, 0)

    def kept(*shape):
        return pl.BlockSpec(
            (batch,) + shape, lambda i, place_ref: (jnp.minimum(i, own // batch - 1),) + (0,) * len(shape)
        )

    rows = pl.BlockSpec((batch, PAD, width), image)
    probs = (width // QUAD, 4 * PAD, PAD)
    return pl.pallas_call(
        functools.partial(attend_kernel, pieces=pieces, own=own),
        out_shape=(
            jax.ShapeDtypeStruct((images, PAD, width), BF16),
            jax.ShapeDtypeStruct((own, PAD, width), F32),
            jax.ShapeDtypeStruct((own, PAD, 3 * width), BF16),
            jax.ShapeDtypeStruct((own,) + probs, BF16),
            jax.ShapeDtypeStruct((own, PAD, width), BF16),
            jax.ShapeDtypeStruct((width, 3 * width), BF16),
            jax.ShapeDtypeStruct((width, width), BF16),
        ),
        grid_spec=pltpu.PrefetchScalarGridSpec(
            num_scalar_prefetch=1,
            grid=(steps,),
            in_specs=[rows, full((1, width)), full((1, width))] + [full(v.shape) for v in (*wq, *wo)],
            out_specs=(
                rows,
                kept(PAD, width),
                kept(PAD, 3 * width),
                kept(*probs),
                kept(PAD, width),
                full((width, 3 * width)),
                full((width, width)),
            ),
            scratch_shapes=[
                pltpu.VMEM((batch * PAD, 3 * width), BF16),
                pltpu.VMEM((batch * PAD, width), BF16),
            ],
        ),
        compiler_params=params(),
        cost_estimate=cost(25),
        name="attend",
    )(place, tok_pad, gain_attn.reshape(1, -1), gain_moe.reshape(1, -1), *wq, *wo)


def expert_kernel(expert_ref, x_ref, cot_ref, wr_ref, *rest, shards, half, block, chunk, begins, ends, steps):
    w1, w2, rest = rest[:shards], rest[shards : 2 * shards], rest[2 * shards :]
    before, rest = ((), rest) if begins else (rest[: 2 * shards], rest[2 * shards + 1 :])
    (gin_ref, out_ref), given, scratch = rest[:2], rest[2 : 2 + 2 * shards], rest[2 + 2 * shards :]
    sums = list(given)
    if ends and shards > 1:
        sums[1], sums[3] = scratch
    dw1, dw2 = sums[0::1][:shards], sums[shards:]
    expert = expert_ref[0]

    @pl.when(pl.program_id(0) == 0)
    def _():
        for k, ref in enumerate(sums):
            ref[...] = jnp.zeros_like(ref) if begins else before[k][...]

    x = x_ref[...]
    rows, width = x.shape
    cot = cot_ref[...].reshape(rows, width).astype(F32)
    logits = nn(x, wr_ref[...])
    ex = jnp.exp(logits - jnp.max(logits, axis=1, keepdims=True))
    mine = iota(ex.shape, 1) == expert
    gate = jnp.sum(jnp.where(mine, ex, 0.0), axis=1, keepdims=True) / jnp.sum(
        ex, axis=1, keepdims=True
    )
    grad_out = (gate * cot).astype(BF16)
    x_t = x.T
    out = jnp.zeros((rows, width), F32)
    gin = jnp.zeros((rows, width), F32)
    c0 = (2.0 / jnp.pi) ** 0.5
    for s in range(shards):
        hidden = w1[s].shape[1]
        size = min(chunk, hidden)
        for c in range(hidden // size):
            cols = slice(c * size, (c + 1) * size)
            u = nn(x, w1[s][:, cols])
            square = u * u
            t = jnp.tanh(u * (c0 + (c0 * 0.044715) * square))
            h = 0.5 + 0.5 * t
            slope = h + (0.5 * u) * (1.0 - t * t) * (c0 + (3 * c0 * 0.044715) * square)
            active = (u * h).astype(BF16)
            out = out + nn(active, w2[s][cols, :])
            grad_pre = (nt(grad_out, w2[s][cols, :]) * slope).astype(BF16)
            gin = gin + nt(grad_pre, w1[s][:, cols])
            dw2[s][cols, :] += tn(active, grad_out)
            dw1[s][:, cols] += nn(x_t, grad_pre)
    out_ref[...] = (gate * out).astype(BF16).reshape(out_ref.shape)
    gate_grad = jnp.sum(cot * out, axis=1, keepdims=True)
    down, across = iota((block, width), 0), iota((block, width), 1)
    for g in range(rows // block):
        span = slice(g * block, (g + 1) * block)
        line = jnp.sum(jnp.where(down == across, gate_grad[span], 0.0), axis=0, keepdims=True)
        high = line.astype(BF16).astype(F32)
        value = jnp.where(down == half, high, jnp.where(down == half + 1, line - high, gin[span]))
        gin_ref[span, :] = value.astype(BF16)

    if ends and shards > 1:

        @pl.when(pl.program_id(0) == steps - 1)
        def _():
            given[1][...] = sums[1][...].astype(BF16)
            given[3][...] = sums[3][...].astype(BF16)


def experts_step(expert, x, cot, before, number, ends, w_router, w1, w2, half, block, step=512, chunk=512):
    rows, width = x.shape
    shards = len(w1)
    hidden = w1[0].shape[1]
    step = min(step, rows)
    row_spec = pl.BlockSpec((step, width), lambda i, _: (i, 0))
    chunk_spec = pl.BlockSpec((step // block, 1, block, width), lambda i, _: (i, number, 0, 0))
    old = [] if before is None else [*before[1:], before[0]]
    shapes = [(width, hidden)] * shards + [(hidden, width)] * shards

    def once(shape):
        return pl.BlockSpec(shape, lambda *_: (0, 0), pipeline_mode=pl.Buffered(1))

    at = 4 + 2 * shards
    alias = {at + 2 * shards: 1} if old else {}
    if old:
        alias |= {at + k: 2 + k for k in range(0, 2 * shards, shards)}
    return pl.pallas_call(
        functools.partial(
            expert_kernel,
            shards=shards,
            half=half,
            block=block,
            chunk=chunk,
            begins=before is None,
            ends=ends,
            steps=rows // step,
        ),
        out_shape=(jax.ShapeDtypeStruct((rows, width), BF16), jax.ShapeDtypeStruct(cot.shape, BF16))
        + tuple(
            jax.ShapeDtypeStruct(v, BF16 if ends and k % shards else F32) for k, v in enumerate(shapes)
        ),
        grid_spec=pltpu.PrefetchScalarGridSpec(
            num_scalar_prefetch=1,
            grid=(rows // step,),
            in_specs=[row_spec, chunk_spec, full(w_router.shape)]
            + [once((width, hidden))] * shards
            + [once((hidden, width))] * shards
            + ([once(v) for v in shapes] + [pl.BlockSpec(memory_space=pl.ANY)] if old else []),
            out_specs=(row_spec, chunk_spec) + tuple(once(v) for v in shapes),
            scratch_shapes=[pltpu.VMEM(shapes[k], F32) for k in range(1, 2 * shards, 2)]
            if ends and shards > 1
            else [],
        ),
        input_output_aliases=alias,
        compiler_params=params(62),
        cost_estimate=cost(20),
        name="experts",
    )(expert, x, cot, w_router, *w1, *w2, *old)


def collect_kernel(first_ref, code_ref, *rest, numbers, half, block, probs, before):
    chunks = len(numbers)
    parts, rest = rest[:chunks], rest[chunks:]
    old, rest = rest[:before], rest[before:]
    out_ref, rest = rest[0], rest[1:]
    count, width = parts[0].shape
    experts = count // block
    own = out_ref.shape[0]
    rows = own * PAD
    codes = code_ref[...]
    across = iota(codes.shape, 1)
    columns = [
        jnp.concatenate(
            [
                jnp.sum(jnp.where(across == (first_ref[0] + g) * 2 + c, codes, 0), axis=1, keepdims=True)
                for g in range(own)
            ],
            axis=0,
        )
        for c in range(2)
    ]
    lane = iota((rows, count), 1)
    total = old[0][...].reshape(rows, width) if old else None
    grads = None
    for c in range(chunks):
        shift = numbers[c] * count
        match = ((lane + shift == columns[0]) | (lane + shift == columns[1])).astype(BF16)
        value = nn(match, parts[c][...])
        total = value if total is None else total + value
        if probs:
            lines = jnp.zeros((experts, 128), F32)
            for e in range(experts):
                tail = parts[c][e * block + block - 16 : (e + 1) * block, 0:128].astype(F32)
                at = half - (block - 16)
                lines = jnp.where(iota(lines.shape, 0) == e, tail[at : at + 1] + tail[at + 1 : at + 2], lines)
            turned = lines.T[:block]
            slot_grads = jnp.concatenate(
                [jnp.where(iota(turned.shape, 1) == e, turned, 0.0) for e in range(experts)], axis=0
            )
            high = slot_grads.astype(BF16)
            low = (slot_grads - high.astype(F32)).astype(BF16)
            value = nn(match, high) + nn(match, low)
            grads = value if grads is None else grads + value
    out_ref[...] = total.astype(out_ref.dtype).reshape(out_ref.shape)
    if probs:
        for g in range(own):
            value = grads[g * PAD : (g + 1) * PAD].T
            rest[0][g] = value + old[1][g] if old else value


def collect(first, code_col, parts, own, dtype, half, block, probs=False, numbers=None, before=()):
    numbers = tuple(range(len(parts))) if numbers is None else numbers
    count, width = parts[0].shape
    outs = [jax.ShapeDtypeStruct((own, PAD, width), dtype)]
    if probs:
        outs.append(jax.ShapeDtypeStruct((own, count // block, PAD), F32))
    return pl.pallas_call(
        functools.partial(
            collect_kernel, numbers=numbers, half=half, block=block, probs=probs, before=len(before)
        ),
        out_shape=tuple(outs),
        in_specs=[pl.BlockSpec(memory_space=pltpu.SMEM), VMEM] + [VMEM] * (len(parts) + len(before)),
        out_specs=(VMEM,) * len(outs),
        compiler_params=params(),
        cost_estimate=cost(7),
        name="collect",
    )(first, code_col, *parts, *before)


def back_kernel(first_ref, *rest, steps, received):
    (sum_ref, gp_ref), rest = rest[:2], rest[2:]
    more, rest = rest[: 2 * received], rest[2 * received :]
    (res_ref, cot_ref, tok_ref, ga_ref, gm_ref, wrt_ref, wq, wo, qkv_ref, prob_ref, att_ref), rest = rest[:11], rest[11:]
    gtok_ref, pack_ref, dwq, dwo, small, gatt_all, dqkv_all = rest
    experts = wrt_ref.shape[0]
    batch, _, model = res_ref.shape
    rows = batch * PAD
    step = pl.program_id(0)

    @pl.when(step == 0)
    def _():
        for ref in (dwq, dwo, small):
            ref[...] = jnp.zeros_like(ref)

    def flat(ref):
        return ref[...].reshape(rows, -1).astype(F32)

    residual = flat(res_ref)
    center = residual - row_mean(residual)
    scale = lax.rsqrt(row_mean(center * center) + EPS)
    xhat = center * scale
    gm = gm_ref[...]
    routed = (xhat * gm).astype(BF16)
    logits = nt(wrt_ref[...], routed)
    ex = jnp.exp(logits - jnp.max(logits, axis=0, keepdims=True))
    probs = ex / jnp.sum(ex, axis=0, keepdims=True)
    grad_probs = gp_ref[...]
    grad_routed = flat(sum_ref)
    if received:
        grad_routed = grad_routed + flat(more[0])
        grad_probs = grad_probs + more[1][...]
    grad_probs = jnp.concatenate([grad_probs[g] for g in range(batch)], axis=1)
    grad_logits = probs * (grad_probs - jnp.sum(probs * grad_probs, axis=0, keepdims=True))
    high = grad_logits.astype(BF16)
    low = (grad_logits - high.astype(F32)).astype(BF16)
    both = jnp.concatenate([high, low], axis=0)
    new = nn(both, routed)
    small[0:experts, :] += new[:experts] + new[experts:]
    grad_routed = grad_routed + tn(both, jnp.concatenate([wrt_ref[...]] * 2, axis=0))
    small[experts + 1 : experts + 2, :] += jnp.sum(grad_routed * xhat, axis=0, keepdims=True)
    g = grad_routed * gm
    grad_res = flat(cot_ref) + scale * (g - row_mean(g) - xhat * row_mean(g * xhat))
    grad_mixed = grad_res.astype(BF16)
    dwo[...] += tn(att_ref[...].reshape(rows, model), grad_mixed)
    gatt_all[...] = nt(grad_mixed, wo[...]).astype(BF16)

    masks = quad_masks()
    for b in range(batch):
        span = slice(b * PAD, (b + 1) * PAD)
        for quad in range(model // QUAD):
            q, k, v = (
                qkv_ref[b, :, j * model + quad * QUAD : j * model + (quad + 1) * QUAD] for j in range(3)
            )
            grad_heads = stacked(gatt_all[span, quad * QUAD : (quad + 1) * QUAD], masks)
            low_probs = prob_ref[b, quad]
            p = low_probs.astype(F32)
            gw = nt(grad_heads, v)
            ds = (p * (gw - jnp.sum(p * gw, axis=1, keepdims=True))).astype(BF16)
            grad_q = unstacked(nn(ds, k), masks) * HEAD_DIM**-0.5
            grad_k = tn(ds, stacked(q, masks))
            grad_v = tn(low_probs, grad_heads)
            for j, value in enumerate((grad_q, grad_k, grad_v)):
                dqkv_all[span, j * model + quad * QUAD : j * model + (quad + 1) * QUAD] = value.astype(BF16)

    tok = flat(tok_ref)
    center = tok - row_mean(tok)
    tok_scale = lax.rsqrt(row_mean(center * center) + EPS)
    xin = center * tok_scale
    ga = ga_ref[...]
    normed = (xin * ga).astype(BF16)
    dwq[...] += tn(normed, dqkv_all[...])
    grad_normed = nt(dqkv_all[...], wq[...])
    small[experts : experts + 1, :] += jnp.sum(grad_normed * xin, axis=0, keepdims=True)
    h = grad_normed * ga
    grad_tok = grad_res + tok_scale * (h - row_mean(h) - xin * row_mean(h * xin))
    gtok_ref[...] = grad_tok.astype(BF16).reshape(gtok_ref.shape)

    @pl.when(step == steps - 1)
    def _():
        shards = pack_ref.shape[0]
        part = model // shards
        for s in range(shards):
            at = 0
            blocks = [dwq[:, j * model + s * part : j * model + (s + 1) * part] for j in range(3)]
            for value in blocks + [dwo[s * part : (s + 1) * part, :], small[...]]:
                for c in range(value.shape[1] // 256):
                    pack_ref[s, at : at + value.shape[0], :] = value[:, c * 256 : (c + 1) * 256].astype(BF16)
                    at += value.shape[0]
            if at < pack_ref.shape[1]:
                pack_ref[s, at:, :] = jnp.zeros((pack_ref.shape[1] - at, 256), BF16)


def small_rows(experts):
    return -(-(experts + 2) // 16) * 16


def pack_rows(width, part, experts, align):
    rows = 3 * width * (part // 256) + part * (width // 256) + small_rows(experts) * (width // 256)
    return -(-rows // align) * align


def back(first, sums, residual, cot_pad, tok_pad, qkv, probs, att, gain_attn, gain_moe, w_router, wq, wo, shards, align, batch=2):
    own, _, width = residual.shape
    batch = batch if own % batch == 0 else 1
    experts = w_router.shape[1]
    rows = pack_rows(width, width // shards, experts, align)

    def mine(*shape):
        return pl.BlockSpec((batch,) + shape, lambda i, f: (i,) + (0,) * len(shape))

    image = pl.BlockSpec((batch, PAD, width), lambda i, f: (i + f[0] // batch, 0, 0))
    flat = [v for pair in sums for v in pair]
    return pl.pallas_call(
        functools.partial(back_kernel, steps=own // batch, received=len(sums) - 1),
        out_shape=(
            jax.ShapeDtypeStruct((own, PAD, width), BF16),
            jax.ShapeDtypeStruct((shards, rows, 256), BF16),
        ),
        grid_spec=pltpu.PrefetchScalarGridSpec(
            num_scalar_prefetch=1,
            grid=(own // batch,),
            in_specs=[mine(PAD, width), mine(experts, PAD)] * len(sums)
            + [
                mine(PAD, width),
                image,
                image,
                full((1, width)),
                full((1, width)),
                full((experts, width)),
                full(wq.shape),
                full(wo.shape),
                mine(*qkv.shape[1:]),
                mine(*probs.shape[1:]),
                mine(*att.shape[1:]),
            ],
            out_specs=(mine(PAD, width), full((shards, rows, 256))),
            scratch_shapes=[
                pltpu.VMEM((width, 3 * width), F32),
                pltpu.VMEM((width, width), F32),
                pltpu.VMEM((small_rows(experts), width), F32),
                pltpu.VMEM((batch * PAD, width), BF16),
                pltpu.VMEM((batch * PAD, 3 * width), BF16),
            ],
        ),
        compiler_params=params(),
        cost_estimate=cost(16),
        name="back",
    )(
        first,
        *flat,
        residual,
        cot_pad,
        tok_pad,
        gain_attn.reshape(1, -1),
        gain_moe.reshape(1, -1),
        w_router.T,
        wq,
        wo,
        qkv,
        probs,
        att,
    )


def unpad_kernel(first_ref, own_ref, peer_ref, out_ref, wide, *, images):
    own = own_ref.shape[0]
    for i in range(images):
        inner = i % own
        mine = first_ref[0] == i - inner
        value = jnp.where(mine, own_ref[inner].astype(F32), peer_ref[inner].astype(F32))
        wide[i * SEQ : (i + 1) * SEQ, :] = value[:SEQ]
    out_ref[...] = wide[0 : images * SEQ, :].astype(out_ref.dtype)


def unpad(first, own, peer, dtype):
    images, width = 2 * own.shape[0], own.shape[2]
    return pl.pallas_call(
        functools.partial(unpad_kernel, images=images),
        out_shape=jax.ShapeDtypeStruct((images * SEQ, width), dtype),
        in_specs=[pl.BlockSpec(memory_space=pltpu.SMEM), VMEM, VMEM],
        out_specs=VMEM,
        scratch_shapes=[wide_scratch(images, width)],
        compiler_params=params(),
        cost_estimate=cost(2),
        name="unpad",
    )(first, own, peer)


def body(tokens, routes, gain_attn, w_qkv, w_attn_out, gain_moe, w_router, w_expert_in, w_expert_out, cotangent, *, ways, groups):
    tok_rows, width = tokens.shape
    experts = w_router.shape[1]
    cap = max(4, (5 * tok_rows // (2 * experts) + 7) // 8 * 8)
    chunks = 2
    half = -(-cap // (ways * chunks))
    block = -(-(half + 2) // 16) * 16
    slots = experts * block
    images = tok_rows // SEQ
    own = images // ways
    rank = lax.axis_index("tensor")
    expert = lax.axis_index("expert")
    first = (rank * own).astype(jnp.int32).reshape(1)
    swap = [(0, 1), (1, 0)]

    def other(v):
        return lax.ppermute(v, "tensor", swap)

    def shards_of(v, axis):
        if ways == 2:
            return [v, other(v)]
        return [lax.all_gather(v, "tensor", axis=axis, tiled=True)]

    def exchange(rows):
        return lax.all_to_all(rows, "expert", split_axis=0, concat_axis=0, tiled=True)

    def after(v, *others):
        return lax.optimization_barrier((v,) + others)[0]

    def rows_of(v):
        return v.reshape(-1, width)

    def collected(number, parts, dtype, probs=False, numbers=None, before=()):
        return collect(number, code_col, parts, own, dtype, half, block, probs, numbers, before)

    if ways == 2:
        core = expert % 2
        near = [(i, i ^ 1) for i in range(groups)]

        def part_of(v, axis):
            size = v.shape[axis] // 2
            return other(lax.dynamic_slice_in_dim(v, core * size, size, axis))

        got_q, got_o = part_of(w_qkv, 2), part_of(w_attn_out, 0)
    else:
        core = 0 * expert
        wq, wo = shards_of(w_qkv, 2), shards_of(w_attn_out, 0)
    cot_pad, cot_slots, code_col, code_row = front(
        rank.astype(jnp.int32).reshape(1), cotangent, routes, experts, cap, half, block, chunks
    )
    if ways == 2:
        cot_slots, got_q, got_o = lax.optimization_barrier((cot_slots, got_q, got_o))
        wq = [w_qkv, got_q, lax.ppermute(got_q, "expert", near)]
        wo = [w_attn_out, got_o, lax.ppermute(got_o, "expert", near)]
    cot_slots = exchange(cot_slots)
    tok_pad = pad(after(tokens, cot_pad))
    w1 = shards_of(after(w_expert_in[0], wq[-1]), 1)
    if ways == 2:
        cut = w_expert_out.shape[1] // 2
        w2_first = other(after(w_expert_out[0, :cut], wq[-1]))
        w2_rest = other(after(w_expert_out[0, cut:], wq[-1]))
    place = jnp.stack([rank * own, core]).astype(jnp.int32)
    routed, residual, qkv, probs, att, wq, wo = attend(place, tok_pad, gain_attn, gain_moe, wq, wo, own)
    x_slots = []
    for c in range(chunks):
        sent = spread(code_row, rows_of(routed), experts, block, 1, c)
        if c == 0:
            sent, cot_slots = lax.optimization_barrier((sent, cot_slots))
            if ways == 2:
                sent = after(sent, w1[-1], w2_first)
        elif ways == 2:
            sent = after(sent, w2_rest)
        x_slots.append(exchange(sent))
    if ways == 2:
        w2 = [w_expert_out[0], jnp.concatenate([w2_first, w2_rest])]
    else:
        w2 = shards_of(w_expert_out[0], 0)
    gin, more = [], None
    expert_number = expert.astype(jnp.int32).reshape(1)
    for c in range(chunks):
        new, *more = experts_step(
            expert_number, rows_of(x_slots[c]), cot_slots, more, c, c == chunks - 1, w_router, w1, w2, half, block
        )
        gin.append(exchange(new.reshape(experts, block, width)))
    gated, *dw = more
    gin = [rows_of(v) for v in gin]
    if ways == 2:
        there = ((1 - rank) * own).astype(jnp.int32).reshape(1)
        dw1_peer = other(dw[1])
        cut = dw[3].shape[0] // 4
        dw2_peer = [other(dw[3][:cut])]
        start = collected(there, gin[:1], F32, True, (0,))
        mine = collected(first, gin[:1], F32, True, (0,))
        gin[1], *start = lax.optimization_barrier((gin[1], *start, *mine))
        start, mine = start[:2], start[2:]
        sent = collected(there, gin[1:], BF16, True, (1,), start)
        received = tuple(other(v) for v in sent)
        mine = collected(first, gin[1:], F32, True, (1,), mine)
        gated = exchange(after(gated, *sent, dw1_peer, dw2_peer[0]))
        grad_w1 = dw[0] + dw1_peer.astype(F32)
        *received, grad_w1 = lax.optimization_barrier((*received, grad_w1, *mine))[:3]
        sums = [mine, received]
        dw2_peer.append(other(after(dw[3][cut:], *received)))
    else:
        gated = exchange(gated)
        every = [collected(jnp.full((1,), r * own, jnp.int32), gin, F32, True) for r in range(ways)]
        sums = [
            tuple(
                lax.psum_scatter(jnp.stack([v[k] for v in every]).astype(t), "tensor", scatter_dimension=0).astype(F32)
                for k, t in ((0, BF16), (1, F32))
            )
        ]
        grad_w1 = lax.psum_scatter(dw[0].astype(BF16), "tensor", scatter_dimension=1, tiled=True).astype(F32)
        grad_w2 = lax.psum_scatter(dw[1].astype(BF16), "tensor", scatter_dimension=0, tiled=True).astype(F32)
    grad_tok, pack = back(
        first, sums, residual, cot_pad, tok_pad, qkv, probs, att, gain_attn, gain_moe, w_router, wq, wo,
        2 if ways == 2 else 1, groups * 8,
    )

    bits = [1 << b for b in range(groups.bit_length() - 1)]
    if ways == 2:

        def swap_bit(v, bit):
            return lax.ppermute(v, "expert", [(i, i ^ bit) for i in range(groups)])

        def add(a, b):
            return (a.astype(F32) + b.astype(F32)).astype(BF16)

        def halves(v, bit):
            size = v.shape[-2] // 2
            upper = (expert // bit) % 2
            keep = lax.dynamic_slice_in_dim(v, upper * size, size, v.ndim - 2)
            give = lax.dynamic_slice_in_dim(v, (1 - upper) * size, size, v.ndim - 2)
            return keep, give

        pack, grad_tok, gated, dw2_peer[1] = lax.optimization_barrier((pack, grad_tok, gated, dw2_peer[1]))
        gated = [rows_of(gated[:, c]) for c in range(chunks)]
        keep, give = halves(pack, bits[0])
        pack = add(keep, swap_bit(give, bits[0]))
        swapped = other(pack[1])
        (mix_there,) = collected(there, gated, BF16)
        mix_peer = other(mix_there)
        grad_peer = other(after(grad_tok, mix_there))
        (mix_here,) = collected(first, [after(gated[0], mix_there), gated[1]], F32)
        total = add(pack[0], swapped)
        total, mix_here = lax.optimization_barrier((total, mix_here))
        keep, give = halves(total, bits[1])
        total = add(keep, swap_bit(give, bits[1]))
        total, mix_peer = lax.optimization_barrier((total, mix_peer))
        result = (residual + (mix_here + mix_peer.astype(F32))).astype(BF16)
        keep, give = halves(total, bits[2])
        total = add(keep, swap_bit(give, bits[2]))
        total, result, grad_w2 = lax.optimization_barrier((total, result, dw[2] + jnp.concatenate(dw2_peer).astype(F32)))
        result_peer = other(result)
        total = add(total, swap_bit(total, bits[3]))
        total, grad_peer = lax.optimization_barrier((total, grad_peer))

        def gathered(v, bit):
            got = swap_bit(v, bit)
            upper = (expert // bit) % 2 == 1
            return jnp.where(upper, jnp.concatenate([got, v]), jnp.concatenate([v, got]))

        for bit in bits[2:0:-1]:
            total = gathered(total, bit)
        grad_tokens = unpad(first, grad_tok, grad_peer, F32)
        total, grad_tokens, result_peer = lax.optimization_barrier((total, grad_tokens, result_peer))
        total = gathered(total, bits[0])
        result = unpad(first, result, result_peer, BF16)
        total = total.astype(F32)
        part = w_qkv.shape[2]
    else:
        gated = [rows_of(gated[:, c]) for c in range(chunks)]
        every = [collected(jnp.full((1,), r * own, jnp.int32), gated, BF16)[0] for r in range(ways)]
        mixture = lax.psum_scatter(jnp.stack(every), "tensor", scatter_dimension=0).astype(F32)

        def whole(v):
            v = lax.all_gather(v, "tensor", axis=0, tiled=True)
            return v[:, :SEQ].reshape(tok_rows, width)

        result = whole((residual + mixture).astype(BF16))
        grad_tokens = whole(grad_tok).astype(F32)
        total = lax.psum(pack[0], ("expert", "tensor")).astype(F32)
        part = width

    def take(at, rows, cols):
        blocks = [total[at + b * rows : at + (b + 1) * rows] for b in range(cols // 256)]
        return jnp.concatenate(blocks, axis=1) if len(blocks) > 1 else blocks[0]

    step = width * (part // 256)
    grad_w_qkv = jnp.stack([take(j * step, width, part) for j in range(3)])
    grad_w_attn_out = take(3 * step, part, width)
    small = take(3 * step + part * (width // 256), small_rows(experts), width)
    if ways != 2:
        grad_w_qkv = lax.dynamic_slice_in_dim(grad_w_qkv, rank * w_qkv.shape[2], w_qkv.shape[2], 2)
        grad_w_attn_out = lax.dynamic_slice_in_dim(grad_w_attn_out, rank * w_qkv.shape[2], w_qkv.shape[2], 0)
    return (
        result,
        grad_tokens,
        small[experts],
        grad_w_qkv,
        grad_w_attn_out,
        small[experts + 1],
        small[:experts].T,
        grad_w1[None],
        grad_w2[None],
    )


def solution(mesh):
    placed = (
        P("expert", None),
        P("expert", None),
        P(),
        P(None, None, "tensor"),
        P("tensor", None),
        P(),
        P(),
        P("expert", None, "tensor"),
        P("expert", "tensor", None),
        P("expert", None),
    )
    return jax.shard_map(
        functools.partial(body, ways=mesh.shape["tensor"], groups=mesh.shape["expert"]),
        mesh=mesh,
        in_specs=placed,
        out_specs=(
            P("expert", None),
            P("expert", None),
            P(),
            P(None, None, "tensor"),
            P("tensor", None),
            P(),
            P(),
            P("expert", None, "tensor"),
            P("expert", "tensor", None),
        ),
        check_vma=False,
    )
```

```python
import functools

import jax
import jax.numpy as jnp
from jax import lax
from jax.experimental import pallas as pl
from jax.experimental.pallas import tpu as pltpu
from jax.sharding import PartitionSpec as P

HEAD_DIM = 64
SEQ = 197
PAD = 208
EPS = 1e-06
F32 = jnp.float32
BF16 = jnp.bfloat16
VMEM = pl.BlockSpec(memory_space=pltpu.VMEM)


def nn(a, b):
    return lax.dot_general(a, b, (((1,), (0,)), ((), ())), preferred_element_type=F32)


def nt(a, b):
    return lax.dot_general(a, b, (((1,), (1,)), ((), ())), preferred_element_type=F32)


def tn(a, b):
    return lax.dot_general(a, b, (((0,), (0,)), ((), ())), preferred_element_type=F32)


def params(mib=56):
    return pltpu.CompilerParams(vmem_limit_bytes=mib << 20)


def cost(us):
    return pl.CostEstimate(flops=0, bytes_accessed=int(us * 3.69e6), transcendentals=0)


def full(shape):
    return pl.BlockSpec(shape, lambda *_: (0,) * len(shape))


def pad_images(source, wide, target):
    wide[0 : source.shape[0], :] = source[...].astype(F32)
    for i in range(target.shape[0]):
        window = wide[i * SEQ : i * SEQ + PAD, :]
        inside = lax.broadcasted_iota(jnp.int32, window.shape, 0) < SEQ
        target[i] = jnp.where(inside, window, 0.0).astype(BF16)


def pad_kernel(source, target, wide):
    pad_images(source, wide, target)


def wide_scratch(images, width):
    return pltpu.VMEM((-(-((images - 1) * SEQ + PAD) // 16) * 16, width), F32)


def pad(rows):
    images, width = rows.shape[0] // SEQ, rows.shape[1]
    return pl.pallas_call(
        pad_kernel,
        out_shape=jax.ShapeDtypeStruct((images, PAD, width), BF16),
        in_specs=[VMEM],
        out_specs=VMEM,
        scratch_shapes=[wide_scratch(images, width)],
        compiler_params=params(),
        cost_estimate=cost(2),
        name="pad",
    )(rows)


def iota(shape, axis):
    return lax.broadcasted_iota(jnp.int32, shape, axis)


def slot_match(code_ref, start, step):
    slot = iota((step, code_ref.shape[1]), 0) + start
    return ((slot == code_ref[0:1, :]) | (slot == code_ref[1:2, :])).astype(BF16)


def front_kernel(rank_ref, cot_ref, col_ref, row_ref, cot_out, slots_out, col_out, row_out, wide, *, cap, half):
    experts, chunks, block, _ = slots_out.shape
    first_slot = rank_ref[0] * (half * chunks)

    def code(expert, position):
        place = position.astype(jnp.int32) - first_slot
        good = (expert >= 0) & (position < cap) & (place >= 0) & (place < half * chunks)
        slot = expert * block + place
        for c in range(1, chunks):
            slot = jnp.where(place >= c * half, slot + (experts * block - half), slot)
        return jnp.where(good, slot, -1)

    lanes = col_ref.shape[1]
    span = lanes * experts
    routes = col_ref[...]
    spread_lanes = (iota((lanes, span), 1) // experts == iota((lanes, span), 0)).astype(BF16)
    gather_lanes = (iota((span, lanes), 0) // experts == iota((span, lanes), 1)).astype(BF16)
    chosen = nn(routes.astype(F32).astype(BF16), spread_lanes) == (iota((PAD, span), 1) % experts).astype(F32)
    ones = chosen.astype(F32)
    lower = (iota((PAD, PAD), 0) > iota((PAD, PAD), 1)).astype(BF16)
    before = nn(lower, ones.astype(BF16))
    totals = jnp.broadcast_to(jnp.sum(ones, axis=0, keepdims=True), (16, span)).astype(BF16)
    source, target = iota((span, span), 0), iota((span, span), 1)
    order_s = (source // experts % 2) * lanes + source // (2 * experts)
    order_t = (target // experts % 2) * lanes + target // (2 * experts)
    earlier = (source % experts == target % experts) & (order_s < order_t)
    before = before + nn(totals, earlier.astype(BF16))[0:1]
    place = nn((jnp.minimum(before, float(cap)) * ones).astype(BF16), gather_lanes)
    col_out[...] = code(routes, place)

    step = 128
    blocks = row_ref.shape[1] // step
    upper = (iota((step, step), 0) < iota((step, step), 1)).astype(BF16)
    order = [(choice, b) for choice in range(2) for b in range(blocks)]
    picked = [row_ref[choice : choice + 1, b * step : (b + 1) * step] for choice, b in order]
    ones = [(p == iota((experts, step), 0)).astype(F32) for p in picked]
    before = nn(jnp.concatenate(ones, axis=0).astype(BF16), upper)
    base = jnp.zeros((experts, 1), F32)
    for k, (choice, b) in enumerate(order):
        position = jnp.sum((before[k * experts : (k + 1) * experts] + base) * ones[k], axis=0, keepdims=True)
        row_out[choice : choice + 1, b * step : (b + 1) * step] = code(picked[k], position)
        base = base + jnp.sum(ones[k], axis=1, keepdims=True)

    pad_images(cot_ref, wide, cot_out)
    rows = cot_out[...].reshape(-1, cot_out.shape[2])
    step = min(512, experts * block)
    per = step // block
    for c in range(chunks):

        def some_slots(k, _):
            value = nn(slot_match(row_out, (c * experts + k * per) * block, step), rows).astype(BF16)
            slots_out[pl.ds(k * per, per), c] = value.reshape(per, block, -1)
            return 0

        lax.fori_loop(0, experts * block // step, some_slots, 0)


def front(rank, cotangent, routes, experts, cap, half, block, chunks):
    rows, width = cotangent.shape
    images = rows // SEQ
    padded = jnp.pad(
        routes.reshape(images, SEQ, 2), ((0, 0), (0, PAD - SEQ), (0, 0)), constant_values=-1
    )
    down = padded.transpose(1, 0, 2).reshape(PAD, images * 2)
    across = padded.reshape(images * PAD, 2).T
    return pl.pallas_call(
        functools.partial(front_kernel, cap=cap, half=half),
        out_shape=(
            jax.ShapeDtypeStruct((images, PAD, width), BF16),
            jax.ShapeDtypeStruct((experts, chunks, block, width), BF16),
            jax.ShapeDtypeStruct(down.shape, jnp.int32),
            jax.ShapeDtypeStruct(across.shape, jnp.int32),
        ),
        in_specs=[pl.BlockSpec(memory_space=pltpu.SMEM)] + [VMEM] * 3,
        out_specs=(VMEM,) * 4,
        scratch_shapes=[wide_scratch(images, width)],
        compiler_params=params(),
        cost_estimate=cost(10),
        name="front",
    )(rank, cotangent, down, across)


def spread_kernel(code_ref, rows_ref, out_ref, *, start, step):
    match = slot_match(code_ref, pl.program_id(0) * step + start, step)
    out_ref[...] = nn(match, rows_ref[...]).astype(BF16).reshape(out_ref.shape)


def spread(code_row, rows, experts, block, chunks, start=0, step=512):
    count, width = rows.shape
    slots = experts * block
    step = min(step, slots)
    per = step // block
    return pl.pallas_call(
        functools.partial(spread_kernel, start=start * slots, step=step),
        out_shape=jax.ShapeDtypeStruct((experts, chunks, block, width), BF16),
        grid=(chunks * slots // step,),
        in_specs=[full((2, count)), full((count, width))],
        out_specs=pl.BlockSpec(
            (per, 1, block, width), lambda i: (i % (experts // per), i // (experts // per), 0, 0)
        ),
        compiler_params=params(),
        cost_estimate=cost(4 * chunks),
        name="spread",
    )(code_row, rows)


def row_mean(v):
    return jnp.mean(v, axis=-1, keepdims=True)


def key_softmax(scores):
    cut = SEQ // 16 * 16
    head, tail = scores[:cut], scores[cut:]
    valid = lax.broadcasted_iota(jnp.int32, tail.shape, 0) < SEQ - cut
    tail = jnp.where(valid, tail, -jnp.inf)
    top = jnp.maximum(jnp.max(head, axis=0, keepdims=True), jnp.max(tail, axis=0, keepdims=True))
    head, tail = jnp.exp(head - top), jnp.exp(tail - top)
    total = jnp.sum(head, axis=0, keepdims=True) + jnp.sum(tail, axis=0, keepdims=True)
    scale = 1.0 / total
    return jnp.concatenate([head * scale, tail * scale], axis=0)


QUAD = 4 * HEAD_DIM


def quad_masks():
    lane = iota((PAD, QUAD), 1)
    return [(lane >= h * HEAD_DIM) & (lane < (h + 1) * HEAD_DIM) for h in range(4)]


def stacked(value, masks):
    return jnp.concatenate([jnp.where(m, value, jnp.zeros_like(value)) for m in masks], axis=0)


def unstacked(value, masks):
    return sum(jnp.where(m, value[h * PAD : (h + 1) * PAD], 0.0) for h, m in enumerate(masks))


def attend_kernel(place_ref, tok_ref, ga_ref, gm_ref, *rest, pieces, own):
    wq, wo, rest = rest[:pieces], rest[pieces : 2 * pieces], rest[2 * pieces :]
    routed_ref, res_ref, qkv_ref, prob_ref, att_ref, wq_all, wo_all, qkv_all, att_all = rest
    batch, _, model = tok_ref.shape
    keep = pl.program_id(0) * batch < own

    @pl.when(pl.program_id(0) == 0)
    def _():
        at = 0
        size = wo[0].shape[0]
        if pieces == 1:
            places = [0]
        else:
            core, small = place_ref[1], wo[1].shape[0]
            places = [0, size + core * small, size + (1 - core) * small]
        for k, start in enumerate(places):
            cols = wo[k].shape[0]
            for j in range(3):
                to = start + j * model
                if k:
                    to = pl.multiple_of(to, 128)
                wq_all[:, pl.ds(to, cols)] = wq[k][j]
            if k:
                start = pl.multiple_of(start, 128)
            wo_all[pl.ds(start, cols), :] = wo[k][...]

    tok = tok_ref[...].reshape(batch * PAD, model).astype(F32)
    center = tok - row_mean(tok)
    normed = (center * lax.rsqrt(row_mean(center * center) + EPS) * ga_ref[...]).astype(BF16)
    value = nn(normed, wq_all[...])
    qkv_all[:, :model] = (value[:, :model] * HEAD_DIM**-0.5).astype(BF16)
    qkv_all[:, model:] = value[:, model:].astype(BF16)
    masks = quad_masks()
    key_ok = iota((4 * PAD, PAD), 1) < SEQ

    def one_image(g, _):
        rows = pl.ds(pl.multiple_of(g * PAD, PAD), PAD)
        for quad in range(model // QUAD):
            q, k, v = (qkv_all[rows, j * model + quad * QUAD : j * model + (quad + 1) * QUAD] for j in range(3))
            scores = jnp.where(key_ok, nt(stacked(q, masks), k), -jnp.inf)
            ex = jnp.exp(scores - jnp.max(scores, axis=1, keepdims=True))
            probs = (ex * (1.0 / jnp.sum(ex, axis=1, keepdims=True))).astype(BF16)

            @pl.when(keep)
            def _():
                prob_ref[g, quad] = probs

            mixed = unstacked(nn(probs, v), masks)
            att_all[rows, quad * QUAD : (quad + 1) * QUAD] = mixed.astype(BF16)
        return 0

    lax.fori_loop(0, batch, one_image, 0)
    residual = tok + nn(att_all[...], wo_all[...])

    @pl.when(keep)
    def _():
        res_ref[...] = residual.reshape(batch, PAD, model)
        qkv_ref[...] = qkv_all[...].reshape(batch, PAD, 3 * model)
        att_ref[...] = att_all[...].reshape(batch, PAD, model)

    center = residual - row_mean(residual)
    normed = center * lax.rsqrt(row_mean(center * center) + EPS) * gm_ref[...]
    routed_ref[...] = normed.astype(BF16).reshape(batch, PAD, model)


def attend(place, tok_pad, gain_attn, gain_moe, wq, wo, own, batch=2):
    images, _, width = tok_pad.shape
    batch = batch if own % batch == 0 else 1
    pieces = len(wq)
    steps = images // batch

    def image(i, place_ref):
        return (lax.rem(i + place_ref[0] // batch, steps), 0, 0)

    def kept(*shape):
        return pl.BlockSpec(
            (batch,) + shape, lambda i, place_ref: (jnp.minimum(i, own // batch - 1),) + (0,) * len(shape)
        )

    rows = pl.BlockSpec((batch, PAD, width), image)
    probs = (width // QUAD, 4 * PAD, PAD)
    return pl.pallas_call(
        functools.partial(attend_kernel, pieces=pieces, own=own),
        out_shape=(
            jax.ShapeDtypeStruct((images, PAD, width), BF16),
            jax.ShapeDtypeStruct((own, PAD, width), F32),
            jax.ShapeDtypeStruct((own, PAD, 3 * width), BF16),
            jax.ShapeDtypeStruct((own,) + probs, BF16),
            jax.ShapeDtypeStruct((own, PAD, width), BF16),
            jax.ShapeDtypeStruct((width, 3 * width), BF16),
            jax.ShapeDtypeStruct((width, width), BF16),
        ),
        grid_spec=pltpu.PrefetchScalarGridSpec(
            num_scalar_prefetch=1,
            grid=(steps,),
            in_specs=[rows, full((1, width)), full((1, width))] + [full(v.shape) for v in (*wq, *wo)],
            out_specs=(
                rows,
                kept(PAD, width),
                kept(PAD, 3 * width),
                kept(*probs),
                kept(PAD, width),
                full((width, 3 * width)),
                full((width, width)),
            ),
            scratch_shapes=[
                pltpu.VMEM((batch * PAD, 3 * width), BF16),
                pltpu.VMEM((batch * PAD, width), BF16),
            ],
        ),
        compiler_params=params(),
        cost_estimate=cost(25),
        name="attend",
    )(place, tok_pad, gain_attn.reshape(1, -1), gain_moe.reshape(1, -1), *wq, *wo)


def expert_kernel(expert_ref, x_ref, cot_ref, wr_ref, *rest, shards, half, block, chunk, begins, ends, steps):
    w1, w2, rest = rest[:shards], rest[shards : 2 * shards], rest[2 * shards :]
    before, rest = ((), rest) if begins else (rest[: 2 * shards], rest[2 * shards + 1 :])
    (gin_ref, out_ref), given, scratch = rest[:2], rest[2 : 2 + 2 * shards], rest[2 + 2 * shards :]
    (out_sum, gin_sum), scratch = scratch[:2], scratch[2:]
    sums = list(given)
    if ends and shards > 1:
        sums[1], sums[3] = scratch
    dw1, dw2 = sums[0::1][:shards], sums[shards:]
    expert = expert_ref[0]

    @pl.when(pl.program_id(0) == 0)
    def _():
        for k, ref in enumerate(sums):
            ref[...] = jnp.zeros_like(ref) if begins else before[k][...]

    x = x_ref[...]
    rows, width = x.shape
    cot = cot_ref[...].reshape(rows, width).astype(F32)
    logits = nn(x, wr_ref[...])
    ex = jnp.exp(logits - jnp.max(logits, axis=1, keepdims=True))
    mine = iota(ex.shape, 1) == expert
    gate = jnp.sum(jnp.where(mine, ex, 0.0), axis=1, keepdims=True) / jnp.sum(
        ex, axis=1, keepdims=True
    )
    grad_out = (gate * cot).astype(BF16)
    x_t = x.T
    out_sum[...] = jnp.zeros_like(out_sum)
    gin_sum[...] = jnp.zeros_like(gin_sum)
    c0 = (2.0 / jnp.pi) ** 0.5
    for s in range(shards):
        hidden = w1[s].shape[1]
        size = min(chunk, hidden)

        def some_hidden(c, _):
            cols = pl.ds(pl.multiple_of(c * size, size), size)
            u = nn(x, w1[s][:, cols])
            square = u * u
            t = jnp.tanh(u * (c0 + (c0 * 0.044715) * square))
            h = 0.5 + 0.5 * t
            slope = h + (0.5 * u) * (1.0 - t * t) * (c0 + (3 * c0 * 0.044715) * square)
            active = (u * h).astype(BF16)
            out_sum[...] += nn(active, w2[s][cols, :])
            grad_pre = (nt(grad_out, w2[s][cols, :]) * slope).astype(BF16)
            gin_sum[...] += nt(grad_pre, w1[s][:, cols])
            dw2[s][cols, :] += tn(active, grad_out)
            dw1[s][:, cols] += nn(x_t, grad_pre)
            return 0

        lax.fori_loop(0, hidden // size, some_hidden, 0)
    out, gin = out_sum[...], gin_sum[...]
    out_ref[...] = (gate * out).astype(BF16).reshape(out_ref.shape)
    gate_grad = jnp.sum(cot * out, axis=1, keepdims=True)
    down, across = iota((block, width), 0), iota((block, width), 1)
    for g in range(rows // block):
        span = slice(g * block, (g + 1) * block)
        line = jnp.sum(jnp.where(down == across, gate_grad[span], 0.0), axis=0, keepdims=True)
        high = line.astype(BF16).astype(F32)
        value = jnp.where(down == half, high, jnp.where(down == half + 1, line - high, gin[span]))
        gin_ref[span, :] = value.astype(BF16)

    if ends and shards > 1:

        @pl.when(pl.program_id(0) == steps - 1)
        def _():
            given[1][...] = sums[1][...].astype(BF16)
            given[3][...] = sums[3][...].astype(BF16)


def experts_step(expert, x, cot, before, number, ends, w_router, w1, w2, half, block, step=512, chunk=512):
    rows, width = x.shape
    shards = len(w1)
    hidden = w1[0].shape[1]
    step = min(step, rows)
    row_spec = pl.BlockSpec((step, width), lambda i, _: (i, 0))
    chunk_spec = pl.BlockSpec((step // block, 1, block, width), lambda i, _: (i, number, 0, 0))
    old = [] if before is None else [*before[1:], before[0]]
    shapes = [(width, hidden)] * shards + [(hidden, width)] * shards

    def once(shape):
        return pl.BlockSpec(shape, lambda *_: (0, 0), pipeline_mode=pl.Buffered(1))

    at = 4 + 2 * shards
    alias = {at + 2 * shards: 1} if old else {}
    if old:
        alias |= {at + k: 2 + k for k in range(0, 2 * shards, shards)}
    return pl.pallas_call(
        functools.partial(
            expert_kernel,
            shards=shards,
            half=half,
            block=block,
            chunk=chunk,
            begins=before is None,
            ends=ends,
            steps=rows // step,
        ),
        out_shape=(jax.ShapeDtypeStruct((rows, width), BF16), jax.ShapeDtypeStruct(cot.shape, BF16))
        + tuple(
            jax.ShapeDtypeStruct(v, BF16 if ends and k % shards else F32) for k, v in enumerate(shapes)
        ),
        grid_spec=pltpu.PrefetchScalarGridSpec(
            num_scalar_prefetch=1,
            grid=(rows // step,),
            in_specs=[row_spec, chunk_spec, full(w_router.shape)]
            + [once((width, hidden))] * shards
            + [once((hidden, width))] * shards
            + ([once(v) for v in shapes] + [pl.BlockSpec(memory_space=pl.ANY)] if old else []),
            out_specs=(row_spec, chunk_spec) + tuple(once(v) for v in shapes),
            scratch_shapes=[pltpu.VMEM((step, width), F32)] * 2
            + ([pltpu.VMEM(shapes[k], F32) for k in range(1, 2 * shards, 2)] if ends and shards > 1 else []),
        ),
        input_output_aliases=alias,
        compiler_params=params(62),
        cost_estimate=cost(20),
        name="experts",
    )(expert, x, cot, w_router, *w1, *w2, *old)


def collect_kernel(first_ref, code_ref, *rest, numbers, half, block, probs, before):
    chunks = len(numbers)
    parts, rest = rest[:chunks], rest[chunks:]
    old, rest = rest[:before], rest[before:]
    out_ref, rest = rest[0], rest[1:]
    count, width = parts[0].shape
    experts = count // block
    rows = PAD
    codes = code_ref[...]
    across = iota(codes.shape, 1)
    at = (first_ref[0] + pl.program_id(0)) * 2
    columns = [jnp.sum(jnp.where(across == at + c, codes, 0), axis=1, keepdims=True) for c in range(2)]
    lane = iota((rows, count), 1)
    total = old[0][0] if old else None
    grads = None
    for c in range(chunks):
        shift = numbers[c] * count
        match = ((lane + shift == columns[0]) | (lane + shift == columns[1])).astype(BF16)
        value = nn(match, parts[c][...])
        total = value if total is None else total + value
        if probs:
            slot_grads = rest[1 + c]

            @pl.when(pl.program_id(0) == 0)
            def _():
                lines = jnp.zeros((experts, 128), F32)
                for e in range(experts):
                    tail = parts[c][e * block + block - 16 : (e + 1) * block, 0:128].astype(F32)
                    here = half - (block - 16)
                    line = tail[here : here + 1] + tail[here + 1 : here + 2]
                    lines = jnp.where(iota(lines.shape, 0) == e, line, lines)
                turned = lines.T[:block]
                high = turned.astype(BF16).astype(F32)
                both = jnp.concatenate([high, turned - high], axis=1)
                for e in range(experts):
                    own_lane = iota(both.shape, 1) % experts == e
                    slot_grads[e * block : (e + 1) * block, :] = jnp.where(own_lane, both, 0.0).astype(BF16)

            value = nn(match, slot_grads[...])
            grads = value if grads is None else grads + value
    out_ref[0] = total.astype(out_ref.dtype)
    if probs:
        turned = grads.T
        value = turned[:experts] + turned[experts:]
        rest[0][0] = value + old[1][0] if old else value


def collect(first, code_col, parts, own, dtype, half, block, probs=False, numbers=None, before=()):
    numbers = tuple(range(len(parts))) if numbers is None else numbers
    count, width = parts[0].shape
    outs = [jax.ShapeDtypeStruct((own, PAD, width), dtype)]
    if probs:
        outs.append(jax.ShapeDtypeStruct((own, count // block, PAD), F32))
    return pl.pallas_call(
        functools.partial(
            collect_kernel, numbers=numbers, half=half, block=block, probs=probs, before=len(before)
        ),
        out_shape=tuple(outs),
        grid_spec=pltpu.PrefetchScalarGridSpec(
            num_scalar_prefetch=1,
            grid=(own,),
            in_specs=[full(code_col.shape)]
            + [full((count, width))] * len(parts)
            + [pl.BlockSpec((1,) + v.shape[1:], lambda i, f: (i, 0, 0)) for v in before],
            out_specs=tuple(pl.BlockSpec((1,) + v.shape[1:], lambda i, f: (i, 0, 0)) for v in outs),
            scratch_shapes=[pltpu.VMEM((count, 2 * (count // block)), BF16)] * (len(parts) if probs else 0),
        ),
        compiler_params=params(),
        cost_estimate=cost(7),
        name="collect",
    )(first, code_col, *parts, *before)


def back_kernel(first_ref, *rest, steps, received):
    (sum_ref, gp_ref), rest = rest[:2], rest[2:]
    more, rest = rest[: 2 * received], rest[2 * received :]
    (res_ref, cot_ref, tok_ref, ga_ref, gm_ref, wrt_ref, wq, wo, qkv_ref, prob_ref, att_ref), rest = rest[:11], rest[11:]
    gtok_ref, pack_ref, dwq, dwo, small, gatt_all, dqkv_all = rest
    experts = wrt_ref.shape[0]
    batch, _, model = res_ref.shape
    rows = batch * PAD
    step = pl.program_id(0)

    @pl.when(step == 0)
    def _():
        for ref in (dwq, dwo, small):
            ref[...] = jnp.zeros_like(ref)

    def flat(ref):
        return ref[...].reshape(rows, -1).astype(F32)

    residual = flat(res_ref)
    center = residual - row_mean(residual)
    scale = lax.rsqrt(row_mean(center * center) + EPS)
    xhat = center * scale
    gm = gm_ref[...]
    routed = (xhat * gm).astype(BF16)
    logits = nt(wrt_ref[...], routed)
    ex = jnp.exp(logits - jnp.max(logits, axis=0, keepdims=True))
    probs = ex / jnp.sum(ex, axis=0, keepdims=True)
    grad_probs = gp_ref[...]
    grad_routed = flat(sum_ref)
    if received:
        grad_routed = grad_routed + flat(more[0])
        grad_probs = grad_probs + more[1][...]
    grad_probs = jnp.concatenate([grad_probs[g] for g in range(batch)], axis=1)
    grad_logits = probs * (grad_probs - jnp.sum(probs * grad_probs, axis=0, keepdims=True))
    high = grad_logits.astype(BF16)
    low = (grad_logits - high.astype(F32)).astype(BF16)
    both = jnp.concatenate([high, low], axis=0)
    new = nn(both, routed)
    small[0:experts, :] += new[:experts] + new[experts:]
    grad_routed = grad_routed + tn(both, jnp.concatenate([wrt_ref[...]] * 2, axis=0))
    small[experts + 1 : experts + 2, :] += jnp.sum(grad_routed * xhat, axis=0, keepdims=True)
    g = grad_routed * gm
    grad_res = flat(cot_ref) + scale * (g - row_mean(g) - xhat * row_mean(g * xhat))
    grad_mixed = grad_res.astype(BF16)
    dwo[...] += tn(att_ref[...].reshape(rows, model), grad_mixed)
    gatt_all[...] = nt(grad_mixed, wo[...]).astype(BF16)

    masks = quad_masks()

    def one_image(b, _):
        span = pl.ds(pl.multiple_of(b * PAD, PAD), PAD)
        for quad in range(model // QUAD):
            q, k, v = (
                qkv_ref[b, :, j * model + quad * QUAD : j * model + (quad + 1) * QUAD] for j in range(3)
            )
            grad_heads = stacked(gatt_all[span, quad * QUAD : (quad + 1) * QUAD], masks)
            low_probs = prob_ref[b, quad]
            p = low_probs.astype(F32)
            gw = nt(grad_heads, v)
            ds = (p * (gw - jnp.sum(p * gw, axis=1, keepdims=True))).astype(BF16)
            grad_q = unstacked(nn(ds, k), masks) * HEAD_DIM**-0.5
            grad_k = tn(ds, stacked(q, masks))
            grad_v = tn(low_probs, grad_heads)
            for j, value in enumerate((grad_q, grad_k, grad_v)):
                dqkv_all[span, j * model + quad * QUAD : j * model + (quad + 1) * QUAD] = value.astype(BF16)
        return 0

    lax.fori_loop(0, batch, one_image, 0)
    tok = flat(tok_ref)
    center = tok - row_mean(tok)
    tok_scale = lax.rsqrt(row_mean(center * center) + EPS)
    xin = center * tok_scale
    ga = ga_ref[...]
    normed = (xin * ga).astype(BF16)
    dwq[...] += tn(normed, dqkv_all[...])
    grad_normed = nt(dqkv_all[...], wq[...])
    small[experts : experts + 1, :] += jnp.sum(grad_normed * xin, axis=0, keepdims=True)
    h = grad_normed * ga
    grad_tok = grad_res + tok_scale * (h - row_mean(h) - xin * row_mean(h * xin))
    gtok_ref[...] = grad_tok.astype(BF16).reshape(gtok_ref.shape)

    @pl.when(step == steps - 1)
    def _():
        shards = pack_ref.shape[0]
        part = model // shards
        for s in range(shards):
            at = 0
            blocks = [dwq[:, j * model + s * part : j * model + (s + 1) * part] for j in range(3)]
            for value in blocks + [dwo[s * part : (s + 1) * part, :], small[...]]:
                for c in range(value.shape[1] // 256):
                    pack_ref[s, at : at + value.shape[0], :] = value[:, c * 256 : (c + 1) * 256].astype(BF16)
                    at += value.shape[0]
            if at < pack_ref.shape[1]:
                pack_ref[s, at:, :] = jnp.zeros((pack_ref.shape[1] - at, 256), BF16)


def small_rows(experts):
    return -(-(experts + 2) // 16) * 16


def pack_rows(width, part, experts, align):
    rows = 3 * width * (part // 256) + part * (width // 256) + small_rows(experts) * (width // 256)
    return -(-rows // align) * align


def back(first, sums, residual, cot_pad, tok_pad, qkv, probs, att, gain_attn, gain_moe, w_router, wq, wo, shards, align, batch=2):
    own, _, width = residual.shape
    batch = batch if own % batch == 0 else 1
    experts = w_router.shape[1]
    rows = pack_rows(width, width // shards, experts, align)

    def mine(*shape):
        return pl.BlockSpec((batch,) + shape, lambda i, f: (i,) + (0,) * len(shape))

    image = pl.BlockSpec((batch, PAD, width), lambda i, f: (i + f[0] // batch, 0, 0))
    flat = [v for pair in sums for v in pair]
    return pl.pallas_call(
        functools.partial(back_kernel, steps=own // batch, received=len(sums) - 1),
        out_shape=(
            jax.ShapeDtypeStruct((own, PAD, width), BF16),
            jax.ShapeDtypeStruct((shards, rows, 256), BF16),
        ),
        grid_spec=pltpu.PrefetchScalarGridSpec(
            num_scalar_prefetch=1,
            grid=(own // batch,),
            in_specs=[mine(PAD, width), mine(experts, PAD)] * len(sums)
            + [
                mine(PAD, width),
                image,
                image,
                full((1, width)),
                full((1, width)),
                full((experts, width)),
                full(wq.shape),
                full(wo.shape),
                mine(*qkv.shape[1:]),
                mine(*probs.shape[1:]),
                mine(*att.shape[1:]),
            ],
            out_specs=(mine(PAD, width), full((shards, rows, 256))),
            scratch_shapes=[
                pltpu.VMEM((width, 3 * width), F32),
                pltpu.VMEM((width, width), F32),
                pltpu.VMEM((small_rows(experts), width), F32),
                pltpu.VMEM((batch * PAD, width), BF16),
                pltpu.VMEM((batch * PAD, 3 * width), BF16),
            ],
        ),
        compiler_params=params(),
        cost_estimate=cost(16),
        name="back",
    )(
        first,
        *flat,
        residual,
        cot_pad,
        tok_pad,
        gain_attn.reshape(1, -1),
        gain_moe.reshape(1, -1),
        w_router.T,
        wq,
        wo,
        qkv,
        probs,
        att,
    )


def unpad_kernel(first_ref, own_ref, peer_ref, out_ref, wide, *, images):
    own = own_ref.shape[0]
    for i in range(images):
        inner = i % own
        mine = first_ref[0] == i - inner
        value = jnp.where(mine, own_ref[inner].astype(F32), peer_ref[inner].astype(F32))
        wide[i * SEQ : (i + 1) * SEQ, :] = value[:SEQ]
    out_ref[...] = wide[0 : images * SEQ, :].astype(out_ref.dtype)


def unpad(first, own, peer, dtype):
    images, width = 2 * own.shape[0], own.shape[2]
    return pl.pallas_call(
        functools.partial(unpad_kernel, images=images),
        out_shape=jax.ShapeDtypeStruct((images * SEQ, width), dtype),
        in_specs=[pl.BlockSpec(memory_space=pltpu.SMEM), VMEM, VMEM],
        out_specs=VMEM,
        scratch_shapes=[wide_scratch(images, width)],
        compiler_params=params(),
        cost_estimate=cost(2),
        name="unpad",
    )(first, own, peer)


def body(tokens, routes, gain_attn, w_qkv, w_attn_out, gain_moe, w_router, w_expert_in, w_expert_out, cotangent, *, ways, groups):
    tok_rows, width = tokens.shape
    experts = w_router.shape[1]
    cap = max(4, (5 * tok_rows // (2 * experts) + 7) // 8 * 8)
    chunks = 2
    half = -(-cap // (ways * chunks))
    block = -(-(half + 2) // 16) * 16
    slots = experts * block
    images = tok_rows // SEQ
    own = images // ways
    rank = lax.axis_index("tensor")
    expert = lax.axis_index("expert")
    first = (rank * own).astype(jnp.int32).reshape(1)
    swap = [(0, 1), (1, 0)]

    def other(v):
        return lax.ppermute(v, "tensor", swap)

    def shards_of(v, axis):
        if ways == 2:
            return [v, other(v)]
        return [lax.all_gather(v, "tensor", axis=axis, tiled=True)]

    def exchange(rows):
        return lax.all_to_all(rows, "expert", split_axis=0, concat_axis=0, tiled=True)

    def after(v, *others):
        return lax.optimization_barrier((v,) + others)[0]

    def rows_of(v):
        return v.reshape(-1, width)

    def collected(number, parts, dtype, probs=False, numbers=None, before=()):
        return collect(number, code_col, parts, own, dtype, half, block, probs, numbers, before)

    if ways == 2:
        core = expert % 2
        near = [(i, i ^ 1) for i in range(groups)]

        def part_of(v, axis):
            size = v.shape[axis] // 2
            return other(lax.dynamic_slice_in_dim(v, core * size, size, axis))

        got_q, got_o = part_of(w_qkv, 2), part_of(w_attn_out, 0)
    else:
        core = 0 * expert
        wq, wo = shards_of(w_qkv, 2), shards_of(w_attn_out, 0)
    cot_pad, cot_slots, code_col, code_row = front(
        rank.astype(jnp.int32).reshape(1), cotangent, routes, experts, cap, half, block, chunks
    )
    if ways == 2:
        cot_slots, got_q, got_o = lax.optimization_barrier((cot_slots, got_q, got_o))
        wq = [w_qkv, got_q, lax.ppermute(got_q, "expert", near)]
        wo = [w_attn_out, got_o, lax.ppermute(got_o, "expert", near)]
    cot_slots = exchange(cot_slots)
    tok_pad = pad(after(tokens, cot_pad))
    w1 = shards_of(after(w_expert_in[0], wq[-1]), 1)
    if ways == 2:
        cut = w_expert_out.shape[1] // 2
        w2_first = other(after(w_expert_out[0, :cut], wq[-1]))
        w2_rest = other(after(w_expert_out[0, cut:], wq[-1]))
    place = jnp.stack([rank * own, core]).astype(jnp.int32)
    routed, residual, qkv, probs, att, wq, wo = attend(place, tok_pad, gain_attn, gain_moe, wq, wo, own)
    x_slots = []
    for c in range(chunks):
        sent = spread(code_row, rows_of(routed), experts, block, 1, c)
        if c == 0:
            sent, cot_slots = lax.optimization_barrier((sent, cot_slots))
            if ways == 2:
                sent = after(sent, w1[-1], w2_first)
        elif ways == 2:
            sent = after(sent, w2_rest)
        x_slots.append(exchange(sent))
    if ways == 2:
        w2 = [w_expert_out[0], jnp.concatenate([w2_first, w2_rest])]
    else:
        w2 = shards_of(w_expert_out[0], 0)
    gin, more = [], None
    expert_number = expert.astype(jnp.int32).reshape(1)
    for c in range(chunks):
        new, *more = experts_step(
            expert_number, rows_of(x_slots[c]), cot_slots, more, c, c == chunks - 1, w_router, w1, w2, half, block
        )
        gin.append(exchange(new.reshape(experts, block, width)))
    gated, *dw = more
    gin = [rows_of(v) for v in gin]
    if ways == 2:
        there = ((1 - rank) * own).astype(jnp.int32).reshape(1)
        dw1_peer = other(dw[1])
        cut = dw[3].shape[0] // 4
        dw2_peer = [other(dw[3][:cut])]
        start = collected(there, gin[:1], F32, True, (0,))
        mine = collected(first, gin[:1], F32, True, (0,))
        gin[1], *start = lax.optimization_barrier((gin[1], *start, *mine))
        start, mine = start[:2], start[2:]
        sent = collected(there, gin[1:], BF16, True, (1,), start)
        received = tuple(other(v) for v in sent)
        mine = collected(first, gin[1:], F32, True, (1,), mine)
        gated = exchange(after(gated, *sent, dw1_peer, dw2_peer[0]))
        grad_w1 = dw[0] + dw1_peer.astype(F32)
        *received, grad_w1 = lax.optimization_barrier((*received, grad_w1, *mine))[:3]
        sums = [mine, received]
        dw2_peer.append(other(after(dw[3][cut:], *received)))
    else:
        gated = exchange(gated)
        every = [collected(jnp.full((1,), r * own, jnp.int32), gin, F32, True) for r in range(ways)]
        sums = [
            tuple(
                lax.psum_scatter(jnp.stack([v[k] for v in every]).astype(t), "tensor", scatter_dimension=0).astype(F32)
                for k, t in ((0, BF16), (1, F32))
            )
        ]
        grad_w1 = lax.psum_scatter(dw[0].astype(BF16), "tensor", scatter_dimension=1, tiled=True).astype(F32)
        grad_w2 = lax.psum_scatter(dw[1].astype(BF16), "tensor", scatter_dimension=0, tiled=True).astype(F32)
    grad_tok, pack = back(
        first, sums, residual, cot_pad, tok_pad, qkv, probs, att, gain_attn, gain_moe, w_router, wq, wo,
        2 if ways == 2 else 1, groups * 8,
    )

    bits = [1 << b for b in range(groups.bit_length() - 1)]
    if ways == 2:

        def swap_bit(v, bit):
            return lax.ppermute(v, "expert", [(i, i ^ bit) for i in range(groups)])

        def add(a, b):
            return (a.astype(F32) + b.astype(F32)).astype(BF16)

        def halves(v, bit):
            size = v.shape[-2] // 2
            upper = (expert // bit) % 2
            keep = lax.dynamic_slice_in_dim(v, upper * size, size, v.ndim - 2)
            give = lax.dynamic_slice_in_dim(v, (1 - upper) * size, size, v.ndim - 2)
            return keep, give

        pack, grad_tok, gated, dw2_peer[1] = lax.optimization_barrier((pack, grad_tok, gated, dw2_peer[1]))
        gated = [rows_of(gated[:, c]) for c in range(chunks)]
        keep, give = halves(pack, bits[0])
        pack = add(keep, swap_bit(give, bits[0]))
        swapped = other(pack[1])
        (mix_there,) = collected(there, gated, BF16)
        mix_peer = other(mix_there)
        grad_peer = other(after(grad_tok, mix_there))
        (mix_here,) = collected(first, [after(gated[0], mix_there), gated[1]], F32)
        total = add(pack[0], swapped)
        total, mix_here = lax.optimization_barrier((total, mix_here))
        keep, give = halves(total, bits[1])
        total = add(keep, swap_bit(give, bits[1]))
        total, mix_peer = lax.optimization_barrier((total, mix_peer))
        result = (residual + (mix_here + mix_peer.astype(F32))).astype(BF16)
        keep, give = halves(total, bits[2])
        total = add(keep, swap_bit(give, bits[2]))
        total, result, grad_w2 = lax.optimization_barrier((total, result, dw[2] + jnp.concatenate(dw2_peer).astype(F32)))
        result_peer = other(result)
        total = add(total, swap_bit(total, bits[3]))
        total, grad_peer = lax.optimization_barrier((total, grad_peer))

        def gathered(v, bit):
            got = swap_bit(v, bit)
            upper = (expert // bit) % 2 == 1
            return jnp.where(upper, jnp.concatenate([got, v]), jnp.concatenate([v, got]))

        for bit in bits[2:0:-1]:
            total = gathered(total, bit)
        grad_tokens = unpad(first, grad_tok, grad_peer, F32)
        total, grad_tokens, result_peer = lax.optimization_barrier((total, grad_tokens, result_peer))
        total = gathered(total, bits[0])
        result = unpad(first, result, result_peer, BF16)
        total = total.astype(F32)
        part = w_qkv.shape[2]
    else:
        gated = [rows_of(gated[:, c]) for c in range(chunks)]
        every = [collected(jnp.full((1,), r * own, jnp.int32), gated, BF16)[0] for r in range(ways)]
        mixture = lax.psum_scatter(jnp.stack(every), "tensor", scatter_dimension=0).astype(F32)

        def whole(v):
            v = lax.all_gather(v, "tensor", axis=0, tiled=True)
            return v[:, :SEQ].reshape(tok_rows, width)

        result = whole((residual + mixture).astype(BF16))
        grad_tokens = whole(grad_tok).astype(F32)
        total = lax.psum(pack[0], ("expert", "tensor")).astype(F32)
        part = width

    def take(at, rows, cols):
        blocks = [total[at + b * rows : at + (b + 1) * rows] for b in range(cols // 256)]
        return jnp.concatenate(blocks, axis=1) if len(blocks) > 1 else blocks[0]

    step = width * (part // 256)
    grad_w_qkv = jnp.stack([take(j * step, width, part) for j in range(3)])
    grad_w_attn_out = take(3 * step, part, width)
    small = take(3 * step + part * (width // 256), small_rows(experts), width)
    if ways != 2:
        grad_w_qkv = lax.dynamic_slice_in_dim(grad_w_qkv, rank * w_qkv.shape[2], w_qkv.shape[2], 2)
        grad_w_attn_out = lax.dynamic_slice_in_dim(grad_w_attn_out, rank * w_qkv.shape[2], w_qkv.shape[2], 0)
    return (
        result,
        grad_tokens,
        small[experts],
        grad_w_qkv,
        grad_w_attn_out,
        small[experts + 1],
        small[:experts].T,
        grad_w1[None],
        grad_w2[None],
    )


def solution(mesh):
    placed = (
        P("expert", None),
        P("expert", None),
        P(),
        P(None, None, "tensor"),
        P("tensor", None),
        P(),
        P(),
        P("expert", None, "tensor"),
        P("expert", "tensor", None),
        P("expert", None),
    )
    return jax.shard_map(
        functools.partial(body, ways=mesh.shape["tensor"], groups=mesh.shape["expert"]),
        mesh=mesh,
        in_specs=placed,
        out_specs=(
            P("expert", None),
            P("expert", None),
            P(),
            P(None, None, "tensor"),
            P("tensor", None),
            P(),
            P(),
            P("expert", None, "tensor"),
            P("expert", "tensor", None),
        ),
        check_vma=False,
    )
```

```python
import functools

import jax
import jax.numpy as jnp
from jax import lax
from jax.experimental import pallas as pl
from jax.experimental.pallas import tpu as pltpu
from jax.sharding import PartitionSpec as P

HEAD_DIM = 64
SEQ = 197
PAD = 208
EPS = 1e-06
F32 = jnp.float32
BF16 = jnp.bfloat16
VMEM = pl.BlockSpec(memory_space=pltpu.VMEM)


def nn(a, b):
    return lax.dot_general(a, b, (((1,), (0,)), ((), ())), preferred_element_type=F32)


def nt(a, b):
    return lax.dot_general(a, b, (((1,), (1,)), ((), ())), preferred_element_type=F32)


def tn(a, b):
    return lax.dot_general(a, b, (((0,), (0,)), ((), ())), preferred_element_type=F32)


def params(mib=56):
    return pltpu.CompilerParams(vmem_limit_bytes=mib << 20)


def cost(us):
    return pl.CostEstimate(flops=0, bytes_accessed=int(us * 3.69e6), transcendentals=0)


def full(shape):
    return pl.BlockSpec(shape, lambda *_: (0,) * len(shape))


def pad_images(source, wide, target):
    wide[0 : source.shape[0], :] = source[...].astype(F32)

    def one_image(i, _):
        off = lax.rem(i * SEQ, 8)
        window = wide[pl.ds(pl.multiple_of(i * SEQ - off, 8), PAD + 8), :]
        window = pltpu.roll(window, lax.rem(PAD + 8 - off, PAD + 8), 0)[:PAD]
        target[i] = jnp.where(iota(window.shape, 0) < SEQ, window, 0.0).astype(BF16)
        return 0

    lax.fori_loop(0, target.shape[0], one_image, 0)


def pad_kernel(source, target, wide):
    pad_images(source, wide, target)


def wide_scratch(images, width):
    return pltpu.VMEM((-(-((images - 1) * SEQ + PAD + 8) // 16) * 16, width), F32)


def pad(rows):
    images, width = rows.shape[0] // SEQ, rows.shape[1]
    return pl.pallas_call(
        pad_kernel,
        out_shape=jax.ShapeDtypeStruct((images, PAD, width), BF16),
        in_specs=[VMEM],
        out_specs=VMEM,
        scratch_shapes=[wide_scratch(images, width)],
        compiler_params=params(),
        cost_estimate=cost(2),
        name="pad",
    )(rows)


def iota(shape, axis):
    return lax.broadcasted_iota(jnp.int32, shape, axis)


def slot_match(code_ref, start, step):
    slot = iota((step, code_ref.shape[1]), 0) + start
    return ((slot == code_ref[0:1, :]) | (slot == code_ref[1:2, :])).astype(BF16)


def front_kernel(rank_ref, cot_ref, col_ref, row_ref, cot_out, slots_out, col_out, row_out, wide, *, cap, half):
    experts, chunks, block, _ = slots_out.shape
    first_slot = rank_ref[0] * (half * chunks)

    def code(expert, position):
        place = position.astype(jnp.int32) - first_slot
        good = (expert >= 0) & (position < cap) & (place >= 0) & (place < half * chunks)
        slot = expert * block + place
        for c in range(1, chunks):
            slot = jnp.where(place >= c * half, slot + (experts * block - half), slot)
        return jnp.where(good, slot, -1)

    lanes = col_ref.shape[1]
    span = lanes * experts
    routes = col_ref[...]
    spread_lanes = (iota((lanes, span), 1) // experts == iota((lanes, span), 0)).astype(BF16)
    gather_lanes = (iota((span, lanes), 0) // experts == iota((span, lanes), 1)).astype(BF16)
    chosen = nn(routes.astype(F32).astype(BF16), spread_lanes) == (iota((PAD, span), 1) % experts).astype(F32)
    ones = chosen.astype(F32)
    lower = (iota((PAD, PAD), 0) > iota((PAD, PAD), 1)).astype(BF16)
    before = nn(lower, ones.astype(BF16))
    totals = jnp.broadcast_to(jnp.sum(ones, axis=0, keepdims=True), (16, span)).astype(BF16)
    source, target = iota((span, span), 0), iota((span, span), 1)
    order_s = (source // experts % 2) * lanes + source // (2 * experts)
    order_t = (target // experts % 2) * lanes + target // (2 * experts)
    earlier = (source % experts == target % experts) & (order_s < order_t)
    before = before + nn(totals, earlier.astype(BF16))[0:1]
    place = nn((jnp.minimum(before, float(cap)) * ones).astype(BF16), gather_lanes)
    col_out[...] = code(routes, place)

    step = 128
    blocks = row_ref.shape[1] // step
    upper = (iota((step, step), 0) < iota((step, step), 1)).astype(BF16)
    order = [(choice, b) for choice in range(2) for b in range(blocks)]
    picked = [row_ref[choice : choice + 1, b * step : (b + 1) * step] for choice, b in order]
    ones = [(p == iota((experts, step), 0)).astype(F32) for p in picked]
    before = nn(jnp.concatenate(ones, axis=0).astype(BF16), upper)
    base = jnp.zeros((experts, 1), F32)
    for k, (choice, b) in enumerate(order):
        position = jnp.sum((before[k * experts : (k + 1) * experts] + base) * ones[k], axis=0, keepdims=True)
        row_out[choice : choice + 1, b * step : (b + 1) * step] = code(picked[k], position)
        base = base + jnp.sum(ones[k], axis=1, keepdims=True)

    pad_images(cot_ref, wide, cot_out)
    rows = cot_out[...].reshape(-1, cot_out.shape[2])
    step = min(512, experts * block)
    per = step // block
    blocks = experts // per

    def some_slots(k, _):
        value = nn(slot_match(row_out, k * step, step), rows).astype(BF16)
        slots_out[pl.ds(lax.rem(k, blocks) * per, per), lax.div(k, blocks)] = value.reshape(per, block, -1)
        return 0

    lax.fori_loop(0, chunks * blocks, some_slots, 0)


def front(rank, cotangent, routes, experts, cap, half, block, chunks):
    rows, width = cotangent.shape
    images = rows // SEQ
    padded = jnp.pad(
        routes.reshape(images, SEQ, 2), ((0, 0), (0, PAD - SEQ), (0, 0)), constant_values=-1
    )
    down = padded.transpose(1, 0, 2).reshape(PAD, images * 2)
    across = padded.reshape(images * PAD, 2).T
    return pl.pallas_call(
        functools.partial(front_kernel, cap=cap, half=half),
        out_shape=(
            jax.ShapeDtypeStruct((images, PAD, width), BF16),
            jax.ShapeDtypeStruct((experts, chunks, block, width), BF16),
            jax.ShapeDtypeStruct(down.shape, jnp.int32),
            jax.ShapeDtypeStruct(across.shape, jnp.int32),
        ),
        in_specs=[pl.BlockSpec(memory_space=pltpu.SMEM)] + [VMEM] * 3,
        out_specs=(VMEM,) * 4,
        scratch_shapes=[wide_scratch(images, width)],
        compiler_params=params(),
        cost_estimate=cost(10),
        name="front",
    )(rank, cotangent, down, across)


def spread_kernel(code_ref, rows_ref, *outs, step, steps):
    number = pl.program_id(0)
    value = nn(slot_match(code_ref, number * step, step), rows_ref[...]).astype(BF16)
    for c, out_ref in enumerate(outs):

        @pl.when(lax.div(number, steps) == c)
        def _():
            out_ref[...] = value.reshape(out_ref.shape)


def spread(code_row, rows, experts, block, chunks, step=512):
    count, width = rows.shape
    step = min(step, experts * block)
    per, steps = step // block, experts * block // step

    def place(c):
        return lambda i: (jnp.clip(i - c * steps, 0, steps - 1), 0, 0)

    return pl.pallas_call(
        functools.partial(spread_kernel, step=step, steps=steps),
        out_shape=(jax.ShapeDtypeStruct((experts, block, width), BF16),) * chunks,
        grid=(chunks * steps,),
        in_specs=[full((2, count)), full((count, width))],
        out_specs=tuple(pl.BlockSpec((per, block, width), place(c)) for c in range(chunks)),
        compiler_params=params(),
        cost_estimate=cost(9),
        name="spread",
    )(code_row, rows)


def row_mean(v):
    return jnp.mean(v, axis=-1, keepdims=True)


def key_softmax(scores):
    cut = SEQ // 16 * 16
    head, tail = scores[:cut], scores[cut:]
    valid = lax.broadcasted_iota(jnp.int32, tail.shape, 0) < SEQ - cut
    tail = jnp.where(valid, tail, -jnp.inf)
    top = jnp.maximum(jnp.max(head, axis=0, keepdims=True), jnp.max(tail, axis=0, keepdims=True))
    head, tail = jnp.exp(head - top), jnp.exp(tail - top)
    total = jnp.sum(head, axis=0, keepdims=True) + jnp.sum(tail, axis=0, keepdims=True)
    scale = 1.0 / total
    return jnp.concatenate([head * scale, tail * scale], axis=0)


QUAD = 4 * HEAD_DIM


def quad_masks():
    lane = iota((PAD, QUAD), 1)
    return [(lane >= h * HEAD_DIM) & (lane < (h + 1) * HEAD_DIM) for h in range(4)]


def stacked(value, masks):
    return jnp.concatenate([jnp.where(m, value, jnp.zeros_like(value)) for m in masks], axis=0)


def unstacked(value, masks):
    return sum(jnp.where(m, value[h * PAD : (h + 1) * PAD], 0.0) for h, m in enumerate(masks))


def attend_kernel(place_ref, tok_ref, ga_ref, gm_ref, *rest, pieces, own):
    wq, wo, rest = rest[:pieces], rest[pieces : 2 * pieces], rest[2 * pieces :]
    routed_ref, res_ref, qkv_ref, prob_ref, att_ref, wq_all, wo_all, qkv_all, att_all = rest
    batch, _, model = tok_ref.shape
    keep = pl.program_id(0) * batch < own

    @pl.when(pl.program_id(0) == 0)
    def _():
        at = 0
        size = wo[0].shape[0]
        if pieces == 1:
            places = [0]
        else:
            core, small = place_ref[1], wo[1].shape[0]
            places = [0, size + core * small, size + (1 - core) * small]
        for k, start in enumerate(places):
            cols = wo[k].shape[0]
            for j in range(3):
                to = start + j * model
                if k:
                    to = pl.multiple_of(to, 128)
                wq_all[:, pl.ds(to, cols)] = wq[k][j]
            if k:
                start = pl.multiple_of(start, 128)
            wo_all[pl.ds(start, cols), :] = wo[k][...]

    tok = tok_ref[...].reshape(batch * PAD, model).astype(F32)
    center = tok - row_mean(tok)
    normed = (center * lax.rsqrt(row_mean(center * center) + EPS) * ga_ref[...]).astype(BF16)
    value = nn(normed, wq_all[...])
    qkv_all[:, :model] = (value[:, :model] * HEAD_DIM**-0.5).astype(BF16)
    qkv_all[:, model:] = value[:, model:].astype(BF16)
    masks = quad_masks()
    key_ok = iota((4 * PAD, PAD), 1) < SEQ
    for g in range(batch):
        rows = slice(g * PAD, (g + 1) * PAD)
        for quad in range(model // QUAD):
            q, k, v = (qkv_all[rows, j * model + quad * QUAD : j * model + (quad + 1) * QUAD] for j in range(3))
            scores = jnp.where(key_ok, nt(stacked(q, masks), k), -jnp.inf)
            ex = jnp.exp(scores - jnp.max(scores, axis=1, keepdims=True))
            probs = (ex * (1.0 / jnp.sum(ex, axis=1, keepdims=True))).astype(BF16)

            @pl.when(keep)
            def _():
                prob_ref[g, quad] = probs

            mixed = unstacked(nn(probs, v), masks)
            att_all[rows, quad * QUAD : (quad + 1) * QUAD] = mixed.astype(BF16)

    residual = tok + nn(att_all[...], wo_all[...])

    @pl.when(keep)
    def _():
        res_ref[...] = residual.reshape(batch, PAD, model)
        qkv_ref[...] = qkv_all[...].reshape(batch, PAD, 3 * model)
        att_ref[...] = att_all[...].reshape(batch, PAD, model)

    center = residual - row_mean(residual)
    normed = center * lax.rsqrt(row_mean(center * center) + EPS) * gm_ref[...]
    routed_ref[...] = normed.astype(BF16).reshape(batch, PAD, model)


def attend(place, tok_pad, gain_attn, gain_moe, wq, wo, own, batch=2):
    images, _, width = tok_pad.shape
    batch = batch if own % batch == 0 else 1
    pieces = len(wq)
    steps = images // batch

    def image(i, place_ref):
        return (lax.rem(i + place_ref[0] // batch, steps), 0, 0)

    def kept(*shape):
        return pl.BlockSpec(
            (batch,) + shape, lambda i, place_ref: (jnp.minimum(i, own // batch - 1),) + (0,) * len(shape)
        )

    rows = pl.BlockSpec((batch, PAD, width), image)
    probs = (width // QUAD, 4 * PAD, PAD)
    return pl.pallas_call(
        functools.partial(attend_kernel, pieces=pieces, own=own),
        out_shape=(
            jax.ShapeDtypeStruct((images, PAD, width), BF16),
            jax.ShapeDtypeStruct((own, PAD, width), F32),
            jax.ShapeDtypeStruct((own, PAD, 3 * width), BF16),
            jax.ShapeDtypeStruct((own,) + probs, BF16),
            jax.ShapeDtypeStruct((own, PAD, width), BF16),
            jax.ShapeDtypeStruct((width, 3 * width), BF16),
            jax.ShapeDtypeStruct((width, width), BF16),
        ),
        grid_spec=pltpu.PrefetchScalarGridSpec(
            num_scalar_prefetch=1,
            grid=(steps,),
            in_specs=[rows, full((1, width)), full((1, width))] + [full(v.shape) for v in (*wq, *wo)],
            out_specs=(
                rows,
                kept(PAD, width),
                kept(PAD, 3 * width),
                kept(*probs),
                kept(PAD, width),
                full((width, 3 * width)),
                full((width, width)),
            ),
            scratch_shapes=[
                pltpu.VMEM((batch * PAD, 3 * width), BF16),
                pltpu.VMEM((batch * PAD, width), BF16),
            ],
        ),
        compiler_params=params(),
        cost_estimate=cost(25),
        name="attend",
    )(place, tok_pad, gain_attn.reshape(1, -1), gain_moe.reshape(1, -1), *wq, *wo)


def expert_kernel(expert_ref, x_ref, cot_ref, wr_ref, *rest, parts, half, block, chunk, begins, ends):
    weights, rest = rest[: len(parts)], rest[len(parts) :]
    w1, w2, dw1, dw2, out_sum, gin_sum, low1, low2, load_sems, store_sems = rest[-10:]
    shards, _, hidden = w1.shape
    before, rest = ((), rest) if begins else (rest[: 2 * shards], rest[2 * shards + 1 :])
    gin_ref, out_ref = rest[:2]
    given = rest[2 : 2 + 2 * shards]
    expert = expert_ref[0]
    size = min(chunk, hidden)
    blocks = hidden // size

    loads = [(s, ref, (w1, w2)[k].at[s, pl.ds(at, ref.shape[0])]) for (k, s, at), ref in zip(parts, weights)]
    loads += [(k % shards, ref, (dw1, dw2)[k // shards].at[k % shards]) for k, ref in enumerate(before)]
    loads = [(s, pltpu.make_async_copy(a, b, load_sems.at[k])) for k, (s, a, b) in enumerate(loads)]
    for s in range(shards):
        for where, copy in loads:
            if where == s:
                copy.start()

    def stores(s, c):
        cols = pl.ds(pl.multiple_of(c * size, size), size)
        if ends and s:
            sources = low1.at[:, cols], low2.at[cols, :]
        else:
            sources = dw1.at[s, :, cols], dw2.at[s, cols, :]
        targets = given[s].at[:, cols], given[shards + s].at[cols, :]
        return [
            pltpu.make_async_copy(a, b, store_sems.at[(s * blocks + c) * 2 + k])
            for k, (a, b) in enumerate(zip(sources, targets))
        ]

    x = x_ref[...]
    rows, width = x.shape
    cot = cot_ref[...].reshape(rows, width).astype(F32)
    logits = nn(x, wr_ref[...])
    ex = jnp.exp(logits - jnp.max(logits, axis=1, keepdims=True))
    mine = iota(ex.shape, 1) == expert
    gate = jnp.sum(jnp.where(mine, ex, 0.0), axis=1, keepdims=True) / jnp.sum(
        ex, axis=1, keepdims=True
    )
    grad_out = (gate * cot).astype(BF16)
    x_t = x.T
    out_sum[...] = jnp.zeros_like(out_sum)
    gin_sum[...] = jnp.zeros_like(gin_sum)
    c0 = (2.0 / jnp.pi) ** 0.5

    def some_hidden(k, _):
        for s in range(shards):

            @pl.when(k == s * blocks)
            def _():
                for where, copy in loads:
                    if where == s:
                        copy.wait()

        shard, at = lax.div(k, blocks), lax.rem(k, blocks)
        cols = pl.ds(pl.multiple_of(at * size, size), size)
        u = nn(x, w1[shard, :, cols])
        square = u * u
        t = jnp.tanh(u * (c0 + (c0 * 0.044715) * square))
        h = 0.5 + 0.5 * t
        slope = h + (0.5 * u) * (1.0 - t * t) * (c0 + (3 * c0 * 0.044715) * square)
        active = (u * h).astype(BF16)
        out_sum[...] += nn(active, w2[shard, cols, :])
        grad_pre = (nt(grad_out, w2[shard, cols, :]) * slope).astype(BF16)
        gin_sum[...] += nt(grad_pre, w1[shard, :, cols])
        first, second = nn(x_t, grad_pre), tn(active, grad_out)
        dw1[shard, :, cols] = first if begins else dw1[shard, :, cols] + first
        dw2[shard, cols, :] = second if begins else dw2[shard, cols, :] + second
        for s in range(shards):

            @pl.when(shard == s)
            def _():
                if ends and s:
                    low1[:, cols] = dw1[shard, :, cols].astype(BF16)
                    low2[cols, :] = dw2[shard, cols, :].astype(BF16)
                for copy in stores(s, at):
                    copy.start()

        return 0

    lax.fori_loop(0, shards * blocks, some_hidden, 0)
    out, gin = out_sum[...], gin_sum[...]
    out_ref[...] = (gate * out).astype(BF16).reshape(out_ref.shape)
    gate_grad = jnp.sum(cot * out, axis=1, keepdims=True)
    down, across = iota((block, width), 0), iota((block, width), 1)
    for g in range(rows // block):
        span = slice(g * block, (g + 1) * block)
        line = jnp.sum(jnp.where(down == across, gate_grad[span], 0.0), axis=0, keepdims=True)
        high = line.astype(BF16).astype(F32)
        value = jnp.where(down == half, high, jnp.where(down == half + 1, line - high, gin[span]))
        gin_ref[span, :] = value.astype(BF16)
    for s in range(shards):
        for c in range(blocks):
            for copy in stores(s, c):
                copy.wait()


def experts_step(expert, x, cot, before, number, ends, w_router, w1, w2, half, block, chunk=512):
    rows, width = x.shape
    shards = len(w1)
    hidden = w1[0][0].shape[1]
    row_spec = full((rows, width))
    chunk_spec = pl.BlockSpec((rows // block, 1, block, width), lambda i, _: (0, number, 0, 0))
    anywhere = pl.BlockSpec(memory_space=pl.ANY)
    old = [] if before is None else [*before[1:], before[0]]
    parts, weights = [], []
    for k, shards_of_one in enumerate((w1, w2)):
        for s, pieces in enumerate(shards_of_one):
            at = 0
            for piece in pieces:
                parts.append((k, s, at))
                weights.append(piece)
                at += piece.shape[0]
    shapes = [(width, hidden)] * shards + [(hidden, width)] * shards
    low = (8, 128) if shards == 1 or not ends else None
    at = 4 + len(weights)
    alias = {at + 2 * shards: 1} if old else {}
    return pl.pallas_call(
        functools.partial(
            expert_kernel,
            parts=parts,
            half=half,
            block=block,
            chunk=chunk,
            begins=before is None,
            ends=ends,
        ),
        out_shape=(jax.ShapeDtypeStruct((rows, width), BF16), jax.ShapeDtypeStruct(cot.shape, BF16))
        + tuple(
            jax.ShapeDtypeStruct(v, BF16 if ends and k % shards else F32) for k, v in enumerate(shapes)
        ),
        grid_spec=pltpu.PrefetchScalarGridSpec(
            num_scalar_prefetch=1,
            grid=(1,),
            in_specs=[row_spec, chunk_spec, full(w_router.shape)] + [anywhere] * (len(weights) + len(old)),
            out_specs=(row_spec, chunk_spec) + (anywhere,) * len(shapes),
            scratch_shapes=[
                pltpu.VMEM((shards, width, hidden), BF16),
                pltpu.VMEM((shards, hidden, width), BF16),
                pltpu.VMEM((shards, width, hidden), F32),
                pltpu.VMEM((shards, hidden, width), F32),
                pltpu.VMEM((rows, width), F32),
                pltpu.VMEM((rows, width), F32),
                pltpu.VMEM(low or (width, hidden), BF16),
                pltpu.VMEM(low or (hidden, width), BF16),
                pltpu.SemaphoreType.DMA((len(weights) + 2 * shards,)),
                pltpu.SemaphoreType.DMA((2 * shards * hidden // min(chunk, hidden),)),
            ],
        ),
        input_output_aliases=alias,
        compiler_params=params(62),
        cost_estimate=cost(20),
        name="experts",
    )(expert, x, cot, w_router, *weights, *old)


def collect_kernel(first_ref, code_ref, *rest, numbers, half, block, probs, before):
    chunks = len(numbers)
    parts, rest = rest[:chunks], rest[chunks:]
    old, rest = rest[:before], rest[before:]
    out_ref, rest = rest[0], rest[1:]
    count, width = parts[0].shape
    experts = count // block
    rows = PAD
    codes = code_ref[...]
    across = iota(codes.shape, 1)
    at = (first_ref[0] + pl.program_id(0)) * 2
    columns = [jnp.sum(jnp.where(across == at + c, codes, 0), axis=1, keepdims=True) for c in range(2)]
    lane = iota((rows, count), 1)
    total = old[0][0] if old else None
    grads = None
    for c in range(chunks):
        shift = numbers[c] * count
        match = ((lane + shift == columns[0]) | (lane + shift == columns[1])).astype(BF16)
        value = nn(match, parts[c][...])
        total = value if total is None else total + value
        if probs:
            slot_grads = rest[1 + c]

            @pl.when(pl.program_id(0) == 0)
            def _():
                lines = jnp.zeros((experts, 128), F32)
                for e in range(experts):
                    tail = parts[c][e * block + block - 16 : (e + 1) * block, 0:128].astype(F32)
                    here = half - (block - 16)
                    line = tail[here : here + 1] + tail[here + 1 : here + 2]
                    lines = jnp.where(iota(lines.shape, 0) == e, line, lines)
                turned = lines.T[:block]
                high = turned.astype(BF16).astype(F32)
                both = jnp.concatenate([high, turned - high], axis=1)
                for e in range(experts):
                    own_lane = iota(both.shape, 1) % experts == e
                    slot_grads[e * block : (e + 1) * block, :] = jnp.where(own_lane, both, 0.0).astype(BF16)

            value = nn(match, slot_grads[...])
            grads = value if grads is None else grads + value
    out_ref[0] = total.astype(out_ref.dtype)
    if probs:
        turned = grads.T
        value = turned[:experts] + turned[experts:]
        rest[0][0] = value + old[1][0] if old else value


def collect(first, code_col, parts, own, dtype, half, block, probs=False, numbers=None, before=()):
    numbers = tuple(range(len(parts))) if numbers is None else numbers
    count, width = parts[0].shape
    outs = [jax.ShapeDtypeStruct((own, PAD, width), dtype)]
    if probs:
        outs.append(jax.ShapeDtypeStruct((own, count // block, PAD), F32))
    return pl.pallas_call(
        functools.partial(
            collect_kernel, numbers=numbers, half=half, block=block, probs=probs, before=len(before)
        ),
        out_shape=tuple(outs),
        grid_spec=pltpu.PrefetchScalarGridSpec(
            num_scalar_prefetch=1,
            grid=(own,),
            in_specs=[full(code_col.shape)]
            + [full((count, width))] * len(parts)
            + [pl.BlockSpec((1,) + v.shape[1:], lambda i, f: (i + f[0], 0, 0)) for v in before],
            out_specs=tuple(pl.BlockSpec((1,) + v.shape[1:], lambda i, f: (i, 0, 0)) for v in outs),
            scratch_shapes=[pltpu.VMEM((count, 2 * (count // block)), BF16)] * (len(parts) if probs else 0),
        ),
        compiler_params=params(),
        cost_estimate=cost(7),
        name="collect",
    )(first, code_col, *parts, *before)


def back_kernel(first_ref, *rest, steps, received):
    (sum_ref, gp_ref), rest = rest[:2], rest[2:]
    more, rest = rest[: 2 * received], rest[2 * received :]
    (res_ref, cot_ref, tok_ref, ga_ref, gm_ref, wrt_ref, wq, wo, qkv_ref, prob_ref, att_ref), rest = rest[:11], rest[11:]
    gtok_ref, pack_ref, dwq, dwo, small, gatt_all, dqkv_all = rest
    experts = wrt_ref.shape[0]
    batch, _, model = res_ref.shape
    rows = batch * PAD
    step = pl.program_id(0)

    @pl.when(step == 0)
    def _():
        for ref in (dwq, dwo, small):
            ref[...] = jnp.zeros_like(ref)

    def flat(ref):
        return ref[...].reshape(rows, -1).astype(F32)

    residual = flat(res_ref)
    center = residual - row_mean(residual)
    scale = lax.rsqrt(row_mean(center * center) + EPS)
    xhat = center * scale
    gm = gm_ref[...]
    routed = (xhat * gm).astype(BF16)
    logits = nt(wrt_ref[...], routed)
    ex = jnp.exp(logits - jnp.max(logits, axis=0, keepdims=True))
    probs = ex / jnp.sum(ex, axis=0, keepdims=True)
    grad_probs = gp_ref[...]
    grad_routed = flat(sum_ref)
    if received:
        grad_routed = grad_routed + flat(more[0])
        grad_probs = grad_probs + more[1][...]
    grad_probs = jnp.concatenate([grad_probs[g] for g in range(batch)], axis=1)
    grad_logits = probs * (grad_probs - jnp.sum(probs * grad_probs, axis=0, keepdims=True))
    high = grad_logits.astype(BF16)
    low = (grad_logits - high.astype(F32)).astype(BF16)
    both = jnp.concatenate([high, low], axis=0)
    new = nn(both, routed)
    small[0:experts, :] += new[:experts] + new[experts:]
    grad_routed = grad_routed + tn(both, jnp.concatenate([wrt_ref[...]] * 2, axis=0))
    small[experts + 1 : experts + 2, :] += jnp.sum(grad_routed * xhat, axis=0, keepdims=True)
    g = grad_routed * gm
    grad_res = flat(cot_ref) + scale * (g - row_mean(g) - xhat * row_mean(g * xhat))
    grad_mixed = grad_res.astype(BF16)
    dwo[...] += tn(att_ref[...].reshape(rows, model), grad_mixed)
    gatt_all[...] = nt(grad_mixed, wo[...]).astype(BF16)

    masks = quad_masks()

    def one_image(b, _):
        span = pl.ds(pl.multiple_of(b * PAD, PAD), PAD)
        for quad in range(model // QUAD):
            q, k, v = (
                qkv_ref[b, :, j * model + quad * QUAD : j * model + (quad + 1) * QUAD] for j in range(3)
            )
            grad_heads = stacked(gatt_all[span, quad * QUAD : (quad + 1) * QUAD], masks)
            low_probs = prob_ref[b, quad]
            p = low_probs.astype(F32)
            gw = nt(grad_heads, v)
            ds = (p * (gw - jnp.sum(p * gw, axis=1, keepdims=True))).astype(BF16)
            grad_q = unstacked(nn(ds, k), masks) * HEAD_DIM**-0.5
            grad_k = tn(ds, stacked(q, masks))
            grad_v = tn(low_probs, grad_heads)
            for j, value in enumerate((grad_q, grad_k, grad_v)):
                dqkv_all[span, j * model + quad * QUAD : j * model + (quad + 1) * QUAD] = value.astype(BF16)
        return 0

    lax.fori_loop(0, batch, one_image, 0)
    tok = flat(tok_ref)
    center = tok - row_mean(tok)
    tok_scale = lax.rsqrt(row_mean(center * center) + EPS)
    xin = center * tok_scale
    ga = ga_ref[...]
    normed = (xin * ga).astype(BF16)
    dwq[...] += tn(normed, dqkv_all[...])
    grad_normed = nt(dqkv_all[...], wq[...])
    small[experts : experts + 1, :] += jnp.sum(grad_normed * xin, axis=0, keepdims=True)
    h = grad_normed * ga
    grad_tok = grad_res + tok_scale * (h - row_mean(h) - xin * row_mean(h * xin))
    gtok_ref[...] = grad_tok.astype(BF16).reshape(gtok_ref.shape)

    @pl.when(step == steps - 1)
    def _():
        shards = pack_ref.shape[0]
        part = model // shards
        for s in range(shards):
            at = 0
            blocks = [dwq[:, j * model + s * part : j * model + (s + 1) * part] for j in range(3)]
            for value in blocks + [dwo[s * part : (s + 1) * part, :], small[...]]:
                for c in range(value.shape[1] // 256):
                    pack_ref[s, at : at + value.shape[0], :] = value[:, c * 256 : (c + 1) * 256].astype(BF16)
                    at += value.shape[0]
            if at < pack_ref.shape[1]:
                pack_ref[s, at:, :] = jnp.zeros((pack_ref.shape[1] - at, 256), BF16)


def small_rows(experts):
    return -(-(experts + 2) // 16) * 16


def pack_rows(width, part, experts, align):
    rows = 3 * width * (part // 256) + part * (width // 256) + small_rows(experts) * (width // 256)
    return -(-rows // align) * align


def back(first, sums, residual, cot_pad, tok_pad, qkv, probs, att, gain_attn, gain_moe, w_router, wq, wo, shards, align, batch=2):
    own, _, width = residual.shape
    batch = batch if own % batch == 0 else 1
    experts = w_router.shape[1]
    rows = pack_rows(width, width // shards, experts, align)

    def mine(*shape):
        return pl.BlockSpec((batch,) + shape, lambda i, f: (i,) + (0,) * len(shape))

    image = pl.BlockSpec((batch, PAD, width), lambda i, f: (i + f[0] // batch, 0, 0))
    flat = [v for pair in sums for v in pair]
    return pl.pallas_call(
        functools.partial(back_kernel, steps=own // batch, received=len(sums) - 1),
        out_shape=(
            jax.ShapeDtypeStruct((own, PAD, width), BF16),
            jax.ShapeDtypeStruct((shards, rows, 256), BF16),
        ),
        grid_spec=pltpu.PrefetchScalarGridSpec(
            num_scalar_prefetch=1,
            grid=(own // batch,),
            in_specs=[mine(PAD, width), mine(experts, PAD)] * len(sums)
            + [
                mine(PAD, width),
                image,
                image,
                full((1, width)),
                full((1, width)),
                full((experts, width)),
                full(wq.shape),
                full(wo.shape),
                mine(*qkv.shape[1:]),
                mine(*probs.shape[1:]),
                mine(*att.shape[1:]),
            ],
            out_specs=(mine(PAD, width), full((shards, rows, 256))),
            scratch_shapes=[
                pltpu.VMEM((width, 3 * width), F32),
                pltpu.VMEM((width, width), F32),
                pltpu.VMEM((small_rows(experts), width), F32),
                pltpu.VMEM((batch * PAD, width), BF16),
                pltpu.VMEM((batch * PAD, 3 * width), BF16),
            ],
        ),
        compiler_params=params(),
        cost_estimate=cost(16),
        name="back",
    )(
        first,
        *flat,
        residual,
        cot_pad,
        tok_pad,
        gain_attn.reshape(1, -1),
        gain_moe.reshape(1, -1),
        w_router.T,
        wq,
        wo,
        qkv,
        probs,
        att,
    )


def unpad_kernel(first_ref, own_ref, peer_ref, out_ref, wide, *, images):
    own = own_ref.shape[0]

    def one_image(i, _):
        inner = lax.rem(i, own)
        mine = first_ref[0] == i - inner
        value = jnp.where(mine, own_ref[inner].astype(F32), peer_ref[inner].astype(F32))
        off = lax.rem(i * SEQ, 8)
        span = pl.ds(pl.multiple_of(i * SEQ - off, 8), PAD + 8)
        value = pltpu.roll(jnp.concatenate([value, jnp.zeros((8, value.shape[1]), F32)], axis=0), off, 0)
        wide[span, :] = jnp.where(iota(value.shape, 0) < off, wide[span, :], value)
        return 0

    lax.fori_loop(0, images, one_image, 0)
    out_ref[...] = wide[0 : images * SEQ, :].astype(out_ref.dtype)


def unpad(first, own, peer, dtype):
    images, width = 2 * own.shape[0], own.shape[2]
    return pl.pallas_call(
        functools.partial(unpad_kernel, images=images),
        out_shape=jax.ShapeDtypeStruct((images * SEQ, width), dtype),
        in_specs=[pl.BlockSpec(memory_space=pltpu.SMEM), VMEM, VMEM],
        out_specs=VMEM,
        scratch_shapes=[wide_scratch(images, width)],
        compiler_params=params(),
        cost_estimate=cost(2),
        name="unpad",
    )(first, own, peer)


def body(tokens, routes, gain_attn, w_qkv, w_attn_out, gain_moe, w_router, w_expert_in, w_expert_out, cotangent, *, ways, groups):
    tok_rows, width = tokens.shape
    experts = w_router.shape[1]
    cap = max(4, (5 * tok_rows // (2 * experts) + 7) // 8 * 8)
    chunks = 2
    half = -(-cap // (ways * chunks))
    block = -(-(half + 2) // 16) * 16
    slots = experts * block
    images = tok_rows // SEQ
    own = images // ways
    rank = lax.axis_index("tensor")
    expert = lax.axis_index("expert")
    first = (rank * own).astype(jnp.int32).reshape(1)
    swap = [(0, 1), (1, 0)]

    def other(v):
        return lax.ppermute(v, "tensor", swap)

    def shards_of(v, axis):
        if ways == 2:
            return [v, other(v)]
        return [lax.all_gather(v, "tensor", axis=axis, tiled=True)]

    def exchange(rows):
        return lax.all_to_all(rows, "expert", split_axis=0, concat_axis=0, tiled=True)

    def after(v, *others):
        return lax.optimization_barrier((v,) + others)[0]

    def rows_of(v):
        return v.reshape(-1, width)

    def collected(number, parts, dtype, probs=False, numbers=None, before=()):
        return collect(number, code_col, parts, own, dtype, half, block, probs, numbers, before)

    if ways == 2:
        core = expert % 2
        near = [(i, i ^ 1) for i in range(groups)]

        def part_of(v, axis):
            size = v.shape[axis] // 2
            return other(lax.dynamic_slice_in_dim(v, core * size, size, axis))

    else:
        core = 0 * expert
        wq, wo = shards_of(w_qkv, 2), shards_of(w_attn_out, 0)
    cot_pad, cot_slots, code_col, code_row = front(
        rank.astype(jnp.int32).reshape(1), cotangent, routes, experts, cap, half, block, chunks
    )
    tok_pad = pad(after(tokens, cot_pad))
    if ways == 2:
        got_q, got_o = part_of(after(w_qkv, cot_slots), 2), part_of(after(w_attn_out, cot_slots), 0)
        got_q, got_o, tok_pad = lax.optimization_barrier((got_q, got_o, tok_pad))
        wq = [w_qkv, got_q, lax.ppermute(got_q, "expert", near)]
        wo = [w_attn_out, got_o, lax.ppermute(got_o, "expert", near)]
    cot_slots = exchange(cot_slots)
    w1 = shards_of(after(w_expert_in[0], wq[-1], wo[-1]), 1)
    if ways == 2:
        cut = w_expert_out.shape[1] // 4
        w2_first = other(after(w_expert_out[0, :cut], wq[-1], wo[-1]))
        w2_rest = other(after(w_expert_out[0, cut:], wq[-1], wo[-1]))
    place = jnp.stack([rank * own, core]).astype(jnp.int32)
    routed, residual, qkv, probs, att, wq, wo = attend(place, tok_pad, gain_attn, gain_moe, wq, wo, own)
    sent, x_slots = spread(code_row, rows_of(routed), experts, block, chunks), []
    for c in range(chunks):
        rows = sent[c]
        if c == 0:
            rows, cot_slots = lax.optimization_barrier((rows, cot_slots))
            if ways == 2:
                rows = after(rows, w1[-1], w2_first)
        elif ways == 2:
            rows = after(rows, w2_rest)
        x_slots.append(exchange(rows))
    if ways == 2:
        w1 = [[v] for v in w1]
        w2 = [[w_expert_out[0]], [w2_first, w2_rest]]
    else:
        w1 = [w1]
        w2 = [shards_of(w_expert_out[0], 0)]
    gin, more = [], None
    expert_number = expert.astype(jnp.int32).reshape(1)
    for c in range(chunks):
        new, *more = experts_step(
            expert_number, rows_of(x_slots[c]), cot_slots, more, c, c == chunks - 1, w_router, w1, w2, half, block
        )
        gin.append(exchange(new.reshape(experts, block, width)))
    gated, *dw = more
    gin = [rows_of(v) for v in gin]
    if ways == 2:
        there = ((1 - rank) * own).astype(jnp.int32).reshape(1)
        dw1_peer = other(dw[1])
        cut = dw[3].shape[0] // 4
        dw2_peer = [other(dw[3][:cut])]
        zero = jnp.zeros((1,), jnp.int32)
        start = collect(zero, code_col, gin[:1], images, F32, half, block, True, (0,))
        gin[1], *start = lax.optimization_barrier((gin[1], *start))
        sent = collected(there, gin[1:], BF16, True, (1,), start)
        received = tuple(other(v) for v in sent)
        mine = collected(first, gin[1:], F32, True, (1,), start)
        gated = exchange(after(gated, *sent, dw1_peer, dw2_peer[0]))
        grad_w1 = dw[0] + dw1_peer.astype(F32)
        *received, grad_w1 = lax.optimization_barrier((*received, grad_w1, *mine))[:3]
        sums = [mine, received]
        dw2_peer.append(other(after(dw[3][cut:], *received)))
    else:
        gated = exchange(gated)
        every = [collected(jnp.full((1,), r * own, jnp.int32), gin, F32, True) for r in range(ways)]
        sums = [
            tuple(
                lax.psum_scatter(jnp.stack([v[k] for v in every]).astype(t), "tensor", scatter_dimension=0).astype(F32)
                for k, t in ((0, BF16), (1, F32))
            )
        ]
        grad_w1 = lax.psum_scatter(dw[0].astype(BF16), "tensor", scatter_dimension=1, tiled=True).astype(F32)
        grad_w2 = lax.psum_scatter(dw[1].astype(BF16), "tensor", scatter_dimension=0, tiled=True).astype(F32)
    grad_tok, pack = back(
        first, sums, residual, cot_pad, tok_pad, qkv, probs, att, gain_attn, gain_moe, w_router, wq, wo,
        2 if ways == 2 else 1, groups * 8,
    )

    bits = [1 << b for b in range(groups.bit_length() - 1)]
    if ways == 2:

        def swap_bit(v, bit):
            return lax.ppermute(v, "expert", [(i, i ^ bit) for i in range(groups)])

        def add(a, b):
            return (a.astype(F32) + b.astype(F32)).astype(BF16)

        def halves(v, bit):
            size = v.shape[-2] // 2
            upper = (expert // bit) % 2
            keep = lax.dynamic_slice_in_dim(v, upper * size, size, v.ndim - 2)
            give = lax.dynamic_slice_in_dim(v, (1 - upper) * size, size, v.ndim - 2)
            return keep, give

        pack, grad_tok, gated, dw2_peer[1] = lax.optimization_barrier((pack, grad_tok, gated, dw2_peer[1]))
        grad_peer = other(grad_tok)
        gated = [rows_of(gated[:, c]) for c in range(chunks)]
        (mix,) = collect(zero, code_col, gated, images, BF16, half, block)
        mix_there = lax.dynamic_slice_in_dim(mix, (1 - rank) * own, own, 0)
        mix_here = lax.dynamic_slice_in_dim(mix, rank * own, own, 0)
        for bit in bits[:2]:
            keep, give = halves(pack, bit)
            pack = add(keep, swap_bit(give, bit))
        pack, grad_peer, mix_there, mix_here, grad_w2 = lax.optimization_barrier(
            (pack, grad_peer, mix_there, mix_here, dw[2] + jnp.concatenate(dw2_peer).astype(F32))
        )
        swapped = other(pack[1])
        mix_peer = other(after(mix_there, pack))
        total = add(pack[0], swapped)

        def gathered(v, bit):
            got = swap_bit(v, bit)
            upper = (expert // bit) % 2 == 1
            return jnp.where(upper, jnp.concatenate([got, v]), jnp.concatenate([v, got]))

        grad_tokens = unpad(first, grad_tok, grad_peer, F32)
        keep, give = halves(total, bits[2])
        total = add(keep, swap_bit(give, bits[2]))
        total = add(total, swap_bit(total, bits[3]))
        total, grad_tokens = lax.optimization_barrier((total, grad_tokens))
        total, mix_peer = lax.optimization_barrier((total, mix_peer))
        result = (residual + (mix_here.astype(F32) + mix_peer.astype(F32))).astype(BF16)
        result_peer = other(result)
        total, result = lax.optimization_barrier((total, result))
        for bit in bits[2:0:-1]:
            total = gathered(total, bit)
        total, result_peer = lax.optimization_barrier((total, result_peer))
        total = gathered(total, bits[0])
        result = unpad(first, result, result_peer, BF16)
        total = total.astype(F32)
        part = w_qkv.shape[2]
    else:
        gated = [rows_of(gated[:, c]) for c in range(chunks)]
        every = [collected(jnp.full((1,), r * own, jnp.int32), gated, BF16)[0] for r in range(ways)]
        mixture = lax.psum_scatter(jnp.stack(every), "tensor", scatter_dimension=0).astype(F32)

        def whole(v):
            v = lax.all_gather(v, "tensor", axis=0, tiled=True)
            return v[:, :SEQ].reshape(tok_rows, width)

        result = whole((residual + mixture).astype(BF16))
        grad_tokens = whole(grad_tok).astype(F32)
        total = lax.psum(pack[0], ("expert", "tensor")).astype(F32)
        part = width

    def take(at, rows, cols):
        blocks = [total[at + b * rows : at + (b + 1) * rows] for b in range(cols // 256)]
        return jnp.concatenate(blocks, axis=1) if len(blocks) > 1 else blocks[0]

    step = width * (part // 256)
    grad_w_qkv = jnp.stack([take(j * step, width, part) for j in range(3)])
    grad_w_attn_out = take(3 * step, part, width)
    small = take(3 * step + part * (width // 256), small_rows(experts), width)
    if ways != 2:
        grad_w_qkv = lax.dynamic_slice_in_dim(grad_w_qkv, rank * w_qkv.shape[2], w_qkv.shape[2], 2)
        grad_w_attn_out = lax.dynamic_slice_in_dim(grad_w_attn_out, rank * w_qkv.shape[2], w_qkv.shape[2], 0)
    return (
        result,
        grad_tokens,
        small[experts],
        grad_w_qkv,
        grad_w_attn_out,
        small[experts + 1],
        small[:experts].T,
        grad_w1[None],
        grad_w2[None],
    )


def solution(mesh):
    placed = (
        P("expert", None),
        P("expert", None),
        P(),
        P(None, None, "tensor"),
        P("tensor", None),
        P(),
        P(),
        P("expert", None, "tensor"),
        P("expert", "tensor", None),
        P("expert", None),
    )
    return jax.shard_map(
        functools.partial(body, ways=mesh.shape["tensor"], groups=mesh.shape["expert"]),
        mesh=mesh,
        in_specs=placed,
        out_specs=(
            P("expert", None),
            P("expert", None),
            P(),
            P(None, None, "tensor"),
            P("tensor", None),
            P(),
            P(),
            P("expert", None, "tensor"),
            P("expert", "tensor", None),
        ),
        check_vma=False,
    )
```

```python
import functools

import jax
import jax.numpy as jnp
from jax import lax
from jax.experimental import pallas as pl
from jax.experimental.pallas import tpu as pltpu
from jax.sharding import PartitionSpec as P

HEAD_DIM = 64
SEQ = 197
PAD = 208
EPS = 1e-06
F32 = jnp.float32
BF16 = jnp.bfloat16
VMEM = pl.BlockSpec(memory_space=pltpu.VMEM)


def nn(a, b):
    return lax.dot_general(a, b, (((1,), (0,)), ((), ())), preferred_element_type=F32)


def nt(a, b):
    return lax.dot_general(a, b, (((1,), (1,)), ((), ())), preferred_element_type=F32)


def tn(a, b):
    return lax.dot_general(a, b, (((0,), (0,)), ((), ())), preferred_element_type=F32)


def params(mib=56):
    return pltpu.CompilerParams(vmem_limit_bytes=mib << 20)


def cost(us):
    return pl.CostEstimate(flops=0, bytes_accessed=int(us * 3.69e6), transcendentals=0)


def full(shape):
    return pl.BlockSpec(shape, lambda *_: (0,) * len(shape))


def pad_images(source, wide, target):
    wide[0 : source.shape[0], :] = source[...].astype(F32)

    def one_image(i, _):
        off = lax.rem(i * SEQ, 8)
        window = wide[pl.ds(pl.multiple_of(i * SEQ - off, 8), PAD + 8), :]
        window = pltpu.roll(window, lax.rem(PAD + 8 - off, PAD + 8), 0)[:PAD]
        target[i] = jnp.where(iota(window.shape, 0) < SEQ, window, 0.0).astype(BF16)
        return 0

    lax.fori_loop(0, target.shape[0], one_image, 0)


def pad_kernel(source, target, wide):
    pad_images(source, wide, target)


def wide_scratch(images, width):
    return pltpu.VMEM((-(-((images - 1) * SEQ + PAD + 8) // 16) * 16, width), F32)


def pad(rows):
    images, width = rows.shape[0] // SEQ, rows.shape[1]
    return pl.pallas_call(
        pad_kernel,
        out_shape=jax.ShapeDtypeStruct((images, PAD, width), BF16),
        in_specs=[VMEM],
        out_specs=VMEM,
        scratch_shapes=[wide_scratch(images, width)],
        compiler_params=params(),
        cost_estimate=cost(2),
        name="pad",
    )(rows)


def iota(shape, axis):
    return lax.broadcasted_iota(jnp.int32, shape, axis)


def slot_match(code_ref, start, step):
    slot = iota((step, code_ref.shape[1]), 0) + start
    return ((slot == code_ref[0:1, :]) | (slot == code_ref[1:2, :])).astype(BF16)


def front_kernel(rank_ref, cot_ref, col_ref, row_ref, cot_out, slots_out, col_out, row_out, wide, *, cap, half):
    experts, chunks, block, _ = slots_out.shape
    first_slot = rank_ref[0] * (half * chunks)

    def code(expert, position):
        place = position.astype(jnp.int32) - first_slot
        good = (expert >= 0) & (position < cap) & (place >= 0) & (place < half * chunks)
        slot = expert * block + place
        for c in range(1, chunks):
            slot = jnp.where(place >= c * half, slot + (experts * block - half), slot)
        return jnp.where(good, slot, -1)

    lanes = col_ref.shape[1]
    span = lanes * experts
    routes = col_ref[...]
    spread_lanes = (iota((lanes, span), 1) // experts == iota((lanes, span), 0)).astype(BF16)
    gather_lanes = (iota((span, lanes), 0) // experts == iota((span, lanes), 1)).astype(BF16)
    chosen = nn(routes.astype(F32).astype(BF16), spread_lanes) == (iota((PAD, span), 1) % experts).astype(F32)
    ones = chosen.astype(F32)
    lower = (iota((PAD, PAD), 0) > iota((PAD, PAD), 1)).astype(BF16)
    before = nn(lower, ones.astype(BF16))
    totals = jnp.broadcast_to(jnp.sum(ones, axis=0, keepdims=True), (16, span)).astype(BF16)
    source, target = iota((span, span), 0), iota((span, span), 1)
    order_s = (source // experts % 2) * lanes + source // (2 * experts)
    order_t = (target // experts % 2) * lanes + target // (2 * experts)
    earlier = (source % experts == target % experts) & (order_s < order_t)
    before = before + nn(totals, earlier.astype(BF16))[0:1]
    place = nn((jnp.minimum(before, float(cap)) * ones).astype(BF16), gather_lanes)
    col_out[...] = code(routes, place)

    step = 128
    blocks = row_ref.shape[1] // step
    upper = (iota((step, step), 0) < iota((step, step), 1)).astype(BF16)
    order = [(choice, b) for choice in range(2) for b in range(blocks)]
    picked = [row_ref[choice : choice + 1, b * step : (b + 1) * step] for choice, b in order]
    ones = [(p == iota((experts, step), 0)).astype(F32) for p in picked]
    before = nn(jnp.concatenate(ones, axis=0).astype(BF16), upper)
    base = jnp.zeros((experts, 1), F32)
    for k, (choice, b) in enumerate(order):
        position = jnp.sum((before[k * experts : (k + 1) * experts] + base) * ones[k], axis=0, keepdims=True)
        row_out[choice : choice + 1, b * step : (b + 1) * step] = code(picked[k], position)
        base = base + jnp.sum(ones[k], axis=1, keepdims=True)

    pad_images(cot_ref, wide, cot_out)
    rows = cot_out[...].reshape(-1, cot_out.shape[2])
    step = min(512, experts * block)
    per = step // block
    blocks = experts // per

    def some_slots(k, _):
        value = nn(slot_match(row_out, k * step, step), rows).astype(BF16)
        slots_out[pl.ds(lax.rem(k, blocks) * per, per), lax.div(k, blocks)] = value.reshape(per, block, -1)
        return 0

    lax.fori_loop(0, chunks * blocks, some_slots, 0)


def front(rank, cotangent, routes, experts, cap, half, block, chunks):
    rows, width = cotangent.shape
    images = rows // SEQ
    padded = jnp.pad(
        routes.reshape(images, SEQ, 2), ((0, 0), (0, PAD - SEQ), (0, 0)), constant_values=-1
    )
    down = padded.transpose(1, 0, 2).reshape(PAD, images * 2)
    across = padded.reshape(images * PAD, 2).T
    return pl.pallas_call(
        functools.partial(front_kernel, cap=cap, half=half),
        out_shape=(
            jax.ShapeDtypeStruct((images, PAD, width), BF16),
            jax.ShapeDtypeStruct((experts, chunks, block, width), BF16),
            jax.ShapeDtypeStruct(down.shape, jnp.int32),
            jax.ShapeDtypeStruct(across.shape, jnp.int32),
        ),
        in_specs=[pl.BlockSpec(memory_space=pltpu.SMEM)] + [VMEM] * 3,
        out_specs=(VMEM,) * 4,
        scratch_shapes=[wide_scratch(images, width)],
        compiler_params=params(),
        cost_estimate=cost(10),
        name="front",
    )(rank, cotangent, down, across)


def spread_kernel(code_ref, rows_ref, out_ref, *, start):
    step = out_ref.shape[0] * out_ref.shape[1]
    value = nn(slot_match(code_ref, pl.program_id(0) * step + start, step), rows_ref[...])
    out_ref[...] = value.astype(BF16).reshape(out_ref.shape)


def spread(code_row, rows, experts, block, chunk, step=256):
    count, width = rows.shape
    slots = experts * block
    per = step // block
    return pl.pallas_call(
        functools.partial(spread_kernel, start=chunk * slots),
        out_shape=jax.ShapeDtypeStruct((experts, block, width), BF16),
        grid=(slots // step,),
        in_specs=[full((2, count)), full((count, width))],
        out_specs=pl.BlockSpec((per, block, width), lambda i: (i, 0, 0)),
        compiler_params=params(),
        cost_estimate=cost(5),
        name="spread",
    )(code_row, rows)


def row_mean(v):
    return jnp.mean(v, axis=-1, keepdims=True)


def key_softmax(scores):
    cut = SEQ // 16 * 16
    head, tail = scores[:cut], scores[cut:]
    valid = lax.broadcasted_iota(jnp.int32, tail.shape, 0) < SEQ - cut
    tail = jnp.where(valid, tail, -jnp.inf)
    top = jnp.maximum(jnp.max(head, axis=0, keepdims=True), jnp.max(tail, axis=0, keepdims=True))
    head, tail = jnp.exp(head - top), jnp.exp(tail - top)
    total = jnp.sum(head, axis=0, keepdims=True) + jnp.sum(tail, axis=0, keepdims=True)
    scale = 1.0 / total
    return jnp.concatenate([head * scale, tail * scale], axis=0)


QUAD = 4 * HEAD_DIM


def quad_masks():
    lane = iota((PAD, QUAD), 1)
    return [(lane >= h * HEAD_DIM) & (lane < (h + 1) * HEAD_DIM) for h in range(4)]


def stacked(value, masks):
    return jnp.concatenate([jnp.where(m, value, jnp.zeros_like(value)) for m in masks], axis=0)


def unstacked(value, masks):
    return sum(jnp.where(m, value[h * PAD : (h + 1) * PAD], 0.0) for h, m in enumerate(masks))


def attend_kernel(place_ref, tok_ref, ga_ref, gm_ref, *rest, pieces, own):
    wq, wo, rest = rest[:pieces], rest[pieces : 2 * pieces], rest[2 * pieces :]
    routed_ref, res_ref, qkv_ref, prob_ref, att_ref, wq_all, wo_all, qkv_all, att_all = rest
    batch, _, model = tok_ref.shape
    keep = pl.program_id(0) * batch < own

    @pl.when(pl.program_id(0) == 0)
    def _():
        at = 0
        size = wo[0].shape[0]
        if pieces == 1:
            places = [0]
        else:
            core, small = place_ref[1], wo[1].shape[0]
            places = [0, size + core * small, size + (1 - core) * small]
        for k, start in enumerate(places):
            cols = wo[k].shape[0]
            for j in range(3):
                to = start + j * model
                if k:
                    to = pl.multiple_of(to, 128)
                wq_all[:, pl.ds(to, cols)] = wq[k][j]
            if k:
                start = pl.multiple_of(start, 128)
            wo_all[pl.ds(start, cols), :] = wo[k][...]

    tok = tok_ref[...].reshape(batch * PAD, model).astype(F32)
    center = tok - row_mean(tok)
    normed = (center * lax.rsqrt(row_mean(center * center) + EPS) * ga_ref[...]).astype(BF16)
    value = nn(normed, wq_all[...])
    qkv_all[:, :model] = (value[:, :model] * HEAD_DIM**-0.5).astype(BF16)
    qkv_all[:, model:] = value[:, model:].astype(BF16)
    masks = quad_masks()
    key_ok = iota((4 * PAD, PAD), 1) < SEQ
    for g in range(batch):
        rows = slice(g * PAD, (g + 1) * PAD)
        for quad in range(model // QUAD):
            q, k, v = (qkv_all[rows, j * model + quad * QUAD : j * model + (quad + 1) * QUAD] for j in range(3))
            scores = jnp.where(key_ok, nt(stacked(q, masks), k), -jnp.inf)
            ex = jnp.exp(scores - jnp.max(scores, axis=1, keepdims=True))
            probs = (ex * (1.0 / jnp.sum(ex, axis=1, keepdims=True))).astype(BF16)

            @pl.when(keep)
            def _():
                prob_ref[g, quad] = probs

            mixed = unstacked(nn(probs, v), masks)
            att_all[rows, quad * QUAD : (quad + 1) * QUAD] = mixed.astype(BF16)

    residual = tok + nn(att_all[...], wo_all[...])

    @pl.when(keep)
    def _():
        res_ref[...] = residual.reshape(batch, PAD, model)
        qkv_ref[...] = qkv_all[...].reshape(batch, PAD, 3 * model)
        att_ref[...] = att_all[...].reshape(batch, PAD, model)

    center = residual - row_mean(residual)
    normed = center * lax.rsqrt(row_mean(center * center) + EPS) * gm_ref[...]
    routed_ref[...] = normed.astype(BF16).reshape(batch, PAD, model)


def attend(place, tok_pad, gain_attn, gain_moe, wq, wo, own, batch=2):
    images, _, width = tok_pad.shape
    batch = batch if own % batch == 0 else 1
    pieces = len(wq)
    steps = images // batch

    def image(i, place_ref):
        return (lax.rem(i + place_ref[0] // batch, steps), 0, 0)

    def kept(*shape):
        return pl.BlockSpec(
            (batch,) + shape, lambda i, place_ref: (jnp.minimum(i, own // batch - 1),) + (0,) * len(shape)
        )

    rows = pl.BlockSpec((batch, PAD, width), image)
    probs = (width // QUAD, 4 * PAD, PAD)
    return pl.pallas_call(
        functools.partial(attend_kernel, pieces=pieces, own=own),
        out_shape=(
            jax.ShapeDtypeStruct((images, PAD, width), BF16),
            jax.ShapeDtypeStruct((own, PAD, width), F32),
            jax.ShapeDtypeStruct((own, PAD, 3 * width), BF16),
            jax.ShapeDtypeStruct((own,) + probs, BF16),
            jax.ShapeDtypeStruct((own, PAD, width), BF16),
            jax.ShapeDtypeStruct((width, 3 * width), BF16),
            jax.ShapeDtypeStruct((width, width), BF16),
        ),
        grid_spec=pltpu.PrefetchScalarGridSpec(
            num_scalar_prefetch=1,
            grid=(steps,),
            in_specs=[rows, full((1, width)), full((1, width))] + [full(v.shape) for v in (*wq, *wo)],
            out_specs=(
                rows,
                kept(PAD, width),
                kept(PAD, 3 * width),
                kept(*probs),
                kept(PAD, width),
                full((width, 3 * width)),
                full((width, width)),
            ),
            scratch_shapes=[
                pltpu.VMEM((batch * PAD, 3 * width), BF16),
                pltpu.VMEM((batch * PAD, width), BF16),
            ],
        ),
        compiler_params=params(),
        cost_estimate=cost(25),
        name="attend",
    )(place, tok_pad, gain_attn.reshape(1, -1), gain_moe.reshape(1, -1), *wq, *wo)


def expert_kernel(expert_ref, x_ref, cot_ref, wr_ref, *rest, parts, half, block, chunk, begins, ends):
    weights, rest = rest[: len(parts)], rest[len(parts) :]
    w1, w2, dw1, dw2, out_sum, gin_sum, low1, low2, gates, load_sems, store_sems = rest[-11:]
    shards, _, hidden = w1.shape
    before, rest = ((), rest) if begins else (rest[: 2 * shards], rest[2 * shards + 1 :])
    gin_ref, out_ref = rest[:2]
    given = rest[2 : 2 + 2 * shards]
    expert = expert_ref[0]
    size = min(chunk, hidden)
    blocks = hidden // size

    loads = [(s, ref, (w1, w2)[k].at[s, pl.ds(at, ref.shape[0])]) for (k, s, at), ref in zip(parts, weights)]
    loads += [(k % shards, ref, (dw1, dw2)[k // shards].at[k % shards]) for k, ref in enumerate(before)]
    loads = [(s, pltpu.make_async_copy(a, b, load_sems.at[k])) for k, (s, a, b) in enumerate(loads)]
    for s in range(shards):
        for where, copy in loads:
            if where == s:
                copy.start()

    def stores(s, c):
        cols = pl.ds(pl.multiple_of(c * size, size), size)
        if ends and s:
            sources = low1.at[:, cols], low2.at[cols, :]
        else:
            sources = dw1.at[s, :, cols], dw2.at[s, cols, :]
        targets = given[s].at[:, cols], given[shards + s].at[cols, :]
        return [
            pltpu.make_async_copy(a, b, store_sems.at[(s * blocks + c) * 2 + k])
            for k, (a, b) in enumerate(zip(sources, targets))
        ]

    x = x_ref[...]
    rows, width = x.shape
    cot = cot_ref[...].reshape(rows, width).astype(F32)
    logits = nn(x, wr_ref[...])
    ex = jnp.exp(logits - jnp.max(logits, axis=1, keepdims=True))
    mine = iota(ex.shape, 1) == expert
    gate = jnp.sum(jnp.where(mine, ex, 0.0), axis=1, keepdims=True) / jnp.sum(
        ex, axis=1, keepdims=True
    )
    grad_out = (gate * cot).astype(BF16)
    x_t = x.T
    out_sum[...] = jnp.zeros_like(out_sum)
    gin_sum[...] = jnp.zeros_like(gin_sum)
    c0 = (2.0 / jnp.pi) ** 0.5

    def some_hidden(k, _):
        for s in range(shards):

            @pl.when(k == s * blocks)
            def _():
                for where, copy in loads:
                    if where == s:
                        copy.wait()

        shard, at = lax.div(k, blocks), lax.rem(k, blocks)
        cols = pl.ds(pl.multiple_of(at * size, size), size)
        u = nn(x, w1[shard, :, cols])
        square = u * u
        t = jnp.tanh(u * (c0 + (c0 * 0.044715) * square))
        h = 0.5 + 0.5 * t
        slope = h + (0.5 * u) * (1.0 - t * t) * (c0 + (3 * c0 * 0.044715) * square)
        active = (u * h).astype(BF16)
        out_sum[...] += nn(active, w2[shard, cols, :])
        grad_pre = (nt(grad_out, w2[shard, cols, :]) * slope).astype(BF16)
        gin_sum[...] += nt(grad_pre, w1[shard, :, cols])
        first, second = nn(x_t, grad_pre), tn(active, grad_out)
        dw1[shard, :, cols] = first if begins else dw1[shard, :, cols] + first
        dw2[shard, cols, :] = second if begins else dw2[shard, cols, :] + second
        for s in range(shards):

            @pl.when(shard == s)
            def _():
                if ends and s:
                    low1[:, cols] = dw1[shard, :, cols].astype(BF16)
                    low2[cols, :] = dw2[shard, cols, :].astype(BF16)
                for copy in stores(s, at):
                    copy.start()

        return 0

    lax.fori_loop(0, shards * blocks, some_hidden, 0)
    down, across = iota((block, width), 0), iota((block, width), 1)
    gates[...] = jnp.broadcast_to(gate, gates.shape)
    group = min(2, rows // block)

    def some_groups(i, _):
        at = pl.multiple_of(i * group * block, group * block)
        span = pl.ds(at, group * block)
        out = out_sum[span, :]
        out_ref[pl.ds(i * group, group), 0] = (gates[span, 0:1] * out).astype(BF16).reshape(group, block, width)
        cot = cot_ref[pl.ds(i * group, group), 0].reshape(group * block, width).astype(F32)
        gate_grad = jnp.sum(cot * out, axis=1, keepdims=True)
        for g in range(group):
            rows_of_one = pl.ds(at + g * block, block)
            line = jnp.where(down == across, gate_grad[g * block : (g + 1) * block], 0.0)
            line = jnp.sum(line, axis=0, keepdims=True)
            high = line.astype(BF16).astype(F32)
            value = jnp.where(down == half + 1, line - high, gin_sum[rows_of_one, :])
            gin_ref[rows_of_one, :] = jnp.where(down == half, high, value).astype(BF16)
        return 0

    lax.fori_loop(0, rows // (group * block), some_groups, 0)
    for s in range(shards):
        for c in range(blocks):
            for copy in stores(s, c):
                copy.wait()


def experts_step(expert, x, cot, before, number, ends, w_router, w1, w2, half, block, chunk=512):
    rows, width = x.shape
    shards = len(w1)
    hidden = w1[0][0].shape[1]
    row_spec = full((rows, width))
    chunk_spec = pl.BlockSpec((rows // block, 1, block, width), lambda i, _: (0, number, 0, 0))
    anywhere = pl.BlockSpec(memory_space=pl.ANY)
    old = [] if before is None else [*before[1:], before[0]]
    parts, weights = [], []
    for k, shards_of_one in enumerate((w1, w2)):
        for s, pieces in enumerate(shards_of_one):
            at = 0
            for piece in pieces:
                parts.append((k, s, at))
                weights.append(piece)
                at += piece.shape[0]
    shapes = [(width, hidden)] * shards + [(hidden, width)] * shards
    low = (8, 128) if shards == 1 or not ends else None
    at = 4 + len(weights)
    alias = {at + 2 * shards: 1} if old else {}
    return pl.pallas_call(
        functools.partial(
            expert_kernel,
            parts=parts,
            half=half,
            block=block,
            chunk=chunk,
            begins=before is None,
            ends=ends,
        ),
        out_shape=(jax.ShapeDtypeStruct((rows, width), BF16), jax.ShapeDtypeStruct(cot.shape, BF16))
        + tuple(
            jax.ShapeDtypeStruct(v, BF16 if ends and k % shards else F32) for k, v in enumerate(shapes)
        ),
        grid_spec=pltpu.PrefetchScalarGridSpec(
            num_scalar_prefetch=1,
            grid=(1,),
            in_specs=[row_spec, chunk_spec, full(w_router.shape)] + [anywhere] * (len(weights) + len(old)),
            out_specs=(row_spec, chunk_spec) + (anywhere,) * len(shapes),
            scratch_shapes=[
                pltpu.VMEM((shards, width, hidden), BF16),
                pltpu.VMEM((shards, hidden, width), BF16),
                pltpu.VMEM((shards, width, hidden), F32),
                pltpu.VMEM((shards, hidden, width), F32),
                pltpu.VMEM((rows, width), F32),
                pltpu.VMEM((rows, width), F32),
                pltpu.VMEM(low or (width, hidden), BF16),
                pltpu.VMEM(low or (hidden, width), BF16),
                pltpu.VMEM((rows, 128), F32),
                pltpu.SemaphoreType.DMA((len(weights) + 2 * shards,)),
                pltpu.SemaphoreType.DMA((2 * shards * hidden // min(chunk, hidden),)),
            ],
        ),
        input_output_aliases=alias,
        compiler_params=params(62),
        cost_estimate=cost(20),
        name="experts",
    )(expert, x, cot, w_router, *weights, *old)


def collect_kernel(first_ref, code_ref, *rest, numbers, half, block, probs, before):
    chunks = len(numbers)
    parts, rest = rest[:chunks], rest[chunks:]
    old, rest = rest[:before], rest[before:]
    out_ref, rest = rest[0], rest[1:]
    count, width = parts[0].shape
    experts = count // block
    rows = PAD
    codes = code_ref[...]
    across = iota(codes.shape, 1)
    at = (first_ref[0] + pl.program_id(0)) * 2
    columns = [jnp.sum(jnp.where(across == at + c, codes, 0), axis=1, keepdims=True) for c in range(2)]
    lane = iota((rows, count), 1)
    total = old[0][0] if old else None
    grads = None
    for c in range(chunks):
        shift = numbers[c] * count
        match = ((lane + shift == columns[0]) | (lane + shift == columns[1])).astype(BF16)
        value = nn(match, parts[c][...])
        total = value if total is None else total + value
        if probs:
            slot_grads = rest[1 + c]

            @pl.when(pl.program_id(0) == 0)
            def _():
                lines = jnp.zeros((experts, 128), F32)
                for e in range(experts):
                    tail = parts[c][e * block + block - 16 : (e + 1) * block, 0:128].astype(F32)
                    here = half - (block - 16)
                    line = tail[here : here + 1] + tail[here + 1 : here + 2]
                    lines = jnp.where(iota(lines.shape, 0) == e, line, lines)
                turned = lines.T[:block]
                high = turned.astype(BF16).astype(F32)
                both = jnp.concatenate([high, turned - high], axis=1)
                for e in range(experts):
                    own_lane = iota(both.shape, 1) % experts == e
                    slot_grads[e * block : (e + 1) * block, :] = jnp.where(own_lane, both, 0.0).astype(BF16)

            value = nn(match, slot_grads[...])
            grads = value if grads is None else grads + value
    out_ref[0] = total.astype(out_ref.dtype)
    if probs:
        turned = grads.T
        value = turned[:experts] + turned[experts:]
        rest[0][0] = value + old[1][0] if old else value


def collect(first, code_col, parts, own, dtype, half, block, probs=False, numbers=None, before=()):
    numbers = tuple(range(len(parts))) if numbers is None else numbers
    count, width = parts[0].shape
    outs = [jax.ShapeDtypeStruct((own, PAD, width), dtype)]
    if probs:
        outs.append(jax.ShapeDtypeStruct((own, count // block, PAD), F32))
    return pl.pallas_call(
        functools.partial(
            collect_kernel, numbers=numbers, half=half, block=block, probs=probs, before=len(before)
        ),
        out_shape=tuple(outs),
        grid_spec=pltpu.PrefetchScalarGridSpec(
            num_scalar_prefetch=1,
            grid=(own,),
            in_specs=[full(code_col.shape)]
            + [full((count, width))] * len(parts)
            + [pl.BlockSpec((1,) + v.shape[1:], lambda i, f: (i + f[0], 0, 0)) for v in before],
            out_specs=tuple(pl.BlockSpec((1,) + v.shape[1:], lambda i, f: (i, 0, 0)) for v in outs),
            scratch_shapes=[pltpu.VMEM((count, 2 * (count // block)), BF16)] * (len(parts) if probs else 0),
        ),
        compiler_params=params(),
        cost_estimate=cost(7),
        name="collect",
    )(first, code_col, *parts, *before)


def back_kernel(first_ref, *rest, steps, received):
    (sum_ref, gp_ref), rest = rest[:2], rest[2:]
    more, rest = rest[: 2 * received], rest[2 * received :]
    (res_ref, cot_ref, tok_ref, ga_ref, gm_ref, wrt_ref, wq, wo, qkv_ref, prob_ref, att_ref), rest = rest[:11], rest[11:]
    gtok_ref, pack_ref, dwq, dwo, small, gatt_all, dqkv_all, wq_here, qkv_here, prob_here, sems = rest
    experts = wrt_ref.shape[0]
    batch, _, model = res_ref.shape
    rows = batch * PAD
    step = pl.program_id(0)

    def loads(number):
        span = pl.ds(number * batch, batch)
        pairs = [(v.at[span], w.at[span]) for v, w in ((qkv_ref, qkv_here), (prob_ref, prob_here))]
        return [pltpu.make_async_copy(a, b, sems.at[number, k]) for k, (a, b) in enumerate(pairs)]

    weights = pltpu.make_async_copy(wq, wq_here, sems.at[0, 2])

    @pl.when(step == 0)
    def _():
        for copy in loads(0) + [weights]:
            copy.start()
        for number in range(1, steps):
            for copy in loads(number):
                copy.start()
        for ref in (dwq, dwo, small):
            ref[...] = jnp.zeros_like(ref)

    def flat(ref):
        return ref[...].reshape(rows, -1).astype(F32)

    residual = flat(res_ref)
    center = residual - row_mean(residual)
    scale = lax.rsqrt(row_mean(center * center) + EPS)
    xhat = center * scale
    gm = gm_ref[...]
    routed = (xhat * gm).astype(BF16)
    logits = nt(wrt_ref[...], routed)
    ex = jnp.exp(logits - jnp.max(logits, axis=0, keepdims=True))
    probs = ex / jnp.sum(ex, axis=0, keepdims=True)
    grad_probs = gp_ref[...]
    grad_routed = flat(sum_ref)
    if received:
        grad_routed = grad_routed + flat(more[0])
        grad_probs = grad_probs + more[1][...]
    grad_probs = jnp.concatenate([grad_probs[g] for g in range(batch)], axis=1)
    grad_logits = probs * (grad_probs - jnp.sum(probs * grad_probs, axis=0, keepdims=True))
    high = grad_logits.astype(BF16)
    low = (grad_logits - high.astype(F32)).astype(BF16)
    both = jnp.concatenate([high, low], axis=0)
    new = nn(both, routed)
    small[0:experts, :] += new[:experts] + new[experts:]
    grad_routed = grad_routed + tn(both, jnp.concatenate([wrt_ref[...]] * 2, axis=0))
    small[experts + 1 : experts + 2, :] += jnp.sum(grad_routed * xhat, axis=0, keepdims=True)
    g = grad_routed * gm
    grad_res = flat(cot_ref) + scale * (g - row_mean(g) - xhat * row_mean(g * xhat))
    grad_mixed = grad_res.astype(BF16)
    dwo[...] += tn(att_ref[...].reshape(rows, model), grad_mixed)
    gatt_all[...] = nt(grad_mixed, wo[...]).astype(BF16)

    masks = quad_masks()
    for number in range(steps):

        @pl.when(step == number)
        def _():
            for copy in loads(number):
                copy.wait()

    for b in range(batch):
        span = slice(b * PAD, (b + 1) * PAD)
        image = step * batch + b
        for quad in range(model // QUAD):
            q, k, v = (
                qkv_here[image, :, j * model + quad * QUAD : j * model + (quad + 1) * QUAD] for j in range(3)
            )
            grad_heads = stacked(gatt_all[span, quad * QUAD : (quad + 1) * QUAD], masks)
            low_probs = prob_here[image, quad]
            p = low_probs.astype(F32)
            gw = nt(grad_heads, v)
            ds = (p * (gw - jnp.sum(p * gw, axis=1, keepdims=True))).astype(BF16)
            grad_q = unstacked(nn(ds, k), masks) * HEAD_DIM**-0.5
            grad_k = tn(ds, stacked(q, masks))
            grad_v = tn(low_probs, grad_heads)
            for j, value in enumerate((grad_q, grad_k, grad_v)):
                dqkv_all[span, j * model + quad * QUAD : j * model + (quad + 1) * QUAD] = value.astype(BF16)

    tok = flat(tok_ref)
    center = tok - row_mean(tok)
    tok_scale = lax.rsqrt(row_mean(center * center) + EPS)
    xin = center * tok_scale
    ga = ga_ref[...]
    normed = (xin * ga).astype(BF16)
    dwq[...] += tn(normed, dqkv_all[...])

    @pl.when(step == 0)
    def _():
        weights.wait()

    grad_normed = nt(dqkv_all[...], wq_here[...])
    small[experts : experts + 1, :] += jnp.sum(grad_normed * xin, axis=0, keepdims=True)
    h = grad_normed * ga
    grad_tok = grad_res + tok_scale * (h - row_mean(h) - xin * row_mean(h * xin))
    gtok_ref[...] = grad_tok.astype(BF16).reshape(gtok_ref.shape)

    @pl.when(step == steps - 1)
    def _():
        shards = pack_ref.shape[0]
        part = model // shards
        for s in range(shards):
            at = 0
            blocks = [dwq[:, j * model + s * part : j * model + (s + 1) * part] for j in range(3)]
            for value in blocks + [dwo[s * part : (s + 1) * part, :], small[...]]:
                for c in range(value.shape[1] // 256):
                    pack_ref[s, at : at + value.shape[0], :] = value[:, c * 256 : (c + 1) * 256].astype(BF16)
                    at += value.shape[0]
            if at < pack_ref.shape[1]:
                pack_ref[s, at:, :] = jnp.zeros((pack_ref.shape[1] - at, 256), BF16)


def small_rows(experts):
    return -(-(experts + 2) // 16) * 16


def pack_rows(width, part, experts, align):
    rows = 3 * width * (part // 256) + part * (width // 256) + small_rows(experts) * (width // 256)
    return -(-rows // align) * align


def back(first, sums, residual, cot_pad, tok_pad, qkv, probs, att, gain_attn, gain_moe, w_router, wq, wo, shards, align, batch=2):
    own, _, width = residual.shape
    batch = batch if own % batch == 0 else 1
    experts = w_router.shape[1]
    rows = pack_rows(width, width // shards, experts, align)

    def mine(*shape):
        return pl.BlockSpec((batch,) + shape, lambda i, f: (i,) + (0,) * len(shape))

    image = pl.BlockSpec((batch, PAD, width), lambda i, f: (i + f[0] // batch, 0, 0))
    flat = [v for pair in sums for v in pair]
    return pl.pallas_call(
        functools.partial(back_kernel, steps=own // batch, received=len(sums) - 1),
        out_shape=(
            jax.ShapeDtypeStruct((own, PAD, width), BF16),
            jax.ShapeDtypeStruct((shards, rows, 256), BF16),
        ),
        grid_spec=pltpu.PrefetchScalarGridSpec(
            num_scalar_prefetch=1,
            grid=(own // batch,),
            in_specs=[mine(PAD, width), mine(experts, PAD)] * len(sums)
            + [
                mine(PAD, width),
                image,
                image,
                full((1, width)),
                full((1, width)),
                full((experts, width)),
                pl.BlockSpec(memory_space=pl.ANY),
                full(wo.shape),
                pl.BlockSpec(memory_space=pl.ANY),
                pl.BlockSpec(memory_space=pl.ANY),
                mine(*att.shape[1:]),
            ],
            out_specs=(mine(PAD, width), full((shards, rows, 256))),
            scratch_shapes=[
                pltpu.VMEM((width, 3 * width), F32),
                pltpu.VMEM((width, width), F32),
                pltpu.VMEM((small_rows(experts), width), F32),
                pltpu.VMEM((batch * PAD, width), BF16),
                pltpu.VMEM((batch * PAD, 3 * width), BF16),
                pltpu.VMEM(wq.shape, BF16),
                pltpu.VMEM(qkv.shape, BF16),
                pltpu.VMEM(probs.shape, BF16),
                pltpu.SemaphoreType.DMA((own // batch, 3)),
            ],
        ),
        compiler_params=params(),
        cost_estimate=cost(16),
        name="back",
    )(
        first,
        *flat,
        residual,
        cot_pad,
        tok_pad,
        gain_attn.reshape(1, -1),
        gain_moe.reshape(1, -1),
        w_router.T,
        wq,
        wo,
        qkv,
        probs,
        att,
    )


def unpad_kernel(first_ref, *refs, images):
    out_ref, wide = refs[-2:]
    pieces = len(refs) // 2 - 1
    parts = refs[:pieces], refs[pieces:-2]
    own, peer = ([(ref, i) for ref in part for i in range(ref.shape[0])] for part in parts)
    for i in range(images):
        inner = i % len(own)
        mine = first_ref[0] == i - inner
        (own_ref, k), (peer_ref, _) = own[inner], peer[inner]
        value = jnp.where(mine, own_ref[k], peer_ref[k]).astype(F32)
        wide[i * SEQ : (i + 1) * SEQ, :] = value[:SEQ]
    out_ref[...] = wide[0 : images * SEQ, :].astype(out_ref.dtype)


def unpad(first, own, peer, dtype):
    images, width = 2 * sum(v.shape[0] for v in own), own[0].shape[2]
    return pl.pallas_call(
        functools.partial(unpad_kernel, images=images),
        out_shape=jax.ShapeDtypeStruct((images * SEQ, width), dtype),
        in_specs=[pl.BlockSpec(memory_space=pltpu.SMEM)] + [VMEM] * (2 * len(own)),
        out_specs=VMEM,
        scratch_shapes=[wide_scratch(images, width)],
        compiler_params=params(),
        cost_estimate=cost(2),
        name="unpad",
    )(first, *own, *peer)


def body(tokens, routes, gain_attn, w_qkv, w_attn_out, gain_moe, w_router, w_expert_in, w_expert_out, cotangent, *, ways, groups):
    tok_rows, width = tokens.shape
    experts = w_router.shape[1]
    cap = max(4, (5 * tok_rows // (2 * experts) + 7) // 8 * 8)
    chunks = 2
    half = -(-cap // (ways * chunks))
    block = -(-(half + 2) // 16) * 16
    slots = experts * block
    images = tok_rows // SEQ
    own = images // ways
    rank = lax.axis_index("tensor")
    expert = lax.axis_index("expert")
    first = (rank * own).astype(jnp.int32).reshape(1)
    swap = [(0, 1), (1, 0)]

    def other(v):
        return lax.ppermute(v, "tensor", swap)

    def shards_of(v, axis):
        if ways == 2:
            return [v, other(v)]
        return [lax.all_gather(v, "tensor", axis=axis, tiled=True)]

    def exchange(rows):
        return lax.all_to_all(rows, "expert", split_axis=0, concat_axis=0, tiled=True)

    def after(v, *others):
        return lax.optimization_barrier((v,) + others)[0]

    def rows_of(v):
        return v.reshape(-1, width)

    def collected(number, parts, dtype, probs=False, numbers=None, before=()):
        return collect(number, code_col, parts, own, dtype, half, block, probs, numbers, before)

    if ways == 2:
        core = expert % 2
        near = [(i, i ^ 1) for i in range(groups)]

        def part_of(v, axis):
            size = v.shape[axis] // 2
            return other(lax.dynamic_slice_in_dim(v, core * size, size, axis))

    else:
        core = 0 * expert
        wq, wo = shards_of(w_qkv, 2), shards_of(w_attn_out, 0)
    cot_pad, cot_slots, code_col, code_row = front(
        rank.astype(jnp.int32).reshape(1), cotangent, routes, experts, cap, half, block, chunks
    )
    tok_pad = pad(after(tokens, cot_pad))
    if ways == 2:
        got_q, got_o = part_of(after(w_qkv, cot_slots), 2), part_of(after(w_attn_out, cot_slots), 0)
        got_q, got_o, tok_pad = lax.optimization_barrier((got_q, got_o, tok_pad))
        wq = [w_qkv, got_q, lax.ppermute(got_q, "expert", near)]
        wo = [w_attn_out, got_o, lax.ppermute(got_o, "expert", near)]
    cot_slots = exchange(cot_slots)
    w1 = shards_of(after(w_expert_in[0], wq[-1], wo[-1]), 1)
    if ways == 2:
        cut = w_expert_out.shape[1] // 4
        w2_first = other(after(w_expert_out[0, :cut], wq[-1], wo[-1]))
        w2_rest = other(after(w_expert_out[0, cut:], wq[-1], wo[-1]))
    place = jnp.stack([rank * own, core]).astype(jnp.int32)
    routed, residual, qkv, probs, att, wq, wo = attend(place, tok_pad, gain_attn, gain_moe, wq, wo, own)
    x_slots = []
    for c in range(chunks):
        rows = spread(code_row, rows_of(routed), experts, block, c)
        if c == 0:
            rows, cot_slots = lax.optimization_barrier((rows, cot_slots))
            if ways == 2:
                rows = after(rows, w1[-1], w2_first)
        elif ways == 2:
            rows = after(rows, w2_rest)
        x_slots.append(exchange(rows))
    if ways == 2:
        w1 = [[v] for v in w1]
        w2 = [[w_expert_out[0]], [w2_first, w2_rest]]
    else:
        w1 = [w1]
        w2 = [shards_of(w_expert_out[0], 0)]
    gin, more = [], None
    expert_number = expert.astype(jnp.int32).reshape(1)
    for c in range(chunks):
        new, *more = experts_step(
            expert_number, rows_of(x_slots[c]), cot_slots, more, c, c == chunks - 1, w_router, w1, w2, half, block
        )
        gin.append(exchange(new.reshape(experts, block, width)))
    gated, *dw = more
    gin = [rows_of(v) for v in gin]
    if ways == 2:
        there = ((1 - rank) * own).astype(jnp.int32).reshape(1)
        dw1_peer = other(dw[1])
        cut = 3 * dw[3].shape[0] // 16
        dw2_peer = [other(dw[3][:cut])]
        zero = jnp.zeros((1,), jnp.int32)
        start = collect(zero, code_col, gin[:1], images, F32, half, block, True, (0,))
        gin[1], *start = lax.optimization_barrier((gin[1], *start))
        sent = collected(there, gin[1:], BF16, True, (1,), start)
        received = tuple(other(v) for v in sent)
        mine = collected(first, gin[1:], F32, True, (1,), start)
        gated = exchange(after(gated, *sent, dw1_peer, dw2_peer[0]))
        grad_w1 = dw[0] + dw1_peer.astype(F32)
        *received, grad_w1 = lax.optimization_barrier((*received, grad_w1, *mine))[:3]
        sums = [mine, received]
        dw2_peer.append(other(after(dw[3][cut:], *received)))
    else:
        gated = exchange(gated)
        every = [collected(jnp.full((1,), r * own, jnp.int32), gin, F32, True) for r in range(ways)]
        sums = [
            tuple(
                lax.psum_scatter(jnp.stack([v[k] for v in every]).astype(t), "tensor", scatter_dimension=0).astype(F32)
                for k, t in ((0, BF16), (1, F32))
            )
        ]
        grad_w1 = lax.psum_scatter(dw[0].astype(BF16), "tensor", scatter_dimension=1, tiled=True).astype(F32)
        grad_w2 = lax.psum_scatter(dw[1].astype(BF16), "tensor", scatter_dimension=0, tiled=True).astype(F32)
    grad_tok, pack = back(
        first, sums, residual, cot_pad, tok_pad, qkv, probs, att, gain_attn, gain_moe, w_router, wq, wo,
        2 if ways == 2 else 1, groups * 8,
    )

    bits = [1 << b for b in range(groups.bit_length() - 1)]
    if ways == 2:

        def swap_bit(v, bit):
            return lax.ppermute(v, "expert", [(i, i ^ bit) for i in range(groups)])

        def add(a, b):
            return (a.astype(F32) + b.astype(F32)).astype(BF16)

        def halves(v, bit):
            size = v.shape[-2] // 2
            upper = (expert // bit) % 2
            keep = lax.dynamic_slice_in_dim(v, upper * size, size, v.ndim - 2)
            give = lax.dynamic_slice_in_dim(v, (1 - upper) * size, size, v.ndim - 2)
            return keep, give

        pack, grad_tok, gated, dw2_peer[1] = lax.optimization_barrier((pack, grad_tok, gated, dw2_peer[1]))
        grad_peer = other(grad_tok)
        gated = [rows_of(gated[:, c]) for c in range(chunks)]
        (mix,) = collect(zero, code_col, gated, images, BF16, half, block)
        mix_there = lax.dynamic_slice_in_dim(mix, (1 - rank) * own, own, 0)
        mix_here = lax.dynamic_slice_in_dim(mix, rank * own, own, 0)
        for bit in bits[:2]:
            keep, give = halves(pack, bit)
            pack = add(keep, swap_bit(give, bit))
        pack, mix_there, grad_peer = lax.optimization_barrier((pack, mix_there, grad_peer))
        mix_peer = other(mix_there)
        keep, give = halves(pack, bits[2])
        pack = add(keep, swap_bit(give, bits[2]))
        grad_tokens = unpad(first, [grad_tok], [grad_peer], F32)
        keep, give = halves(pack, bits[3])
        pack, grad_w2, mix_here = lax.optimization_barrier(
            (add(keep, swap_bit(give, bits[3])), dw[2] + jnp.concatenate(dw2_peer).astype(F32), mix_here)
        )
        pack, mix_peer, grad_tokens = lax.optimization_barrier((pack, mix_peer, grad_tokens))
        swapped = other(pack[1])
        result = (residual + (mix_here.astype(F32) + mix_peer.astype(F32))).astype(BF16)
        swapped, result = lax.optimization_barrier((swapped, result))
        result_peer = other(result)
        total = add(pack[0], swapped)

        def gathered(v, bit):
            got = swap_bit(v, bit)
            upper = (expert // bit) % 2 == 1
            return jnp.where(upper, jnp.concatenate([got, v]), jnp.concatenate([v, got]))

        for bit in bits[3:1:-1]:
            total = gathered(total, bit)
        total = gathered(total, bits[1])
        total, result_peer = lax.optimization_barrier((total, result_peer))
        total = gathered(total, bits[0])
        total = total.astype(F32)
        part = w_qkv.shape[2]
    else:
        gated = [rows_of(gated[:, c]) for c in range(chunks)]
        every = [collected(jnp.full((1,), r * own, jnp.int32), gated, BF16)[0] for r in range(ways)]
        mixture = lax.psum_scatter(jnp.stack(every), "tensor", scatter_dimension=0).astype(F32)

        def whole(v):
            v = lax.all_gather(v, "tensor", axis=0, tiled=True)
            return v[:, :SEQ].reshape(tok_rows, width)

        result = whole((residual + mixture).astype(BF16))
        grad_tokens = whole(grad_tok).astype(F32)
        total = lax.psum(pack[0], ("expert", "tensor")).astype(F32)
        part = width

    def take(at, rows, cols):
        blocks = [total[at + b * rows : at + (b + 1) * rows] for b in range(cols // 256)]
        return jnp.concatenate(blocks, axis=1) if len(blocks) > 1 else blocks[0]

    step = width * (part // 256)
    grad_w_qkv = jnp.stack([take(j * step, width, part) for j in range(3)])
    grad_w_attn_out = take(3 * step, part, width)
    small = take(3 * step + part * (width // 256), small_rows(experts), width)
    if ways != 2:
        grad_w_qkv = lax.dynamic_slice_in_dim(grad_w_qkv, rank * w_qkv.shape[2], w_qkv.shape[2], 2)
        grad_w_attn_out = lax.dynamic_slice_in_dim(grad_w_attn_out, rank * w_qkv.shape[2], w_qkv.shape[2], 0)
    sums = (small[experts], grad_w_qkv, grad_w_attn_out, small[experts + 1], small[:experts].T)
    if ways == 2:
        result = unpad(first, [result], [result_peer], BF16)
    return (result, grad_tokens, *sums, grad_w1[None], grad_w2[None])


def solution(mesh):
    placed = (
        P("expert", None),
        P("expert", None),
        P(),
        P(None, None, "tensor"),
        P("tensor", None),
        P(),
        P(),
        P("expert", None, "tensor"),
        P("expert", "tensor", None),
        P("expert", None),
    )
    return jax.shard_map(
        functools.partial(body, ways=mesh.shape["tensor"], groups=mesh.shape["expert"]),
        mesh=mesh,
        in_specs=placed,
        out_specs=(
            P("expert", None),
            P("expert", None),
            P(),
            P(None, None, "tensor"),
            P("tensor", None),
            P(),
            P(),
            P("expert", None, "tensor"),
            P("expert", "tensor", None),
        ),
        check_vma=False,
    )
```

```python
import functools

import jax
import jax.numpy as jnp
from jax import lax
from jax.experimental import pallas as pl
from jax.experimental.pallas import tpu as pltpu
from jax.sharding import PartitionSpec as P

HEAD_DIM = 64
SEQ = 197
PAD = 208
EPS = 1e-06
F32 = jnp.float32
BF16 = jnp.bfloat16
VMEM = pl.BlockSpec(memory_space=pltpu.VMEM)


def nn(a, b):
    return lax.dot_general(a, b, (((1,), (0,)), ((), ())), preferred_element_type=F32)


def nt(a, b):
    return lax.dot_general(a, b, (((1,), (1,)), ((), ())), preferred_element_type=F32)


def tn(a, b):
    return lax.dot_general(a, b, (((0,), (0,)), ((), ())), preferred_element_type=F32)


def params(mib=56):
    return pltpu.CompilerParams(vmem_limit_bytes=mib << 20)


def cost(us):
    return pl.CostEstimate(flops=0, bytes_accessed=int(us * 3.69e6), transcendentals=0)


def full(shape):
    return pl.BlockSpec(shape, lambda *_: (0,) * len(shape))


def pad_images(source, wide, target):
    wide[0 : source.shape[0], :] = source[...].astype(F32)

    def one_image(i, _):
        off = lax.rem(i * SEQ, 8)
        window = wide[pl.ds(pl.multiple_of(i * SEQ - off, 8), PAD + 8), :]
        window = pltpu.roll(window, lax.rem(PAD + 8 - off, PAD + 8), 0)[:PAD]
        target[i] = jnp.where(iota(window.shape, 0) < SEQ, window, 0.0).astype(BF16)
        return 0

    lax.fori_loop(0, target.shape[0], one_image, 0)


def pad_kernel(source, target, wide):
    pad_images(source, wide, target)


def wide_scratch(images, width):
    return pltpu.VMEM((-(-((images - 1) * SEQ + PAD + 8) // 16) * 16, width), F32)


def pad(rows):
    images, width = rows.shape[0] // SEQ, rows.shape[1]
    return pl.pallas_call(
        pad_kernel,
        out_shape=jax.ShapeDtypeStruct((images, PAD, width), BF16),
        in_specs=[VMEM],
        out_specs=VMEM,
        scratch_shapes=[wide_scratch(images, width)],
        compiler_params=params(),
        cost_estimate=cost(2),
        name="pad",
    )(rows)


def iota(shape, axis):
    return lax.broadcasted_iota(jnp.int32, shape, axis)


def slot_match(code_ref, start, step):
    slot = iota((step, code_ref.shape[1]), 0) + start
    return ((slot == code_ref[0:1, :]) | (slot == code_ref[1:2, :])).astype(BF16)


def front_kernel(rank_ref, cot_ref, col_ref, row_ref, cot_out, slots_out, col_out, row_out, wide, *, cap, half):
    experts, chunks, block, _ = slots_out.shape
    first_slot = rank_ref[0] * (half * chunks)

    def code(expert, position):
        place = position.astype(jnp.int32) - first_slot
        good = (expert >= 0) & (position < cap) & (place >= 0) & (place < half * chunks)
        slot = expert * block + place
        for c in range(1, chunks):
            slot = jnp.where(place >= c * half, slot + (experts * block - half), slot)
        return jnp.where(good, slot, -1)

    lanes = col_ref.shape[0]
    span = lanes * experts
    routes = col_ref[...].astype(F32).T.astype(jnp.int32)
    spread_lanes = (iota((lanes, span), 1) // experts == iota((lanes, span), 0)).astype(BF16)
    gather_lanes = (iota((span, lanes), 0) // experts == iota((span, lanes), 1)).astype(BF16)
    chosen = nn(routes.astype(F32).astype(BF16), spread_lanes) == (iota((PAD, span), 1) % experts).astype(F32)
    ones = chosen.astype(F32)
    lower = (iota((PAD, PAD), 0) > iota((PAD, PAD), 1)).astype(BF16)
    before = nn(lower, ones.astype(BF16))
    totals = jnp.broadcast_to(jnp.sum(ones, axis=0, keepdims=True), (16, span)).astype(BF16)
    source, target = iota((span, span), 0), iota((span, span), 1)
    earlier = (source % experts == target % experts) & (source // experts < target // experts)
    before = before + nn(totals, earlier.astype(BF16))[0:1]
    place = nn((jnp.minimum(before, float(cap)) * ones).astype(BF16), gather_lanes)
    col_out[...] = code(routes, place)

    step = 128
    blocks = row_ref.shape[1] // step
    upper = (iota((step, step), 0) < iota((step, step), 1)).astype(BF16)
    order = [(choice, b) for choice in range(2) for b in range(blocks)]
    picked = [row_ref[choice : choice + 1, b * step : (b + 1) * step] for choice, b in order]
    ones = [(p == iota((experts, step), 0)).astype(F32) for p in picked]
    before = nn(jnp.concatenate(ones, axis=0).astype(BF16), upper)
    base = jnp.zeros((experts, 1), F32)
    for k, (choice, b) in enumerate(order):
        position = jnp.sum((before[k * experts : (k + 1) * experts] + base) * ones[k], axis=0, keepdims=True)
        row_out[choice : choice + 1, b * step : (b + 1) * step] = code(picked[k], position)
        base = base + jnp.sum(ones[k], axis=1, keepdims=True)

    pad_images(cot_ref, wide, cot_out)
    rows = cot_out[...].reshape(-1, cot_out.shape[2])
    step = min(512, experts * block)
    per = step // block
    blocks = experts // per

    def some_slots(k, _):
        value = nn(slot_match(row_out, k * step, step), rows).astype(BF16)
        slots_out[pl.ds(lax.rem(k, blocks) * per, per), lax.div(k, blocks)] = value.reshape(per, block, -1)
        return 0

    lax.fori_loop(0, chunks * blocks, some_slots, 0)


def front(rank, cotangent, routes, experts, cap, half, block, chunks):
    rows, width = cotangent.shape
    images = rows // SEQ
    padded = jnp.pad(
        routes.T.reshape(2, images, SEQ), ((0, 0), (0, 0), (0, PAD - SEQ)), constant_values=-1
    )
    down = padded.reshape(2 * images, PAD)
    across = padded.reshape(2, images * PAD)
    return pl.pallas_call(
        functools.partial(front_kernel, cap=cap, half=half),
        out_shape=(
            jax.ShapeDtypeStruct((images, PAD, width), BF16),
            jax.ShapeDtypeStruct((experts, chunks, block, width), BF16),
            jax.ShapeDtypeStruct(down.shape[::-1], jnp.int32),
            jax.ShapeDtypeStruct(across.shape, jnp.int32),
        ),
        in_specs=[pl.BlockSpec(memory_space=pltpu.SMEM)] + [VMEM] * 3,
        out_specs=(VMEM,) * 4,
        scratch_shapes=[wide_scratch(images, width)],
        compiler_params=params(),
        cost_estimate=cost(10),
        name="front",
    )(rank, cotangent, down, across)


def spread_kernel(code_ref, rows_ref, out_ref, *, start):
    step = out_ref.shape[0] * out_ref.shape[1]
    value = nn(slot_match(code_ref, pl.program_id(0) * step + start, step), rows_ref[...])
    out_ref[...] = value.astype(BF16).reshape(out_ref.shape)


def spread(code_row, rows, experts, block, chunk, step=256):
    count, width = rows.shape
    slots = experts * block
    per = step // block
    return pl.pallas_call(
        functools.partial(spread_kernel, start=chunk * slots),
        out_shape=jax.ShapeDtypeStruct((experts, block, width), BF16),
        grid=(slots // step,),
        in_specs=[full((2, count)), full((count, width))],
        out_specs=pl.BlockSpec((per, block, width), lambda i: (i, 0, 0)),
        compiler_params=params(),
        cost_estimate=cost(5),
        name="spread",
    )(code_row, rows)


def row_mean(v):
    return jnp.mean(v, axis=-1, keepdims=True)


def key_softmax(scores):
    cut = SEQ // 16 * 16
    head, tail = scores[:cut], scores[cut:]
    valid = lax.broadcasted_iota(jnp.int32, tail.shape, 0) < SEQ - cut
    tail = jnp.where(valid, tail, -jnp.inf)
    top = jnp.maximum(jnp.max(head, axis=0, keepdims=True), jnp.max(tail, axis=0, keepdims=True))
    head, tail = jnp.exp(head - top), jnp.exp(tail - top)
    total = jnp.sum(head, axis=0, keepdims=True) + jnp.sum(tail, axis=0, keepdims=True)
    scale = 1.0 / total
    return jnp.concatenate([head * scale, tail * scale], axis=0)


QUAD = 4 * HEAD_DIM


def quad_masks():
    lane = iota((PAD, QUAD), 1)
    return [(lane >= h * HEAD_DIM) & (lane < (h + 1) * HEAD_DIM) for h in range(4)]


def stacked(value, masks):
    return jnp.concatenate([jnp.where(m, value, jnp.zeros_like(value)) for m in masks], axis=0)


def unstacked(value, masks):
    return sum(jnp.where(m, value[h * PAD : (h + 1) * PAD], 0.0) for h, m in enumerate(masks))


def attend_kernel(place_ref, tok_ref, ga_ref, gm_ref, *rest, pieces, own):
    wq, wo, rest = rest[:pieces], rest[pieces : 2 * pieces], rest[2 * pieces :]
    routed_ref, res_ref, qkv_ref, prob_ref, att_ref, wq_all, wo_all, qkv_all, att_all = rest
    batch, _, model = tok_ref.shape
    keep = pl.program_id(0) * batch < own

    @pl.when(pl.program_id(0) == 0)
    def _():
        at = 0
        size = wo[0].shape[0]
        if pieces == 1:
            places = [0]
        else:
            core, small = place_ref[1], wo[1].shape[0]
            places = [0, size + core * small, size + (1 - core) * small]
        for k, start in enumerate(places):
            cols = wo[k].shape[0]
            for j in range(3):
                to = start + j * model
                if k:
                    to = pl.multiple_of(to, 128)
                wq_all[:, pl.ds(to, cols)] = wq[k][j]
            if k:
                start = pl.multiple_of(start, 128)
            wo_all[pl.ds(start, cols), :] = wo[k][...]

    tok = tok_ref[...].reshape(batch * PAD, model).astype(F32)
    center = tok - row_mean(tok)
    normed = (center * lax.rsqrt(row_mean(center * center) + EPS) * ga_ref[...]).astype(BF16)
    value = nn(normed, wq_all[...])
    qkv_all[:, :model] = (value[:, :model] * HEAD_DIM**-0.5).astype(BF16)
    qkv_all[:, model:] = value[:, model:].astype(BF16)
    masks = quad_masks()
    key_ok = iota((4 * PAD, PAD), 1) < SEQ
    for g in range(batch):
        rows = slice(g * PAD, (g + 1) * PAD)
        for quad in range(model // QUAD):
            q, k, v = (qkv_all[rows, j * model + quad * QUAD : j * model + (quad + 1) * QUAD] for j in range(3))
            scores = jnp.where(key_ok, nt(stacked(q, masks), k), -jnp.inf)
            ex = jnp.exp(scores - jnp.max(scores, axis=1, keepdims=True))
            probs = (ex * (1.0 / jnp.sum(ex, axis=1, keepdims=True))).astype(BF16)

            @pl.when(keep)
            def _():
                prob_ref[g, quad] = probs

            mixed = unstacked(nn(probs, v), masks)
            att_all[rows, quad * QUAD : (quad + 1) * QUAD] = mixed.astype(BF16)

    residual = tok + nn(att_all[...], wo_all[...])

    @pl.when(keep)
    def _():
        res_ref[...] = residual.reshape(batch, PAD, model)
        qkv_ref[...] = qkv_all[...].reshape(batch, PAD, 3 * model)
        att_ref[...] = att_all[...].reshape(batch, PAD, model)

    center = residual - row_mean(residual)
    normed = center * lax.rsqrt(row_mean(center * center) + EPS) * gm_ref[...]
    routed_ref[...] = normed.astype(BF16).reshape(batch, PAD, model)


def attend(place, tok_pad, gain_attn, gain_moe, wq, wo, own, batch=2):
    images, _, width = tok_pad.shape
    batch = batch if own % batch == 0 else 1
    pieces = len(wq)
    steps = images // batch

    def image(i, place_ref):
        return (lax.rem(i + place_ref[0] // batch, steps), 0, 0)

    def kept(*shape):
        return pl.BlockSpec(
            (batch,) + shape, lambda i, place_ref: (jnp.minimum(i, own // batch - 1),) + (0,) * len(shape)
        )

    rows = pl.BlockSpec((batch, PAD, width), image)
    probs = (width // QUAD, 4 * PAD, PAD)
    return pl.pallas_call(
        functools.partial(attend_kernel, pieces=pieces, own=own),
        out_shape=(
            jax.ShapeDtypeStruct((images, PAD, width), BF16),
            jax.ShapeDtypeStruct((own, PAD, width), F32),
            jax.ShapeDtypeStruct((own, PAD, 3 * width), BF16),
            jax.ShapeDtypeStruct((own,) + probs, BF16),
            jax.ShapeDtypeStruct((own, PAD, width), BF16),
            jax.ShapeDtypeStruct((width, 3 * width), BF16),
            jax.ShapeDtypeStruct((width, width), BF16),
        ),
        grid_spec=pltpu.PrefetchScalarGridSpec(
            num_scalar_prefetch=1,
            grid=(steps,),
            in_specs=[rows, full((1, width)), full((1, width))] + [full(v.shape) for v in (*wq, *wo)],
            out_specs=(
                rows,
                kept(PAD, width),
                kept(PAD, 3 * width),
                kept(*probs),
                kept(PAD, width),
                full((width, 3 * width)),
                full((width, width)),
            ),
            scratch_shapes=[
                pltpu.VMEM((batch * PAD, 3 * width), BF16),
                pltpu.VMEM((batch * PAD, width), BF16),
            ],
        ),
        compiler_params=params(),
        cost_estimate=cost(25),
        name="attend",
    )(place, tok_pad, gain_attn.reshape(1, -1), gain_moe.reshape(1, -1), *wq, *wo)


def expert_kernel(expert_ref, x_ref, cot_ref, wr_ref, *rest, parts, half, block, chunk, begins, ends):
    weights, rest = rest[: len(parts)], rest[len(parts) :]
    w1, w2, dw1, dw2, out_sum, gin_sum, low1, low2, gates, load_sems, store_sems = rest[-11:]
    shards, _, hidden = w1.shape
    before, rest = ((), rest) if begins else (rest[: 2 * shards], rest[2 * shards + 1 :])
    gin_ref, out_ref = rest[:2]
    given = rest[2 : 2 + 2 * shards]
    expert = expert_ref[0]
    size = min(chunk, hidden)
    blocks = hidden // size

    loads = [(s, ref, (w1, w2)[k].at[s, pl.ds(at, ref.shape[0])]) for (k, s, at), ref in zip(parts, weights)]
    loads += [(k % shards, ref, (dw1, dw2)[k // shards].at[k % shards]) for k, ref in enumerate(before)]
    loads = [(s, pltpu.make_async_copy(a, b, load_sems.at[k])) for k, (s, a, b) in enumerate(loads)]
    for s in range(shards):
        for where, copy in loads:
            if where == s:
                copy.start()

    def stores(s, c):
        cols = pl.ds(pl.multiple_of(c * size, size), size)
        if ends and s:
            sources = low1.at[:, cols], low2.at[cols, :]
        else:
            sources = dw1.at[s, :, cols], dw2.at[s, cols, :]
        targets = given[s].at[:, cols], given[shards + s].at[cols, :]
        return [
            pltpu.make_async_copy(a, b, store_sems.at[(s * blocks + c) * 2 + k])
            for k, (a, b) in enumerate(zip(sources, targets))
        ]

    x = x_ref[...]
    rows, width = x.shape
    cot = cot_ref[...].reshape(rows, width).astype(F32)
    logits = nt(x, wr_ref[...])
    ex = jnp.exp(logits - jnp.max(logits, axis=1, keepdims=True))
    mine = iota(ex.shape, 1) == expert
    gate = jnp.sum(jnp.where(mine, ex, 0.0), axis=1, keepdims=True) / jnp.sum(
        ex, axis=1, keepdims=True
    )
    grad_out = (gate * cot).astype(BF16)
    x_t = x.T
    out_sum[...] = jnp.zeros_like(out_sum)
    gin_sum[...] = jnp.zeros_like(gin_sum)
    c0 = (2.0 / jnp.pi) ** 0.5

    def some_hidden(k, _):
        for s in range(shards):

            @pl.when(k == s * blocks)
            def _():
                for where, copy in loads:
                    if where == s:
                        copy.wait()

        shard, at = lax.div(k, blocks), lax.rem(k, blocks)
        cols = pl.ds(pl.multiple_of(at * size, size), size)
        u = nn(x, w1[shard, :, cols])
        square = u * u
        t = jnp.tanh(u * (c0 + (c0 * 0.044715) * square))
        h = 0.5 + 0.5 * t
        slope = h + (0.5 * u) * (1.0 - t * t) * (c0 + (3 * c0 * 0.044715) * square)
        active = (u * h).astype(BF16)
        out_sum[...] += nn(active, w2[shard, cols, :])
        grad_pre = (nt(grad_out, w2[shard, cols, :]) * slope).astype(BF16)
        gin_sum[...] += nt(grad_pre, w1[shard, :, cols])
        first, second = nn(x_t, grad_pre), tn(active, grad_out)
        dw1[shard, :, cols] = first if begins else dw1[shard, :, cols] + first
        dw2[shard, cols, :] = second if begins else dw2[shard, cols, :] + second
        for s in range(shards):

            @pl.when(shard == s)
            def _():
                if ends and s:
                    low1[:, cols] = dw1[shard, :, cols].astype(BF16)
                    low2[cols, :] = dw2[shard, cols, :].astype(BF16)
                for copy in stores(s, at):
                    copy.start()

        return 0

    lax.fori_loop(0, shards * blocks, some_hidden, 0)
    down, across = iota((block, width), 0), iota((block, width), 1)
    gates[...] = jnp.broadcast_to(gate, gates.shape)
    group = min(2, rows // block)

    def some_groups(i, _):
        at = pl.multiple_of(i * group * block, group * block)
        span = pl.ds(at, group * block)
        out = out_sum[span, :]
        out_ref[pl.ds(i * group, group), 0] = (gates[span, 0:1] * out).astype(BF16).reshape(group, block, width)
        cot = cot_ref[pl.ds(i * group, group), 0].reshape(group * block, width).astype(F32)
        gate_grad = jnp.sum(cot * out, axis=1, keepdims=True)
        for g in range(group):
            rows_of_one = pl.ds(at + g * block, block)
            line = jnp.where(down == across, gate_grad[g * block : (g + 1) * block], 0.0)
            line = jnp.sum(line, axis=0, keepdims=True)
            high = line.astype(BF16).astype(F32)
            value = jnp.where(down == half + 1, line - high, gin_sum[rows_of_one, :])
            gin_ref[rows_of_one, :] = jnp.where(down == half, high, value).astype(BF16)
        return 0

    lax.fori_loop(0, rows // (group * block), some_groups, 0)
    for s in range(shards):
        for c in range(blocks):
            for copy in stores(s, c):
                copy.wait()


def experts_step(expert, x, cot, before, number, ends, w_router, w1, w2, half, block, chunk=512):
    rows, width = x.shape
    shards = len(w1)
    hidden = w1[0][0].shape[1]
    row_spec = full((rows, width))
    chunk_spec = pl.BlockSpec((rows // block, 1, block, width), lambda i, _: (0, number, 0, 0))
    anywhere = pl.BlockSpec(memory_space=pl.ANY)
    old = [] if before is None else [*before[1:], before[0]]
    parts, weights = [], []
    for k, shards_of_one in enumerate((w1, w2)):
        for s, pieces in enumerate(shards_of_one):
            at = 0
            for piece in pieces:
                parts.append((k, s, at))
                weights.append(piece)
                at += piece.shape[0]
    shapes = [(width, hidden)] * shards + [(hidden, width)] * shards
    low = (8, 128) if shards == 1 or not ends else None
    at = 4 + len(weights)
    alias = {at + 2 * shards: 1} if old else {}
    return pl.pallas_call(
        functools.partial(
            expert_kernel,
            parts=parts,
            half=half,
            block=block,
            chunk=chunk,
            begins=before is None,
            ends=ends,
        ),
        out_shape=(jax.ShapeDtypeStruct((rows, width), BF16), jax.ShapeDtypeStruct(cot.shape, BF16))
        + tuple(
            jax.ShapeDtypeStruct(v, BF16 if ends and k % shards else F32) for k, v in enumerate(shapes)
        ),
        grid_spec=pltpu.PrefetchScalarGridSpec(
            num_scalar_prefetch=1,
            grid=(1,),
            in_specs=[row_spec, chunk_spec, full(w_router.shape[::-1])] + [anywhere] * (len(weights) + len(old)),
            out_specs=(row_spec, chunk_spec) + (anywhere,) * len(shapes),
            scratch_shapes=[
                pltpu.VMEM((shards, width, hidden), BF16),
                pltpu.VMEM((shards, hidden, width), BF16),
                pltpu.VMEM((shards, width, hidden), F32),
                pltpu.VMEM((shards, hidden, width), F32),
                pltpu.VMEM((rows, width), F32),
                pltpu.VMEM((rows, width), F32),
                pltpu.VMEM(low or (width, hidden), BF16),
                pltpu.VMEM(low or (hidden, width), BF16),
                pltpu.VMEM((rows, 128), F32),
                pltpu.SemaphoreType.DMA((len(weights) + 2 * shards,)),
                pltpu.SemaphoreType.DMA((2 * shards * hidden // min(chunk, hidden),)),
            ],
        ),
        input_output_aliases=alias,
        compiler_params=params(62),
        cost_estimate=cost(20),
        name="experts",
    )(expert, x, cot, w_router.T, *weights, *old)


def collect_kernel(first_ref, code_ref, *rest, numbers, half, block, probs, before):
    chunks = len(numbers)
    parts, rest = rest[:chunks], rest[chunks:]
    old, rest = rest[:before], rest[before:]
    out_ref, rest = rest[0], rest[1:]
    count, width = parts[0].shape
    experts = count // block
    rows = PAD
    codes = code_ref[...]
    across = iota(codes.shape, 1)
    at = first_ref[0] + pl.program_id(0)
    images = codes.shape[1] // 2
    columns = [
        jnp.sum(jnp.where(across == at + c * images, codes, 0), axis=1, keepdims=True) for c in range(2)
    ]
    lane = iota((rows, count), 1)
    total = old[0][0] if old else None
    grads = None
    for c in range(chunks):
        shift = numbers[c] * count
        match = ((lane + shift == columns[0]) | (lane + shift == columns[1])).astype(BF16)
        value = nn(match, parts[c][...])
        total = value if total is None else total + value
        if probs:
            slot_grads = rest[1 + c]

            @pl.when(pl.program_id(0) == 0)
            def _():
                lines = jnp.zeros((experts, 128), F32)
                for e in range(experts):
                    tail = parts[c][e * block + block - 16 : (e + 1) * block, 0:128].astype(F32)
                    here = half - (block - 16)
                    line = tail[here : here + 1] + tail[here + 1 : here + 2]
                    lines = jnp.where(iota(lines.shape, 0) == e, line, lines)
                turned = lines.T[:block]
                high = turned.astype(BF16).astype(F32)
                both = jnp.concatenate([high, turned - high], axis=1)
                for e in range(experts):
                    own_lane = iota(both.shape, 1) % experts == e
                    slot_grads[e * block : (e + 1) * block, :] = jnp.where(own_lane, both, 0.0).astype(BF16)

            value = nn(match, slot_grads[...])
            grads = value if grads is None else grads + value
    out_ref[0] = total.astype(out_ref.dtype)
    if probs:
        turned = grads.T
        value = turned[:experts] + turned[experts:]
        rest[0][0] = value + old[1][0] if old else value


def collect(first, code_col, parts, own, dtype, half, block, probs=False, numbers=None, before=()):
    numbers = tuple(range(len(parts))) if numbers is None else numbers
    count, width = parts[0].shape
    outs = [jax.ShapeDtypeStruct((own, PAD, width), dtype)]
    if probs:
        outs.append(jax.ShapeDtypeStruct((own, count // block, PAD), F32))
    return pl.pallas_call(
        functools.partial(
            collect_kernel, numbers=numbers, half=half, block=block, probs=probs, before=len(before)
        ),
        out_shape=tuple(outs),
        grid_spec=pltpu.PrefetchScalarGridSpec(
            num_scalar_prefetch=1,
            grid=(own,),
            in_specs=[full(code_col.shape)]
            + [full((count, width))] * len(parts)
            + [pl.BlockSpec((1,) + v.shape[1:], lambda i, f: (i + f[0], 0, 0)) for v in before],
            out_specs=tuple(pl.BlockSpec((1,) + v.shape[1:], lambda i, f: (i, 0, 0)) for v in outs),
            scratch_shapes=[pltpu.VMEM((count, 2 * (count // block)), BF16)] * (len(parts) if probs else 0),
        ),
        compiler_params=params(),
        cost_estimate=cost(7),
        name="collect",
    )(first, code_col, *parts, *before)


def back_kernel(place_ref, *rest, steps, received, split):
    (sum_ref, gp_ref), rest = rest[:2], rest[2:]
    more, rest = rest[: 2 * received], rest[2 * received :]
    (res_ref, cot_ref, tok_ref, ga_ref, gm_ref, wrt_ref, wq, wo, qkv_ref, prob_ref, att_ref), rest = rest[:11], rest[11:]
    gtok_ref, packs, rest = rest[0], rest[1 : 2 + split], rest[2 + split :]
    dwq, dwo, small, gatt_all, dqkv_all, wq_here, qkv_here, prob_here, pack_ref, sems = rest
    experts = wrt_ref.shape[0]
    batch, _, model = res_ref.shape
    rows = batch * PAD
    step = pl.program_id(0)

    def loads(number):
        span = pl.ds(number * batch, batch)
        pairs = [(v.at[span], w.at[span]) for v, w in ((qkv_ref, qkv_here), (prob_ref, prob_here))]
        return [pltpu.make_async_copy(a, b, sems.at[number, k]) for k, (a, b) in enumerate(pairs)]

    weights = pltpu.make_async_copy(wq, wq_here, sems.at[0, 2])

    @pl.when(step == 0)
    def _():
        for copy in loads(0) + [weights]:
            copy.start()
        for number in range(1, steps):
            for copy in loads(number):
                copy.start()
        for ref in (dwq, dwo, small):
            ref[...] = jnp.zeros_like(ref)

    def flat(ref):
        return ref[...].reshape(rows, -1).astype(F32)

    residual = flat(res_ref)
    center = residual - row_mean(residual)
    scale = lax.rsqrt(row_mean(center * center) + EPS)
    xhat = center * scale
    gm = gm_ref[...]
    routed = (xhat * gm).astype(BF16)
    logits = nt(wrt_ref[...], routed)
    ex = jnp.exp(logits - jnp.max(logits, axis=0, keepdims=True))
    probs = ex / jnp.sum(ex, axis=0, keepdims=True)
    grad_probs = gp_ref[...]
    grad_routed = flat(sum_ref)
    if received:
        grad_routed = grad_routed + flat(more[0])
        grad_probs = grad_probs + more[1][...]
    grad_probs = jnp.concatenate([grad_probs[g] for g in range(batch)], axis=1)
    grad_logits = probs * (grad_probs - jnp.sum(probs * grad_probs, axis=0, keepdims=True))
    high = grad_logits.astype(BF16)
    low = (grad_logits - high.astype(F32)).astype(BF16)
    both = jnp.concatenate([high, low], axis=0)
    new = nn(both, routed)
    small[0:experts, :] += new[:experts] + new[experts:]
    grad_routed = grad_routed + tn(both, jnp.concatenate([wrt_ref[...]] * 2, axis=0))
    small[experts + 1 : experts + 2, :] += jnp.sum(grad_routed * xhat, axis=0, keepdims=True)
    g = grad_routed * gm
    grad_res = flat(cot_ref) + scale * (g - row_mean(g) - xhat * row_mean(g * xhat))
    grad_mixed = grad_res.astype(BF16)
    dwo[...] += tn(att_ref[...].reshape(rows, model), grad_mixed)
    gatt_all[...] = nt(grad_mixed, wo[...]).astype(BF16)

    masks = quad_masks()
    for number in range(steps):

        @pl.when(step == number)
        def _():
            for copy in loads(number):
                copy.wait()

    for b in range(batch):
        span = slice(b * PAD, (b + 1) * PAD)
        image = step * batch + b
        for quad in range(model // QUAD):
            q, k, v = (
                qkv_here[image, :, j * model + quad * QUAD : j * model + (quad + 1) * QUAD] for j in range(3)
            )
            grad_heads = stacked(gatt_all[span, quad * QUAD : (quad + 1) * QUAD], masks)
            low_probs = prob_here[image, quad]
            p = low_probs.astype(F32)
            gw = nt(grad_heads, v)
            ds = (p * (gw - jnp.sum(p * gw, axis=1, keepdims=True))).astype(BF16)
            grad_q = unstacked(nn(ds, k), masks) * HEAD_DIM**-0.5
            grad_k = tn(ds, stacked(q, masks))
            grad_v = tn(low_probs, grad_heads)
            for j, value in enumerate((grad_q, grad_k, grad_v)):
                dqkv_all[span, j * model + quad * QUAD : j * model + (quad + 1) * QUAD] = value.astype(BF16)

    tok = flat(tok_ref)
    center = tok - row_mean(tok)
    tok_scale = lax.rsqrt(row_mean(center * center) + EPS)
    xin = center * tok_scale
    ga = ga_ref[...]
    normed = (xin * ga).astype(BF16)
    dwq[...] += tn(normed, dqkv_all[...])

    @pl.when(step == 0)
    def _():
        weights.wait()

    grad_normed = nt(dqkv_all[...], wq_here[...])
    small[experts : experts + 1, :] += jnp.sum(grad_normed * xin, axis=0, keepdims=True)
    h = grad_normed * ga
    grad_tok = grad_res + tok_scale * (h - row_mean(h) - xin * row_mean(h * xin))
    gtok_ref[...] = grad_tok.astype(BF16).reshape(gtok_ref.shape)

    @pl.when(step == steps - 1)
    def _():
        shards = pack_ref.shape[0]
        part = model // shards
        for s in range(shards):
            at = 0
            blocks = [dwq[:, j * model + s * part : j * model + (s + 1) * part] for j in range(3)]
            for value in blocks + [dwo[s * part : (s + 1) * part, :], small[...]]:
                for c in range(value.shape[1] // 256):
                    pack_ref[s, at : at + value.shape[0], :] = value[:, c * 256 : (c + 1) * 256].astype(BF16)
                    at += value.shape[0]
            if at < pack_ref.shape[1]:
                pack_ref[s, at:, :] = jnp.zeros((pack_ref.shape[1] - at, 256), BF16)
        if split:
            size = packs[0].shape[1]
            at = pl.multiple_of(place_ref[1] * size, size)
            packs[0][...] = pack_ref[:, pl.ds(at, size), :]
            packs[1][...] = pack_ref[:, pl.ds(pl.multiple_of(size - at, size), size), :]
        else:
            packs[0][...] = pack_ref[...]


def small_rows(experts):
    return -(-(experts + 2) // 16) * 16


def pack_rows(width, part, experts, align):
    rows = 3 * width * (part // 256) + part * (width // 256) + small_rows(experts) * (width // 256)
    return -(-rows // align) * align


def back(place, sums, residual, cot_pad, tok_pad, qkv, probs, att, gain_attn, gain_moe, w_router, wq, wo, shards, align, batch=2):
    own, _, width = residual.shape
    batch = batch if own % batch == 0 else 1
    experts = w_router.shape[1]
    rows = pack_rows(width, width // shards, experts, align)
    split = int(shards == 2)

    def mine(*shape):
        return pl.BlockSpec((batch,) + shape, lambda i, f: (i,) + (0,) * len(shape))

    image = pl.BlockSpec((batch, PAD, width), lambda i, f: (i + f[0] // batch, 0, 0))
    flat = [v for pair in sums for v in pair]
    return pl.pallas_call(
        functools.partial(back_kernel, steps=own // batch, received=len(sums) - 1, split=split),
        out_shape=(jax.ShapeDtypeStruct((own, PAD, width), BF16),)
        + (jax.ShapeDtypeStruct((shards, rows // (1 + split), 256), BF16),) * (1 + split),
        grid_spec=pltpu.PrefetchScalarGridSpec(
            num_scalar_prefetch=1,
            grid=(own // batch,),
            in_specs=[mine(PAD, width), mine(experts, PAD)] * len(sums)
            + [
                mine(PAD, width),
                image,
                image,
                full((1, width)),
                full((1, width)),
                full((experts, width)),
                pl.BlockSpec(memory_space=pl.ANY),
                full(wo.shape),
                pl.BlockSpec(memory_space=pl.ANY),
                pl.BlockSpec(memory_space=pl.ANY),
                mine(*att.shape[1:]),
            ],
            out_specs=(mine(PAD, width),) + (full((shards, rows // (1 + split), 256)),) * (1 + split),
            scratch_shapes=[
                pltpu.VMEM((width, 3 * width), F32),
                pltpu.VMEM((width, width), F32),
                pltpu.VMEM((small_rows(experts), width), F32),
                pltpu.VMEM((batch * PAD, width), BF16),
                pltpu.VMEM((batch * PAD, 3 * width), BF16),
                pltpu.VMEM(wq.shape, BF16),
                pltpu.VMEM(qkv.shape, BF16),
                pltpu.VMEM(probs.shape, BF16),
                pltpu.VMEM((shards, rows, 256), BF16),
                pltpu.SemaphoreType.DMA((own // batch, 3)),
            ],
        ),
        compiler_params=params(),
        cost_estimate=cost(16),
        name="back",
    )(
        place,
        *flat,
        residual,
        cot_pad,
        tok_pad,
        gain_attn.reshape(1, -1),
        gain_moe.reshape(1, -1),
        w_router.T,
        wq,
        wo,
        qkv,
        probs,
        att,
    )


def unpad_kernel(first_ref, *refs, images):
    out_ref, wide = refs[-2:]
    pieces = len(refs) // 2 - 1
    parts = refs[:pieces], refs[pieces:-2]
    own, peer = ([(ref, i) for ref in part for i in range(ref.shape[0])] for part in parts)
    for i in range(images):
        inner = i % len(own)
        mine = first_ref[0] == i - inner
        (own_ref, k), (peer_ref, _) = own[inner], peer[inner]
        value = jnp.where(mine, own_ref[k], peer_ref[k]).astype(F32)
        wide[i * SEQ : (i + 1) * SEQ, :] = value[:SEQ]
    out_ref[...] = wide[0 : images * SEQ, :].astype(out_ref.dtype)


def unpad(first, own, peer, dtype):
    images, width = 2 * sum(v.shape[0] for v in own), own[0].shape[2]
    return pl.pallas_call(
        functools.partial(unpad_kernel, images=images),
        out_shape=jax.ShapeDtypeStruct((images * SEQ, width), dtype),
        in_specs=[pl.BlockSpec(memory_space=pltpu.SMEM)] + [VMEM] * (2 * len(own)),
        out_specs=VMEM,
        scratch_shapes=[wide_scratch(images, width)],
        compiler_params=params(),
        cost_estimate=cost(2),
        name="unpad",
    )(first, *own, *peer)


def body(tokens, routes, gain_attn, w_qkv, w_attn_out, gain_moe, w_router, w_expert_in, w_expert_out, cotangent, *, ways, groups):
    tok_rows, width = tokens.shape
    experts = w_router.shape[1]
    cap = max(4, (5 * tok_rows // (2 * experts) + 7) // 8 * 8)
    chunks = 2
    half = -(-cap // (ways * chunks))
    block = -(-(half + 2) // 16) * 16
    slots = experts * block
    images = tok_rows // SEQ
    own = images // ways
    rank = lax.axis_index("tensor")
    expert = lax.axis_index("expert")
    first = (rank * own).astype(jnp.int32).reshape(1)
    swap = [(0, 1), (1, 0)]

    def other(v):
        return lax.ppermute(v, "tensor", swap)

    def shards_of(v, axis):
        if ways == 2:
            return [v, other(v)]
        return [lax.all_gather(v, "tensor", axis=axis, tiled=True)]

    def exchange(rows):
        return lax.all_to_all(rows, "expert", split_axis=0, concat_axis=0, tiled=True)

    def after(v, *others):
        return lax.optimization_barrier((v,) + others)[0]

    def rows_of(v):
        return v.reshape(-1, width)

    def collected(number, parts, dtype, probs=False, numbers=None, before=()):
        return collect(number, code_col, parts, own, dtype, half, block, probs, numbers, before)

    if ways == 2:
        core = expert % 2
        near = [(i, i ^ 1) for i in range(groups)]

        def part_of(v, axis):
            size = v.shape[axis] // 2
            return other(lax.dynamic_slice_in_dim(v, core * size, size, axis))

    else:
        core = 0 * expert
        wq, wo = shards_of(w_qkv, 2), shards_of(w_attn_out, 0)
    cot_pad, cot_slots, code_col, code_row = front(
        rank.astype(jnp.int32).reshape(1), cotangent, routes, experts, cap, half, block, chunks
    )
    tok_pad = pad(after(tokens, cot_pad))
    if ways == 2:
        got_q, got_o = part_of(after(w_qkv, cot_slots), 2), part_of(after(w_attn_out, cot_slots), 0)
        got_q, got_o, tok_pad = lax.optimization_barrier((got_q, got_o, tok_pad))
        wq = [w_qkv, got_q, lax.ppermute(got_q, "expert", near)]
        wo = [w_attn_out, got_o, lax.ppermute(got_o, "expert", near)]
    cot_slots = exchange(cot_slots)
    w1 = shards_of(after(w_expert_in[0], wq[-1], wo[-1]), 1)
    if ways == 2:
        cut = w_expert_out.shape[1] // 4
        w2_first = other(after(w_expert_out[0, :cut], wq[-1], wo[-1]))
        w2_rest = other(after(w_expert_out[0, cut:], wq[-1], wo[-1]))
    place = jnp.stack([rank * own, core]).astype(jnp.int32)
    routed, residual, qkv, probs, att, wq, wo = attend(place, tok_pad, gain_attn, gain_moe, wq, wo, own)
    x_slots = []
    for c in range(chunks):
        rows = spread(code_row, rows_of(routed), experts, block, c)
        if c == 0:
            rows, cot_slots = lax.optimization_barrier((rows, cot_slots))
            if ways == 2:
                rows = after(rows, w1[-1], w2_first)
        elif ways == 2:
            rows = after(rows, w2_rest)
        x_slots.append(exchange(rows))
    if ways == 2:
        w1 = [[v] for v in w1]
        w2 = [[w_expert_out[0]], [w2_first, w2_rest]]
    else:
        w1 = [w1]
        w2 = [shards_of(w_expert_out[0], 0)]
    gin, more = [], None
    expert_number = expert.astype(jnp.int32).reshape(1)
    for c in range(chunks):
        new, *more = experts_step(
            expert_number, rows_of(x_slots[c]), cot_slots, more, c, c == chunks - 1, w_router, w1, w2, half, block
        )
        gin.append(exchange(new.reshape(experts, block, width)))
    gated, *dw = more
    gin = [rows_of(v) for v in gin]
    if ways == 2:
        there = ((1 - rank) * own).astype(jnp.int32).reshape(1)
        dw1_peer = other(dw[1])
        cut = 3 * dw[3].shape[0] // 16
        dw2_peer = [other(dw[3][:cut])]
        zero = jnp.zeros((1,), jnp.int32)
        start = collect(zero, code_col, gin[:1], images, F32, half, block, True, (0,))
        gin[1], *start = lax.optimization_barrier((gin[1], *start))
        sent = collected(there, gin[1:], BF16, True, (1,), start)
        received = tuple(other(v) for v in sent)
        mine = collected(first, gin[1:], F32, True, (1,), start)
        gated = exchange(after(gated, *sent, dw1_peer, dw2_peer[0]))
        grad_w1 = dw[0] + dw1_peer.astype(F32)
        *received, grad_w1 = lax.optimization_barrier((*received, grad_w1, *mine))[:3]
        sums = [mine, received]
        dw2_peer.append(other(after(dw[3][cut:], *received)))
    else:
        gated = exchange(gated)
        every = [collected(jnp.full((1,), r * own, jnp.int32), gin, F32, True) for r in range(ways)]
        sums = [
            tuple(
                lax.psum_scatter(jnp.stack([v[k] for v in every]).astype(t), "tensor", scatter_dimension=0).astype(F32)
                for k, t in ((0, BF16), (1, F32))
            )
        ]
        grad_w1 = lax.psum_scatter(dw[0].astype(BF16), "tensor", scatter_dimension=1, tiled=True).astype(F32)
        grad_w2 = lax.psum_scatter(dw[1].astype(BF16), "tensor", scatter_dimension=0, tiled=True).astype(F32)
    grad_tok, *pack = back(
        place, sums, residual, cot_pad, tok_pad, qkv, probs, att, gain_attn, gain_moe, w_router, wq, wo,
        2 if ways == 2 else 1, groups * 8,
    )

    bits = [1 << b for b in range(groups.bit_length() - 1)]
    if ways == 2:

        def swap_bit(v, bit):
            return lax.ppermute(v, "expert", [(i, i ^ bit) for i in range(groups)])

        def add(a, b):
            return (a.astype(F32) + b.astype(F32)).astype(BF16)

        def halves(v, bit):
            size = v.shape[-2] // 2
            upper = (expert // bit) % 2
            keep = lax.dynamic_slice_in_dim(v, upper * size, size, v.ndim - 2)
            give = lax.dynamic_slice_in_dim(v, (1 - upper) * size, size, v.ndim - 2)
            return keep, give

        keep, give, grad_tok, gated, dw2_peer[1] = lax.optimization_barrier((*pack, grad_tok, gated, dw2_peer[1]))
        grad_peer = other(grad_tok)
        gated = [rows_of(gated[:, c]) for c in range(chunks)]
        (mix,) = collect(zero, code_col, gated, images, BF16, half, block)
        mix_there = lax.dynamic_slice_in_dim(mix, (1 - rank) * own, own, 0)
        mix_here = lax.dynamic_slice_in_dim(mix, rank * own, own, 0)
        pack = add(keep, swap_bit(give, bits[0]))
        keep, give = halves(pack, bits[1])
        pack = add(keep, swap_bit(give, bits[1]))
        mix_peer = other(mix_there)
        pack, mix_there, grad_peer = lax.optimization_barrier((pack, mix_there, grad_peer))
        keep, give = halves(pack, bits[2])
        pack = add(keep, swap_bit(give, bits[2]))
        grad_tokens = unpad(first, [grad_tok], [grad_peer], F32)
        keep, give = halves(pack, bits[3])
        pack, grad_w2, mix_here = lax.optimization_barrier(
            (add(keep, swap_bit(give, bits[3])), dw[2] + jnp.concatenate(dw2_peer).astype(F32), mix_here)
        )
        pack, mix_peer, grad_tokens = lax.optimization_barrier((pack, mix_peer, grad_tokens))
        swapped = other(pack[1])
        result = (residual + (mix_here.astype(F32) + mix_peer.astype(F32))).astype(BF16)
        swapped, result = lax.optimization_barrier((swapped, result))
        result_peer = other(result)
        total = add(pack[0], swapped)

        def gathered(v, bit):
            got = swap_bit(v, bit)
            upper = (expert // bit) % 2 == 1
            return jnp.where(upper, jnp.concatenate([got, v]), jnp.concatenate([v, got]))

        for bit in bits[3:1:-1]:
            total = gathered(total, bit)
        total = gathered(total, bits[1])
        total, result_peer = lax.optimization_barrier((total, result_peer))
        total = gathered(total, bits[0])
        total = total.astype(F32)
        part = w_qkv.shape[2]
    else:
        gated = [rows_of(gated[:, c]) for c in range(chunks)]
        every = [collected(jnp.full((1,), r * own, jnp.int32), gated, BF16)[0] for r in range(ways)]
        mixture = lax.psum_scatter(jnp.stack(every), "tensor", scatter_dimension=0).astype(F32)

        def whole(v):
            v = lax.all_gather(v, "tensor", axis=0, tiled=True)
            return v[:, :SEQ].reshape(tok_rows, width)

        result = whole((residual + mixture).astype(BF16))
        grad_tokens = whole(grad_tok).astype(F32)
        total = lax.psum(pack[0][0], ("expert", "tensor")).astype(F32)
        part = width

    def take(at, rows, cols):
        blocks = [total[at + b * rows : at + (b + 1) * rows] for b in range(cols // 256)]
        return jnp.concatenate(blocks, axis=1) if len(blocks) > 1 else blocks[0]

    step = width * (part // 256)
    grad_w_qkv = jnp.stack([take(j * step, width, part) for j in range(3)])
    grad_w_attn_out = take(3 * step, part, width)
    small = take(3 * step + part * (width // 256), small_rows(experts), width)
    if ways != 2:
        grad_w_qkv = lax.dynamic_slice_in_dim(grad_w_qkv, rank * w_qkv.shape[2], w_qkv.shape[2], 2)
        grad_w_attn_out = lax.dynamic_slice_in_dim(grad_w_attn_out, rank * w_qkv.shape[2], w_qkv.shape[2], 0)
    sums = (small[experts], grad_w_qkv, grad_w_attn_out, small[experts + 1], small[:experts].T)
    if ways == 2:
        result = unpad(first, [result], [result_peer], BF16)
    return (result, grad_tokens, *sums, grad_w1[None], grad_w2[None])


def solution(mesh):
    placed = (
        P("expert", None),
        P("expert", None),
        P(),
        P(None, None, "tensor"),
        P("tensor", None),
        P(),
        P(),
        P("expert", None, "tensor"),
        P("expert", "tensor", None),
        P("expert", None),
    )
    return jax.shard_map(
        functools.partial(body, ways=mesh.shape["tensor"], groups=mesh.shape["expert"]),
        mesh=mesh,
        in_specs=placed,
        out_specs=(
            P("expert", None),
            P("expert", None),
            P(),
            P(None, None, "tensor"),
            P("tensor", None),
            P(),
            P(),
            P("expert", None, "tensor"),
            P("expert", "tensor", None),
        ),
        check_vma=False,
    )
```

```python
import functools

import jax
import jax.numpy as jnp
from jax import lax
from jax.experimental import pallas as pl
from jax.experimental.pallas import tpu as pltpu
from jax.sharding import PartitionSpec as P

HEAD_DIM = 64
SEQ = 197
PAD = 208
SENT = 200
EPS = 1e-06
F32 = jnp.float32
BF16 = jnp.bfloat16
VMEM = pl.BlockSpec(memory_space=pltpu.VMEM)


def nn(a, b):
    return lax.dot_general(a, b, (((1,), (0,)), ((), ())), preferred_element_type=F32)


def nt(a, b):
    return lax.dot_general(a, b, (((1,), (1,)), ((), ())), preferred_element_type=F32)


def tn(a, b):
    return lax.dot_general(a, b, (((0,), (0,)), ((), ())), preferred_element_type=F32)


def params(mib=56):
    return pltpu.CompilerParams(vmem_limit_bytes=mib << 20)


def cost(us):
    return pl.CostEstimate(flops=0, bytes_accessed=int(us * 3.69e6), transcendentals=0)


def full(shape):
    return pl.BlockSpec(shape, lambda *_: (0,) * len(shape))


def pad_images(source, wide, target):
    wide[0 : source.shape[0], :] = source[...].astype(F32)

    def one_image(i, _):
        off = lax.rem(i * SEQ, 8)
        window = wide[pl.ds(pl.multiple_of(i * SEQ - off, 8), PAD + 8), :]
        window = pltpu.roll(window, lax.rem(PAD + 8 - off, PAD + 8), 0)[:PAD]
        target[i] = jnp.where(iota(window.shape, 0) < SEQ, window, 0.0).astype(BF16)
        return 0

    lax.fori_loop(0, target.shape[0], one_image, 0)


def pad_kernel(source, target, wide):
    pad_images(source, wide, target)


def wide_scratch(images, width):
    return pltpu.VMEM((-(-((images - 1) * SEQ + PAD + 8) // 16) * 16, width), F32)


def pad(rows):
    images, width = rows.shape[0] // SEQ, rows.shape[1]
    return pl.pallas_call(
        pad_kernel,
        out_shape=jax.ShapeDtypeStruct((images, PAD, width), BF16),
        in_specs=[VMEM],
        out_specs=VMEM,
        scratch_shapes=[wide_scratch(images, width)],
        compiler_params=params(),
        cost_estimate=cost(2),
        name="pad",
    )(rows)


def iota(shape, axis):
    return lax.broadcasted_iota(jnp.int32, shape, axis)


def slot_match(code_ref, start, step):
    slot = iota((step, code_ref.shape[1]), 0) + start
    return ((slot == code_ref[0:1, :]) | (slot == code_ref[1:2, :])).astype(BF16)


def front_kernel(rank_ref, cot_ref, col_ref, row_ref, cot_out, slots_out, col_out, row_out, wide, *, cap, half):
    experts, chunks, block, _ = slots_out.shape
    first_slot = rank_ref[0] * (half * chunks)

    def code(expert, position):
        place = position.astype(jnp.int32) - first_slot
        good = (expert >= 0) & (position < cap) & (place >= 0) & (place < half * chunks)
        slot = expert * block + place
        for c in range(1, chunks):
            slot = jnp.where(place >= c * half, slot + (experts * block - half), slot)
        return jnp.where(good, slot, -1)

    lanes = col_ref.shape[0]
    span = lanes * experts
    routes = col_ref[...].astype(F32).T.astype(jnp.int32)
    spread_lanes = (iota((lanes, span), 1) // experts == iota((lanes, span), 0)).astype(BF16)
    gather_lanes = (iota((span, lanes), 0) // experts == iota((span, lanes), 1)).astype(BF16)
    chosen = nn(routes.astype(F32).astype(BF16), spread_lanes) == (iota((PAD, span), 1) % experts).astype(F32)
    ones = chosen.astype(F32)
    lower = (iota((PAD, PAD), 0) > iota((PAD, PAD), 1)).astype(BF16)
    before = nn(lower, ones.astype(BF16))
    totals = jnp.broadcast_to(jnp.sum(ones, axis=0, keepdims=True), (16, span)).astype(BF16)
    source, target = iota((span, span), 0), iota((span, span), 1)
    earlier = (source % experts == target % experts) & (source // experts < target // experts)
    before = before + nn(totals, earlier.astype(BF16))[0:1]
    place = nn((jnp.minimum(before, float(cap)) * ones).astype(BF16), gather_lanes)
    col_out[...] = code(routes, place)

    step = 128
    blocks = row_ref.shape[1] // step
    upper = (iota((step, step), 0) < iota((step, step), 1)).astype(BF16)
    order = [(choice, b) for choice in range(2) for b in range(blocks)]
    picked = [row_ref[choice : choice + 1, b * step : (b + 1) * step] for choice, b in order]
    ones = [(p == iota((experts, step), 0)).astype(F32) for p in picked]
    before = nn(jnp.concatenate(ones, axis=0).astype(BF16), upper)
    base = jnp.zeros((experts, 1), F32)
    for k, (choice, b) in enumerate(order):
        position = jnp.sum((before[k * experts : (k + 1) * experts] + base) * ones[k], axis=0, keepdims=True)
        row_out[choice : choice + 1, b * step : (b + 1) * step] = code(picked[k], position)
        base = base + jnp.sum(ones[k], axis=1, keepdims=True)

    pad_images(cot_ref, wide, cot_out)
    rows = cot_out[...].reshape(-1, cot_out.shape[2])
    step = min(512, experts * block)
    per = step // block
    blocks = experts // per

    def some_slots(k, _):
        value = nn(slot_match(row_out, k * step, step), rows).astype(BF16)
        slots_out[pl.ds(lax.rem(k, blocks) * per, per), lax.div(k, blocks)] = value.reshape(per, block, -1)
        return 0

    lax.fori_loop(0, chunks * blocks, some_slots, 0)


def front(rank, cotangent, routes, experts, cap, half, block, chunks):
    rows, width = cotangent.shape
    images = rows // SEQ
    padded = jnp.pad(
        routes.T.reshape(2, images, SEQ), ((0, 0), (0, 0), (0, PAD - SEQ)), constant_values=-1
    )
    down = padded.reshape(2 * images, PAD)
    across = padded.reshape(2, images * PAD)
    return pl.pallas_call(
        functools.partial(front_kernel, cap=cap, half=half),
        out_shape=(
            jax.ShapeDtypeStruct((images, PAD, width), BF16),
            jax.ShapeDtypeStruct((experts, chunks, block, width), BF16),
            jax.ShapeDtypeStruct(down.shape[::-1], jnp.int32),
            jax.ShapeDtypeStruct(across.shape, jnp.int32),
        ),
        in_specs=[pl.BlockSpec(memory_space=pltpu.SMEM)] + [VMEM] * 3,
        out_specs=(VMEM,) * 4,
        scratch_shapes=[wide_scratch(images, width)],
        compiler_params=params(),
        cost_estimate=cost(10),
        name="front",
    )(rank, cotangent, down, across)


def spread_kernel(code_ref, rows_ref, out_ref, *, start):
    step = out_ref.shape[0] * out_ref.shape[1]
    value = nn(slot_match(code_ref, pl.program_id(0) * step + start, step), rows_ref[...])
    out_ref[...] = value.astype(BF16).reshape(out_ref.shape)


def spread(code_row, rows, experts, block, chunk, step=256):
    count, width = rows.shape
    slots = experts * block
    per = step // block
    return pl.pallas_call(
        functools.partial(spread_kernel, start=chunk * slots),
        out_shape=jax.ShapeDtypeStruct((experts, block, width), BF16),
        grid=(slots // step,),
        in_specs=[full((2, count)), full((count, width))],
        out_specs=pl.BlockSpec((per, block, width), lambda i: (i, 0, 0)),
        compiler_params=params(),
        cost_estimate=cost(5),
        name="spread",
    )(code_row, rows)


def row_mean(v):
    return jnp.mean(v, axis=-1, keepdims=True)


def key_softmax(scores):
    cut = SEQ // 16 * 16
    head, tail = scores[:cut], scores[cut:]
    valid = lax.broadcasted_iota(jnp.int32, tail.shape, 0) < SEQ - cut
    tail = jnp.where(valid, tail, -jnp.inf)
    top = jnp.maximum(jnp.max(head, axis=0, keepdims=True), jnp.max(tail, axis=0, keepdims=True))
    head, tail = jnp.exp(head - top), jnp.exp(tail - top)
    total = jnp.sum(head, axis=0, keepdims=True) + jnp.sum(tail, axis=0, keepdims=True)
    scale = 1.0 / total
    return jnp.concatenate([head * scale, tail * scale], axis=0)


QUAD = 4 * HEAD_DIM


def quad_masks():
    lane = iota((PAD, QUAD), 1)
    return [(lane >= h * HEAD_DIM) & (lane < (h + 1) * HEAD_DIM) for h in range(4)]


def stacked(value, masks):
    return jnp.concatenate([jnp.where(m, value, jnp.zeros_like(value)) for m in masks], axis=0)


def unstacked(value, masks):
    return sum(jnp.where(m, value[h * PAD : (h + 1) * PAD], 0.0) for h, m in enumerate(masks))


def attend_kernel(place_ref, tok_ref, ga_ref, gm_ref, *rest, pieces, own):
    wq, wo, rest = rest[:pieces], rest[pieces : 2 * pieces], rest[2 * pieces :]
    routed_ref, res_ref, qkv_ref, prob_ref, att_ref, wq_all, wo_all, qkv_all, att_all = rest
    batch, _, model = tok_ref.shape
    keep = pl.program_id(0) * batch < own

    @pl.when(pl.program_id(0) == 0)
    def _():
        at = 0
        size = wo[0].shape[0]
        if pieces == 1:
            places = [0]
        else:
            core, small = place_ref[1], wo[1].shape[0]
            places = [0, size + core * small, size + (1 - core) * small]
        for k, start in enumerate(places):
            cols = wo[k].shape[0]
            for j in range(3):
                to = start + j * model
                if k:
                    to = pl.multiple_of(to, 128)
                wq_all[:, pl.ds(to, cols)] = wq[k][j]
            if k:
                start = pl.multiple_of(start, 128)
            wo_all[pl.ds(start, cols), :] = wo[k][...]

    tok = tok_ref[...].reshape(batch * PAD, model).astype(F32)
    center = tok - row_mean(tok)
    normed = (center * lax.rsqrt(row_mean(center * center) + EPS) * ga_ref[...]).astype(BF16)
    value = nn(normed, wq_all[...])
    qkv_all[:, :model] = (value[:, :model] * HEAD_DIM**-0.5).astype(BF16)
    qkv_all[:, model:] = value[:, model:].astype(BF16)
    masks = quad_masks()
    key_ok = iota((4 * PAD, PAD), 1) < SEQ
    for g in range(batch):
        rows = slice(g * PAD, (g + 1) * PAD)
        for quad in range(model // QUAD):
            q, k, v = (qkv_all[rows, j * model + quad * QUAD : j * model + (quad + 1) * QUAD] for j in range(3))
            scores = jnp.where(key_ok, nt(stacked(q, masks), k), -jnp.inf)
            ex = jnp.exp(scores - jnp.max(scores, axis=1, keepdims=True))
            probs = (ex * (1.0 / jnp.sum(ex, axis=1, keepdims=True))).astype(BF16)

            @pl.when(keep)
            def _():
                prob_ref[g, quad] = probs

            mixed = unstacked(nn(probs, v), masks)
            att_all[rows, quad * QUAD : (quad + 1) * QUAD] = mixed.astype(BF16)

    residual = tok + nn(att_all[...], wo_all[...])

    @pl.when(keep)
    def _():
        res_ref[...] = residual.reshape(batch, PAD, model)
        qkv_ref[...] = qkv_all[...].reshape(batch, PAD, 3 * model)
        att_ref[...] = att_all[...].reshape(batch, PAD, model)

    center = residual - row_mean(residual)
    normed = center * lax.rsqrt(row_mean(center * center) + EPS) * gm_ref[...]
    routed_ref[...] = normed.astype(BF16).reshape(batch, PAD, model)


def attend(place, tok_pad, gain_attn, gain_moe, wq, wo, own, batch=2):
    images, _, width = tok_pad.shape
    batch = batch if own % batch == 0 else 1
    pieces = len(wq)
    steps = images // batch

    def image(i, place_ref):
        return (lax.rem(i + place_ref[0] // batch, steps), 0, 0)

    def kept(*shape):
        return pl.BlockSpec(
            (batch,) + shape, lambda i, place_ref: (jnp.minimum(i, own // batch - 1),) + (0,) * len(shape)
        )

    rows = pl.BlockSpec((batch, PAD, width), image)
    probs = (width // QUAD, 4 * PAD, PAD)
    return pl.pallas_call(
        functools.partial(attend_kernel, pieces=pieces, own=own),
        out_shape=(
            jax.ShapeDtypeStruct((images, PAD, width), BF16),
            jax.ShapeDtypeStruct((own, PAD, width), F32),
            jax.ShapeDtypeStruct((own, PAD, 3 * width), BF16),
            jax.ShapeDtypeStruct((own,) + probs, BF16),
            jax.ShapeDtypeStruct((own, PAD, width), BF16),
            jax.ShapeDtypeStruct((width, 3 * width), BF16),
            jax.ShapeDtypeStruct((width, width), BF16),
        ),
        grid_spec=pltpu.PrefetchScalarGridSpec(
            num_scalar_prefetch=1,
            grid=(steps,),
            in_specs=[rows, full((1, width)), full((1, width))] + [full(v.shape) for v in (*wq, *wo)],
            out_specs=(
                rows,
                kept(PAD, width),
                kept(PAD, 3 * width),
                kept(*probs),
                kept(PAD, width),
                full((width, 3 * width)),
                full((width, width)),
            ),
            scratch_shapes=[
                pltpu.VMEM((batch * PAD, 3 * width), BF16),
                pltpu.VMEM((batch * PAD, width), BF16),
            ],
        ),
        compiler_params=params(),
        cost_estimate=cost(25),
        name="attend",
    )(place, tok_pad, gain_attn.reshape(1, -1), gain_moe.reshape(1, -1), *wq, *wo)


def expert_kernel(expert_ref, x_ref, cot_ref, wr_ref, *rest, parts, half, block, chunk, begins, ends):
    weights, rest = rest[: len(parts)], rest[len(parts) :]
    w1, w2, dw1, dw2, out_sum, gin_sum, low1, low2, gates, load_sems, store_sems = rest[-11:]
    shards, _, hidden = w1.shape
    before, rest = ((), rest) if begins else (rest[: 2 * shards], rest[2 * shards + 1 :])
    gin_ref, out_ref = rest[:2]
    given = rest[2 : 2 + 2 * shards]
    expert = expert_ref[0]
    size = min(chunk, hidden)
    blocks = hidden // size

    loads = [(s, ref, (w1, w2)[k].at[s, pl.ds(at, ref.shape[0])]) for (k, s, at), ref in zip(parts, weights)]
    loads += [(k % shards, ref, (dw1, dw2)[k // shards].at[k % shards]) for k, ref in enumerate(before)]
    loads = [(s, pltpu.make_async_copy(a, b, load_sems.at[k])) for k, (s, a, b) in enumerate(loads)]
    for s in range(shards):
        for where, copy in loads:
            if where == s:
                copy.start()

    def stores(s, c):
        cols = pl.ds(pl.multiple_of(c * size, size), size)
        if ends and s:
            sources = low1.at[:, cols], low2.at[cols, :]
        else:
            sources = dw1.at[s, :, cols], dw2.at[s, cols, :]
        targets = given[s].at[:, cols], given[shards + s].at[cols, :]
        return [
            pltpu.make_async_copy(a, b, store_sems.at[(s * blocks + c) * 2 + k])
            for k, (a, b) in enumerate(zip(sources, targets))
        ]

    x = x_ref[...]
    rows, width = x.shape
    cot = cot_ref[...].reshape(rows, width).astype(F32)
    logits = nt(x, wr_ref[...])
    ex = jnp.exp(logits - jnp.max(logits, axis=1, keepdims=True))
    mine = iota(ex.shape, 1) == expert
    gate = jnp.sum(jnp.where(mine, ex, 0.0), axis=1, keepdims=True) / jnp.sum(
        ex, axis=1, keepdims=True
    )
    grad_out = (gate * cot).astype(BF16)
    x_t = x.T
    out_sum[...] = jnp.zeros_like(out_sum)
    gin_sum[...] = jnp.zeros_like(gin_sum)
    c0 = (2.0 / jnp.pi) ** 0.5

    def some_hidden(k, _):
        for s in range(shards):

            @pl.when(k == s * blocks)
            def _():
                for where, copy in loads:
                    if where == s:
                        copy.wait()

        shard, at = lax.div(k, blocks), lax.rem(k, blocks)
        cols = pl.ds(pl.multiple_of(at * size, size), size)
        u = nn(x, w1[shard, :, cols])
        square = u * u
        t = jnp.tanh(u * (c0 + (c0 * 0.044715) * square))
        h = 0.5 + 0.5 * t
        slope = h + (0.5 * u) * (1.0 - t * t) * (c0 + (3 * c0 * 0.044715) * square)
        active = (u * h).astype(BF16)
        out_sum[...] += nn(active, w2[shard, cols, :])
        grad_pre = (nt(grad_out, w2[shard, cols, :]) * slope).astype(BF16)
        gin_sum[...] += nt(grad_pre, w1[shard, :, cols])
        first, second = nn(x_t, grad_pre), tn(active, grad_out)
        dw1[shard, :, cols] = first if begins else dw1[shard, :, cols] + first
        dw2[shard, cols, :] = second if begins else dw2[shard, cols, :] + second
        for s in range(shards):

            @pl.when(shard == s)
            def _():
                if ends and s:
                    low1[:, cols] = dw1[shard, :, cols].astype(BF16)
                    low2[cols, :] = dw2[shard, cols, :].astype(BF16)
                for copy in stores(s, at):
                    copy.start()

        return 0

    lax.fori_loop(0, shards * blocks, some_hidden, 0)
    down, across = iota((block, width), 0), iota((block, width), 1)
    gates[...] = jnp.broadcast_to(gate, gates.shape)
    group = min(2, rows // block)

    def some_groups(i, _):
        at = pl.multiple_of(i * group * block, group * block)
        span = pl.ds(at, group * block)
        out = out_sum[span, :]
        out_ref[pl.ds(i * group, group), 0] = (gates[span, 0:1] * out).astype(BF16).reshape(group, block, width)
        cot = cot_ref[pl.ds(i * group, group), 0].reshape(group * block, width).astype(F32)
        gate_grad = jnp.sum(cot * out, axis=1, keepdims=True)
        for g in range(group):
            rows_of_one = pl.ds(at + g * block, block)
            line = jnp.where(down == across, gate_grad[g * block : (g + 1) * block], 0.0)
            line = jnp.sum(line, axis=0, keepdims=True)
            high = line.astype(BF16).astype(F32)
            value = jnp.where(down == half + 1, line - high, gin_sum[rows_of_one, :])
            gin_ref[rows_of_one, :] = jnp.where(down == half, high, value).astype(BF16)
        return 0

    lax.fori_loop(0, rows // (group * block), some_groups, 0)
    for s in range(shards):
        for c in range(blocks):
            for copy in stores(s, c):
                copy.wait()


def experts_step(expert, x, cot, before, number, ends, w_router, w1, w2, half, block, chunk=512):
    rows, width = x.shape
    shards = len(w1)
    hidden = w1[0][0].shape[1]
    row_spec = full((rows, width))
    chunk_spec = pl.BlockSpec((rows // block, 1, block, width), lambda i, _: (0, number, 0, 0))
    anywhere = pl.BlockSpec(memory_space=pl.ANY)
    old = [] if before is None else [*before[1:], before[0]]
    parts, weights = [], []
    for k, shards_of_one in enumerate((w1, w2)):
        for s, pieces in enumerate(shards_of_one):
            at = 0
            for piece in pieces:
                parts.append((k, s, at))
                weights.append(piece)
                at += piece.shape[0]
    shapes = [(width, hidden)] * shards + [(hidden, width)] * shards
    low = (8, 128) if shards == 1 or not ends else None
    at = 4 + len(weights)
    alias = {at + 2 * shards: 1} if old else {}
    return pl.pallas_call(
        functools.partial(
            expert_kernel,
            parts=parts,
            half=half,
            block=block,
            chunk=chunk,
            begins=before is None,
            ends=ends,
        ),
        out_shape=(jax.ShapeDtypeStruct((rows, width), BF16), jax.ShapeDtypeStruct(cot.shape, BF16))
        + tuple(
            jax.ShapeDtypeStruct(v, BF16 if ends and k % shards else F32) for k, v in enumerate(shapes)
        ),
        grid_spec=pltpu.PrefetchScalarGridSpec(
            num_scalar_prefetch=1,
            grid=(1,),
            in_specs=[row_spec, chunk_spec, full(w_router.shape[::-1])] + [anywhere] * (len(weights) + len(old)),
            out_specs=(row_spec, chunk_spec) + (anywhere,) * len(shapes),
            scratch_shapes=[
                pltpu.VMEM((shards, width, hidden), BF16),
                pltpu.VMEM((shards, hidden, width), BF16),
                pltpu.VMEM((shards, width, hidden), F32),
                pltpu.VMEM((shards, hidden, width), F32),
                pltpu.VMEM((rows, width), F32),
                pltpu.VMEM((rows, width), F32),
                pltpu.VMEM(low or (width, hidden), BF16),
                pltpu.VMEM(low or (hidden, width), BF16),
                pltpu.VMEM((rows, 128), F32),
                pltpu.SemaphoreType.DMA((len(weights) + 2 * shards,)),
                pltpu.SemaphoreType.DMA((2 * shards * hidden // min(chunk, hidden),)),
            ],
        ),
        input_output_aliases=alias,
        compiler_params=params(62),
        cost_estimate=cost(20),
        name="experts",
    )(expert, x, cot, w_router.T, *weights, *old)


def collect_kernel(first_ref, code_ref, *rest, numbers, half, block, probs, before):
    chunks = len(numbers)
    parts, rest = rest[:chunks], rest[chunks:]
    old, rest = rest[:before], rest[before:]
    out_ref, rest = rest[0], rest[1:]
    count, width = parts[0].shape
    experts = count // block
    rows = PAD
    codes = code_ref[...]
    across = iota(codes.shape, 1)
    at = first_ref[0] + pl.program_id(0)
    images = codes.shape[1] // 2
    columns = [
        jnp.sum(jnp.where(across == at + c * images, codes, 0), axis=1, keepdims=True) for c in range(2)
    ]
    lane = iota((rows, count), 1)
    total = old[0][0] if old else None
    grads = None
    for c in range(chunks):
        shift = numbers[c] * count
        match = ((lane + shift == columns[0]) | (lane + shift == columns[1])).astype(BF16)
        value = nn(match, parts[c][...])
        total = value if total is None else total + value
        if probs:
            slot_grads = rest[1 + c]

            @pl.when(pl.program_id(0) == 0)
            def _():
                lines = jnp.zeros((experts, 128), F32)
                for e in range(experts):
                    tail = parts[c][e * block + block - 16 : (e + 1) * block, 0:128].astype(F32)
                    here = half - (block - 16)
                    line = tail[here : here + 1] + tail[here + 1 : here + 2]
                    lines = jnp.where(iota(lines.shape, 0) == e, line, lines)
                turned = lines.T[:block]
                high = turned.astype(BF16).astype(F32)
                both = jnp.concatenate([high, turned - high], axis=1)
                for e in range(experts):
                    own_lane = iota(both.shape, 1) % experts == e
                    slot_grads[e * block : (e + 1) * block, :] = jnp.where(own_lane, both, 0.0).astype(BF16)

            value = nn(match, slot_grads[...])
            grads = value if grads is None else grads + value
    out_ref[0] = total[: out_ref.shape[1]].astype(out_ref.dtype)
    if probs:
        turned = grads.T
        value = turned[:experts] + turned[experts:]
        rest[0][0] = value + old[1][0] if old else value


def collect(first, code_col, parts, own, dtype, half, block, probs=False, numbers=None, before=(), rows=PAD):
    numbers = tuple(range(len(parts))) if numbers is None else numbers
    count, width = parts[0].shape
    outs = [jax.ShapeDtypeStruct((own, rows, width), dtype)]
    if probs:
        outs.append(jax.ShapeDtypeStruct((own, count // block, PAD), F32))
    return pl.pallas_call(
        functools.partial(
            collect_kernel, numbers=numbers, half=half, block=block, probs=probs, before=len(before)
        ),
        out_shape=tuple(outs),
        grid_spec=pltpu.PrefetchScalarGridSpec(
            num_scalar_prefetch=1,
            grid=(own,),
            in_specs=[full(code_col.shape)]
            + [full((count, width))] * len(parts)
            + [pl.BlockSpec((1,) + v.shape[1:], lambda i, f: (i + f[0], 0, 0)) for v in before],
            out_specs=tuple(pl.BlockSpec((1,) + v.shape[1:], lambda i, f: (i, 0, 0)) for v in outs),
            scratch_shapes=[pltpu.VMEM((count, 2 * (count // block)), BF16)] * (len(parts) if probs else 0),
        ),
        compiler_params=params(),
        cost_estimate=cost(7),
        name="collect",
    )(first, code_col, *parts, *before)


def back_kernel(place_ref, *rest, steps, received, split):
    (sum_ref, gp_ref), rest = rest[:2], rest[2:]
    more, rest = rest[: 2 * received], rest[2 * received :]
    (res_ref, cot_ref, tok_ref, ga_ref, gm_ref, wrt_ref, wq, wo, qkv_ref, prob_ref, att_ref), rest = rest[:11], rest[11:]
    gtok_ref, packs, rest = rest[0], rest[1 : 2 + split], rest[2 + split :]
    dwq, dwo, small, gatt_all, dqkv_all, wq_here, qkv_here, prob_here, pack_ref, sems = rest
    experts = wrt_ref.shape[0]
    batch, _, model = res_ref.shape
    rows = batch * PAD
    step = pl.program_id(0)

    def loads(number):
        span = pl.ds(number * batch, batch)
        pairs = [(v.at[span], w.at[span]) for v, w in ((qkv_ref, qkv_here), (prob_ref, prob_here))]
        return [pltpu.make_async_copy(a, b, sems.at[number, k]) for k, (a, b) in enumerate(pairs)]

    weights = pltpu.make_async_copy(wq, wq_here, sems.at[0, 2])

    @pl.when(step == 0)
    def _():
        for copy in loads(0) + [weights]:
            copy.start()
        for number in range(1, steps):
            for copy in loads(number):
                copy.start()
        for ref in (dwq, dwo, small):
            ref[...] = jnp.zeros_like(ref)

    def flat(ref):
        return ref[...].reshape(rows, -1).astype(F32)

    residual = flat(res_ref)
    center = residual - row_mean(residual)
    scale = lax.rsqrt(row_mean(center * center) + EPS)
    xhat = center * scale
    gm = gm_ref[...]
    routed = (xhat * gm).astype(BF16)
    logits = nt(wrt_ref[...], routed)
    ex = jnp.exp(logits - jnp.max(logits, axis=0, keepdims=True))
    probs = ex / jnp.sum(ex, axis=0, keepdims=True)
    grad_probs = gp_ref[...]
    grad_routed = flat(sum_ref)
    if received:
        tail = jnp.zeros((PAD - more[0].shape[1], model), F32)
        both = [v for b in range(batch) for v in (more[0][b].astype(F32), tail)]
        grad_routed = grad_routed + jnp.concatenate(both, axis=0)
        grad_probs = grad_probs + more[1][...]
    grad_probs = jnp.concatenate([grad_probs[g] for g in range(batch)], axis=1)
    grad_logits = probs * (grad_probs - jnp.sum(probs * grad_probs, axis=0, keepdims=True))
    high = grad_logits.astype(BF16)
    low = (grad_logits - high.astype(F32)).astype(BF16)
    both = jnp.concatenate([high, low], axis=0)
    new = nn(both, routed)
    small[0:experts, :] += new[:experts] + new[experts:]
    grad_routed = grad_routed + tn(both, jnp.concatenate([wrt_ref[...]] * 2, axis=0))
    small[experts + 1 : experts + 2, :] += jnp.sum(grad_routed * xhat, axis=0, keepdims=True)
    g = grad_routed * gm
    grad_res = flat(cot_ref) + scale * (g - row_mean(g) - xhat * row_mean(g * xhat))
    grad_mixed = grad_res.astype(BF16)
    dwo[...] += tn(att_ref[...].reshape(rows, model), grad_mixed)
    gatt_all[...] = nt(grad_mixed, wo[...]).astype(BF16)

    masks = quad_masks()
    for number in range(steps):

        @pl.when(step == number)
        def _():
            for copy in loads(number):
                copy.wait()

    for b in range(batch):
        span = slice(b * PAD, (b + 1) * PAD)
        image = step * batch + b
        for quad in range(model // QUAD):
            q, k, v = (
                qkv_here[image, :, j * model + quad * QUAD : j * model + (quad + 1) * QUAD] for j in range(3)
            )
            grad_heads = stacked(gatt_all[span, quad * QUAD : (quad + 1) * QUAD], masks)
            low_probs = prob_here[image, quad]
            p = low_probs.astype(F32)
            gw = nt(grad_heads, v)
            ds = (p * (gw - jnp.sum(p * gw, axis=1, keepdims=True))).astype(BF16)
            grad_q = unstacked(nn(ds, k), masks) * HEAD_DIM**-0.5
            grad_k = tn(ds, stacked(q, masks))
            grad_v = tn(low_probs, grad_heads)
            for j, value in enumerate((grad_q, grad_k, grad_v)):
                dqkv_all[span, j * model + quad * QUAD : j * model + (quad + 1) * QUAD] = value.astype(BF16)

    tok = flat(tok_ref)
    center = tok - row_mean(tok)
    tok_scale = lax.rsqrt(row_mean(center * center) + EPS)
    xin = center * tok_scale
    ga = ga_ref[...]
    normed = (xin * ga).astype(BF16)
    dwq[...] += tn(normed, dqkv_all[...])

    @pl.when(step == 0)
    def _():
        weights.wait()

    grad_normed = nt(dqkv_all[...], wq_here[...])
    small[experts : experts + 1, :] += jnp.sum(grad_normed * xin, axis=0, keepdims=True)
    h = grad_normed * ga
    grad_tok = grad_res + tok_scale * (h - row_mean(h) - xin * row_mean(h * xin))
    for b in range(batch):
        gtok_ref[b] = grad_tok[b * PAD : b * PAD + gtok_ref.shape[1]].astype(BF16)

    @pl.when(step == steps - 1)
    def _():
        shards = pack_ref.shape[0]
        part = model // shards
        for s in range(shards):
            at = 0
            blocks = [dwq[:, j * model + s * part : j * model + (s + 1) * part] for j in range(3)]
            for value in blocks + [dwo[s * part : (s + 1) * part, :], small[...]]:
                for c in range(value.shape[1] // 256):
                    pack_ref[s, at : at + value.shape[0], :] = value[:, c * 256 : (c + 1) * 256].astype(BF16)
                    at += value.shape[0]
            if at < pack_ref.shape[1]:
                pack_ref[s, at:, :] = jnp.zeros((pack_ref.shape[1] - at, 256), BF16)
        if split:
            size = packs[0].shape[1]
            at = pl.multiple_of(place_ref[1] * size, size)
            packs[0][...] = pack_ref[:, pl.ds(at, size), :]
            packs[1][...] = pack_ref[:, pl.ds(pl.multiple_of(size - at, size), size), :]
        else:
            packs[0][...] = pack_ref[...]


def small_rows(experts):
    return -(-(experts + 2) // 16) * 16


def pack_rows(width, part, experts, align):
    rows = 3 * width * (part // 256) + part * (width // 256) + small_rows(experts) * (width // 256)
    return -(-rows // align) * align


def back(place, sums, residual, cot_pad, tok_pad, qkv, probs, att, gain_attn, gain_moe, w_router, wq, wo, shards, align, batch=2):
    own, _, width = residual.shape
    batch = batch if own % batch == 0 else 1
    experts = w_router.shape[1]
    rows = pack_rows(width, width // shards, experts, align)
    split = int(shards == 2)

    def mine(*shape):
        return pl.BlockSpec((batch,) + shape, lambda i, f: (i,) + (0,) * len(shape))

    image = pl.BlockSpec((batch, PAD, width), lambda i, f: (i + f[0] // batch, 0, 0))
    flat = [v for pair in sums for v in pair]
    return pl.pallas_call(
        functools.partial(back_kernel, steps=own // batch, received=len(sums) - 1, split=split),
        out_shape=(jax.ShapeDtypeStruct((own, SENT, width), BF16),)
        + (jax.ShapeDtypeStruct((shards, rows // (1 + split), 256), BF16),) * (1 + split),
        grid_spec=pltpu.PrefetchScalarGridSpec(
            num_scalar_prefetch=1,
            grid=(own // batch,),
            in_specs=[mine(*v.shape[1:]) for v in flat]
            + [
                mine(PAD, width),
                image,
                image,
                full((1, width)),
                full((1, width)),
                full((experts, width)),
                pl.BlockSpec(memory_space=pl.ANY),
                full(wo.shape),
                pl.BlockSpec(memory_space=pl.ANY),
                pl.BlockSpec(memory_space=pl.ANY),
                mine(*att.shape[1:]),
            ],
            out_specs=(mine(SENT, width),) + (full((shards, rows // (1 + split), 256)),) * (1 + split),
            scratch_shapes=[
                pltpu.VMEM((width, 3 * width), F32),
                pltpu.VMEM((width, width), F32),
                pltpu.VMEM((small_rows(experts), width), F32),
                pltpu.VMEM((batch * PAD, width), BF16),
                pltpu.VMEM((batch * PAD, 3 * width), BF16),
                pltpu.VMEM(wq.shape, BF16),
                pltpu.VMEM(qkv.shape, BF16),
                pltpu.VMEM(probs.shape, BF16),
                pltpu.VMEM((shards, rows, 256), BF16),
                pltpu.SemaphoreType.DMA((own // batch, 3)),
            ],
        ),
        compiler_params=params(),
        cost_estimate=cost(16),
        name="back",
    )(
        place,
        *flat,
        residual,
        cot_pad,
        tok_pad,
        gain_attn.reshape(1, -1),
        gain_moe.reshape(1, -1),
        w_router.T,
        wq,
        wo,
        qkv,
        probs,
        att,
    )


def unpad_kernel(first_ref, *refs, images):
    out_ref, wide = refs[-2:]
    pieces = len(refs) // 2 - 1
    parts = refs[:pieces], refs[pieces:-2]
    own, peer = ([(ref, i) for ref in part for i in range(ref.shape[0])] for part in parts)
    for i in range(images):
        inner = i % len(own)
        mine = first_ref[0] == i - inner
        (own_ref, k), (peer_ref, _) = own[inner], peer[inner]
        value = jnp.where(mine, own_ref[k], peer_ref[k]).astype(F32)
        wide[i * SEQ : (i + 1) * SEQ, :] = value[:SEQ]
    out_ref[...] = wide[0 : images * SEQ, :].astype(out_ref.dtype)


def unpad(first, own, peer, dtype):
    images, width = 2 * sum(v.shape[0] for v in own), own[0].shape[2]
    return pl.pallas_call(
        functools.partial(unpad_kernel, images=images),
        out_shape=jax.ShapeDtypeStruct((images * SEQ, width), dtype),
        in_specs=[pl.BlockSpec(memory_space=pltpu.SMEM)] + [VMEM] * (2 * len(own)),
        out_specs=VMEM,
        scratch_shapes=[wide_scratch(images, width)],
        compiler_params=params(),
        cost_estimate=cost(2),
        name="unpad",
    )(first, *own, *peer)


def body(tokens, routes, gain_attn, w_qkv, w_attn_out, gain_moe, w_router, w_expert_in, w_expert_out, cotangent, *, ways, groups):
    tok_rows, width = tokens.shape
    experts = w_router.shape[1]
    cap = max(4, (5 * tok_rows // (2 * experts) + 7) // 8 * 8)
    chunks = 2
    half = -(-cap // (ways * chunks))
    block = -(-(half + 2) // 16) * 16
    slots = experts * block
    images = tok_rows // SEQ
    own = images // ways
    rank = lax.axis_index("tensor")
    expert = lax.axis_index("expert")
    first = (rank * own).astype(jnp.int32).reshape(1)
    swap = [(0, 1), (1, 0)]

    def other(v):
        return lax.ppermute(v, "tensor", swap)

    def shards_of(v, axis):
        if ways == 2:
            return [v, other(v)]
        return [lax.all_gather(v, "tensor", axis=axis, tiled=True)]

    def exchange(rows):
        return lax.all_to_all(rows, "expert", split_axis=0, concat_axis=0, tiled=True)

    def after(v, *others):
        return lax.optimization_barrier((v,) + others)[0]

    def rows_of(v):
        return v.reshape(-1, width)

    def collected(number, parts, dtype, probs=False, numbers=None, before=(), rows=PAD):
        return collect(number, code_col, parts, own, dtype, half, block, probs, numbers, before, rows)

    if ways == 2:
        core = expert % 2
        near = [(i, i ^ 1) for i in range(groups)]

        def part_of(v, axis):
            size = v.shape[axis] // 2
            return other(lax.dynamic_slice_in_dim(v, core * size, size, axis))

    else:
        core = 0 * expert
        wq, wo = shards_of(w_qkv, 2), shards_of(w_attn_out, 0)
    cot_pad, cot_slots, code_col, code_row = front(
        rank.astype(jnp.int32).reshape(1), cotangent, routes, experts, cap, half, block, chunks
    )
    tok_pad = pad(after(tokens, cot_pad))
    if ways == 2:
        got_q, got_o = part_of(after(w_qkv, cot_slots), 2), part_of(after(w_attn_out, cot_slots), 0)
        got_q, got_o, tok_pad = lax.optimization_barrier((got_q, got_o, tok_pad))
        wq = [w_qkv, got_q, lax.ppermute(got_q, "expert", near)]
        wo = [w_attn_out, got_o, lax.ppermute(got_o, "expert", near)]
    cot_slots = exchange(cot_slots)
    w1 = shards_of(after(w_expert_in[0], wq[-1], wo[-1]), 1)
    if ways == 2:
        cut = w_expert_out.shape[1] // 4
        w2_first = other(after(w_expert_out[0, :cut], wq[-1], wo[-1]))
        w2_rest = other(after(w_expert_out[0, cut:], wq[-1], wo[-1]))
    place = jnp.stack([rank * own, core]).astype(jnp.int32)
    routed, residual, qkv, probs, att, wq, wo = attend(place, tok_pad, gain_attn, gain_moe, wq, wo, own)
    x_slots = []
    for c in range(chunks):
        rows = spread(code_row, rows_of(routed), experts, block, c)
        if c == 0:
            rows, cot_slots = lax.optimization_barrier((rows, cot_slots))
            if ways == 2:
                rows = after(rows, w1[-1], w2_first)
        elif ways == 2:
            rows = after(rows, w2_rest)
        x_slots.append(exchange(rows))
    if ways == 2:
        w1 = [[v] for v in w1]
        w2 = [[w_expert_out[0]], [w2_first, w2_rest]]
    else:
        w1 = [w1]
        w2 = [shards_of(w_expert_out[0], 0)]
    gin, more = [], None
    expert_number = expert.astype(jnp.int32).reshape(1)
    for c in range(chunks):
        new, *more = experts_step(
            expert_number, rows_of(x_slots[c]), cot_slots, more, c, c == chunks - 1, w_router, w1, w2, half, block
        )
        gin.append(exchange(new.reshape(experts, block, width)))
    gated, *dw = more
    gin = [rows_of(v) for v in gin]
    if ways == 2:
        there = ((1 - rank) * own).astype(jnp.int32).reshape(1)
        dw1_peer = other(dw[1])
        cut = 3 * dw[3].shape[0] // 16
        dw2_peer = [other(dw[3][:cut])]
        zero = jnp.zeros((1,), jnp.int32)
        start = collect(zero, code_col, gin[:1], images, F32, half, block, True, (0,))
        gin[1], *start = lax.optimization_barrier((gin[1], *start))
        sent = collected(there, gin[1:], BF16, True, (1,), start, SENT)
        received = tuple(other(v) for v in sent)
        mine = collected(first, gin[1:], F32, True, (1,), start)
        gated = exchange(after(gated, *sent, dw1_peer, dw2_peer[0]))
        grad_w1 = dw[0] + dw1_peer.astype(F32)
        *received, grad_w1 = lax.optimization_barrier((*received, grad_w1, *mine))[:3]
        sums = [mine, received]
        dw2_peer.append(other(after(dw[3][cut:], *received)))
    else:
        gated = exchange(gated)
        every = [collected(jnp.full((1,), r * own, jnp.int32), gin, F32, True) for r in range(ways)]
        sums = [
            tuple(
                lax.psum_scatter(jnp.stack([v[k] for v in every]).astype(t), "tensor", scatter_dimension=0).astype(F32)
                for k, t in ((0, BF16), (1, F32))
            )
        ]
        grad_w1 = lax.psum_scatter(dw[0].astype(BF16), "tensor", scatter_dimension=1, tiled=True).astype(F32)
        grad_w2 = lax.psum_scatter(dw[1].astype(BF16), "tensor", scatter_dimension=0, tiled=True).astype(F32)
    grad_tok, *pack = back(
        place, sums, residual, cot_pad, tok_pad, qkv, probs, att, gain_attn, gain_moe, w_router, wq, wo,
        2 if ways == 2 else 1, groups * 8,
    )

    bits = [1 << b for b in range(groups.bit_length() - 1)]
    if ways == 2:

        def swap_bit(v, bit):
            return lax.ppermute(v, "expert", [(i, i ^ bit) for i in range(groups)])

        def add(a, b):
            return (a.astype(F32) + b.astype(F32)).astype(BF16)

        def halves(v, bit):
            size = v.shape[-2] // 2
            upper = (expert // bit) % 2
            keep = lax.dynamic_slice_in_dim(v, upper * size, size, v.ndim - 2)
            give = lax.dynamic_slice_in_dim(v, (1 - upper) * size, size, v.ndim - 2)
            return keep, give

        keep, give, grad_tok, gated, dw2_peer[1] = lax.optimization_barrier((*pack, grad_tok, gated, dw2_peer[1]))
        grad_peer = other(grad_tok)
        gated = [rows_of(gated[:, c]) for c in range(chunks)]
        (mix,) = collect(zero, code_col, gated, images, BF16, half, block, rows=SENT)
        mix_there = lax.dynamic_slice_in_dim(mix, (1 - rank) * own, own, 0)
        mix_here = lax.dynamic_slice_in_dim(mix, rank * own, own, 0)
        pack = add(keep, swap_bit(give, bits[0]))
        keep, give = halves(pack, bits[1])
        pack = add(keep, swap_bit(give, bits[1]))
        mix_peer = other(mix_there)
        pack, mix_there, grad_peer = lax.optimization_barrier((pack, mix_there, grad_peer))
        keep, give = halves(pack, bits[2])
        pack = add(keep, swap_bit(give, bits[2]))
        grad_tokens = unpad(first, [grad_tok], [grad_peer], F32)
        keep, give = halves(pack, bits[3])
        pack, grad_w2, mix_here = lax.optimization_barrier(
            (add(keep, swap_bit(give, bits[3])), dw[2] + jnp.concatenate(dw2_peer).astype(F32), mix_here)
        )
        pack, mix_peer, grad_tokens = lax.optimization_barrier((pack, mix_peer, grad_tokens))
        swapped = other(pack[1])
        result = (residual[:, :SENT] + (mix_here.astype(F32) + mix_peer.astype(F32))).astype(BF16)
        swapped, result = lax.optimization_barrier((swapped, result))
        result_peer = other(result)
        total = add(pack[0], swapped)

        def gathered(v, bit):
            got = swap_bit(v, bit)
            upper = (expert // bit) % 2 == 1
            return jnp.where(upper, jnp.concatenate([got, v]), jnp.concatenate([v, got]))

        for bit in bits[3:1:-1]:
            total = gathered(total, bit)
        total = gathered(total, bits[1])
        total, result_peer = lax.optimization_barrier((total, result_peer))
        total = gathered(total, bits[0])
        total = total.astype(F32)
        part = w_qkv.shape[2]
    else:
        gated = [rows_of(gated[:, c]) for c in range(chunks)]
        every = [collected(jnp.full((1,), r * own, jnp.int32), gated, BF16)[0] for r in range(ways)]
        mixture = lax.psum_scatter(jnp.stack(every), "tensor", scatter_dimension=0).astype(F32)

        def whole(v):
            v = lax.all_gather(v, "tensor", axis=0, tiled=True)
            return v[:, :SEQ].reshape(tok_rows, width)

        result = whole((residual + mixture).astype(BF16))
        grad_tokens = whole(grad_tok).astype(F32)
        total = lax.psum(pack[0][0], ("expert", "tensor")).astype(F32)
        part = width

    def take(at, rows, cols):
        blocks = [total[at + b * rows : at + (b + 1) * rows] for b in range(cols // 256)]
        return jnp.concatenate(blocks, axis=1) if len(blocks) > 1 else blocks[0]

    step = width * (part // 256)
    grad_w_qkv = jnp.stack([take(j * step, width, part) for j in range(3)])
    grad_w_attn_out = take(3 * step, part, width)
    small = take(3 * step + part * (width // 256), small_rows(experts), width)
    if ways != 2:
        grad_w_qkv = lax.dynamic_slice_in_dim(grad_w_qkv, rank * w_qkv.shape[2], w_qkv.shape[2], 2)
        grad_w_attn_out = lax.dynamic_slice_in_dim(grad_w_attn_out, rank * w_qkv.shape[2], w_qkv.shape[2], 0)
    sums = (small[experts], grad_w_qkv, grad_w_attn_out, small[experts + 1], small[:experts].T)
    if ways == 2:
        result = unpad(first, [result], [result_peer], BF16)
    return (result, grad_tokens, *sums, grad_w1[None], grad_w2[None])


def solution(mesh):
    placed = (
        P("expert", None),
        P("expert", None),
        P(),
        P(None, None, "tensor"),
        P("tensor", None),
        P(),
        P(),
        P("expert", None, "tensor"),
        P("expert", "tensor", None),
        P("expert", None),
    )
    return jax.shard_map(
        functools.partial(body, ways=mesh.shape["tensor"], groups=mesh.shape["expert"]),
        mesh=mesh,
        in_specs=placed,
        out_specs=(
            P("expert", None),
            P("expert", None),
            P(),
            P(None, None, "tensor"),
            P("tensor", None),
            P(),
            P(),
            P("expert", None, "tensor"),
            P("expert", "tensor", None),
        ),
        check_vma=False,
    )
```

```python
import functools

import jax
import jax.numpy as jnp
from jax import lax
from jax.experimental import pallas as pl
from jax.experimental.pallas import tpu as pltpu
from jax.sharding import PartitionSpec as P

HEAD_DIM = 64
SEQ = 197
PAD = 208
SENT = 200
EPS = 1e-06
F32 = jnp.float32
BF16 = jnp.bfloat16
VMEM = pl.BlockSpec(memory_space=pltpu.VMEM)


def nn(a, b):
    return lax.dot_general(a, b, (((1,), (0,)), ((), ())), preferred_element_type=F32)


def nt(a, b):
    return lax.dot_general(a, b, (((1,), (1,)), ((), ())), preferred_element_type=F32)


def tn(a, b):
    return lax.dot_general(a, b, (((0,), (0,)), ((), ())), preferred_element_type=F32)


def params(mib=56):
    return pltpu.CompilerParams(vmem_limit_bytes=mib << 20)


def cost(us):
    return pl.CostEstimate(flops=0, bytes_accessed=int(us * 3.69e6), transcendentals=0)


def full(shape):
    return pl.BlockSpec(shape, lambda *_: (0,) * len(shape))


def pad_images(source, wide, target):
    wide[0 : source.shape[0], :] = source[...].astype(F32)

    def one_image(i, _):
        off = lax.rem(i * SEQ, 8)
        window = wide[pl.ds(pl.multiple_of(i * SEQ - off, 8), PAD + 8), :]
        window = pltpu.roll(window, lax.rem(PAD + 8 - off, PAD + 8), 0)[:PAD]
        target[i] = jnp.where(iota(window.shape, 0) < SEQ, window, 0.0).astype(BF16)
        return 0

    lax.fori_loop(0, target.shape[0], one_image, 0)


def pad_kernel(source, target, wide):
    pad_images(source, wide, target)


def wide_scratch(images, width):
    return pltpu.VMEM((-(-((images - 1) * SEQ + PAD + 8) // 16) * 16, width), F32)


def pad(rows):
    images, width = rows.shape[0] // SEQ, rows.shape[1]
    return pl.pallas_call(
        pad_kernel,
        out_shape=jax.ShapeDtypeStruct((images, PAD, width), BF16),
        in_specs=[VMEM],
        out_specs=VMEM,
        scratch_shapes=[wide_scratch(images, width)],
        compiler_params=params(),
        cost_estimate=cost(2),
        name="pad",
    )(rows)


def iota(shape, axis):
    return lax.broadcasted_iota(jnp.int32, shape, axis)


def slot_match(code_ref, start, step):
    slot = iota((step, code_ref.shape[1]), 0) + start
    return ((slot == code_ref[0:1, :]) | (slot == code_ref[1:2, :])).astype(BF16)


def front_kernel(rank_ref, cot_ref, col_ref, row_ref, cot_out, slots_out, col_out, row_out, wide, *, cap, half):
    experts, chunks, block, _ = slots_out.shape
    first_slot = rank_ref[0] * (half * chunks)

    def code(expert, position):
        place = position.astype(jnp.int32) - first_slot
        good = (expert >= 0) & (position < cap) & (place >= 0) & (place < half * chunks)
        slot = expert * block + place
        for c in range(1, chunks):
            slot = jnp.where(place >= c * half, slot + (experts * block - half), slot)
        return jnp.where(good, slot, -1)

    lanes = col_ref.shape[0]
    span = lanes * experts
    routes = col_ref[...].astype(F32).T.astype(jnp.int32)
    spread_lanes = (iota((lanes, span), 1) // experts == iota((lanes, span), 0)).astype(BF16)
    gather_lanes = (iota((span, lanes), 0) // experts == iota((span, lanes), 1)).astype(BF16)
    chosen = nn(routes.astype(F32).astype(BF16), spread_lanes) == (iota((PAD, span), 1) % experts).astype(F32)
    ones = chosen.astype(F32)
    lower = (iota((PAD, PAD), 0) > iota((PAD, PAD), 1)).astype(BF16)
    before = nn(lower, ones.astype(BF16))
    totals = jnp.broadcast_to(jnp.sum(ones, axis=0, keepdims=True), (16, span)).astype(BF16)
    source, target = iota((span, span), 0), iota((span, span), 1)
    earlier = (source % experts == target % experts) & (source // experts < target // experts)
    before = before + nn(totals, earlier.astype(BF16))[0:1]
    place = nn((jnp.minimum(before, float(cap)) * ones).astype(BF16), gather_lanes)
    col_out[...] = code(routes, place)

    step = 128
    blocks = row_ref.shape[1] // step
    upper = (iota((step, step), 0) < iota((step, step), 1)).astype(BF16)
    order = [(choice, b) for choice in range(2) for b in range(blocks)]
    picked = [row_ref[choice : choice + 1, b * step : (b + 1) * step] for choice, b in order]
    ones = [(p == iota((experts, step), 0)).astype(F32) for p in picked]
    before = nn(jnp.concatenate(ones, axis=0).astype(BF16), upper)
    base = jnp.zeros((experts, 1), F32)
    for k, (choice, b) in enumerate(order):
        position = jnp.sum((before[k * experts : (k + 1) * experts] + base) * ones[k], axis=0, keepdims=True)
        row_out[choice : choice + 1, b * step : (b + 1) * step] = code(picked[k], position)
        base = base + jnp.sum(ones[k], axis=1, keepdims=True)

    pad_images(cot_ref, wide, cot_out)
    rows = cot_out[...].reshape(-1, cot_out.shape[2])
    step = min(512, experts * block)
    per = step // block
    blocks = experts // per

    def some_slots(k, _):
        value = nn(slot_match(row_out, k * step, step), rows).astype(BF16)
        slots_out[pl.ds(lax.rem(k, blocks) * per, per), lax.div(k, blocks)] = value.reshape(per, block, -1)
        return 0

    lax.fori_loop(0, chunks * blocks, some_slots, 0)


def front(rank, cotangent, routes, experts, cap, half, block, chunks):
    rows, width = cotangent.shape
    images = rows // SEQ
    padded = jnp.pad(
        routes.T.reshape(2, images, SEQ), ((0, 0), (0, 0), (0, PAD - SEQ)), constant_values=-1
    )
    down = padded.reshape(2 * images, PAD)
    across = padded.reshape(2, images * PAD)
    return pl.pallas_call(
        functools.partial(front_kernel, cap=cap, half=half),
        out_shape=(
            jax.ShapeDtypeStruct((images, PAD, width), BF16),
            jax.ShapeDtypeStruct((experts, chunks, block, width), BF16),
            jax.ShapeDtypeStruct(down.shape[::-1], jnp.int32),
            jax.ShapeDtypeStruct(across.shape, jnp.int32),
        ),
        in_specs=[pl.BlockSpec(memory_space=pltpu.SMEM)] + [VMEM] * 3,
        out_specs=(VMEM,) * 4,
        scratch_shapes=[wide_scratch(images, width)],
        compiler_params=params(),
        cost_estimate=cost(10),
        name="front",
    )(rank, cotangent, down, across)


def spread_kernel(code_ref, rows_ref, out_ref, *, start):
    step = out_ref.shape[0] * out_ref.shape[1]
    value = nn(slot_match(code_ref, pl.program_id(0) * step + start, step), rows_ref[...])
    out_ref[...] = value.astype(BF16).reshape(out_ref.shape)


def spread(code_row, rows, experts, block, chunk, step=256):
    count, width = rows.shape
    slots = experts * block
    per = step // block
    return pl.pallas_call(
        functools.partial(spread_kernel, start=chunk * slots),
        out_shape=jax.ShapeDtypeStruct((experts, block, width), BF16),
        grid=(slots // step,),
        in_specs=[full((2, count)), full((count, width))],
        out_specs=pl.BlockSpec((per, block, width), lambda i: (i, 0, 0)),
        compiler_params=params(),
        cost_estimate=cost(5),
        name="spread",
    )(code_row, rows)


def row_mean(v):
    return jnp.mean(v, axis=-1, keepdims=True)


def key_softmax(scores):
    cut = SEQ // 16 * 16
    head, tail = scores[:cut], scores[cut:]
    valid = lax.broadcasted_iota(jnp.int32, tail.shape, 0) < SEQ - cut
    tail = jnp.where(valid, tail, -jnp.inf)
    top = jnp.maximum(jnp.max(head, axis=0, keepdims=True), jnp.max(tail, axis=0, keepdims=True))
    head, tail = jnp.exp(head - top), jnp.exp(tail - top)
    total = jnp.sum(head, axis=0, keepdims=True) + jnp.sum(tail, axis=0, keepdims=True)
    scale = 1.0 / total
    return jnp.concatenate([head * scale, tail * scale], axis=0)


QUAD = 4 * HEAD_DIM


def quad_masks():
    lane = iota((PAD, QUAD), 1)
    return [(lane >= h * HEAD_DIM) & (lane < (h + 1) * HEAD_DIM) for h in range(4)]


def stacked(value, masks):
    return jnp.concatenate([jnp.where(m, value, jnp.zeros_like(value)) for m in masks], axis=0)


def unstacked(value, masks):
    return sum(jnp.where(m, value[h * PAD : (h + 1) * PAD], 0.0) for h, m in enumerate(masks))


def attend_kernel(place_ref, tok_ref, ga_ref, gm_ref, *rest, pieces, own):
    wq, wo, rest = rest[:pieces], rest[pieces : 2 * pieces], rest[2 * pieces :]
    routed_ref, res_ref, qkv_ref, prob_ref, att_ref, wq_all, wo_all, qkv_all, att_all = rest
    batch, _, model = tok_ref.shape
    keep = pl.program_id(0) * batch < own

    @pl.when(pl.program_id(0) == 0)
    def _():
        at = 0
        size = wo[0].shape[0]
        if pieces == 1:
            places = [0]
        else:
            core, small = place_ref[1], wo[1].shape[0]
            places = [0, size + core * small, size + (1 - core) * small]
        for k, start in enumerate(places):
            cols = wo[k].shape[0]
            for j in range(3):
                to = start + j * model
                if k:
                    to = pl.multiple_of(to, 128)
                wq_all[:, pl.ds(to, cols)] = wq[k][j]
            if k:
                start = pl.multiple_of(start, 128)
            wo_all[pl.ds(start, cols), :] = wo[k][...]

    tok = tok_ref[...].reshape(batch * PAD, model).astype(F32)
    center = tok - row_mean(tok)
    normed = (center * lax.rsqrt(row_mean(center * center) + EPS) * ga_ref[...]).astype(BF16)
    value = nn(normed, wq_all[...])
    qkv_all[:, :model] = (value[:, :model] * HEAD_DIM**-0.5).astype(BF16)
    qkv_all[:, model:] = value[:, model:].astype(BF16)
    masks = quad_masks()
    key_ok = iota((4 * PAD, PAD), 1) < SEQ
    for g in range(batch):
        rows = slice(g * PAD, (g + 1) * PAD)
        for quad in range(model // QUAD):
            q, k, v = (qkv_all[rows, j * model + quad * QUAD : j * model + (quad + 1) * QUAD] for j in range(3))
            scores = jnp.where(key_ok, nt(stacked(q, masks), k), -jnp.inf)
            ex = jnp.exp(scores - jnp.max(scores, axis=1, keepdims=True))
            probs = (ex * (1.0 / jnp.sum(ex, axis=1, keepdims=True))).astype(BF16)

            @pl.when(keep)
            def _():
                prob_ref[g, quad] = probs

            mixed = unstacked(nn(probs, v), masks)
            att_all[rows, quad * QUAD : (quad + 1) * QUAD] = mixed.astype(BF16)

    residual = tok + nn(att_all[...], wo_all[...])

    @pl.when(keep)
    def _():
        res_ref[...] = residual.reshape(batch, PAD, model)
        qkv_ref[...] = qkv_all[...].reshape(batch, PAD, 3 * model)
        att_ref[...] = att_all[...].reshape(batch, PAD, model)

    center = residual - row_mean(residual)
    normed = center * lax.rsqrt(row_mean(center * center) + EPS) * gm_ref[...]
    routed_ref[...] = normed.astype(BF16).reshape(batch, PAD, model)


def attend(place, tok_pad, gain_attn, gain_moe, wq, wo, own, batch=2):
    images, _, width = tok_pad.shape
    batch = batch if own % batch == 0 else 1
    pieces = len(wq)
    steps = images // batch

    def image(i, place_ref):
        return (lax.rem(i + place_ref[0] // batch, steps), 0, 0)

    def kept(*shape):
        return pl.BlockSpec(
            (batch,) + shape, lambda i, place_ref: (jnp.minimum(i, own // batch - 1),) + (0,) * len(shape)
        )

    rows = pl.BlockSpec((batch, PAD, width), image)
    probs = (width // QUAD, 4 * PAD, PAD)
    return pl.pallas_call(
        functools.partial(attend_kernel, pieces=pieces, own=own),
        out_shape=(
            jax.ShapeDtypeStruct((images, PAD, width), BF16),
            jax.ShapeDtypeStruct((own, PAD, width), F32),
            jax.ShapeDtypeStruct((own, PAD, 3 * width), BF16),
            jax.ShapeDtypeStruct((own,) + probs, BF16),
            jax.ShapeDtypeStruct((own, PAD, width), BF16),
            jax.ShapeDtypeStruct((width, 3 * width), BF16),
            jax.ShapeDtypeStruct((width, width), BF16),
        ),
        grid_spec=pltpu.PrefetchScalarGridSpec(
            num_scalar_prefetch=1,
            grid=(steps,),
            in_specs=[rows, full((1, width)), full((1, width))] + [full(v.shape) for v in (*wq, *wo)],
            out_specs=(
                rows,
                kept(PAD, width),
                kept(PAD, 3 * width),
                kept(*probs),
                kept(PAD, width),
                full((width, 3 * width)),
                full((width, width)),
            ),
            scratch_shapes=[
                pltpu.VMEM((batch * PAD, 3 * width), BF16),
                pltpu.VMEM((batch * PAD, width), BF16),
            ],
        ),
        compiler_params=params(),
        cost_estimate=cost(25),
        name="attend",
    )(place, tok_pad, gain_attn.reshape(1, -1), gain_moe.reshape(1, -1), *wq, *wo)


def expert_kernel(expert_ref, x_ref, cot_ref, wr_ref, *rest, parts, half, block, chunk, begins, ends):
    weights, rest = rest[: len(parts)], rest[len(parts) :]
    w1, w2, dw1, dw2, out_sum, gin_sum, low1, low2, gates, load_sems, store_sems = rest[-11:]
    shards, _, hidden = w1.shape
    before, rest = ((), rest) if begins else (rest[: 2 * shards], rest[2 * shards + 1 :])
    gin_ref, out_ref = rest[:2]
    given = rest[2 : 2 + 2 * shards]
    expert = expert_ref[0]
    size = min(chunk, hidden)
    blocks = hidden // size

    loads = [(s, ref, (w1, w2)[k].at[s, pl.ds(at, ref.shape[0])]) for (k, s, at), ref in zip(parts, weights)]
    loads += [(k % shards, ref, (dw1, dw2)[k // shards].at[k % shards]) for k, ref in enumerate(before)]
    loads = [(s, pltpu.make_async_copy(a, b, load_sems.at[k])) for k, (s, a, b) in enumerate(loads)]
    for s in range(shards):
        for where, copy in loads:
            if where == s:
                copy.start()

    def stores(s, c):
        cols = pl.ds(pl.multiple_of(c * size, size), size)
        if ends and s:
            sources = low1.at[:, cols], low2.at[cols, :]
        else:
            sources = dw1.at[s, :, cols], dw2.at[s, cols, :]
        targets = given[s].at[:, cols], given[shards + s].at[cols, :]
        return [
            pltpu.make_async_copy(a, b, store_sems.at[(s * blocks + c) * 2 + k])
            for k, (a, b) in enumerate(zip(sources, targets))
        ]

    x = x_ref[...]
    rows, width = x.shape
    cot = cot_ref[...].reshape(rows, width).astype(F32)
    logits = nt(x, wr_ref[...])
    ex = jnp.exp(logits - jnp.max(logits, axis=1, keepdims=True))
    mine = iota(ex.shape, 1) == expert
    gate = jnp.sum(jnp.where(mine, ex, 0.0), axis=1, keepdims=True) / jnp.sum(
        ex, axis=1, keepdims=True
    )
    grad_out = (gate * cot).astype(BF16)
    x_t = x.T
    out_sum[...] = jnp.zeros_like(out_sum)
    gin_sum[...] = jnp.zeros_like(gin_sum)
    c0 = (2.0 / jnp.pi) ** 0.5

    def some_hidden(k, _):
        for s in range(shards):

            @pl.when(k == s * blocks)
            def _():
                for where, copy in loads:
                    if where == s:
                        copy.wait()

        shard, at = lax.div(k, blocks), lax.rem(k, blocks)
        cols = pl.ds(pl.multiple_of(at * size, size), size)
        u = nn(x, w1[shard, :, cols])
        square = u * u
        t = jnp.tanh(u * (c0 + (c0 * 0.044715) * square))
        h = 0.5 + 0.5 * t
        slope = h + (0.5 * u) * (1.0 - t * t) * (c0 + (3 * c0 * 0.044715) * square)
        active = (u * h).astype(BF16)
        out_sum[...] += nn(active, w2[shard, cols, :])
        grad_pre = (nt(grad_out, w2[shard, cols, :]) * slope).astype(BF16)
        gin_sum[...] += nt(grad_pre, w1[shard, :, cols])
        first, second = nn(x_t, grad_pre), tn(active, grad_out)
        dw1[shard, :, cols] = first if begins else dw1[shard, :, cols] + first
        dw2[shard, cols, :] = second if begins else dw2[shard, cols, :] + second
        for s in range(shards):

            @pl.when(shard == s)
            def _():
                if ends and s:
                    low1[:, cols] = dw1[shard, :, cols].astype(BF16)
                    low2[cols, :] = dw2[shard, cols, :].astype(BF16)
                for copy in stores(s, at):
                    copy.start()

        return 0

    lax.fori_loop(0, shards * blocks, some_hidden, 0)
    down, across = iota((block, width), 0), iota((block, width), 1)
    gates[...] = jnp.broadcast_to(gate, gates.shape)
    group = min(2, rows // block)

    def some_groups(i, _):
        at = pl.multiple_of(i * group * block, group * block)
        span = pl.ds(at, group * block)
        out = out_sum[span, :]
        out_ref[pl.ds(i * group, group), 0] = (gates[span, 0:1] * out).astype(BF16).reshape(group, block, width)
        cot = cot_ref[pl.ds(i * group, group), 0].reshape(group * block, width).astype(F32)
        gate_grad = jnp.sum(cot * out, axis=1, keepdims=True)
        for g in range(group):
            rows_of_one = pl.ds(at + g * block, block)
            line = jnp.where(down == across, gate_grad[g * block : (g + 1) * block], 0.0)
            line = jnp.sum(line, axis=0, keepdims=True)
            high = line.astype(BF16).astype(F32)
            value = jnp.where(down == half + 1, line - high, gin_sum[rows_of_one, :])
            gin_ref[rows_of_one, :] = jnp.where(down == half, high, value).astype(BF16)
        return 0

    lax.fori_loop(0, rows // (group * block), some_groups, 0)
    for s in range(shards):
        for c in range(blocks):
            for copy in stores(s, c):
                copy.wait()


def experts_step(expert, x, cot, before, number, ends, w_router, w1, w2, half, block, chunk=512):
    rows, width = x.shape
    shards = len(w1)
    hidden = w1[0][0].shape[1]
    row_spec = full((rows, width))
    chunk_spec = pl.BlockSpec((rows // block, 1, block, width), lambda i, _: (0, number, 0, 0))
    anywhere = pl.BlockSpec(memory_space=pl.ANY)
    old = [] if before is None else [*before[1:], before[0]]
    parts, weights = [], []
    for k, shards_of_one in enumerate((w1, w2)):
        for s, pieces in enumerate(shards_of_one):
            at = 0
            for piece in pieces:
                parts.append((k, s, at))
                weights.append(piece)
                at += piece.shape[0]
    shapes = [(width, hidden)] * shards + [(hidden, width)] * shards
    low = (8, 128) if shards == 1 or not ends else None
    at = 4 + len(weights)
    alias = {at + 2 * shards: 1} if old else {}
    return pl.pallas_call(
        functools.partial(
            expert_kernel,
            parts=parts,
            half=half,
            block=block,
            chunk=chunk,
            begins=before is None,
            ends=ends,
        ),
        out_shape=(jax.ShapeDtypeStruct((rows, width), BF16), jax.ShapeDtypeStruct(cot.shape, BF16))
        + tuple(
            jax.ShapeDtypeStruct(v, BF16 if ends and k % shards else F32) for k, v in enumerate(shapes)
        ),
        grid_spec=pltpu.PrefetchScalarGridSpec(
            num_scalar_prefetch=1,
            grid=(1,),
            in_specs=[row_spec, chunk_spec, full(w_router.shape[::-1])] + [anywhere] * (len(weights) + len(old)),
            out_specs=(row_spec, chunk_spec) + (anywhere,) * len(shapes),
            scratch_shapes=[
                pltpu.VMEM((shards, width, hidden), BF16),
                pltpu.VMEM((shards, hidden, width), BF16),
                pltpu.VMEM((shards, width, hidden), F32),
                pltpu.VMEM((shards, hidden, width), F32),
                pltpu.VMEM((rows, width), F32),
                pltpu.VMEM((rows, width), F32),
                pltpu.VMEM(low or (width, hidden), BF16),
                pltpu.VMEM(low or (hidden, width), BF16),
                pltpu.VMEM((rows, 128), F32),
                pltpu.SemaphoreType.DMA((len(weights) + 2 * shards,)),
                pltpu.SemaphoreType.DMA((2 * shards * hidden // min(chunk, hidden),)),
            ],
        ),
        input_output_aliases=alias,
        compiler_params=params(62),
        cost_estimate=cost(20),
        name="experts",
    )(expert, x, cot, w_router.T, *weights, *old)


def collect_kernel(first_ref, code_ref, *rest, numbers, half, block, probs, before):
    chunks = len(numbers)
    parts, rest = rest[:chunks], rest[chunks:]
    old, rest = rest[:before], rest[before:]
    out_ref, rest = rest[0], rest[1:]
    count, width = parts[0].shape
    experts = count // block
    rows = PAD
    codes = code_ref[...]
    across = iota(codes.shape, 1)
    at = first_ref[0] + pl.program_id(0)
    images = codes.shape[1] // 2
    columns = [
        jnp.sum(jnp.where(across == at + c * images, codes, 0), axis=1, keepdims=True) for c in range(2)
    ]
    lane = iota((rows, count), 1)
    total = old[0][0] if old else None
    grads = None
    for c in range(chunks):
        shift = numbers[c] * count
        match = ((lane + shift == columns[0]) | (lane + shift == columns[1])).astype(BF16)
        value = nn(match, parts[c][...])
        total = value if total is None else total + value
        if probs:
            slot_grads = rest[1 + c]

            @pl.when(pl.program_id(0) == 0)
            def _():
                lines = jnp.zeros((experts, 128), F32)
                for e in range(experts):
                    tail = parts[c][e * block + block - 16 : (e + 1) * block, 0:128].astype(F32)
                    here = half - (block - 16)
                    line = tail[here : here + 1] + tail[here + 1 : here + 2]
                    lines = jnp.where(iota(lines.shape, 0) == e, line, lines)
                turned = lines.T[:block]
                high = turned.astype(BF16).astype(F32)
                both = jnp.concatenate([high, turned - high], axis=1)
                for e in range(experts):
                    own_lane = iota(both.shape, 1) % experts == e
                    slot_grads[e * block : (e + 1) * block, :] = jnp.where(own_lane, both, 0.0).astype(BF16)

            value = nn(match, slot_grads[...])
            grads = value if grads is None else grads + value
    out_ref[0] = total[: out_ref.shape[1]].astype(out_ref.dtype)
    if probs:
        turned = grads.T
        value = turned[:experts] + turned[experts:]
        value = value + old[1][0] if old else value
        rest[0][0] = value.astype(rest[0].dtype)


def collect(first, code_col, parts, own, dtype, half, block, probs=False, numbers=None, before=(), rows=PAD):
    numbers = tuple(range(len(parts))) if numbers is None else numbers
    count, width = parts[0].shape
    outs = [jax.ShapeDtypeStruct((own, rows, width), dtype)]
    if probs:
        outs.append(jax.ShapeDtypeStruct((own, count // block, PAD), dtype))
    return pl.pallas_call(
        functools.partial(
            collect_kernel, numbers=numbers, half=half, block=block, probs=probs, before=len(before)
        ),
        out_shape=tuple(outs),
        grid_spec=pltpu.PrefetchScalarGridSpec(
            num_scalar_prefetch=1,
            grid=(own,),
            in_specs=[full(code_col.shape)]
            + [full((count, width))] * len(parts)
            + [pl.BlockSpec((1,) + v.shape[1:], lambda i, f: (i + f[0], 0, 0)) for v in before],
            out_specs=tuple(pl.BlockSpec((1,) + v.shape[1:], lambda i, f: (i, 0, 0)) for v in outs),
            scratch_shapes=[pltpu.VMEM((count, 2 * (count // block)), BF16)] * (len(parts) if probs else 0),
        ),
        compiler_params=params(),
        cost_estimate=cost(7),
        name="collect",
    )(first, code_col, *parts, *before)


def back_kernel(place_ref, *rest, steps, received, split):
    (sum_ref, gp_ref), rest = rest[:2], rest[2:]
    more, rest = rest[: 2 * received], rest[2 * received :]
    (res_ref, cot_ref, tok_ref, ga_ref, gm_ref, wrt_ref, wq, wo, qkv_ref, prob_ref, att_ref), rest = rest[:11], rest[11:]
    gtok_ref, packs, rest = rest[0], rest[1 : 2 + split], rest[2 + split :]
    dwq, dwo, small, gatt_all, dqkv_all, wq_here, qkv_here, prob_here, pack_ref, sems = rest
    experts = wrt_ref.shape[0]
    batch, _, model = res_ref.shape
    rows = batch * PAD
    step = pl.program_id(0)

    def loads(number):
        span = pl.ds(number * batch, batch)
        pairs = [(v.at[span], w.at[span]) for v, w in ((qkv_ref, qkv_here), (prob_ref, prob_here))]
        return [pltpu.make_async_copy(a, b, sems.at[number, k]) for k, (a, b) in enumerate(pairs)]

    weights = pltpu.make_async_copy(wq, wq_here, sems.at[0, 2])

    @pl.when(step == 0)
    def _():
        for copy in loads(0) + [weights]:
            copy.start()
        for number in range(1, steps):
            for copy in loads(number):
                copy.start()
        for ref in (dwq, dwo, small):
            ref[...] = jnp.zeros_like(ref)

    def flat(ref):
        return ref[...].reshape(rows, -1).astype(F32)

    residual = flat(res_ref)
    center = residual - row_mean(residual)
    scale = lax.rsqrt(row_mean(center * center) + EPS)
    xhat = center * scale
    gm = gm_ref[...]
    routed = (xhat * gm).astype(BF16)
    logits = nt(wrt_ref[...], routed)
    ex = jnp.exp(logits - jnp.max(logits, axis=0, keepdims=True))
    probs = ex / jnp.sum(ex, axis=0, keepdims=True)
    grad_probs = gp_ref[...]
    grad_routed = flat(sum_ref)
    if received:
        tail = jnp.zeros((PAD - more[0].shape[1], model), F32)
        both = [v for b in range(batch) for v in (more[0][b].astype(F32), tail)]
        grad_routed = grad_routed + jnp.concatenate(both, axis=0)
        grad_probs = grad_probs + more[1][...].astype(F32)
    grad_probs = jnp.concatenate([grad_probs[g] for g in range(batch)], axis=1)
    grad_logits = probs * (grad_probs - jnp.sum(probs * grad_probs, axis=0, keepdims=True))
    high = grad_logits.astype(BF16)
    low = (grad_logits - high.astype(F32)).astype(BF16)
    both = jnp.concatenate([high, low], axis=0)
    new = nn(both, routed)
    small[0:experts, :] += new[:experts] + new[experts:]
    grad_routed = grad_routed + tn(both, jnp.concatenate([wrt_ref[...]] * 2, axis=0))
    small[experts + 1 : experts + 2, :] += jnp.sum(grad_routed * xhat, axis=0, keepdims=True)
    g = grad_routed * gm
    grad_res = flat(cot_ref) + scale * (g - row_mean(g) - xhat * row_mean(g * xhat))
    grad_mixed = grad_res.astype(BF16)
    dwo[...] += tn(att_ref[...].reshape(rows, model), grad_mixed)
    gatt_all[...] = nt(grad_mixed, wo[...]).astype(BF16)

    masks = quad_masks()
    for number in range(steps):

        @pl.when(step == number)
        def _():
            for copy in loads(number):
                copy.wait()

    for b in range(batch):
        span = slice(b * PAD, (b + 1) * PAD)
        image = step * batch + b
        for quad in range(model // QUAD):
            q, k, v = (
                qkv_here[image, :, j * model + quad * QUAD : j * model + (quad + 1) * QUAD] for j in range(3)
            )
            grad_heads = stacked(gatt_all[span, quad * QUAD : (quad + 1) * QUAD], masks)
            low_probs = prob_here[image, quad]
            p = low_probs.astype(F32)
            gw = nt(grad_heads, v)
            ds = (p * (gw - jnp.sum(p * gw, axis=1, keepdims=True))).astype(BF16)
            grad_q = unstacked(nn(ds, k), masks) * HEAD_DIM**-0.5
            grad_k = tn(ds, stacked(q, masks))
            grad_v = tn(low_probs, grad_heads)
            for j, value in enumerate((grad_q, grad_k, grad_v)):
                dqkv_all[span, j * model + quad * QUAD : j * model + (quad + 1) * QUAD] = value.astype(BF16)

    tok = flat(tok_ref)
    center = tok - row_mean(tok)
    tok_scale = lax.rsqrt(row_mean(center * center) + EPS)
    xin = center * tok_scale
    ga = ga_ref[...]
    normed = (xin * ga).astype(BF16)
    dwq[...] += tn(normed, dqkv_all[...])

    @pl.when(step == 0)
    def _():
        weights.wait()

    grad_normed = nt(dqkv_all[...], wq_here[...])
    small[experts : experts + 1, :] += jnp.sum(grad_normed * xin, axis=0, keepdims=True)
    h = grad_normed * ga
    grad_tok = grad_res + tok_scale * (h - row_mean(h) - xin * row_mean(h * xin))
    for b in range(batch):
        gtok_ref[b] = grad_tok[b * PAD : b * PAD + gtok_ref.shape[1]].astype(BF16)

    @pl.when(step == steps - 1)
    def _():
        shards = pack_ref.shape[0]
        part = model // shards
        for s in range(shards):
            at = 0
            blocks = [dwq[:, j * model + s * part : j * model + (s + 1) * part] for j in range(3)]
            for value in blocks + [dwo[s * part : (s + 1) * part, :], small[...]]:
                for c in range(value.shape[1] // 256):
                    pack_ref[s, at : at + value.shape[0], :] = value[:, c * 256 : (c + 1) * 256].astype(BF16)
                    at += value.shape[0]
            if at < pack_ref.shape[1]:
                pack_ref[s, at:, :] = jnp.zeros((pack_ref.shape[1] - at, 256), BF16)
        if split:
            size = packs[0].shape[1]
            at = pl.multiple_of(place_ref[1] * size, size)
            packs[0][...] = pack_ref[:, pl.ds(at, size), :]
            packs[1][...] = pack_ref[:, pl.ds(pl.multiple_of(size - at, size), size), :]
        else:
            packs[0][...] = pack_ref[...]


def small_rows(experts):
    return -(-(experts + 2) // 16) * 16


def pack_rows(width, part, experts, align):
    rows = 3 * width * (part // 256) + part * (width // 256) + small_rows(experts) * (width // 256)
    return -(-rows // align) * align


def back(place, sums, residual, cot_pad, tok_pad, qkv, probs, att, gain_attn, gain_moe, w_router, wq, wo, shards, align, batch=2):
    own, _, width = residual.shape
    batch = batch if own % batch == 0 else 1
    experts = w_router.shape[1]
    rows = pack_rows(width, width // shards, experts, align)
    split = int(shards == 2)

    def mine(*shape):
        return pl.BlockSpec((batch,) + shape, lambda i, f: (i,) + (0,) * len(shape))

    image = pl.BlockSpec((batch, PAD, width), lambda i, f: (i + f[0] // batch, 0, 0))
    flat = [v for pair in sums for v in pair]
    return pl.pallas_call(
        functools.partial(back_kernel, steps=own // batch, received=len(sums) - 1, split=split),
        out_shape=(jax.ShapeDtypeStruct((own, SENT, width), BF16),)
        + (jax.ShapeDtypeStruct((shards, rows // (1 + split), 256), BF16),) * (1 + split),
        grid_spec=pltpu.PrefetchScalarGridSpec(
            num_scalar_prefetch=1,
            grid=(own // batch,),
            in_specs=[mine(*v.shape[1:]) for v in flat]
            + [
                mine(PAD, width),
                image,
                image,
                full((1, width)),
                full((1, width)),
                full((experts, width)),
                pl.BlockSpec(memory_space=pl.ANY),
                full(wo.shape),
                pl.BlockSpec(memory_space=pl.ANY),
                pl.BlockSpec(memory_space=pl.ANY),
                mine(*att.shape[1:]),
            ],
            out_specs=(mine(SENT, width),) + (full((shards, rows // (1 + split), 256)),) * (1 + split),
            scratch_shapes=[
                pltpu.VMEM((width, 3 * width), F32),
                pltpu.VMEM((width, width), F32),
                pltpu.VMEM((small_rows(experts), width), F32),
                pltpu.VMEM((batch * PAD, width), BF16),
                pltpu.VMEM((batch * PAD, 3 * width), BF16),
                pltpu.VMEM(wq.shape, BF16),
                pltpu.VMEM(qkv.shape, BF16),
                pltpu.VMEM(probs.shape, BF16),
                pltpu.VMEM((shards, rows, 256), BF16),
                pltpu.SemaphoreType.DMA((own // batch, 3)),
            ],
        ),
        compiler_params=params(),
        cost_estimate=cost(16),
        name="back",
    )(
        place,
        *flat,
        residual,
        cot_pad,
        tok_pad,
        gain_attn.reshape(1, -1),
        gain_moe.reshape(1, -1),
        w_router.T,
        wq,
        wo,
        qkv,
        probs,
        att,
    )


def unpad_kernel(first_ref, *refs, images):
    out_ref, wide = refs[-2:]
    pieces = len(refs) // 2 - 1
    parts = refs[:pieces], refs[pieces:-2]
    own, peer = ([(ref, i) for ref in part for i in range(ref.shape[0])] for part in parts)
    for i in range(images):
        inner = i % len(own)
        mine = first_ref[0] == i - inner
        (own_ref, k), (peer_ref, _) = own[inner], peer[inner]
        value = jnp.where(mine, own_ref[k], peer_ref[k]).astype(F32)
        wide[i * SEQ : (i + 1) * SEQ, :] = value[:SEQ]
    out_ref[...] = wide[0 : images * SEQ, :].astype(out_ref.dtype)


def unpad(first, own, peer, dtype):
    images, width = 2 * sum(v.shape[0] for v in own), own[0].shape[2]
    return pl.pallas_call(
        functools.partial(unpad_kernel, images=images),
        out_shape=jax.ShapeDtypeStruct((images * SEQ, width), dtype),
        in_specs=[pl.BlockSpec(memory_space=pltpu.SMEM)] + [VMEM] * (2 * len(own)),
        out_specs=VMEM,
        scratch_shapes=[wide_scratch(images, width)],
        compiler_params=params(),
        cost_estimate=cost(2),
        name="unpad",
    )(first, *own, *peer)


def body(tokens, routes, gain_attn, w_qkv, w_attn_out, gain_moe, w_router, w_expert_in, w_expert_out, cotangent, *, ways, groups):
    tok_rows, width = tokens.shape
    experts = w_router.shape[1]
    cap = max(4, (5 * tok_rows // (2 * experts) + 7) // 8 * 8)
    chunks = 2
    half = -(-cap // (ways * chunks))
    block = -(-(half + 2) // 16) * 16
    slots = experts * block
    images = tok_rows // SEQ
    own = images // ways
    rank = lax.axis_index("tensor")
    expert = lax.axis_index("expert")
    first = (rank * own).astype(jnp.int32).reshape(1)
    swap = [(0, 1), (1, 0)]

    def other(v):
        return lax.ppermute(v, "tensor", swap)

    def shards_of(v, axis):
        if ways == 2:
            return [v, other(v)]
        return [lax.all_gather(v, "tensor", axis=axis, tiled=True)]

    def exchange(rows):
        return lax.all_to_all(rows, "expert", split_axis=0, concat_axis=0, tiled=True)

    def after(v, *others):
        return lax.optimization_barrier((v,) + others)[0]

    def rows_of(v):
        return v.reshape(-1, width)

    def collected(number, parts, dtype, probs=False, numbers=None, before=(), rows=PAD):
        return collect(number, code_col, parts, own, dtype, half, block, probs, numbers, before, rows)

    if ways == 2:
        core = expert % 2
        near = [(i, i ^ 1) for i in range(groups)]

        def part_of(v, axis):
            size = v.shape[axis] // 2
            return other(lax.dynamic_slice_in_dim(v, core * size, size, axis))

    else:
        core = 0 * expert
        wq, wo = shards_of(w_qkv, 2), shards_of(w_attn_out, 0)
    cot_pad, cot_slots, code_col, code_row = front(
        rank.astype(jnp.int32).reshape(1), cotangent, routes, experts, cap, half, block, chunks
    )
    tok_pad = pad(after(tokens, cot_pad))
    if ways == 2:
        got_q, got_o = part_of(after(w_qkv, cot_slots), 2), part_of(after(w_attn_out, cot_slots), 0)
        got_q, got_o, tok_pad = lax.optimization_barrier((got_q, got_o, tok_pad))
        wq = [w_qkv, got_q, lax.ppermute(got_q, "expert", near)]
        wo = [w_attn_out, got_o, lax.ppermute(got_o, "expert", near)]
    cot_slots = exchange(cot_slots)
    w1 = shards_of(after(w_expert_in[0], wq[-1], wo[-1]), 1)
    if ways == 2:
        cut = 3 * w_expert_out.shape[1] // 16
        w2_first = other(after(w_expert_out[0, :cut], wq[-1], wo[-1]))
        w2_rest = other(after(w_expert_out[0, cut:], wq[-1], wo[-1]))
    place = jnp.stack([rank * own, core]).astype(jnp.int32)
    routed, residual, qkv, probs, att, wq, wo = attend(place, tok_pad, gain_attn, gain_moe, wq, wo, own)
    x_slots = []
    for c in range(chunks):
        rows = spread(code_row, rows_of(routed), experts, block, c)
        if c == 0:
            rows, cot_slots = lax.optimization_barrier((rows, cot_slots))
            if ways == 2:
                rows = after(rows, w1[-1], w2_first)
        elif ways == 2:
            rows = after(rows, w2_rest)
        x_slots.append(exchange(rows))
    if ways == 2:
        w1 = [[v] for v in w1]
        w2 = [[w_expert_out[0]], [w2_first, w2_rest]]
    else:
        w1 = [w1]
        w2 = [shards_of(w_expert_out[0], 0)]
    gin, more = [], None
    expert_number = expert.astype(jnp.int32).reshape(1)
    for c in range(chunks):
        new, *more = experts_step(
            expert_number, rows_of(x_slots[c]), cot_slots, more, c, c == chunks - 1, w_router, w1, w2, half, block
        )
        gin.append(exchange(new.reshape(experts, block, width)))
    gated, *dw = more
    gin = [rows_of(v) for v in gin]
    if ways == 2:
        there = ((1 - rank) * own).astype(jnp.int32).reshape(1)
        dw1_peer = other(dw[1])
        cut = 3 * dw[3].shape[0] // 16
        dw2_peer = [other(dw[3][:cut])]
        zero = jnp.zeros((1,), jnp.int32)
        start = collect(zero, code_col, gin[:1], images, F32, half, block, True, (0,))
        gin[1], *start = lax.optimization_barrier((gin[1], *start))
        sent = collected(there, gin[1:], BF16, True, (1,), start, SENT)
        received = tuple(other(v) for v in sent)
        mine = collected(first, gin[1:], F32, True, (1,), start)
        gated = exchange(after(gated, *sent, dw1_peer, dw2_peer[0]))
        grad_w1 = dw[0] + dw1_peer.astype(F32)
        *received, grad_w1 = lax.optimization_barrier((*received, grad_w1, *mine))[:3]
        sums = [mine, received]
        dw2_peer.append(other(after(dw[3][cut:], *received)))
    else:
        gated = exchange(gated)
        every = [collected(jnp.full((1,), r * own, jnp.int32), gin, F32, True) for r in range(ways)]
        sums = [
            tuple(
                lax.psum_scatter(jnp.stack([v[k] for v in every]).astype(t), "tensor", scatter_dimension=0).astype(F32)
                for k, t in ((0, BF16), (1, F32))
            )
        ]
        grad_w1 = lax.psum_scatter(dw[0].astype(BF16), "tensor", scatter_dimension=1, tiled=True).astype(F32)
        grad_w2 = lax.psum_scatter(dw[1].astype(BF16), "tensor", scatter_dimension=0, tiled=True).astype(F32)
    grad_tok, *pack = back(
        place, sums, residual, cot_pad, tok_pad, qkv, probs, att, gain_attn, gain_moe, w_router, wq, wo,
        2 if ways == 2 else 1, groups * 8,
    )

    bits = [1 << b for b in range(groups.bit_length() - 1)]
    if ways == 2:

        def swap_bit(v, bit):
            return lax.ppermute(v, "expert", [(i, i ^ bit) for i in range(groups)])

        def add(a, b):
            return (a.astype(F32) + b.astype(F32)).astype(BF16)

        def halves(v, bit):
            size = v.shape[-2] // 2
            upper = (expert // bit) % 2
            keep = lax.dynamic_slice_in_dim(v, upper * size, size, v.ndim - 2)
            give = lax.dynamic_slice_in_dim(v, (1 - upper) * size, size, v.ndim - 2)
            return keep, give

        keep, give, grad_tok, gated, dw2_peer[1] = lax.optimization_barrier((*pack, grad_tok, gated, dw2_peer[1]))
        grad_peer = other(grad_tok)
        gated = [rows_of(gated[:, c]) for c in range(chunks)]
        (mix,) = collect(zero, code_col, gated, images, BF16, half, block, rows=SENT)
        mix_there = lax.dynamic_slice_in_dim(mix, (1 - rank) * own, own, 0)
        mix_here = lax.dynamic_slice_in_dim(mix, rank * own, own, 0)
        pack = add(keep, swap_bit(give, bits[0]))
        keep, give = halves(pack, bits[1])
        pack = add(keep, swap_bit(give, bits[1]))
        mix_peer = other(mix_there)
        pack, mix_there, grad_peer = lax.optimization_barrier((pack, mix_there, grad_peer))
        keep, give = halves(pack, bits[2])
        pack = add(keep, swap_bit(give, bits[2]))
        grad_tokens = unpad(first, [grad_tok], [grad_peer], F32)
        keep, give = halves(pack, bits[3])
        pack, grad_w2, mix_here = lax.optimization_barrier(
            (add(keep, swap_bit(give, bits[3])), dw[2] + jnp.concatenate(dw2_peer).astype(F32), mix_here)
        )
        pack, mix_peer, grad_tokens = lax.optimization_barrier((pack, mix_peer, grad_tokens))
        swapped = other(pack[1])
        result = (residual[:, :SENT] + (mix_here.astype(F32) + mix_peer.astype(F32))).astype(BF16)
        swapped, result = lax.optimization_barrier((swapped, result))
        result_peer = other(result)
        total = add(pack[0], swapped)

        def gathered(v, bit):
            got = swap_bit(v, bit)
            upper = (expert // bit) % 2 == 1
            return jnp.where(upper, jnp.concatenate([got, v]), jnp.concatenate([v, got]))

        for bit in bits[3:1:-1]:
            total = gathered(total, bit)
        total = gathered(total, bits[1])
        total, result_peer = lax.optimization_barrier((total, result_peer))
        total = gathered(total, bits[0])
        total = total.astype(F32)
        part = w_qkv.shape[2]
    else:
        gated = [rows_of(gated[:, c]) for c in range(chunks)]
        every = [collected(jnp.full((1,), r * own, jnp.int32), gated, BF16)[0] for r in range(ways)]
        mixture = lax.psum_scatter(jnp.stack(every), "tensor", scatter_dimension=0).astype(F32)

        def whole(v):
            v = lax.all_gather(v, "tensor", axis=0, tiled=True)
            return v[:, :SEQ].reshape(tok_rows, width)

        result = whole((residual + mixture).astype(BF16))
        grad_tokens = whole(grad_tok).astype(F32)
        total = lax.psum(pack[0][0], ("expert", "tensor")).astype(F32)
        part = width

    def take(at, rows, cols):
        blocks = [total[at + b * rows : at + (b + 1) * rows] for b in range(cols // 256)]
        return jnp.concatenate(blocks, axis=1) if len(blocks) > 1 else blocks[0]

    step = width * (part // 256)
    grad_w_qkv = jnp.stack([take(j * step, width, part) for j in range(3)])
    grad_w_attn_out = take(3 * step, part, width)
    small = take(3 * step + part * (width // 256), small_rows(experts), width)
    if ways != 2:
        grad_w_qkv = lax.dynamic_slice_in_dim(grad_w_qkv, rank * w_qkv.shape[2], w_qkv.shape[2], 2)
        grad_w_attn_out = lax.dynamic_slice_in_dim(grad_w_attn_out, rank * w_qkv.shape[2], w_qkv.shape[2], 0)
    sums = (small[experts], grad_w_qkv, grad_w_attn_out, small[experts + 1], small[:experts].T)
    if ways == 2:
        result = unpad(first, [result], [result_peer], BF16)
    return (result, grad_tokens, *sums, grad_w1[None], grad_w2[None])


def solution(mesh):
    placed = (
        P("expert", None),
        P("expert", None),
        P(),
        P(None, None, "tensor"),
        P("tensor", None),
        P(),
        P(),
        P("expert", None, "tensor"),
        P("expert", "tensor", None),
        P("expert", None),
    )
    return jax.shard_map(
        functools.partial(body, ways=mesh.shape["tensor"], groups=mesh.shape["expert"]),
        mesh=mesh,
        in_specs=placed,
        out_specs=(
            P("expert", None),
            P("expert", None),
            P(),
            P(None, None, "tensor"),
            P("tensor", None),
            P(),
            P(),
            P("expert", None, "tensor"),
            P("expert", "tensor", None),
        ),
        check_vma=False,
    )
```
